32 devices in a mesh: section: 2 (over core), dp: 8 (over z, x), seq: 2 (over y).
Axes of the slice: x: 2, y: 2, z: 4, core: 2. Of those that a mesh axis runs over, the one named last changes fastest.
Arguments:
- inputs: bfloat16 [2, 16, 256, 384], P(None, 'dp', 'seq'), may hold values from -6 to 6
- cotangent: bfloat16 [2, 16, 256, 384], P(None, 'dp', 'seq'), may hold values from -6 to 6
- time_ids: int32 [2, 16], replicated, may hold values from 0 to 999
- row_counts: int32 [2, 8], P(None, 'dp'), may hold values from 1 to 2, as said below
- cond_table: bfloat16 [1000, 384], replicated, may hold values from -6 to 6
- modulation_weight: bfloat16 [2, 384, 2304], P('section', ('dp', 'seq')), may hold values from -0.3125 to 0.3125
- attention_weight: bfloat16 [2, 384, 1152], P('section', ('dp', 'seq')), may hold values from -0.3125 to 0.3125
- output_weight: bfloat16 [2, 384, 384], P('section', ('dp', 'seq')), may hold values from -1.25 to 1.25
- expand_weight: bfloat16 [2, 384, 1536], P('section', ('dp', 'seq')), may hold values from -0.3125 to 0.3125
- shrink_weight: bfloat16 [2, 1536, 384], P('section', ('dp', 'seq')), may hold values from -0.15625 to 0.15625
- biases: bfloat16 [2, 5376], P('section', ('dp', 'seq')), may hold values from -1.5 to 1.5
Outputs:
- activations: bfloat16 [2, 2, 16, 256, 384], P('section', None, 'dp', 'seq')
- input_grads: float32 [2, 2, 16, 256, 384], P('section', None, 'dp', 'seq')
- table_grad: float32 [1000, 384], replicated
- modulation_grad: float32 [2, 384, 2304], P('section', ('dp', 'seq'))
- attention_grad: float32 [2, 384, 1152], P('section', ('dp', 'seq'))
- output_grad: float32 [2, 384, 384], P('section', ('dp', 'seq'))
- expand_grad: float32 [2, 384, 1536], P('section', ('dp', 'seq'))
- shrink_grad: float32 [2, 1536, 384], P('section', ('dp', 'seq'))
- biases_grad: float32 [2, 5376], P('section', ('dp', 'seq'))
The draws below stay inside these ranges and needn't reach their ends.
Inputs may be any that keep to these rules, and one draw needn't show every extreme that they name: `row_counts`: entry [m, r] is how many latents data row r holds in micro-batch m: its slots r * 2 to r * 2 + entry - 1 are live, the others are padding. In every micro-batch some row holds 2.
All inputs are finite; a program needn't handle non-finite values.
Results may differ from the reference program's by a relative error of at most 0.018.
The reference program's roundings to bfloat16 on the way count: a program that leaves them out, or rounds other values in their place, can miss the bound.
Values may be sent and summed in bfloat16 or wider, within the bound.
No kernel may reach another device: no remote copies, remote signals or barrier semaphores. Data moves between devices by JAX's collectives and lax.ppermute only.
A program may use at most 128 MiB of HBM per device.

```python
import math
import jax
import jax.numpy as jnp
from jax import lax

D = 384
HEADS = 6
HEAD = 64
FF = 1536
STEPS = 1000
MICRO = 2
SLOT_CAP = 2
LENGTH = 256
SLOTS = 16
N_DP = 8


def draw_row_counts(key, part):
    key = jax.random.fold_in(key, 7)
    count_key, fuller_key = jax.random.split(key)
    counts = jax.random.randint(count_key, (MICRO, N_DP), 1, SLOT_CAP + 1)
    fullest = jax.random.randint(fuller_key, (MICRO, 1), 0, N_DP)
    columns = jnp.arange(N_DP, dtype=jnp.int32)[None, :]
    return jnp.where(columns == fullest, SLOT_CAP, counts).astype(jnp.int32)


def plant(array, key, low, top_value):
    longest = array.shape.index(max(array.shape))
    spots = []
    for shift in (0, 1):
        where = [jax.random.randint(jax.random.fold_in(key, axis), (), 0, length) for axis, length in enumerate(array.shape)]
        where[longest] = (where[longest] + shift) % array.shape[longest]
        spots.append(tuple(where))
    return array.at[spots[0]].set(low).at[spots[1]].set(top_value)


def level_of(rng, extent, cuts, low, high):
    factor_of = 1.0
    for axis_at, blocks in cuts:
        draws = jax.random.uniform(jax.random.fold_in(jax.random.fold_in(rng, 6), axis_at), (blocks,), jnp.float32, low / len(cuts), high / len(cuts))
        factor_of = factor_of * jnp.repeat(jnp.exp(draws), extent[axis_at] // blocks).reshape((-1,) + (1,) * (len(extent) - 1 - axis_at))
    return factor_of


def gaussian(rng, extent, deviation, most, cuts=(), kind=jnp.bfloat16):
    gain = level_of(rng, extent, cuts, -0.22, 0.18) if cuts else 1.0
    drawn = jax.random.normal(rng, extent, jnp.float32) * deviation * gain
    return jnp.minimum(jnp.maximum(drawn, -most), most).astype(kind)


def setup_inputs(seed: int = 0) -> dict:
    arg_keys = jax.random.split(jax.random.key(seed), 12)
    inputs = gaussian(arg_keys[0], (MICRO, SLOTS, LENGTH, D), 1.0, 6.0, ((1, 8), (2, 2)))
    cotangent = gaussian(arg_keys[1], (MICRO, SLOTS, LENGTH, D), 1.0, 6.0, ((1, 8), (2, 2)))
    time_ids = plant(jax.random.randint(arg_keys[2], (MICRO, SLOTS), 0, STEPS), jax.random.fold_in(arg_keys[2], 1), 0, STEPS - 1).astype(jnp.int32)
    row_counts = draw_row_counts(jax.random.fold_in(arg_keys[11], 71), 0)
    cond_table = gaussian(arg_keys[4], (STEPS, D), 1.0, 6.0)
    modulation_weight = gaussian(arg_keys[5], (2, D, 6 * D), D ** -0.5, 0.3125, ((0, 2), (1, 16)))
    attention_weight = gaussian(arg_keys[6], (2, D, 3 * D), D ** -0.5, 0.3125, ((0, 2), (1, 16)))
    output_weight = gaussian(arg_keys[7], (2, D, D), (D // 16) ** -0.5, 1.25, ((0, 2), (1, 16)))
    expand_weight = gaussian(arg_keys[8], (2, D, FF), D ** -0.5, 0.3125, ((0, 2), (1, 16)))
    shrink_weight = gaussian(arg_keys[9], (2, FF, D), FF ** -0.5, 0.15625, ((0, 2), (1, 16)))
    biases = gaussian(arg_keys[10], (2, 10 * D + FF), 0.3, 1.5, ((0, 2), (1, 16)))
    return {"inputs": inputs, "cotangent": cotangent, "time_ids": time_ids, "row_counts": row_counts, "cond_table": cond_table, "modulation_weight": modulation_weight, "attention_weight": attention_weight, "output_weight": output_weight, "expand_weight": expand_weight, "shrink_weight": shrink_weight, "biases": biases}


@jax.custom_vjp
def low(v):
    return lax.optimization_barrier(v.astype(jnp.bfloat16)).astype(jnp.float32)

@jax.custom_vjp
def low_back(v):
    return v

def low_keep(v):
    return (low(v), None)

def low_pass(kept, grad):
    return (grad,)

def back_keep(v):
    return (v, None)

def back_low(kept, grad):
    return (low(grad),)
low.defvjp(low_keep, low_pass)
low_back.defvjp(back_keep, back_low)
epsilon = 1e-06

def dense(former, latter):
    return jnp.dot(former, latter, precision=lax.Precision.HIGHEST)

def normalize(values):
    centre = lax.optimization_barrier(jnp.mean(values, axis=-1, keepdims=True))
    centred = values - centre
    spread = lax.optimization_barrier(jnp.mean(centred * centred, axis=-1, keepdims=True))
    return centred * lax.rsqrt(spread + epsilon)

def modulation_parts(modulation):
    return [member[:, None, :] for member in jnp.split(modulation, 6, axis=-1)]

def layer_forward(inputs, silu_cond, params):
    modulation_matrix, attention_matrix, output_matrix, expand_matrix, shrink_matrix, bias_values = params
    model_width = inputs.shape[-1]
    hidden_width = expand_matrix.shape[1]
    boundaries = [6 * model_width, 7 * model_width, 8 * model_width, 9 * model_width, 9 * model_width + hidden_width]
    bias_ada, bias_query, bias_value, bias_output, bias_expand, bias_shrink = jnp.split(bias_values, boundaries)
    modulation = low_back(dense(silu_cond, modulation_matrix) + bias_ada)
    members = modulation_parts(modulation)
    hidden_one = low(normalize(inputs) * (1.0 + members[1]) + members[0])
    projected = dense(hidden_one, attention_matrix)
    query_rows = low(low_back(projected[..., :model_width] + bias_query))
    key_rows = low(low_back(projected[..., model_width:2 * model_width]))
    value_rows = low(low_back(projected[..., 2 * model_width:] + bias_value))
    latents, length = (inputs.shape[0], inputs.shape[1])
    head_query = query_rows.reshape(latents, length, HEADS, HEAD)
    head_key = key_rows.reshape(latents, length, HEADS, HEAD)
    head_value = value_rows.reshape(latents, length, HEADS, HEAD)
    scores = low_back(jnp.einsum('blhe,bmhe->bhlm', head_query, head_key, precision=lax.Precision.HIGHEST) * HEAD ** (-0.5))
    highest = lax.optimization_barrier(jnp.max(scores, axis=-1, keepdims=True))
    log_total = highest + jnp.log(lax.optimization_barrier(jnp.sum(jnp.exp(scores - highest), axis=-1, keepdims=True)))
    soft_weights = low(jnp.exp(scores - log_total))
    attended = jnp.einsum('bhlm,bmhe->blhe', soft_weights, head_value, precision=lax.Precision.HIGHEST)
    attended = low(low_back(attended.reshape(latents, length, model_width)))
    attention_branch = low_back(dense(attended, output_matrix) + bias_output)
    middle = inputs + members[2] * attention_branch
    hidden_two = low(normalize(middle) * (1.0 + members[4]) + members[3])
    expanded = low_back(dense(hidden_two, expand_matrix) + bias_expand)
    activated = low(jax.nn.gelu(expanded, approximate=True))
    branch = low_back(dense(activated, shrink_matrix) + bias_shrink)
    return middle + members[5] * branch

def two_sections(block_inputs, block_ids, block_hook, table_values, params_first, params_second):
    conditions = jnp.take(table_values, block_ids, axis=0)
    silu_cond = low(jax.nn.silu(conditions))
    first_out = layer_forward(block_inputs, silu_cond, params_first)
    second_input = low(low_back(first_out)) + block_hook
    second_out = layer_forward(second_input, silu_cond, params_second)
    return (second_out, first_out)

def reference(inputs, cotangent, time_ids, row_counts, cond_table, modulation_weight, attention_weight, output_weight, expand_weight, shrink_weight, biases):
    batches, slot_count, length, model_width = inputs.shape
    row_count = row_counts.shape[1]
    capacity = slot_count // row_count
    slot_index = jnp.arange(slot_count, dtype=jnp.int32)
    live_mask = ((slot_index % capacity)[None, :] < jnp.take(row_counts, slot_index // capacity, axis=1)).astype(jnp.float32)
    latent_count = batches * slot_count
    group_size = math.gcd(latent_count, max(1, 4096 // length))
    blocks = latent_count // group_size
    flat_inputs = inputs.astype(jnp.float32).reshape(blocks, group_size, length, model_width)
    flat_ids = time_ids.reshape(blocks, group_size).astype(jnp.int32)
    flat_cotangent = (cotangent.astype(jnp.float32) * live_mask[:, :, None, None]).reshape(blocks, group_size, length, model_width)
    section_hook = jnp.zeros_like(flat_inputs)
    table_values = cond_table.astype(jnp.float32)
    matrices = (modulation_weight, attention_weight, output_weight, expand_weight, shrink_weight, biases)
    params_first = tuple((matrix[0].astype(jnp.float32) for matrix in matrices))
    params_second = tuple((matrix[1].astype(jnp.float32) for matrix in matrices))

    def run_all(inputs_all, table_all, hook_all, first_params, second_params):

        def block_step(carried, pieces):
            second_out, first_out = jax.checkpoint(two_sections)(pieces[0], pieces[1], pieces[2], table_all, first_params, second_params)
            return (carried, (second_out, first_out))
        _, (seconds, firsts) = lax.scan(block_step, jnp.zeros((), jnp.float32), (inputs_all, flat_ids, hook_all))
        return (seconds, firsts)
    seconds, pullback, firsts = jax.vjp(run_all, flat_inputs, table_values, section_hook, params_first, params_second, has_aux=True)
    grad_inputs, grad_table, grad_hook, grads_first, grads_second = pullback(flat_cotangent)
    full_shape = (batches, slot_count, length, model_width)
    activations = (jnp.stack([firsts.reshape(full_shape), seconds.reshape(full_shape)]) * live_mask[None, :, :, None, None]).astype(jnp.bfloat16)
    input_grads = jnp.stack([grad_inputs.reshape(full_shape), grad_hook.reshape(full_shape)])
    stacked = [jnp.stack([grads_first[member_index], grads_second[member_index]]) for member_index in range(6)]
    return (activations, input_grads, grad_table, stacked[0], stacked[1], stacked[2], stacked[3], stacked[4], stacked[5])
```

```python
from functools import partial

import jax
import jax.numpy as jnp
from jax import lax
from jax.sharding import PartitionSpec as P

HEADS = 6
HEAD = 64
SCALE = HEAD ** (-0.5)
epsilon = 1e-06
RING = ("dp", "seq")


def normalize_rows(values):
    centre = jnp.mean(values, axis=-1, keepdims=True)
    centred = values - centre
    spread = jnp.mean(centred * centred, axis=-1, keepdims=True)
    factor = lax.rsqrt(spread + epsilon)
    return (centred * factor, factor)


def normalize_back(normed, factor, grad_normed):
    mean_grad = jnp.mean(grad_normed, axis=-1, keepdims=True)
    mean_cross = jnp.mean(grad_normed * normed, axis=-1, keepdims=True)
    return factor * (grad_normed - mean_grad - normed * mean_cross)


def matmul(former, latter):
    return jnp.dot(former, latter, preferred_element_type=jnp.float32)


def matmul_transposed(former, latter):
    return lax.dot_general(
        former, latter, (((1,), (1,)), ((), ())), preferred_element_type=jnp.float32
    )


def outer_sum(former, latter):
    return lax.dot_general(
        former, latter, (((0,), (0,)), ((), ())), preferred_element_type=jnp.float32
    )


def split_heads(tensor):
    return tensor.reshape(tensor.shape[0], HEADS, HEAD)


def forward(inputs_wide, members, weights):
    attention_matrix, output_matrix, expand_matrix, shrink_matrix, biases = weights
    width = inputs_wide.shape[-1]
    shift_one, scale_one, gate_one, shift_two, scale_two, gate_two = members
    normed_one, _ = normalize_rows(inputs_wide)
    hidden_one = (normed_one * (1.0 + scale_one) + shift_one).astype(jnp.bfloat16)
    projected = matmul(hidden_one, attention_matrix)
    queries = (projected[:, :width] + biases[1]).astype(jnp.bfloat16)
    keys = projected[:, width : 2 * width].astype(jnp.bfloat16)
    values = (projected[:, 2 * width :] + biases[2]).astype(jnp.bfloat16)
    scores = (
        jnp.einsum(
            "the,lhe->htl",
            split_heads(queries),
            split_heads(keys),
            preferred_element_type=jnp.float32,
        )
        * SCALE
    )
    highest = jnp.max(scores, axis=-1, keepdims=True)
    log_total = highest + jnp.log(jnp.sum(jnp.exp(scores - highest), axis=-1, keepdims=True))
    soft = jnp.exp(scores - log_total).astype(jnp.bfloat16)
    attended = jnp.einsum(
        "htl,lhe->the", soft, split_heads(values), preferred_element_type=jnp.float32
    )
    attended = attended.reshape(inputs_wide.shape).astype(jnp.bfloat16)
    branch_one = matmul(attended, output_matrix) + biases[3]
    middle = inputs_wide + gate_one * branch_one
    normed_two, _ = normalize_rows(middle)
    hidden_two = (normed_two * (1.0 + scale_two) + shift_two).astype(jnp.bfloat16)
    expanded = matmul(hidden_two, expand_matrix) + biases[4]
    activated = jax.nn.gelu(expanded, approximate=True).astype(jnp.bfloat16)
    branch_two = matmul(activated, shrink_matrix) + biases[5]
    result = middle + gate_two * branch_two
    kept = (queries, keys, values, log_total, attended, branch_one, expanded, branch_two)
    return result, kept


def backward(grad_out, inputs_wide, members, weights, kept):
    attention_matrix, output_matrix, expand_matrix, shrink_matrix, _ = weights
    queries, keys, values, log_total, attended, branch_one, expanded, branch_two = kept
    shift_one, scale_one, gate_one, shift_two, scale_two, gate_two = members
    shape = inputs_wide.shape
    normed_one, factor_one = normalize_rows(inputs_wide)
    hidden_one = (normed_one * (1.0 + scale_one) + shift_one).astype(jnp.bfloat16)
    middle = inputs_wide + gate_one * branch_one
    normed_two, factor_two = normalize_rows(middle)
    hidden_two = (normed_two * (1.0 + scale_two) + shift_two).astype(jnp.bfloat16)
    grad_branch = (gate_two * grad_out).astype(jnp.bfloat16)
    gate_two_grad = jnp.sum(grad_out * branch_two, axis=0)
    grad_activated = matmul_transposed(grad_branch, shrink_matrix)
    activated, gelu_back = jax.vjp(partial(jax.nn.gelu, approximate=True), expanded)
    activated = activated.astype(jnp.bfloat16)
    grad_expanded = gelu_back(grad_activated)[0].astype(jnp.bfloat16)
    grad_hidden_two = matmul_transposed(grad_expanded, expand_matrix)
    shift_two_grad = jnp.sum(grad_hidden_two, axis=0)
    scale_two_grad = jnp.sum(grad_hidden_two * normed_two, axis=0)
    grad_middle = grad_out + normalize_back(
        normed_two, factor_two, grad_hidden_two * (1.0 + scale_two)
    )
    gate_one_grad = jnp.sum(grad_middle * branch_one, axis=0)
    grad_attention = (gate_one * grad_middle).astype(jnp.bfloat16)
    grad_attended = matmul_transposed(grad_attention, output_matrix).astype(jnp.bfloat16)
    scores = (
        jnp.einsum(
            "the,lhe->htl",
            split_heads(queries),
            split_heads(keys),
            preferred_element_type=jnp.float32,
        )
        * SCALE
    )
    soft_exact = jnp.exp(scores - log_total)
    grad_soft = jnp.einsum(
        "the,lhe->htl",
        split_heads(grad_attended),
        split_heads(values),
        preferred_element_type=jnp.float32,
    )
    inner = jnp.sum(grad_soft * soft_exact, axis=-1, keepdims=True)
    grad_scores = (soft_exact * (grad_soft - inner)).astype(jnp.bfloat16)
    grad_queries = (
        jnp.einsum(
            "htl,lhe->the", grad_scores, split_heads(keys), preferred_element_type=jnp.float32
        )
        * SCALE
    )
    grad_keys = (
        jnp.einsum(
            "htl,the->lhe", grad_scores, split_heads(queries), preferred_element_type=jnp.float32
        )
        * SCALE
    )
    grad_values = jnp.einsum(
        "htl,the->lhe",
        soft_exact.astype(jnp.bfloat16),
        split_heads(grad_attended),
        preferred_element_type=jnp.float32,
    )
    grad_projected = jnp.concatenate(
        [
            member.reshape(shape).astype(jnp.bfloat16)
            for member in (grad_queries, grad_keys, grad_values)
        ],
        axis=-1,
    )
    grad_hidden_one = matmul_transposed(grad_projected, attention_matrix)
    shift_one_grad = jnp.sum(grad_hidden_one, axis=0)
    scale_one_grad = jnp.sum(grad_hidden_one * normed_one, axis=0)
    grad_inputs = grad_middle + normalize_back(
        normed_one, factor_one, grad_hidden_one * (1.0 + scale_one)
    )
    grad_modulation = jnp.concatenate(
        [
            shift_one_grad,
            scale_one_grad,
            gate_one_grad,
            shift_two_grad,
            scale_two_grad,
            gate_two_grad,
        ]
    ).astype(jnp.bfloat16)
    width = shape[1]
    column_sums = [
        jnp.sum(member, axis=0, dtype=jnp.float32)
        for member in (
            grad_projected[:, :width],
            grad_projected[:, 2 * width :],
            grad_attention,
            grad_expanded,
            grad_branch,
        )
    ]
    matrix_grads = (
        outer_sum(hidden_one, grad_projected),
        outer_sum(attended, grad_attention),
        outer_sum(hidden_two, grad_expanded),
        outer_sum(activated, grad_branch),
    )
    return grad_inputs, grad_modulation, jnp.concatenate(column_sums), matrix_grads


def pair_swap(block, axis):
    return lax.ppermute(block, axis, [(0, 1), (1, 0)])


def ring_exchange(block, size, step):
    route = [(i, step(i)) for i in range(size)]
    return lax.ppermute(block, RING, route)


def scatter_sum(block, rank, size):
    half = block.shape[-1] // 2
    pieces = [block[..., :half], block[..., half:]]
    left = size
    low_bits = 0
    while left > 4:
        orders = [(0, 1), (1, 0)] if left % 4 == 0 and left >= 16 else [(0,), (0,)]
        for turn in range(len(orders[0])):
            updated = []
            for piece, order in zip(pieces, orders):
                bit = low_bits + order[turn]
                mine = (rank >> bit) & 1
                if len(order) == 2 and turn == 0:
                    shaped = piece.reshape(-1, 2, 2, *piece.shape[1:])
                    at = 2 - order[turn]
                else:
                    shaped = piece.reshape(-1, 2, *piece.shape[1:])
                    at = 1
                keep = lax.dynamic_index_in_dim(shaped, mine, at, keepdims=False)
                send = lax.dynamic_index_in_dim(shaped, 1 - mine, at, keepdims=False)
                got = ring_exchange(send, size, lambda i, bit=bit: i ^ (1 << bit))
                total = (keep.astype(jnp.float32) + got.astype(jnp.float32)).astype(jnp.bfloat16)
                updated.append(total.reshape(-1, *piece.shape[1:]))
            pieces = updated
        low_bits += len(orders[0])
        left //= 2 ** len(orders[0])
    block = jnp.concatenate(pieces, axis=-1)
    high = rank >> low_bits
    total = lax.dynamic_index_in_dim(block, high, 0, keepdims=False).astype(jnp.float32)
    stride = 1 << low_bits
    for turn in range(1, left):
        send = lax.dynamic_index_in_dim(block, (high + turn) % left, 0, keepdims=False)
        got = ring_exchange(send, size, lambda i, turn=turn: (i + turn * stride) % size)
        total = total + got.astype(jnp.float32)
    return total


def per_device(
    inputs,
    cotangent,
    time_ids,
    row_counts,
    cond_table,
    modulation_weight,
    attention_weight,
    output_weight,
    expand_weight,
    shrink_weight,
    biases,
):
    section_rank = lax.axis_index("section")
    data_rank = lax.axis_index("dp")
    seq_rank = lax.axis_index("seq")
    sections = lax.axis_size("section")
    seq_size = lax.axis_size("seq")
    ring_size = lax.axis_size("dp") * seq_size
    ring_rank = data_rank * seq_size + seq_rank
    batches, slots, tokens, width = inputs.shape
    assert batches == sections == 2 and seq_size % slots == 0
    sharers = seq_size // slots
    slot = seq_rank // sharers
    length = tokens * seq_size
    rows = attention_weight.shape[1]
    ratio = shrink_weight.shape[1] // rows
    hidden = ratio * width
    bias_columns = biases.shape[1] // rows
    table_rows = cond_table.shape[0]

    packed = jnp.concatenate(
        [
            attention_weight[0],
            output_weight[0],
            expand_weight[0],
            shrink_weight[0].reshape(rows, ratio, width).reshape(rows, ratio * width),
            modulation_weight[0],
            jnp.pad(biases.reshape(rows, bias_columns), ((0, 0), (0, 128 - bias_columns))),
        ],
        axis=1,
    )
    own_pack = lax.all_gather(packed, RING, axis=0, tiled=True)
    other_pack = pair_swap(own_pack, "section")

    def unpack(pack):
        edges = [0, 3 * width, 4 * width, 4 * width + hidden, 4 * width + 2 * hidden]
        att, out, up, down = [pack[:, a:b] for a, b in zip(edges[:-1], edges[1:])]
        down = down.reshape(hidden, width)
        modulation_matrix = pack[:, edges[-1] : edges[-1] + 6 * width]
        bias = pack[:, edges[-1] + 6 * width :][:, :bias_columns].reshape(-1).astype(jnp.float32)
        cuts = [6 * width, 7 * width, 8 * width, 9 * width, 9 * width + hidden]
        return modulation_matrix, (att, out, up, down, jnp.split(bias, cuts))

    is_first = section_rank == 0
    first_mod, first_weights = unpack(jnp.where(is_first, own_pack, other_pack))
    second_mod, second_weights = unpack(jnp.where(is_first, other_pack, own_pack))

    both = jnp.stack(
        [
            lax.dynamic_index_in_dim(inputs, section_rank, 0, keepdims=False),
            lax.dynamic_index_in_dim(cotangent, section_rank, 0, keepdims=False),
        ],
        axis=1,
    )
    both = jnp.repeat(both, sharers, axis=0)
    both = lax.all_to_all(both, "seq", 0, 0, tiled=True)
    both = jnp.swapaxes(both, 0, 1).reshape(2, length, width)
    live = (
        slot < lax.dynamic_index_in_dim(row_counts, section_rank, 0, keepdims=False)[0]
    ).astype(jnp.float32)
    flat_ids = time_ids.reshape(-1)
    selector = (
        flat_ids[:, None] == jnp.arange(table_rows, dtype=jnp.int32)[None, :]
    ).astype(jnp.bfloat16)
    conditions = matmul(selector, cond_table)
    silu_all = jax.nn.silu(conditions).astype(jnp.bfloat16)
    latent = section_rank * time_ids.shape[1] + data_rank * slots + slot
    condition = lax.dynamic_slice_in_dim(conditions, latent, 1, 0)
    silu_now = lax.dynamic_slice_in_dim(silu_all, latent, 1, 0)

    def members_of(modulation_matrix, weights):
        return jnp.split(matmul(silu_now, modulation_matrix) + weights[4][0], 6, axis=-1)

    first_input = both[0].astype(jnp.float32)
    first_members = members_of(first_mod, first_weights)
    second_members = members_of(second_mod, second_weights)
    first_out, first_kept = forward(first_input, first_members, first_weights)
    first_low = first_out.astype(jnp.bfloat16)
    second_input = first_low.astype(jnp.float32)
    second_out, second_kept = forward(second_input, second_members, second_weights)
    second_grad, second_dmod, second_sums, second_terms = backward(
        both[1].astype(jnp.float32) * live,
        second_input,
        second_members,
        second_weights,
        second_kept,
    )
    second_grad_low = second_grad.astype(jnp.bfloat16)
    first_grad, first_dmod, first_sums, first_terms = backward(
        second_grad_low.astype(jnp.float32),
        first_input,
        first_members,
        first_weights,
        first_kept,
    )

    def to_owners(first, second):
        pieces = jnp.stack([first, second]).reshape(2 * seq_size, tokens, width)
        pieces = lax.all_to_all(pieces, ("section", "seq"), 0, 0, tiled=True)
        return pieces.reshape(batches, slots, sharers, tokens, width)[:, :, 0]

    live_low = live.astype(jnp.bfloat16)
    activations = to_owners(first_low * live_low, second_out.astype(jnp.bfloat16) * live_low)
    input_grads = to_owners(first_grad.astype(jnp.bfloat16), second_grad_low).astype(jnp.float32)

    def pack_terms(terms):
        att, out, up, down = [term * (1.0 / sharers) for term in terms]
        down = down.reshape(width, ratio * width)
        whole = jnp.concatenate([att, out, up, down], axis=1).astype(jnp.bfloat16)
        half = whole.shape[1] // 2
        return jnp.stack([whole[:, :half], whole[:, half:]])

    halves = jnp.stack([pack_terms(first_terms), pack_terms(second_terms)], axis=1)
    keep = lax.dynamic_index_in_dim(halves, section_rank, 0, keepdims=False)
    send = lax.dynamic_index_in_dim(halves, 1 - section_rank, 0, keepdims=False)
    chip_sum = (
        keep.astype(jnp.float32) + pair_swap(send, "section").astype(jnp.float32)
    ).astype(jnp.bfloat16)
    half = chip_sum.shape[-1]
    ring_terms = jnp.swapaxes(chip_sum.reshape(2, ring_size, rows, half), 0, 1)
    owned = scatter_sum(ring_terms.reshape(ring_size, 2 * rows, half), ring_rank, ring_size)
    owned = owned.reshape(2, rows, half)
    mine = lax.dynamic_index_in_dim(owned, section_rank, 0, keepdims=False)
    theirs = pair_swap(
        lax.dynamic_index_in_dim(owned, 1 - section_rank, 0, keepdims=False), "section"
    )
    full = jnp.where(
        is_first,
        jnp.concatenate([mine, theirs], axis=1),
        jnp.concatenate([theirs, mine], axis=1),
    )
    edges = [0, 3 * width, 4 * width, 4 * width + hidden, 4 * width + 2 * hidden]
    att, out, up, down = [full[:, a:b] for a, b in zip(edges[:-1], edges[1:])]
    down = down.reshape(rows * ratio, width)

    _, silu_back = jax.vjp(jax.nn.silu, condition)
    grad_condition = silu_back(
        matmul_transposed(first_dmod[None], first_mod)
        + matmul_transposed(second_dmod[None], second_mod)
    )[0][0]
    row = jnp.concatenate(
        [
            first_dmod.astype(jnp.float32),
            first_sums,
            second_dmod.astype(jnp.float32),
            second_sums,
            grad_condition,
        ]
    )
    every = lax.all_gather(row[None], ("section", "dp", "seq"), axis=0, tiled=True)
    every = every[::sharers]
    per_section = every[:, : 2 * bias_columns * width].reshape(every.shape[0], 2, -1)
    section_rows = lax.dynamic_index_in_dim(per_section, section_rank, 1, keepdims=False)
    bias_total = jnp.sum(section_rows, axis=0)
    bias_grad = lax.dynamic_slice_in_dim(
        bias_total, ring_rank * biases.shape[1], biases.shape[1], 0
    )
    silu_own = lax.dynamic_slice_in_dim(silu_all, ring_rank * rows, rows, 1)
    modulation_grad = outer_sum(silu_own, section_rows[:, : 6 * width].astype(jnp.bfloat16))
    table_grad = lax.dot_general(
        selector.astype(jnp.float32),
        every[:, 2 * bias_columns * width :],
        (((0,), (0,)), ((), ())),
        precision=lax.Precision.HIGHEST,
        preferred_element_type=jnp.float32,
    )
    return (
        activations[None],
        input_grads[None],
        table_grad,
        modulation_grad[None],
        att[None],
        out[None],
        up[None],
        down[None],
        bias_grad[None],
    )


def solution(mesh):
    shard = P("section", ("dp", "seq"), None)
    in_specs = (
        P(None, "dp", "seq", None),
        P(None, "dp", "seq", None),
        P(),
        P(None, "dp"),
        P(),
        shard,
        shard,
        shard,
        shard,
        shard,
        P("section", ("dp", "seq")),
    )
    out_specs = (
        P("section", None, "dp", "seq", None),
        P("section", None, "dp", "seq", None),
        P(),
        shard,
        shard,
        shard,
        shard,
        shard,
        P("section", ("dp", "seq")),
    )
    return jax.shard_map(
        per_device, mesh=mesh, in_specs=in_specs, out_specs=out_specs, check_vma=False
    )
```

```python
from functools import partial

import jax
import jax.numpy as jnp
from jax import lax
from jax.experimental import pallas as pl
from jax.experimental.pallas import tpu as pltpu
from jax.sharding import PartitionSpec as P

HEADS = 6
HEAD = 64
SCALE = HEAD ** (-0.5)
epsilon = 1e-06
RING = ("dp", "seq")
INNER = (2.0 / 3.141592653589793) ** 0.5
CUBE = 0.044715


def matmul(former, latter):
    return jnp.dot(former, latter, preferred_element_type=jnp.float32)


def matmul_transposed(former, latter):
    return lax.dot_general(
        former, latter, (((1,), (1,)), ((), ())), preferred_element_type=jnp.float32
    )


def outer_sum(former, latter):
    return lax.dot_general(
        former, latter, (((0,), (0,)), ((), ())), preferred_element_type=jnp.float32
    )


def low(values):
    return values.astype(jnp.bfloat16)


def normalize_rows(values):
    centre = jnp.mean(values, axis=-1, keepdims=True)
    centred = values - centre
    spread = jnp.mean(centred * centred, axis=-1, keepdims=True)
    factor = lax.rsqrt(spread + epsilon)
    return (centred * factor, factor)


def normalize_back(normed, factor, grad_normed):
    mean_grad = jnp.mean(grad_normed, axis=-1, keepdims=True)
    mean_cross = jnp.mean(grad_normed * normed, axis=-1, keepdims=True)
    return factor * (grad_normed - mean_grad - normed * mean_cross)


def column_sum(values):
    return jnp.sum(values.astype(jnp.float32), axis=0, keepdims=True)


def section_kernel(layout, backward, *refs):
    width, hidden, rows, ratio, ring_size, share, bias_count = layout
    own_ref, x_ref, silu_ref = refs[:3]
    refs = refs[3:]
    if backward:
        dy_ref = refs[0]
        refs = refs[1:]
    pack_refs = refs[:2]
    refs = refs[2:]
    if backward:
        y_ref, dx_ref, row_ref, keep_ref, send_ref = refs[:5]
        refs = refs[5:]
    else:
        y_ref = refs[0]
        refs = refs[1:]
    mod_w, att_w, out_w, up_w, down_p, bias_p, sems = refs[:7]
    bias_s, down_w, down_s, block_s, qkv_s, att_s, u_s = refs[7:14]
    if backward:
        soft_s, slope_s, da_s, dqkv_s, halves, out_sems = refs[14:]

    own = own_ref[0] == 1
    held = (att_w, out_w, up_w, mod_w, down_p, bias_p)
    sizes = (3 * width, width, hidden, 6 * width, hidden, 128)
    starts = [sum(sizes[:i]) for i in range(len(sizes))]

    def fetches(source):
        return [
            pltpu.make_async_copy(
                pack_refs[source].at[:, start : start + size], target, sems.at[i]
            )
            for i, (target, start, size) in enumerate(zip(held, starts, sizes))
        ]

    @pl.when(own)
    def _():
        for copy in fetches(0):
            copy.start()

    @pl.when(jnp.logical_not(own))
    def _():
        for copy in fetches(1):
            copy.start()

    arrivals = fetches(0)

    def bias(a, b):
        return bias_s[:, a:b]

    x = x_ref[...].astype(jnp.float32)
    normed_one, factor_one = normalize_rows(x)
    arrivals[5].wait()
    bias_rows = bias_p[...].astype(jnp.float32)
    for d in range(ring_size):
        for i in range(0, bias_count, 128):
            wide = min(128, bias_count - i)
            start = d * bias_count + i
            row = d * rows + i // 128
            bias_s[:, start : start + wide] = bias_rows[row : row + 1, :wide]
    arrivals[3].wait()
    modulation = matmul(silu_ref[...], mod_w[...])[0:1, :] + bias(0, 6 * width)
    shift_one, scale_one, gate_one, shift_two, scale_two, gate_two = [
        modulation[:, i * width : (i + 1) * width] for i in range(6)
    ]
    hidden_one = low(normed_one * (1.0 + scale_one) + shift_one)
    at = 6 * width
    arrivals[0].wait()
    qkv_s[:, :width] = low(matmul(hidden_one, att_w[:, :width]) + bias(at, at + width))
    qkv_s[:, width : 2 * width] = low(matmul(hidden_one, att_w[:, width : 2 * width]))
    qkv_s[:, 2 * width :] = low(
        matmul(hidden_one, att_w[:, 2 * width :]) + bias(at + width, at + 2 * width)
    )

    def part(ref, member, head):
        start = member * width + head * HEAD
        return ref[:, start : start + HEAD]

    for head in range(HEADS):
        scores = matmul_transposed(part(qkv_s, 0, head), part(qkv_s, 1, head)) * SCALE
        raised = jnp.exp(scores - jnp.max(scores, axis=-1, keepdims=True))
        soft = raised * (1.0 / jnp.sum(raised, axis=-1, keepdims=True))
        if backward:
            soft_s[head] = soft
        attended = matmul(low(soft), part(qkv_s, 2, head))
        att_s[:, head * HEAD : (head + 1) * HEAD] = low(attended)
    arrivals[1].wait()
    branch_one = matmul(att_s[...], out_w[...]) + bias(at + 2 * width, at + 3 * width)
    middle = x + gate_one * branch_one
    normed_two, factor_two = normalize_rows(middle)
    hidden_two = low(normed_two * (1.0 + scale_two) + shift_two)
    arrivals[2].wait()
    at += 3 * width
    for j in range(ratio):
        cut = slice(j * width, (j + 1) * width)
        a = matmul(hidden_two, up_w[:, cut]) + bias(at + j * width, at + (j + 1) * width)
        square = a * a
        turn = jnp.tanh(INNER * (a + CUBE * (a * square)))
        half_one = 0.5 * (1.0 + turn)
        u_s[:, cut] = low(a * half_one)
        if backward:
            slope_s[:, cut] = half_one + (0.5 * INNER) * a * (1.0 - turn * turn) * (
                1.0 + (3.0 * CUBE) * square
            )
    arrivals[4].wait()
    block_s[...] = down_p[...].astype(jnp.float32)
    for d in range(ring_size):
        for j in range(ratio):
            down_s[(d * ratio + j) * rows : (d * ratio + j + 1) * rows, :] = block_s[
                d * rows : (d + 1) * rows, j * width : (j + 1) * width
            ]
    down_w[...] = low(down_s[...])
    branch_two = matmul(u_s[...], down_w[...]) + bias(at + hidden, at + hidden + width)
    y_ref[...] = low(middle + gate_two * branch_two)
    if not backward:
        return

    grad_out = dy_ref[...].astype(jnp.float32)
    grad_branch = low(gate_two * grad_out)
    sums_at = 6 * width
    row_ref[:, 5 * width : 6 * width] = column_sum(grad_out * branch_two)
    row_ref[:, sums_at + 3 * width + hidden : sums_at + 4 * width + hidden] = column_sum(
        grad_branch
    )
    for j in range(ratio):
        cut = slice(j * width, (j + 1) * width)
        grad_expanded = low(slope_s[:, cut] * matmul_transposed(grad_branch, down_w[cut, :]))
        da_s[:, cut] = grad_expanded
        row_ref[:, sums_at + (3 + j) * width : sums_at + (4 + j) * width] = column_sum(
            grad_expanded
        )
    split = (4 * width + 2 * hidden) // 2 - 4 * width
    up_first = low(outer_sum(hidden_two, da_s[:, :split]) * share)
    halves[0, :, 4 * width :] = up_first
    halves[1, :, : hidden - split] = low(outer_sum(hidden_two, da_s[:, split:]) * share)
    down_s[...] = outer_sum(u_s[...], grad_branch) * share
    for d in range(ring_size):
        for j in range(ratio):
            block_s[d * rows : (d + 1) * rows, j * width : (j + 1) * width] = down_s[
                (d * ratio + j) * rows : (d * ratio + j + 1) * rows, :
            ]
    halves[1, :, hidden - split :] = low(block_s[...])
    rank = own_ref[1]
    second_out = [
        pltpu.make_async_copy(halves.at[1], keep_ref, out_sems.at[1]),
        pltpu.make_async_copy(halves.at[1], send_ref, out_sems.at[1]),
    ]

    @pl.when(rank == 1)
    def _():
        second_out[0].start()

    @pl.when(rank != 1)
    def _():
        second_out[1].start()

    grad_hidden_two = matmul_transposed(da_s[...], up_w[...])
    row_ref[:, 3 * width : 4 * width] = column_sum(grad_hidden_two)
    row_ref[:, 4 * width : 5 * width] = column_sum(grad_hidden_two * normed_two)
    grad_middle = grad_out + normalize_back(
        normed_two, factor_two, grad_hidden_two * (1.0 + scale_two)
    )
    row_ref[:, 2 * width : 3 * width] = column_sum(grad_middle * branch_one)
    grad_attention = low(gate_one * grad_middle)
    row_ref[:, sums_at + 2 * width : sums_at + 3 * width] = column_sum(grad_attention)
    halves[0, :, 3 * width : 4 * width] = low(outer_sum(att_s[...], grad_attention) * share)
    grad_attended = low(matmul_transposed(grad_attention, out_w[...]))
    for head in range(HEADS):
        soft = soft_s[head]
        grad_head = grad_attended[:, head * HEAD : (head + 1) * HEAD]
        grad_soft = matmul_transposed(grad_head, part(qkv_s, 2, head))
        inner = jnp.sum(grad_soft * soft, axis=-1, keepdims=True)
        grad_scores = low(soft * (grad_soft - inner))
        grads = (
            matmul(grad_scores, part(qkv_s, 1, head)) * SCALE,
            outer_sum(grad_scores, part(qkv_s, 0, head)) * SCALE,
            outer_sum(low(soft), grad_head),
        )
        for member, grad in enumerate(grads):
            start = member * width + head * HEAD
            dqkv_s[:, start : start + HEAD] = low(grad)
    row_ref[:, sums_at : sums_at + width] = column_sum(dqkv_s[:, :width])
    row_ref[:, sums_at + width : sums_at + 2 * width] = column_sum(dqkv_s[:, 2 * width :])
    halves[0, :, : 3 * width] = low(outer_sum(hidden_one, dqkv_s[...]) * share)
    first_out = [
        pltpu.make_async_copy(halves.at[0], keep_ref, out_sems.at[0]),
        pltpu.make_async_copy(halves.at[0], send_ref, out_sems.at[0]),
    ]

    @pl.when(rank == 0)
    def _():
        first_out[0].start()

    @pl.when(rank != 0)
    def _():
        first_out[1].start()

    grad_hidden_one = matmul_transposed(dqkv_s[...], att_w[...])
    row_ref[:, :width] = column_sum(grad_hidden_one)
    row_ref[:, width : 2 * width] = column_sum(grad_hidden_one * normed_one)
    dx_ref[...] = low(
        grad_middle
        + normalize_back(normed_one, factor_one, grad_hidden_one * (1.0 + scale_one))
    )
    grad_modulation = low(row_ref[:, : 6 * width])
    row_ref[:, : 6 * width] = grad_modulation.astype(jnp.float32)
    spread = jnp.broadcast_to(row_ref[:, : 6 * width], (16, 6 * width))
    row_ref[:, sums_at + 4 * width + hidden :] = matmul_transposed(low(spread), mod_w[...])[0:1, :]
    second_out[0].wait()
    first_out[0].wait()


def run_section(layout, flags, x, silu, packs, dy=None):
    width, hidden, rows, ratio, ring_size, share, bias_count = layout
    length = x.shape[0]
    backward = dy is not None
    vmem = pl.BlockSpec(memory_space=pltpu.VMEM)
    hbm = pl.BlockSpec(memory_space=pl.ANY)
    bf16, f32 = jnp.bfloat16, jnp.float32
    half = 2 * width + hidden
    shapes = [jax.ShapeDtypeStruct((length, width), bf16)]
    out_specs = [vmem]
    scratch = [
        pltpu.VMEM((width, 6 * width), bf16),
        pltpu.VMEM((width, 3 * width), bf16),
        pltpu.VMEM((width, width), bf16),
        pltpu.VMEM((width, hidden), bf16),
        pltpu.VMEM((width, hidden), bf16),
        pltpu.VMEM((width, 128), bf16),
        pltpu.SemaphoreType.DMA((6,)),
        pltpu.VMEM((1, bias_count * ring_size), f32),
        pltpu.VMEM((hidden, width), bf16),
        pltpu.VMEM((hidden, width), f32),
        pltpu.VMEM((width, hidden), f32),
        pltpu.VMEM((length, 3 * width), bf16),
        pltpu.VMEM((length, width), bf16),
        pltpu.VMEM((length, hidden), bf16),
    ]
    operands = [flags, x, silu]
    if backward:
        operands.append(dy)
        shapes += [
            jax.ShapeDtypeStruct((length, width), bf16),
            jax.ShapeDtypeStruct((1, 11 * width + hidden), f32),
            jax.ShapeDtypeStruct((width, half), bf16),
            jax.ShapeDtypeStruct((width, half), bf16),
        ]
        out_specs += [vmem, vmem, hbm, hbm]
        scratch += [
            pltpu.VMEM((HEADS, length, length), f32),
            pltpu.VMEM((length, hidden), f32),
            pltpu.VMEM((length, hidden), bf16),
            pltpu.VMEM((length, 3 * width), bf16),
            pltpu.VMEM((2, width, half), bf16),
            pltpu.SemaphoreType.DMA((2,)),
        ]
    specs = [pl.BlockSpec(memory_space=pltpu.SMEM)] + [vmem] * (len(operands) - 1) + [hbm] * 2
    work = 2 * length * width * (4 * width + 2 * hidden + 2 * length)
    moved = 2 * width * (10 * width + 2 * hidden)
    return pl.pallas_call(
        partial(section_kernel, layout, backward),
        out_shape=shapes,
        in_specs=specs,
        out_specs=out_specs,
        scratch_shapes=scratch,
        compiler_params=pltpu.CompilerParams(
            vmem_limit_bytes=(36 if length <= 256 else 56) * 1024 * 1024
        ),
        cost_estimate=pl.CostEstimate(
            flops=(3 if backward else 1) * work,
            bytes_accessed=(2 if backward else 1) * moved,
            transcendentals=HEADS * length * length + length * hidden,
        ),
    )(*operands, *packs)


def pair_swap(block, axis):
    return lax.ppermute(block, axis, [(0, 1), (1, 0)])


def ring_exchange(block, size, step):
    route = [(i, step(i)) for i in range(size)]
    return lax.ppermute(block, RING, route)


def scatter_sum(block, rank, size):
    half = block.shape[-1] // 2
    pieces = [block[..., :half], block[..., half:]]
    left = size
    low_bits = 0
    while left > 4:
        orders = [(0, 1), (1, 0)] if left % 4 == 0 and left >= 16 else [(0,), (0,)]
        for turn in range(len(orders[0])):
            updated = []
            for piece, order in zip(pieces, orders):
                bit = low_bits + order[turn]
                mine = (rank >> bit) & 1
                if len(order) == 2 and turn == 0:
                    shaped = piece.reshape(-1, 2, 2, *piece.shape[1:])
                    at = 2 - order[turn]
                else:
                    shaped = piece.reshape(-1, 2, *piece.shape[1:])
                    at = 1
                keep = lax.dynamic_index_in_dim(shaped, mine, at, keepdims=False)
                send = lax.dynamic_index_in_dim(shaped, 1 - mine, at, keepdims=False)
                got = ring_exchange(send, size, lambda i, bit=bit: i ^ (1 << bit))
                total = (keep.astype(jnp.float32) + got.astype(jnp.float32)).astype(jnp.bfloat16)
                updated.append(total.reshape(-1, *piece.shape[1:]))
            pieces = updated
        low_bits += len(orders[0])
        left //= 2 ** len(orders[0])
    block = jnp.concatenate(pieces, axis=-1)
    high = rank >> low_bits
    total = lax.dynamic_index_in_dim(block, high, 0, keepdims=False).astype(jnp.float32)
    stride = 1 << low_bits
    for turn in range(1, left):
        send = lax.dynamic_index_in_dim(block, (high + turn) % left, 0, keepdims=False)
        got = ring_exchange(send, size, lambda i, turn=turn: (i + turn * stride) % size)
        total = total + got.astype(jnp.float32)
    return total


def per_device(
    inputs,
    cotangent,
    time_ids,
    row_counts,
    cond_table,
    modulation_weight,
    attention_weight,
    output_weight,
    expand_weight,
    shrink_weight,
    biases,
):
    section_rank = lax.axis_index("section")
    data_rank = lax.axis_index("dp")
    seq_rank = lax.axis_index("seq")
    sections = lax.axis_size("section")
    seq_size = lax.axis_size("seq")
    ring_size = lax.axis_size("dp") * seq_size
    ring_rank = data_rank * seq_size + seq_rank
    batches, slots, tokens, width = inputs.shape
    assert batches == sections == 2 and seq_size % slots == 0
    sharers = seq_size // slots
    slot = seq_rank // sharers
    length = tokens * seq_size
    rows = attention_weight.shape[1]
    ratio = shrink_weight.shape[1] // rows
    hidden = ratio * width
    bias_count = biases.shape[1]
    bias_rows = -(-bias_count // 128)
    assert bias_rows <= rows and hidden == expand_weight.shape[2]
    table_rows = cond_table.shape[0]
    is_first = section_rank == 0
    layout = (width, hidden, rows, ratio, ring_size, 1.0 / sharers, bias_count)

    bias_block = jnp.pad(biases[0], (0, bias_rows * 128 - bias_count)).reshape(bias_rows, 128)
    packed = jnp.concatenate(
        [
            attention_weight[0],
            output_weight[0],
            expand_weight[0],
            modulation_weight[0],
            *[shrink_weight[0, j * rows : (j + 1) * rows] for j in range(ratio)],
            jnp.pad(bias_block, ((0, rows - bias_rows), (0, 0))),
        ],
        axis=1,
    )
    own_pack = lax.all_gather(packed, RING, axis=0, tiled=True)
    packs = (own_pack, pair_swap(own_pack, "section"))

    live = (
        slot < lax.dynamic_index_in_dim(row_counts, section_rank, 0, keepdims=False)[0]
    ).astype(jnp.bfloat16)
    both = jnp.stack(
        [
            lax.dynamic_index_in_dim(inputs, section_rank, 0, keepdims=False),
            lax.dynamic_index_in_dim(cotangent, section_rank, 0, keepdims=False),
        ],
        axis=1,
    )
    both = jnp.repeat(both, sharers, axis=0)
    both = lax.all_to_all(both, "seq", 0, 0, tiled=True)
    first_input = both[:, 0].reshape(length, width)
    last_grad = both[:, 1].reshape(length, width) * live
    flat_ids = time_ids.reshape(-1)
    selector = (
        flat_ids[:, None] == jnp.arange(table_rows, dtype=jnp.int32)[None, :]
    ).astype(jnp.bfloat16)
    conditions = matmul(selector, cond_table)
    silu_all = jax.nn.silu(conditions).astype(jnp.bfloat16)
    latent = section_rank * time_ids.shape[1] + data_rank * slots + slot
    condition = lax.dynamic_slice_in_dim(conditions, latent, 1, 0)
    silu_now = jnp.broadcast_to(lax.dynamic_slice_in_dim(silu_all, latent, 1, 0), (16, width))

    first_flags = jnp.stack([is_first, ~is_first]).astype(jnp.int32)
    second_flags = jnp.stack([~is_first, ~is_first]).astype(jnp.int32)
    (first_low,) = run_section(layout, first_flags, first_input, silu_now, packs)
    second_low, second_grad, second_row, second_keep, second_send = run_section(
        layout, second_flags, first_low, silu_now, packs, last_grad
    )
    second_got = pair_swap(second_send, "section")
    _, first_grad, first_row, first_keep, first_send = run_section(
        layout, first_flags, first_input, silu_now, packs, second_grad
    )
    first_got = pair_swap(first_send, "section")

    def to_owners(first, second):
        pieces = jnp.stack([first, second]).reshape(2 * seq_size, tokens, width)
        pieces = lax.all_to_all(pieces, ("section", "seq"), 0, 0, tiled=True)
        return pieces.reshape(batches, slots, sharers, tokens, width)[:, :, 0]

    activations = to_owners(first_low * live, second_low * live)
    input_grads = to_owners(first_grad, second_grad).astype(jnp.float32)

    half = first_keep.shape[1]

    def chip_sum(keep, got):
        total = keep.astype(jnp.float32) + got.astype(jnp.float32)
        return total.astype(jnp.bfloat16).reshape(ring_size, 1, rows, half)

    ring_terms = jnp.concatenate(
        [chip_sum(first_keep, first_got), chip_sum(second_keep, second_got)], axis=1
    )
    owned = scatter_sum(ring_terms.reshape(ring_size, 2 * rows, half), ring_rank, ring_size)
    owned = owned.reshape(2, rows, half)
    mine = lax.dynamic_index_in_dim(owned, section_rank, 0, keepdims=False)
    theirs = pair_swap(
        lax.dynamic_index_in_dim(owned, 1 - section_rank, 0, keepdims=False), "section"
    )
    full = jnp.where(
        is_first,
        jnp.concatenate([mine, theirs], axis=1),
        jnp.concatenate([theirs, mine], axis=1),
    )
    edges = [0, 3 * width, 4 * width, 4 * width + hidden]
    att, out, up = [full[:, a:b] for a, b in zip(edges[:-1], edges[1:])]
    down = jnp.concatenate(
        [full[:, edges[3] + j * width : edges[3] + (j + 1) * width] for j in range(ratio)], axis=0
    )

    per_row = 10 * width + hidden
    _, silu_back = jax.vjp(jax.nn.silu, condition)
    grad_condition = silu_back(first_row[:, per_row:] + second_row[:, per_row:])[0]
    row = jnp.concatenate([first_row[:, :per_row], second_row[:, :per_row], grad_condition], axis=1)
    every = lax.all_gather(row, ("section", "dp", "seq"), axis=0, tiled=True)[::sharers]
    section_rows = jnp.where(is_first, every[:, :per_row], every[:, per_row : 2 * per_row])
    bias_total = jnp.sum(section_rows, axis=0)
    bias_grad = lax.dynamic_slice_in_dim(bias_total, ring_rank * bias_count, bias_count, 0)
    silu_own = lax.dynamic_slice_in_dim(silu_all, ring_rank * rows, rows, 1)
    modulation_grad = outer_sum(silu_own, section_rows[:, : 6 * width].astype(jnp.bfloat16))
    table_grad = lax.dot_general(
        selector.astype(jnp.float32),
        every[:, 2 * per_row :],
        (((0,), (0,)), ((), ())),
        precision=lax.Precision.HIGHEST,
        preferred_element_type=jnp.float32,
    )
    return (
        activations[None],
        input_grads[None],
        table_grad,
        modulation_grad[None],
        att[None],
        out[None],
        up[None],
        down[None],
        bias_grad[None],
    )


def solution(mesh):
    shard = P("section", ("dp", "seq"), None)
    in_specs = (
        P(None, "dp", "seq", None),
        P(None, "dp", "seq", None),
        P(),
        P(None, "dp"),
        P(),
        shard,
        shard,
        shard,
        shard,
        shard,
        P("section", ("dp", "seq")),
    )
    out_specs = (
        P("section", None, "dp", "seq", None),
        P("section", None, "dp", "seq", None),
        P(),
        shard,
        shard,
        shard,
        shard,
        shard,
        P("section", ("dp", "seq")),
    )
    return jax.shard_map(
        per_device, mesh=mesh, in_specs=in_specs, out_specs=out_specs, check_vma=False
    )
```

```python
from functools import partial

import jax
import jax.numpy as jnp
from jax import lax
from jax.experimental import pallas as pl
from jax.experimental.pallas import tpu as pltpu
from jax.sharding import PartitionSpec as P

HEADS = 6
HEAD = 64
SCALE = HEAD ** (-0.5)
epsilon = 1e-06
RING = ("dp", "seq")
INNER = (2.0 / 3.141592653589793) ** 0.5
CUBE = 0.044715


def matmul(former, latter):
    return jnp.dot(former, latter, preferred_element_type=jnp.float32)


def matmul_transposed(former, latter):
    return lax.dot_general(
        former, latter, (((1,), (1,)), ((), ())), preferred_element_type=jnp.float32
    )


def outer_sum(former, latter):
    return lax.dot_general(
        former, latter, (((0,), (0,)), ((), ())), preferred_element_type=jnp.float32
    )


def low(values):
    return values.astype(jnp.bfloat16)


def normalize_rows(values):
    centre = jnp.mean(values, axis=-1, keepdims=True)
    centred = values - centre
    spread = jnp.mean(centred * centred, axis=-1, keepdims=True)
    factor = lax.rsqrt(spread + epsilon)
    return (centred * factor, factor)


def normalize_back(normed, factor, grad_normed):
    mean_grad = jnp.mean(grad_normed, axis=-1, keepdims=True)
    mean_cross = jnp.mean(grad_normed * normed, axis=-1, keepdims=True)
    return factor * (grad_normed - mean_grad - normed * mean_cross)


def column_sum(values):
    return jnp.sum(values.astype(jnp.float32), axis=0, keepdims=True)


def section_kernel(layout, backward, *refs):
    width, hidden, rows, ratio, ring_size, share, bias_count = layout
    own_ref, x_ref, modulation_ref = refs[:3]
    refs = refs[3:]
    if backward:
        dy_ref = refs[0]
        refs = refs[1:]
    pack_refs = refs[:2]
    refs = refs[2:]
    if backward:
        y_ref, dx_ref, row_ref, keep_ref, send_ref = refs[:5]
        refs = refs[5:]
    else:
        y_ref = refs[0]
        refs = refs[1:]
    att_w, out_w, up_w, down_p, bias_p, sems = refs[:6]
    bias_s, down_w, down_s, block_s, qkv_s, att_s, u_s = refs[6:13]
    if backward:
        soft_s, slope_s, da_s, dqkv_s, halves, out_sems = refs[13:]

    own = own_ref[0] == 1
    held = (att_w, out_w, up_w, down_p, bias_p)
    sizes = (3 * width, width, hidden, hidden, 128)
    starts = [sum(sizes[:i]) for i in range(len(sizes))]

    def fetches(source):
        return [
            pltpu.make_async_copy(
                pack_refs[source].at[:, start : start + size], target, sems.at[i]
            )
            for i, (target, start, size) in enumerate(zip(held, starts, sizes))
        ]

    @pl.when(own)
    def _():
        for copy in fetches(0):
            copy.start()

    @pl.when(jnp.logical_not(own))
    def _():
        for copy in fetches(1):
            copy.start()

    arrivals = fetches(0)

    def bias(a, b):
        return bias_s[:, a:b]

    x = x_ref[...].astype(jnp.float32)
    normed_one, factor_one = normalize_rows(x)
    arrivals[4].wait()
    bias_rows = bias_p[...].astype(jnp.float32)
    for d in range(ring_size):
        for i in range(0, bias_count, 128):
            wide = min(128, bias_count - i)
            start = d * bias_count + i
            row = d * rows + i // 128
            bias_s[:, start : start + wide] = bias_rows[row : row + 1, :wide]
    modulation = modulation_ref[...] + bias(0, 6 * width)
    shift_one, scale_one, gate_one, shift_two, scale_two, gate_two = [
        modulation[:, i * width : (i + 1) * width] for i in range(6)
    ]
    hidden_one = low(normed_one * (1.0 + scale_one) + shift_one)
    at = 6 * width
    arrivals[0].wait()
    qkv_s[:, :width] = low(matmul(hidden_one, att_w[:, :width]) + bias(at, at + width))
    qkv_s[:, width : 2 * width] = low(matmul(hidden_one, att_w[:, width : 2 * width]))
    qkv_s[:, 2 * width :] = low(
        matmul(hidden_one, att_w[:, 2 * width :]) + bias(at + width, at + 2 * width)
    )

    def part(ref, member, head):
        start = member * width + head * HEAD
        return ref[:, start : start + HEAD]

    for head in range(HEADS):
        scores = matmul_transposed(part(qkv_s, 0, head), part(qkv_s, 1, head)) * SCALE
        raised = jnp.exp(scores - jnp.max(scores, axis=-1, keepdims=True))
        soft = raised * (1.0 / jnp.sum(raised, axis=-1, keepdims=True))
        if backward:
            soft_s[head] = soft
        attended = matmul(low(soft), part(qkv_s, 2, head))
        att_s[:, head * HEAD : (head + 1) * HEAD] = low(attended)
    arrivals[1].wait()
    branch_one = matmul(att_s[...], out_w[...]) + bias(at + 2 * width, at + 3 * width)
    middle = x + gate_one * branch_one
    normed_two, factor_two = normalize_rows(middle)
    hidden_two = low(normed_two * (1.0 + scale_two) + shift_two)
    arrivals[2].wait()
    at += 3 * width
    for j in range(ratio):
        cut = slice(j * width, (j + 1) * width)
        a = matmul(hidden_two, up_w[:, cut]) + bias(at + j * width, at + (j + 1) * width)
        square = a * a
        turn = jnp.tanh(INNER * (a + CUBE * (a * square)))
        half_one = 0.5 * (1.0 + turn)
        u_s[:, cut] = low(a * half_one)
        if backward:
            slope_s[:, cut] = half_one + (0.5 * INNER) * a * (1.0 - turn * turn) * (
                1.0 + (3.0 * CUBE) * square
            )
    arrivals[3].wait()
    block_s[...] = down_p[...].astype(jnp.float32)
    for d in range(ring_size):
        for j in range(ratio):
            down_s[(d * ratio + j) * rows : (d * ratio + j + 1) * rows, :] = block_s[
                d * rows : (d + 1) * rows, j * width : (j + 1) * width
            ]
    down_w[...] = low(down_s[...])
    branch_two = matmul(u_s[...], down_w[...]) + bias(at + hidden, at + hidden + width)
    y_ref[...] = low(middle + gate_two * branch_two)
    if not backward:
        return

    grad_out = dy_ref[...].astype(jnp.float32)
    grad_branch = low(gate_two * grad_out)
    sums_at = 6 * width
    row_ref[:, 5 * width : 6 * width] = column_sum(grad_out * branch_two)
    row_ref[:, sums_at + 3 * width + hidden : sums_at + 4 * width + hidden] = column_sum(
        grad_branch
    )
    for j in range(ratio):
        cut = slice(j * width, (j + 1) * width)
        grad_expanded = low(slope_s[:, cut] * matmul_transposed(grad_branch, down_w[cut, :]))
        da_s[:, cut] = grad_expanded
        row_ref[:, sums_at + (3 + j) * width : sums_at + (4 + j) * width] = column_sum(
            grad_expanded
        )
    split = (4 * width + 2 * hidden) // 2 - 4 * width
    up_first = low(outer_sum(hidden_two, da_s[:, :split]) * share)
    halves[0, :, 4 * width :] = up_first
    halves[1, :, : hidden - split] = low(outer_sum(hidden_two, da_s[:, split:]) * share)
    down_s[...] = outer_sum(u_s[...], grad_branch) * share
    for d in range(ring_size):
        for j in range(ratio):
            block_s[d * rows : (d + 1) * rows, j * width : (j + 1) * width] = down_s[
                (d * ratio + j) * rows : (d * ratio + j + 1) * rows, :
            ]
    halves[1, :, hidden - split :] = low(block_s[...])
    rank = own_ref[1]
    second_out = [
        pltpu.make_async_copy(halves.at[1], keep_ref, out_sems.at[1]),
        pltpu.make_async_copy(halves.at[1], send_ref, out_sems.at[1]),
    ]

    @pl.when(rank == 1)
    def _():
        second_out[0].start()

    @pl.when(rank != 1)
    def _():
        second_out[1].start()

    grad_hidden_two = matmul_transposed(da_s[...], up_w[...])
    row_ref[:, 3 * width : 4 * width] = column_sum(grad_hidden_two)
    row_ref[:, 4 * width : 5 * width] = column_sum(grad_hidden_two * normed_two)
    grad_middle = grad_out + normalize_back(
        normed_two, factor_two, grad_hidden_two * (1.0 + scale_two)
    )
    row_ref[:, 2 * width : 3 * width] = column_sum(grad_middle * branch_one)
    grad_attention = low(gate_one * grad_middle)
    row_ref[:, sums_at + 2 * width : sums_at + 3 * width] = column_sum(grad_attention)
    halves[0, :, 3 * width : 4 * width] = low(outer_sum(att_s[...], grad_attention) * share)
    grad_attended = low(matmul_transposed(grad_attention, out_w[...]))
    for head in range(HEADS):
        soft = soft_s[head]
        grad_head = grad_attended[:, head * HEAD : (head + 1) * HEAD]
        grad_soft = matmul_transposed(grad_head, part(qkv_s, 2, head))
        inner = jnp.sum(grad_soft * soft, axis=-1, keepdims=True)
        grad_scores = low(soft * (grad_soft - inner))
        grads = (
            matmul(grad_scores, part(qkv_s, 1, head)) * SCALE,
            outer_sum(grad_scores, part(qkv_s, 0, head)) * SCALE,
            outer_sum(low(soft), grad_head),
        )
        for member, grad in enumerate(grads):
            start = member * width + head * HEAD
            dqkv_s[:, start : start + HEAD] = low(grad)
    row_ref[:, sums_at : sums_at + width] = column_sum(dqkv_s[:, :width])
    row_ref[:, sums_at + width : sums_at + 2 * width] = column_sum(dqkv_s[:, 2 * width :])
    halves[0, :, : 3 * width] = low(outer_sum(hidden_one, dqkv_s[...]) * share)
    first_out = [
        pltpu.make_async_copy(halves.at[0], keep_ref, out_sems.at[0]),
        pltpu.make_async_copy(halves.at[0], send_ref, out_sems.at[0]),
    ]

    @pl.when(rank == 0)
    def _():
        first_out[0].start()

    @pl.when(rank != 0)
    def _():
        first_out[1].start()

    grad_hidden_one = matmul_transposed(dqkv_s[...], att_w[...])
    row_ref[:, :width] = column_sum(grad_hidden_one)
    row_ref[:, width : 2 * width] = column_sum(grad_hidden_one * normed_one)
    dx_ref[...] = low(
        grad_middle
        + normalize_back(normed_one, factor_one, grad_hidden_one * (1.0 + scale_one))
    )
    row_ref[:, : 6 * width] = low(row_ref[:, : 6 * width]).astype(jnp.float32)
    second_out[0].wait()
    first_out[0].wait()


def run_section(layout, flags, x, modulation, packs, dy=None):
    width, hidden, rows, ratio, ring_size, share, bias_count = layout
    length = x.shape[0]
    backward = dy is not None
    vmem = pl.BlockSpec(memory_space=pltpu.VMEM)
    hbm = pl.BlockSpec(memory_space=pl.ANY)
    bf16, f32 = jnp.bfloat16, jnp.float32
    half = 2 * width + hidden
    shapes = [jax.ShapeDtypeStruct((length, width), bf16)]
    out_specs = [vmem]
    scratch = [
        pltpu.VMEM((width, 3 * width), bf16),
        pltpu.VMEM((width, width), bf16),
        pltpu.VMEM((width, hidden), bf16),
        pltpu.VMEM((width, hidden), bf16),
        pltpu.VMEM((width, 128), bf16),
        pltpu.SemaphoreType.DMA((5,)),
        pltpu.VMEM((1, bias_count * ring_size), f32),
        pltpu.VMEM((hidden, width), bf16),
        pltpu.VMEM((hidden, width), f32),
        pltpu.VMEM((width, hidden), f32),
        pltpu.VMEM((length, 3 * width), bf16),
        pltpu.VMEM((length, width), bf16),
        pltpu.VMEM((length, hidden), bf16),
    ]
    operands = [flags, x, modulation]
    if backward:
        operands.append(dy)
        shapes += [
            jax.ShapeDtypeStruct((length, width), bf16),
            jax.ShapeDtypeStruct((1, 10 * width + hidden), f32),
            jax.ShapeDtypeStruct((width, half), bf16),
            jax.ShapeDtypeStruct((width, half), bf16),
        ]
        out_specs += [vmem, vmem, hbm, hbm]
        scratch += [
            pltpu.VMEM((HEADS, length, length), f32),
            pltpu.VMEM((length, hidden), f32),
            pltpu.VMEM((length, hidden), bf16),
            pltpu.VMEM((length, 3 * width), bf16),
            pltpu.VMEM((2, width, half), bf16),
            pltpu.SemaphoreType.DMA((2,)),
        ]
    specs = [pl.BlockSpec(memory_space=pltpu.SMEM)] + [vmem] * (len(operands) - 1) + [hbm] * 2
    work = 2 * length * width * (4 * width + 2 * hidden + 2 * length)
    moved = 2 * width * (10 * width + 2 * hidden)
    return pl.pallas_call(
        partial(section_kernel, layout, backward),
        out_shape=shapes,
        in_specs=specs,
        out_specs=out_specs,
        scratch_shapes=scratch,
        compiler_params=pltpu.CompilerParams(
            vmem_limit_bytes=(36 if length <= 256 else 56) * 1024 * 1024
        ),
        cost_estimate=pl.CostEstimate(
            flops=(3 if backward else 1) * work,
            bytes_accessed=(2 if backward else 1) * moved,
            transcendentals=HEADS * length * length + length * hidden,
        ),
    )(*operands, *packs)


def pack_kernel(rows, ratio, att_ref, out_ref, up_ref, down_ref, bias_ref, packed_ref):
    width = out_ref.shape[1]
    at = 0
    for ref in (att_ref, out_ref, up_ref):
        packed_ref[:, at : at + ref.shape[1]] = ref[...]
        at += ref.shape[1]
    down = down_ref[...].astype(jnp.float32)
    for j in range(ratio):
        packed_ref[:, at : at + width] = low(down[j * rows : (j + 1) * rows])
        at += width
    packed_ref[:, at:] = bias_ref[...]


def copy_all(copies):
    for copy in copies:
        copy.start()
    for copy in copies:
        copy.wait()


def stack_kernel(high, split, place_ref, *refs):
    pieces, (first_ref, second_ref), sems = refs[:high], refs[high:-1], refs[-1]
    copies = []
    for turn, piece in enumerate(pieces):
        place = lax.rem(place_ref[0] + (high - turn), high)
        copies += [
            pltpu.make_async_copy(piece.at[:, :split], first_ref.at[place], sems.at[turn, 0]),
            pltpu.make_async_copy(piece.at[:, split:], second_ref.at[place], sems.at[turn, 1]),
        ]
    copy_all(copies)


def weave_kernel(split, place_ref, *refs):
    pieces, full_ref, sems = refs[:8], refs[8], refs[9]
    x, y = place_ref[1], place_ref[2]
    copies = []
    for i, piece in enumerate(pieces):
        other_x, other_y = (i % 4) & 1, (i % 4) >> 1
        row = x if not other_x else 1 - x
        column = y if not other_y else 1 - y
        lanes = pl.ds(0, split) if i < 4 else pl.ds(split, piece.shape[2])
        copies.append(
            pltpu.make_async_copy(piece, full_ref.at[:, row, column, :, lanes], sems.at[i])
        )
    copy_all(copies)


def chip_sum_kernel(high, place_ref, *refs):
    terms, (first_keep, first_send, second_keep, second_send) = refs[:4], refs[4:]
    x, y = place_ref[1], place_ref[2]
    rows, half = terms[0].shape[1:]
    lanes = half // 2
    for z in range(high):
        for other in range(2):
            for keep, target, span, chunk in (
                (True, first_keep, slice(0, lanes), z * 4 + x * 2 + other),
                (False, first_send, slice(0, lanes), z * 4 + (1 - x) * 2 + other),
                (True, second_keep, slice(lanes, half), z * 4 + other * 2 + y),
                (False, second_send, slice(lanes, half), z * 4 + other * 2 + (1 - y)),
            ):
                for section in range(2):
                    mine, got = terms[2 * section : 2 * section + 2]
                    target[z, other, section] = low(
                        mine[chunk, :, span].astype(jnp.float32)
                        + got[chunk, :, span].astype(jnp.float32)
                    )


def in_memory(kernel, shapes, operands, scalars=1, scratch=(), memory=pl.ANY, limit=24):
    specs = [pl.BlockSpec(memory_space=pltpu.SMEM)] * scalars
    specs += [pl.BlockSpec(memory_space=memory)] * (len(operands) - scalars)
    moved = sum(2 * shape.size for shape in shapes)
    return pl.pallas_call(
        kernel,
        out_shape=shapes,
        in_specs=specs,
        out_specs=[pl.BlockSpec(memory_space=memory)] * len(shapes),
        scratch_shapes=list(scratch),
        compiler_params=pltpu.CompilerParams(vmem_limit_bytes=limit * 1024 * 1024),
        cost_estimate=pl.CostEstimate(flops=0, bytes_accessed=2 * moved, transcendentals=0),
    )(*operands)


def pair_swap(block, axis):
    return lax.ppermute(block, axis, [(0, 1), (1, 0)])


def ring_exchange(block, size, step):
    return lax.ppermute(block, RING, [(i, step(i)) for i in range(size)])


def flip(block, size, bit):
    return ring_exchange(block, size, lambda i: i ^ (1 << bit))


def rotate(block, size, turn):
    return ring_exchange(block, size, lambda i: (i + 4 * turn) % size)


def gather_compact(packed, place, size, split):
    high = size // 4
    rows, lanes = packed.shape
    shards = [packed] + [rotate(packed, size, turn) for turn in range(1, high)]
    first, second = in_memory(
        partial(stack_kernel, high, split),
        [
            jax.ShapeDtypeStruct((high, rows, wide), packed.dtype)
            for wide in (split, lanes - split)
        ],
        [place, *shards],
        scratch=[pltpu.SemaphoreType.DMA((high, 2))],
    )
    first_x, second_y = flip(first, size, 1), flip(second, size, 0)
    first_y, second_x = flip(first, size, 0), flip(second, size, 1)
    first_both, second_both = flip(first_x, size, 0), flip(second_y, size, 1)
    (full,) = in_memory(
        partial(weave_kernel, split),
        [jax.ShapeDtypeStruct((high, 2, 2, rows, lanes), packed.dtype)],
        [place, first, first_x, first_y, first_both, second, second_x, second_y, second_both],
        scratch=[pltpu.SemaphoreType.DMA((8,))],
    )
    return full.reshape(size * rows, lanes)


def scatter_compact(terms, place, rank, size):
    high = size // 4
    rows, half = terms[0].shape[1:]
    lanes = half // 2
    shape = jax.ShapeDtypeStruct((high, 2, 2, rows, lanes), jnp.bfloat16)
    first_keep, first_send, second_keep, second_send = in_memory(
        partial(chip_sum_kernel, high),
        [shape] * 4,
        [place, *terms],
        memory=pltpu.VMEM,
        limit=32,
    )
    first_got, second_got = flip(first_send, size, 1), flip(second_send, size, 0)

    def second_stage(keep, got, mine, bit):
        total = low(keep.astype(jnp.float32) + got.astype(jnp.float32))
        kept = lax.dynamic_index_in_dim(total, mine, 1, keepdims=False)
        sent = lax.dynamic_index_in_dim(total, 1 - mine, 1, keepdims=False)
        return low(kept.astype(jnp.float32) + flip(sent, size, bit).astype(jnp.float32))

    first = second_stage(first_keep, first_got, rank & 1, 0)
    second = second_stage(second_keep, second_got, (rank >> 1) & 1, 1)
    block = jnp.concatenate([first, second], axis=-1)
    place_high = rank >> 2
    total = lax.dynamic_index_in_dim(block, place_high, 0, keepdims=False).astype(jnp.float32)
    for turn in range(1, high):
        sent = lax.dynamic_index_in_dim(block, (place_high + turn) % high, 0, keepdims=False)
        total = total + rotate(sent, size, turn).astype(jnp.float32)
    return total


def scatter_sum(block, rank, size):
    half = block.shape[-1] // 2
    pieces = [block[..., :half], block[..., half:]]
    left = size
    low_bits = 0
    while left > 4:
        orders = [(0, 1), (1, 0)] if left % 4 == 0 and left >= 16 else [(0,), (0,)]
        for turn in range(len(orders[0])):
            updated = []
            for piece, order in zip(pieces, orders):
                bit = low_bits + order[turn]
                mine = (rank >> bit) & 1
                if len(order) == 2 and turn == 0:
                    shaped = piece.reshape(-1, 2, 2, *piece.shape[1:])
                    at = 2 - order[turn]
                else:
                    shaped = piece.reshape(-1, 2, *piece.shape[1:])
                    at = 1
                keep = lax.dynamic_index_in_dim(shaped, mine, at, keepdims=False)
                send = lax.dynamic_index_in_dim(shaped, 1 - mine, at, keepdims=False)
                got = ring_exchange(send, size, lambda i, bit=bit: i ^ (1 << bit))
                total = (keep.astype(jnp.float32) + got.astype(jnp.float32)).astype(jnp.bfloat16)
                updated.append(total.reshape(-1, *piece.shape[1:]))
            pieces = updated
        low_bits += len(orders[0])
        left //= 2 ** len(orders[0])
    block = jnp.concatenate(pieces, axis=-1)
    high = rank >> low_bits
    total = lax.dynamic_index_in_dim(block, high, 0, keepdims=False).astype(jnp.float32)
    stride = 1 << low_bits
    for turn in range(1, left):
        send = lax.dynamic_index_in_dim(block, (high + turn) % left, 0, keepdims=False)
        got = ring_exchange(send, size, lambda i, turn=turn: (i + turn * stride) % size)
        total = total + got.astype(jnp.float32)
    return total


def per_device(
    inputs,
    cotangent,
    time_ids,
    row_counts,
    cond_table,
    modulation_weight,
    attention_weight,
    output_weight,
    expand_weight,
    shrink_weight,
    biases,
):
    section_rank = lax.axis_index("section")
    data_rank = lax.axis_index("dp")
    seq_rank = lax.axis_index("seq")
    sections = lax.axis_size("section")
    seq_size = lax.axis_size("seq")
    ring_size = lax.axis_size("dp") * seq_size
    ring_rank = data_rank * seq_size + seq_rank
    batches, slots, tokens, width = inputs.shape
    assert batches == sections == 2 and seq_size % slots == 0
    sharers = seq_size // slots
    slot = seq_rank // sharers
    length = tokens * seq_size
    rows = attention_weight.shape[1]
    ratio = shrink_weight.shape[1] // rows
    hidden = ratio * width
    bias_count = biases.shape[1]
    bias_rows = -(-bias_count // 128)
    assert bias_rows <= rows and hidden == expand_weight.shape[2]
    table_rows = cond_table.shape[0]
    is_first = section_rank == 0
    layout = (width, hidden, rows, ratio, ring_size, 1.0 / sharers, bias_count)
    compact = ring_size in (8, 16) and seq_size == slots == 2
    place = jnp.stack([ring_rank >> 2, (ring_rank >> 1) & 1, ring_rank & 1]).astype(jnp.int32)

    flat_ids = time_ids.reshape(-1)
    selector = (
        flat_ids[:, None] == jnp.arange(table_rows, dtype=jnp.int32)[None, :]
    ).astype(jnp.bfloat16)
    conditions = matmul(selector, cond_table)
    silu_all = jax.nn.silu(conditions).astype(jnp.bfloat16)
    silu_own = lax.dynamic_slice_in_dim(silu_all, ring_rank * rows, rows, 1)
    products = jnp.repeat(matmul(silu_own, modulation_weight[0]), sharers, axis=0)
    products = lax.all_to_all(
        products[:, None], ("section", "dp", "seq"), 0, 0, tiled=True
    ).reshape(sections, ring_size, 6 * width)
    first_modulation, second_modulation = jnp.split(jnp.sum(products, axis=1), 2, axis=0)

    lanes = 4 * width + 2 * hidden + 128
    bias_block = jnp.pad(biases[0], (0, bias_rows * 128 - bias_count)).reshape(bias_rows, 128)
    bias_block = jnp.pad(bias_block, ((0, rows - bias_rows), (0, 0)))
    (packed,) = in_memory(
        partial(pack_kernel, rows, ratio),
        [jax.ShapeDtypeStruct((rows, lanes), jnp.bfloat16)],
        [attention_weight[0], output_weight[0], expand_weight[0], shrink_weight[0], bias_block],
        scalars=0,
        memory=pltpu.VMEM,
    )
    if compact:
        own_pack = gather_compact(packed, place, ring_size, (4 * width + 2 * hidden) // 2)
    else:
        own_pack = lax.all_gather(packed, RING, axis=0, tiled=True)
    packs = (own_pack, pair_swap(own_pack, "section"))
    own_matrix = lax.all_gather(modulation_weight[0], RING, axis=0, tiled=True)
    other_matrix = pair_swap(own_matrix, "section")

    live = (
        slot < lax.dynamic_index_in_dim(row_counts, section_rank, 0, keepdims=False)[0]
    ).astype(jnp.bfloat16)
    both = jnp.stack(
        [
            lax.dynamic_index_in_dim(inputs, section_rank, 0, keepdims=False),
            lax.dynamic_index_in_dim(cotangent, section_rank, 0, keepdims=False),
        ],
        axis=1,
    )

    def side_by_side(mine, got, axis):
        return jnp.where(
            seq_rank == 0,
            jnp.concatenate([mine, got], axis=axis),
            jnp.concatenate([got, mine], axis=axis),
        )

    if compact:
        mine = lax.dynamic_index_in_dim(both, seq_rank, 0, keepdims=False)
        sent = lax.dynamic_index_in_dim(both, 1 - seq_rank, 0, keepdims=False)
        both = side_by_side(mine, pair_swap(sent, "seq"), 1)
    else:
        both = lax.all_to_all(jnp.repeat(both, sharers, axis=0), "seq", 0, 0, tiled=True)
        both = jnp.swapaxes(both, 0, 1).reshape(2, length, width)
    first_input = both[0]
    last_grad = both[1] * live

    first_flags = jnp.stack([is_first, ~is_first]).astype(jnp.int32)
    second_flags = jnp.stack([~is_first, ~is_first]).astype(jnp.int32)
    (first_low,) = run_section(layout, first_flags, first_input, first_modulation, packs)
    second_low, second_grad, second_row, second_keep, second_send = run_section(
        layout, second_flags, first_low, second_modulation, packs, last_grad
    )
    second_got = pair_swap(second_send, "section")
    _, first_grad, first_row, first_keep, first_send = run_section(
        layout, first_flags, first_input, first_modulation, packs, second_grad
    )
    first_got = pair_swap(first_send, "section")

    early = jnp.stack([first_low * live, second_low * live, second_grad])
    if compact:

        def halves_of(block):
            return block.reshape(-1, 2, tokens, width)

        def to_slots(block):
            block = halves_of(block)
            mine = lax.dynamic_index_in_dim(block, seq_rank, 1, keepdims=True)
            sent = lax.dynamic_index_in_dim(block, 1 - seq_rank, 1, keepdims=True)
            return side_by_side(mine, pair_swap(sent, "seq"), 1)

        early, late = to_slots(early), to_slots(first_grad)
        per_first = jnp.stack([early[0], late[0]])
        per_second = early[1:]
        mine = jnp.where(is_first, per_first, per_second)
        got = pair_swap(jnp.where(is_first, per_second, per_first), "section")
        outputs = jnp.where(is_first, jnp.stack([mine, got], 1), jnp.stack([got, mine], 1))
    else:
        pieces = jnp.stack([early[0], first_grad, early[1], early[2]])
        pieces = jnp.swapaxes(pieces.reshape(2, 2, seq_size, tokens, width), 1, 2)
        pieces = pieces.reshape(2 * seq_size, 2, tokens, width)
        pieces = lax.all_to_all(pieces, ("section", "seq"), 0, 0, tiled=True)
        pieces = pieces.reshape(batches, slots, sharers, 2, tokens, width)[:, :, 0]
        outputs = jnp.moveaxis(pieces, 2, 0)
    activations = outputs[0]
    input_grads = outputs[1].astype(jnp.float32)

    half = first_keep.shape[1]
    if compact:
        terms = [
            term.reshape(ring_size, rows, half)
            for term in (first_keep, first_got, second_keep, second_got)
        ]
        owned = scatter_compact(terms, place, ring_rank, ring_size)
    else:

        def chip_sum(keep, got):
            total = keep.astype(jnp.float32) + got.astype(jnp.float32)
            return total.astype(jnp.bfloat16).reshape(ring_size, 1, rows, half)

        ring_terms = jnp.concatenate(
            [chip_sum(first_keep, first_got), chip_sum(second_keep, second_got)], axis=1
        )
        owned = scatter_sum(ring_terms.reshape(ring_size, 2 * rows, half), ring_rank, ring_size)
        owned = owned.reshape(2, rows, half)
    mine = lax.dynamic_index_in_dim(owned, section_rank, 0, keepdims=False)
    theirs = pair_swap(
        lax.dynamic_index_in_dim(owned, 1 - section_rank, 0, keepdims=False), "section"
    )
    full = jnp.where(
        is_first,
        jnp.concatenate([mine, theirs], axis=1),
        jnp.concatenate([theirs, mine], axis=1),
    )
    edges = [0, 3 * width, 4 * width, 4 * width + hidden]
    att, out, up = [full[:, a:b] for a, b in zip(edges[:-1], edges[1:])]
    down = jnp.concatenate(
        [full[:, edges[3] + j * width : edges[3] + (j + 1) * width] for j in range(ratio)], axis=0
    )

    row = jnp.concatenate([first_row, second_row], axis=1)
    per_row = first_row.shape[1]
    every = lax.all_gather(row, ("section", "dp", "seq"), axis=0, tiled=True)[::sharers]
    first_rows, second_rows = every[:, :per_row], every[:, per_row:]
    own_rows = jnp.where(is_first, first_rows, second_rows)
    other_rows = jnp.where(is_first, second_rows, first_rows)[:, : 6 * width]
    bias_total = jnp.sum(own_rows, axis=0)
    bias_grad = lax.dynamic_slice_in_dim(bias_total, ring_rank * bias_count, bias_count, 0)
    own_rows = low(own_rows[:, : 6 * width])
    modulation_grad = outer_sum(silu_own, own_rows)
    _, silu_back = jax.vjp(jax.nn.silu, conditions)
    grad_conditions = silu_back(
        matmul_transposed(own_rows, own_matrix) + matmul_transposed(low(other_rows), other_matrix)
    )[0]
    table_grad = lax.dot_general(
        selector.astype(jnp.float32),
        grad_conditions,
        (((0,), (0,)), ((), ())),
        precision=lax.Precision.HIGHEST,
        preferred_element_type=jnp.float32,
    )
    return (
        activations[None],
        input_grads[None],
        table_grad,
        modulation_grad[None],
        att[None],
        out[None],
        up[None],
        down[None],
        bias_grad[None],
    )


def solution(mesh):
    shard = P("section", ("dp", "seq"), None)
    in_specs = (
        P(None, "dp", "seq", None),
        P(None, "dp", "seq", None),
        P(),
        P(None, "dp"),
        P(),
        shard,
        shard,
        shard,
        shard,
        shard,
        P("section", ("dp", "seq")),
    )
    out_specs = (
        P("section", None, "dp", "seq", None),
        P("section", None, "dp", "seq", None),
        P(),
        shard,
        shard,
        shard,
        shard,
        shard,
        P("section", ("dp", "seq")),
    )
    return jax.shard_map(
        per_device, mesh=mesh, in_specs=in_specs, out_specs=out_specs, check_vma=False
    )
```

```python
from functools import partial

import jax
import jax.numpy as jnp
from jax import lax
from jax.experimental import pallas as pl
from jax.experimental.pallas import tpu as pltpu
from jax.sharding import PartitionSpec as P

HEADS = 6
HEAD = 64
SCALE = HEAD ** (-0.5)
epsilon = 1e-06
RING = ("dp", "seq")
INNER = (2.0 / 3.141592653589793) ** 0.5
CUBE = 0.044715


def matmul(former, latter):
    return jnp.dot(former, latter, preferred_element_type=jnp.float32)


def matmul_transposed(former, latter):
    return lax.dot_general(
        former, latter, (((1,), (1,)), ((), ())), preferred_element_type=jnp.float32
    )


def outer_sum(former, latter):
    return lax.dot_general(
        former, latter, (((0,), (0,)), ((), ())), preferred_element_type=jnp.float32
    )


def low(values):
    return values.astype(jnp.bfloat16)


def normalize_rows(values):
    centre = jnp.mean(values, axis=-1, keepdims=True)
    centred = values - centre
    spread = jnp.mean(centred * centred, axis=-1, keepdims=True)
    factor = lax.rsqrt(spread + epsilon)
    return (centred * factor, factor)


def normalize_back(normed, factor, grad_normed):
    mean_grad = jnp.mean(grad_normed, axis=-1, keepdims=True)
    mean_cross = jnp.mean(grad_normed * normed, axis=-1, keepdims=True)
    return factor * (grad_normed - mean_grad - normed * mean_cross)


def column_sum(values):
    return jnp.sum(values.astype(jnp.float32), axis=0, keepdims=True)


def section_kernel(layout, backward, after, *refs):
    width, hidden, rows, ratio, ring_size, share, bias_count = layout
    rank_ref, x_ref, modulation_ref, bias_ref = refs[:4]
    refs = refs[4:]
    if backward:
        dy_ref = refs[0]
        refs = refs[1:]
    mine_ref, theirs_ref = refs[:2]
    refs = refs[2 + after :]
    if backward:
        y_ref, dx_ref, row_ref, keep_ref, send_ref = refs[:5]
        refs = refs[5:]
    else:
        y_ref = refs[0]
        refs = refs[1:]
    att_w, out_w, up_w, down_p, sems = refs[:5]
    bias_s, down_w, down_s, block_s, qkv_s, att_s, u_s = refs[5:12]
    if backward:
        soft_s, slope_s, da_s, dqkv_s, halves, out_sems = refs[12:]

    rank = rank_ref[0]
    split = hidden - 2 * width

    def fetches(first, second):
        moves = (
            (first.at[:, : 3 * width], att_w),
            (first.at[:, 3 * width : 4 * width], out_w),
            (first.at[:, 4 * width :], up_w.at[:, :split]),
            (second.at[:, : hidden - split], up_w.at[:, split:]),
            (second.at[:, hidden - split :], down_p),
        )
        return [
            pltpu.make_async_copy(source, target, sems.at[i])
            for i, (source, target) in enumerate(moves)
        ]

    @pl.when(rank == 0)
    def _():
        for copy in fetches(mine_ref, theirs_ref):
            copy.start()

    @pl.when(rank != 0)
    def _():
        for copy in fetches(theirs_ref, mine_ref):
            copy.start()

    arrivals = fetches(mine_ref, theirs_ref)

    def bias(a, b):
        return bias_s[:, a:b]

    x = x_ref[...].astype(jnp.float32)
    normed_one, factor_one = normalize_rows(x)
    for d in range(ring_size):
        bias_s[:, d * bias_count : (d + 1) * bias_count] = bias_ref[d : d + 1, :]
    modulation = modulation_ref[...] + bias(0, 6 * width)
    shift_one, scale_one, gate_one, shift_two, scale_two, gate_two = [
        modulation[:, i * width : (i + 1) * width] for i in range(6)
    ]
    hidden_one = low(normed_one * (1.0 + scale_one) + shift_one)
    at = 6 * width
    arrivals[0].wait()
    qkv_s[:, :width] = low(matmul(hidden_one, att_w[:, :width]) + bias(at, at + width))
    qkv_s[:, width : 2 * width] = low(matmul(hidden_one, att_w[:, width : 2 * width]))
    qkv_s[:, 2 * width :] = low(
        matmul(hidden_one, att_w[:, 2 * width :]) + bias(at + width, at + 2 * width)
    )

    def part(ref, member, head):
        start = member * width + head * HEAD
        return ref[:, start : start + HEAD]

    for head in range(HEADS):
        scores = matmul_transposed(part(qkv_s, 0, head), part(qkv_s, 1, head)) * SCALE
        raised = jnp.exp(scores - jnp.max(scores, axis=-1, keepdims=True))
        soft = raised * (1.0 / jnp.sum(raised, axis=-1, keepdims=True))
        if backward:
            soft_s[head] = soft
        attended = matmul(low(soft), part(qkv_s, 2, head))
        att_s[:, head * HEAD : (head + 1) * HEAD] = low(attended)
    arrivals[1].wait()
    branch_one = matmul(att_s[...], out_w[...]) + bias(at + 2 * width, at + 3 * width)
    middle = x + gate_one * branch_one
    normed_two, factor_two = normalize_rows(middle)
    hidden_two = low(normed_two * (1.0 + scale_two) + shift_two)
    arrivals[2].wait()
    arrivals[3].wait()
    at += 3 * width
    for j in range(ratio):
        cut = slice(j * width, (j + 1) * width)
        a = matmul(hidden_two, up_w[:, cut]) + bias(at + j * width, at + (j + 1) * width)
        square = a * a
        turn = jnp.tanh(INNER * (a + CUBE * (a * square)))
        half_one = 0.5 * (1.0 + turn)
        u_s[:, cut] = low(a * half_one)
        if backward:
            slope_s[:, cut] = half_one + (0.5 * INNER) * a * (1.0 - turn * turn) * (
                1.0 + (3.0 * CUBE) * square
            )
    arrivals[4].wait()
    block_s[...] = down_p[...].astype(jnp.float32)
    for d in range(ring_size):
        for j in range(ratio):
            down_s[(d * ratio + j) * rows : (d * ratio + j + 1) * rows, :] = block_s[
                d * rows : (d + 1) * rows, j * width : (j + 1) * width
            ]
    down_w[...] = low(down_s[...])
    branch_two = matmul(u_s[...], down_w[...]) + bias(at + hidden, at + hidden + width)
    y_ref[...] = low(middle + gate_two * branch_two)
    if not backward:
        return

    grad_out = dy_ref[...].astype(jnp.float32)
    grad_branch = low(gate_two * grad_out)
    sums_at = 6 * width
    row_ref[:, 5 * width : 6 * width] = column_sum(grad_out * branch_two)
    row_ref[:, sums_at + 3 * width + hidden : sums_at + 4 * width + hidden] = column_sum(
        grad_branch
    )
    for j in range(ratio):
        cut = slice(j * width, (j + 1) * width)
        grad_expanded = low(slope_s[:, cut] * matmul_transposed(grad_branch, down_w[cut, :]))
        da_s[:, cut] = grad_expanded
        row_ref[:, sums_at + (3 + j) * width : sums_at + (4 + j) * width] = column_sum(
            grad_expanded
        )
    up_first = low(outer_sum(hidden_two, da_s[:, :split]) * share)
    halves[0, :, 4 * width :] = up_first
    halves[1, :, : hidden - split] = low(outer_sum(hidden_two, da_s[:, split:]) * share)
    down_s[...] = outer_sum(u_s[...], grad_branch) * share
    for d in range(ring_size):
        for j in range(ratio):
            block_s[d * rows : (d + 1) * rows, j * width : (j + 1) * width] = down_s[
                (d * ratio + j) * rows : (d * ratio + j + 1) * rows, :
            ]
    halves[1, :, hidden - split :] = low(block_s[...])
    second_out = [
        pltpu.make_async_copy(halves.at[1], keep_ref, out_sems.at[1]),
        pltpu.make_async_copy(halves.at[1], send_ref, out_sems.at[1]),
    ]

    @pl.when(rank == 1)
    def _():
        second_out[0].start()

    @pl.when(rank != 1)
    def _():
        second_out[1].start()

    grad_hidden_two = matmul_transposed(da_s[...], up_w[...])
    row_ref[:, 3 * width : 4 * width] = column_sum(grad_hidden_two)
    row_ref[:, 4 * width : 5 * width] = column_sum(grad_hidden_two * normed_two)
    grad_middle = grad_out + normalize_back(
        normed_two, factor_two, grad_hidden_two * (1.0 + scale_two)
    )
    row_ref[:, 2 * width : 3 * width] = column_sum(grad_middle * branch_one)
    grad_attention = low(gate_one * grad_middle)
    row_ref[:, sums_at + 2 * width : sums_at + 3 * width] = column_sum(grad_attention)
    halves[0, :, 3 * width : 4 * width] = low(outer_sum(att_s[...], grad_attention) * share)
    grad_attended = low(matmul_transposed(grad_attention, out_w[...]))
    for head in range(HEADS):
        soft = soft_s[head]
        grad_head = grad_attended[:, head * HEAD : (head + 1) * HEAD]
        grad_soft = matmul_transposed(grad_head, part(qkv_s, 2, head))
        inner = jnp.sum(grad_soft * soft, axis=-1, keepdims=True)
        grad_scores = low(soft * (grad_soft - inner))
        grads = (
            matmul(grad_scores, part(qkv_s, 1, head)) * SCALE,
            outer_sum(grad_scores, part(qkv_s, 0, head)) * SCALE,
            outer_sum(low(soft), grad_head),
        )
        for member, grad in enumerate(grads):
            start = member * width + head * HEAD
            dqkv_s[:, start : start + HEAD] = low(grad)
    row_ref[:, sums_at : sums_at + width] = column_sum(dqkv_s[:, :width])
    row_ref[:, sums_at + width : sums_at + 2 * width] = column_sum(dqkv_s[:, 2 * width :])
    halves[0, :, : 3 * width] = low(outer_sum(hidden_one, dqkv_s[...]) * share)
    first_out = [
        pltpu.make_async_copy(halves.at[0], keep_ref, out_sems.at[0]),
        pltpu.make_async_copy(halves.at[0], send_ref, out_sems.at[0]),
    ]

    @pl.when(rank == 0)
    def _():
        first_out[0].start()

    @pl.when(rank != 0)
    def _():
        first_out[1].start()

    grad_hidden_one = matmul_transposed(dqkv_s[...], att_w[...])
    row_ref[:, :width] = column_sum(grad_hidden_one)
    row_ref[:, width : 2 * width] = column_sum(grad_hidden_one * normed_one)
    dx_ref[...] = low(
        grad_middle
        + normalize_back(normed_one, factor_one, grad_hidden_one * (1.0 + scale_one))
    )
    row_ref[:, : 6 * width] = low(row_ref[:, : 6 * width]).astype(jnp.float32)
    second_out[0].wait()
    first_out[0].wait()


def run_section(layout, rank, x, modulation, bias, halves, dy=None, after=()):
    width, hidden, rows, ratio, ring_size, share, bias_count = layout
    length = x.shape[0]
    backward = dy is not None
    vmem = pl.BlockSpec(memory_space=pltpu.VMEM)
    hbm = pl.BlockSpec(memory_space=pl.ANY)
    bf16, f32 = jnp.bfloat16, jnp.float32
    half = 2 * width + hidden
    shapes = [jax.ShapeDtypeStruct((length, width), bf16)]
    out_specs = [vmem]
    scratch = [
        pltpu.VMEM((width, 3 * width), bf16),
        pltpu.VMEM((width, width), bf16),
        pltpu.VMEM((width, hidden), bf16),
        pltpu.VMEM((width, hidden), bf16),
        pltpu.SemaphoreType.DMA((5,)),
        pltpu.VMEM((1, bias_count * ring_size), f32),
        pltpu.VMEM((hidden, width), bf16),
        pltpu.VMEM((hidden, width), f32),
        pltpu.VMEM((width, hidden), f32),
        pltpu.VMEM((length, 3 * width), bf16),
        pltpu.VMEM((length, width), bf16),
        pltpu.VMEM((length, hidden), bf16),
    ]
    operands = [rank, x, modulation, bias]
    if backward:
        operands.append(dy)
        shapes += [
            jax.ShapeDtypeStruct((length, width), bf16),
            jax.ShapeDtypeStruct((1, 10 * width + hidden), f32),
            jax.ShapeDtypeStruct((width, half), bf16),
            jax.ShapeDtypeStruct((width, half), bf16),
        ]
        out_specs += [vmem, vmem, hbm, hbm]
        scratch += [
            pltpu.VMEM((HEADS, length, length), f32),
            pltpu.VMEM((length, hidden), f32),
            pltpu.VMEM((length, hidden), bf16),
            pltpu.VMEM((length, 3 * width), bf16),
            pltpu.VMEM((2, width, half), bf16),
            pltpu.SemaphoreType.DMA((2,)),
        ]
    specs = [pl.BlockSpec(memory_space=pltpu.SMEM)] + [vmem] * (len(operands) - 1) + [hbm] * (2 + len(after))
    work = 2 * length * width * (4 * width + 2 * hidden + 2 * length)
    moved = 2 * width * (10 * width + 2 * hidden)
    return pl.pallas_call(
        partial(section_kernel, layout, backward, len(after)),
        out_shape=shapes,
        in_specs=specs,
        out_specs=out_specs,
        scratch_shapes=scratch,
        compiler_params=pltpu.CompilerParams(
            vmem_limit_bytes=(36 if length <= 256 else 56) * 1024 * 1024
        ),
        cost_estimate=pl.CostEstimate(
            flops=(3 if backward else 1) * work,
            bytes_accessed=(2 if backward else 1) * moved,
            transcendentals=HEADS * length * length + length * hidden,
        ),
    )(*operands, *halves, *after)


def copy_all(copies):
    for copy in copies:
        copy.start()
    for copy in copies:
        copy.wait()


def pack_kernel(rank_ref, att_ref, out_ref, up_ref, down_ref, keep_ref, send_ref, sems):
    ratio, rows, width = down_ref.shape
    split = (ratio - 2) * width

    def copies(first, second):
        moves = [
            (att_ref, first.at[:, : 3 * width]),
            (out_ref, first.at[:, 3 * width : 4 * width]),
            (up_ref.at[:, :split], first.at[:, 4 * width :]),
            (up_ref.at[:, split:], second.at[:, : 2 * width]),
        ]
        for j in range(ratio):
            moves.append((down_ref.at[j], second.at[:, (2 + j) * width : (3 + j) * width]))
        return [
            pltpu.make_async_copy(source, target, sems.at[i])
            for i, (source, target) in enumerate(moves)
        ]

    @pl.when(rank_ref[0] == 0)
    def _():
        copy_all(copies(keep_ref, send_ref))

    @pl.when(rank_ref[0] != 0)
    def _():
        copy_all(copies(send_ref, keep_ref))


def stack_kernel(high, split, place_ref, *refs):
    pieces, sems = refs[:high], refs[-1]
    targets = refs[-1 - (2 if split else 1) : -1]
    copies = []
    for turn, piece in enumerate(pieces):
        place = lax.rem(place_ref[0] + (high - turn), high)
        parts = (piece.at[:, :split], piece.at[:, split:]) if split else (piece,)
        for i, (part, target) in enumerate(zip(parts, targets)):
            copies.append(pltpu.make_async_copy(part, target.at[place], sems.at[turn, i]))
    copy_all(copies)


def weave_kernel(split, place_ref, *refs):
    pieces, full_ref, sems = refs[:-2], refs[-2], refs[-1]
    x, y = place_ref[1], place_ref[2]
    copies = []
    for i, piece in enumerate(pieces):
        other_x, other_y = (i % 4) & 1, (i % 4) >> 1
        row = x if not other_x else 1 - x
        column = y if not other_y else 1 - y
        target = full_ref.at[:, row, column]
        if split:
            target = full_ref.at[:, row, column, :, pl.ds((i // 4) * split, split)]
        copies.append(pltpu.make_async_copy(piece, target, sems.at[i]))
    copy_all(copies)


def added(former, latter):
    return former.astype(jnp.float32) + latter.astype(jnp.float32)


def chip_sum_kernel(high, place_ref, mine, got, first_keep, first_send, second_keep, second_send):
    x, y = place_ref[1], place_ref[2]
    half = mine.shape[2]
    lanes = half // 2
    for z in range(high):
        for other in range(2):
            for target, span, chunk in (
                (first_keep, slice(0, lanes), z * 4 + x * 2 + other),
                (first_send, slice(0, lanes), z * 4 + (1 - x) * 2 + other),
                (second_keep, slice(lanes, half), z * 4 + other * 2 + y),
                (second_send, slice(lanes, half), z * 4 + other * 2 + (1 - y)),
            ):
                target[z, other] = low(added(mine[chunk, :, span], got[chunk, :, span]))


def turn_kernel(high, place_ref, *refs):
    for part, own in ((0, place_ref[2]), (1, place_ref[1])):
        kept, got = refs[2 * part : 2 * part + 2]
        keep, send = refs[4 + 2 * part : 6 + 2 * part]
        for z in range(high):
            keep[z] = low(added(kept[z, own], got[z, own]))
            send[z] = low(added(kept[z, 1 - own], got[z, 1 - own]))


def rise_kernel(high, place_ref, *refs):
    targets = refs[4:]
    lanes = refs[0].shape[2]
    for turn in range(high):
        chunk = lax.rem(place_ref[0] + turn, high)
        for part in range(2):
            kept, got = refs[2 * part : 2 * part + 2]
            total = added(kept[chunk], got[chunk])
            span = slice(part * lanes, (part + 1) * lanes)
            targets[turn][:, span] = total.astype(targets[turn].dtype)


def close_kernel(high, rank_ref, *refs):
    keep, send = refs[-2:]
    totals = []
    for section in range(2):
        pieces = refs[section * high : (section + 1) * high]
        total = pieces[0][...].astype(jnp.float32)
        for piece in pieces[1:]:
            total = total + piece[...].astype(jnp.float32)
        totals.append(total)
    first = rank_ref[0] == 0
    keep[...] = jnp.where(first, totals[0], totals[1])
    send[...] = jnp.where(first, totals[1], totals[0])


def spread_kernel(rank_ref, mine, got, att_ref, out_ref, up_ref, down_ref):
    rows, width = out_ref.shape
    split = up_ref.shape[1] - 2 * width
    first = rank_ref[0] == 0
    lower = jnp.where(first, mine[...], got[...])
    upper = jnp.where(first, got[...], mine[...])
    att_ref[...] = lower[:, : 3 * width]
    out_ref[...] = lower[:, 3 * width : 4 * width]
    up_ref[:, :split] = lower[:, 4 * width :]
    up_ref[:, split:] = upper[:, : 2 * width]
    for j in range(down_ref.shape[0] // rows):
        down_ref[j * rows : (j + 1) * rows, :] = upper[:, (2 + j) * width : (3 + j) * width]


def in_memory(kernel, shapes, operands, scratch=(), memory=pltpu.VMEM, after=(), limit=32):
    specs = [pl.BlockSpec(memory_space=pltpu.SMEM)]
    specs += [pl.BlockSpec(memory_space=memory)] * (len(operands) - 1)
    specs += [pl.BlockSpec(memory_space=pl.ANY)] * len(after)
    count = len(operands)

    def body(*refs):
        kernel(*refs[:count], *refs[count + len(after) :])

    moved = sum(shape.size * shape.dtype.itemsize for shape in shapes)
    return pl.pallas_call(
        body,
        out_shape=shapes,
        in_specs=specs,
        out_specs=[pl.BlockSpec(memory_space=memory)] * len(shapes),
        scratch_shapes=list(scratch),
        compiler_params=pltpu.CompilerParams(vmem_limit_bytes=limit * 1024 * 1024),
        cost_estimate=pl.CostEstimate(flops=0, bytes_accessed=3 * moved, transcendentals=0),
    )(*operands, *after)


def pair_swap(block, axis):
    return lax.ppermute(block, axis, [(0, 1), (1, 0)])


def ring_exchange(block, size, step):
    return lax.ppermute(block, RING, [(i, step(i)) for i in range(size)])


def flip(block, size, mask):
    return ring_exchange(block, size, lambda i: i ^ mask)


def rotate(block, size, turn):
    return ring_exchange(block, size, lambda i: (i + 4 * turn) % size)


def rotations(block, size):
    return [block] + [rotate(block, size, turn) for turn in range(1, size // 4)]


def gather_along_z(shard, place, size, after=()):
    high = size // 4
    rows, lanes = shard.shape
    return in_memory(
        partial(stack_kernel, high, lanes // 2),
        [jax.ShapeDtypeStruct((high, rows, lanes // 2), shard.dtype)] * 2,
        [place, *rotations(shard, size)],
        scratch=[pltpu.SemaphoreType.DMA((high, 2))],
        memory=pl.ANY,
        after=after,
    )


def gather_across(first, second, place, size):
    high, rows, lanes = first.shape
    first_x, second_y = flip(first, size, 2), flip(second, size, 1)
    first_y, second_x = flip(first, size, 1), flip(second, size, 2)
    first_both, second_both = flip(first_x, size, 1), flip(second_y, size, 2)
    (full,) = in_memory(
        partial(weave_kernel, lanes),
        [jax.ShapeDtypeStruct((high, 2, 2, rows, 2 * lanes), first.dtype)],
        [place, first, first_x, first_y, first_both, second, second_x, second_y, second_both],
        scratch=[pltpu.SemaphoreType.DMA((8,))],
        memory=pl.ANY,
    )
    return full.reshape(size * rows, 2 * lanes)


def gather_rows(block, place, size):
    high = size // 4
    (stacked,) = in_memory(
        partial(stack_kernel, high, 0),
        [jax.ShapeDtypeStruct((high, *block.shape), block.dtype)],
        [place, *rotations(block, size)],
        scratch=[pltpu.SemaphoreType.DMA((high, 1))],
        memory=pl.ANY,
    )
    (full,) = in_memory(
        partial(weave_kernel, 0),
        [jax.ShapeDtypeStruct((high, 2, 2, *block.shape), block.dtype)],
        [place, stacked, *[flip(stacked, size, mask) for mask in (2, 1, 3)]],
        scratch=[pltpu.SemaphoreType.DMA((4,))],
        memory=pl.ANY,
    )
    return full.reshape(size, *block.shape)


def scatter_first(mine, got, place, size):
    rows, half = mine.shape[1:]
    shape = jax.ShapeDtypeStruct((size // 4, 2, rows, half // 2), jnp.bfloat16)
    return in_memory(partial(chip_sum_kernel, size // 4), [shape] * 4, [place, mine, got])


def scatter_flips(sorted_terms, size):
    first_keep, first_send, second_keep, second_send = sorted_terms
    return first_keep, flip(first_send, size, 2), second_keep, flip(second_send, size, 1)


def scatter_rest(received, place, size):
    high, _, rows, lanes = received[0].shape
    shape = jax.ShapeDtypeStruct((high, rows, lanes), jnp.bfloat16)
    first_keep, first_send, second_keep, second_send = in_memory(
        partial(turn_kernel, high), [shape] * 4, [place, *received]
    )
    first_got, second_got = flip(first_send, size, 1), flip(second_send, size, 2)
    chunk = (rows, 2 * lanes)
    own, *sent = in_memory(
        partial(rise_kernel, high),
        [jax.ShapeDtypeStruct(chunk, jnp.float32)]
        + [jax.ShapeDtypeStruct(chunk, jnp.bfloat16)] * (high - 1),
        [place, first_keep, first_got, second_keep, second_got],
    )
    return [own] + [rotate(block, size, turn + 1) for turn, block in enumerate(sent)]


def scatter_sum(block, rank, size):
    half = block.shape[-1] // 2
    pieces = [block[..., :half], block[..., half:]]
    left = size
    low_bits = 0
    while left > 4:
        orders = [(0, 1), (1, 0)] if left % 4 == 0 and left >= 16 else [(0,), (0,)]
        for turn in range(len(orders[0])):
            updated = []
            for piece, order in zip(pieces, orders):
                bit = low_bits + order[turn]
                mine = (rank >> bit) & 1
                if len(order) == 2 and turn == 0:
                    shaped = piece.reshape(-1, 2, 2, *piece.shape[1:])
                    at = 2 - order[turn]
                else:
                    shaped = piece.reshape(-1, 2, *piece.shape[1:])
                    at = 1
                keep = lax.dynamic_index_in_dim(shaped, mine, at, keepdims=False)
                send = lax.dynamic_index_in_dim(shaped, 1 - mine, at, keepdims=False)
                got = ring_exchange(send, size, lambda i, bit=bit: i ^ (1 << bit))
                total = (keep.astype(jnp.float32) + got.astype(jnp.float32)).astype(jnp.bfloat16)
                updated.append(total.reshape(-1, *piece.shape[1:]))
            pieces = updated
        low_bits += len(orders[0])
        left //= 2 ** len(orders[0])
    block = jnp.concatenate(pieces, axis=-1)
    high = rank >> low_bits
    total = lax.dynamic_index_in_dim(block, high, 0, keepdims=False).astype(jnp.float32)
    stride = 1 << low_bits
    for turn in range(1, left):
        send = lax.dynamic_index_in_dim(block, (high + turn) % left, 0, keepdims=False)
        got = ring_exchange(send, size, lambda i, turn=turn: (i + turn * stride) % size)
        total = total + got.astype(jnp.float32)
    return total


def per_device(
    inputs,
    cotangent,
    time_ids,
    row_counts,
    cond_table,
    modulation_weight,
    attention_weight,
    output_weight,
    expand_weight,
    shrink_weight,
    biases,
):
    section_rank = lax.axis_index("section")
    data_rank = lax.axis_index("dp")
    seq_rank = lax.axis_index("seq")
    sections = lax.axis_size("section")
    seq_size = lax.axis_size("seq")
    ring_size = lax.axis_size("dp") * seq_size
    ring_rank = data_rank * seq_size + seq_rank
    batches, slots, tokens, width = inputs.shape
    assert batches == sections == 2 and seq_size % slots == 0
    sharers = seq_size // slots
    slot = seq_rank // sharers
    length = tokens * seq_size
    rows = attention_weight.shape[1]
    ratio = shrink_weight.shape[1] // rows
    hidden = ratio * width
    bias_count = biases.shape[1]
    half = 2 * width + hidden
    assert hidden == expand_weight.shape[2] and ratio >= 2
    table_rows = cond_table.shape[0]
    is_first = section_rank == 0
    layout = (width, hidden, rows, ratio, ring_size, 1.0 / sharers, bias_count)
    compact = ring_size in (8, 16) and seq_size == slots == 2
    rank = section_rank.astype(jnp.int32).reshape(1)
    place = jnp.stack([ring_rank >> 2, (ring_rank >> 1) & 1, ring_rank & 1]).astype(jnp.int32)

    keep, send = in_memory(
        pack_kernel,
        [jax.ShapeDtypeStruct((rows, half), jnp.bfloat16)] * 2,
        [
            rank,
            attention_weight[0],
            output_weight[0],
            expand_weight[0],
            shrink_weight[0].reshape(ratio, rows, width),
        ],
        scratch=[pltpu.SemaphoreType.DMA((4 + ratio,))],
        memory=pl.ANY,
    )
    got = pair_swap(send, "section")
    first_shard = jnp.where(is_first, keep, got)
    second_shard = jnp.where(is_first, got, keep)

    live = (
        slot < lax.dynamic_index_in_dim(row_counts, section_rank, 0, keepdims=False)[0]
    ).astype(jnp.bfloat16)
    both = jnp.stack(
        [
            lax.dynamic_index_in_dim(inputs, section_rank, 0, keepdims=False),
            lax.dynamic_index_in_dim(cotangent, section_rank, 0, keepdims=False),
        ],
        axis=1,
    )

    def side_by_side(mine, got, axis):
        return jnp.where(
            seq_rank == 0,
            jnp.concatenate([mine, got], axis=axis),
            jnp.concatenate([got, mine], axis=axis),
        )

    if compact:
        mine = lax.dynamic_index_in_dim(both, seq_rank, 0, keepdims=False)
        sent = lax.dynamic_index_in_dim(both, 1 - seq_rank, 0, keepdims=False)
        both = side_by_side(mine, pair_swap(sent, "seq"), 1)
    else:
        both = lax.all_to_all(jnp.repeat(both, sharers, axis=0), "seq", 0, 0, tiled=True)
        both = jnp.swapaxes(both, 0, 1).reshape(2, length, width)
    first_input = both[0]
    last_grad = both[1] * live

    flat_ids = time_ids.reshape(-1)
    selector = (
        flat_ids[:, None] == jnp.arange(table_rows, dtype=jnp.int32)[None, :]
    ).astype(jnp.bfloat16)
    conditions = matmul(selector, cond_table)
    silu_all = jax.nn.silu(conditions).astype(jnp.bfloat16)
    silu_own = lax.dynamic_slice_in_dim(silu_all, ring_rank * rows, rows, 1)
    products = matmul(silu_own, modulation_weight[0])
    own_bias = jnp.broadcast_to(biases.astype(jnp.float32), (products.shape[0], bias_count))
    products = jnp.repeat(jnp.concatenate([products, own_bias], axis=1), sharers, axis=0)
    products = lax.all_to_all(
        products[:, None], ("section", "dp", "seq"), 0, 0, tiled=True
    ).reshape(sections, ring_size, 6 * width + bias_count)
    first_modulation, second_modulation = jnp.split(
        jnp.sum(products[:, :, : 6 * width], axis=1), 2, axis=0
    )
    first_bias, second_bias = products[0, :, 6 * width :], products[1, :, 6 * width :]

    if compact:
        first_parts = gather_along_z(first_shard, place, ring_size, after=(products, both))
        second_parts = gather_along_z(second_shard, place, ring_size)
        first_pack = gather_across(*first_parts, place, ring_size)
        second_pack = gather_across(*second_parts, place, ring_size)
    else:
        first_pack = lax.all_gather(first_shard, RING, axis=0, tiled=True)
        second_pack = lax.all_gather(second_shard, RING, axis=0, tiled=True)
    first_halves = (first_pack, pair_swap(first_pack, "section"))
    second_halves = (second_pack, pair_swap(second_pack, "section"))
    own_matrix = lax.all_gather(modulation_weight[0], RING, axis=0, tiled=True)

    first = (first_input, first_modulation, first_bias, first_halves)
    (first_low,) = run_section(layout, rank, *first)
    second_low, second_grad, second_row, second_keep, second_send = run_section(
        layout, rank, first_low, second_modulation, second_bias, second_halves, last_grad
    )
    second_got = pair_swap(second_send, "section")

    def ring_terms(term):
        return term.reshape(ring_size, rows, half)

    after = ()
    if compact:
        second_sorted = scatter_first(
            ring_terms(second_keep), ring_terms(second_got), place, ring_size
        )
        after = (second_sorted[0],)
        second_received = scatter_flips(second_sorted, ring_size)
    _, first_grad, first_row, first_keep, first_send = run_section(
        layout, rank, *first, second_grad, after
    )
    first_got = pair_swap(first_send, "section")

    shard = jax.ShapeDtypeStruct((rows, half), jnp.float32)
    if compact:
        second_pieces = scatter_rest(second_received, place, ring_size)
        first_sorted = scatter_first(
            ring_terms(first_keep), ring_terms(first_got), place, ring_size
        )
        first_pieces = scatter_rest(scatter_flips(first_sorted, ring_size), place, ring_size)
    else:

        def chip_sum(keep, got):
            return ring_terms(low(added(keep, got)))

        first_pieces, second_pieces = [
            [scatter_sum(chip_sum(keep, got), ring_rank, ring_size)]
            for keep, got in ((first_keep, first_got), (second_keep, second_got))
        ]
    mine, send = in_memory(
        partial(close_kernel, len(first_pieces)),
        [shard, shard],
        [rank, *first_pieces, *second_pieces],
    )
    att, out, up, down = in_memory(
        spread_kernel,
        [
            jax.ShapeDtypeStruct(extent, jnp.float32)
            for extent in (
                (rows, 3 * width),
                (rows, width),
                (rows, hidden),
                (rows * ratio, width),
            )
        ],
        [rank, mine, pair_swap(send, "section")],
    )

    early = jnp.stack([first_low * live, second_low * live, second_grad])
    if compact:

        def to_slots(block):
            block = block.reshape(-1, 2, tokens, width)
            mine = lax.dynamic_index_in_dim(block, seq_rank, 1, keepdims=True)
            sent = lax.dynamic_index_in_dim(block, 1 - seq_rank, 1, keepdims=True)
            return side_by_side(mine, pair_swap(sent, "seq"), 1)

        early, late = to_slots(early), to_slots(first_grad)
        per_first = jnp.stack([early[0], late[0]])
        per_second = early[1:]
        mine = jnp.where(is_first, per_first, per_second)
        got = pair_swap(jnp.where(is_first, per_second, per_first), "section")
        outputs = jnp.where(is_first, jnp.stack([mine, got], 1), jnp.stack([got, mine], 1))
    else:
        pieces = jnp.stack([early[0], first_grad, early[1], early[2]])
        pieces = jnp.swapaxes(pieces.reshape(2, 2, seq_size, tokens, width), 1, 2)
        pieces = pieces.reshape(2 * seq_size, 2, tokens, width)
        pieces = lax.all_to_all(pieces, ("section", "seq"), 0, 0, tiled=True)
        pieces = pieces.reshape(batches, slots, sharers, 2, tokens, width)[:, :, 0]
        outputs = jnp.moveaxis(pieces, 2, 0)
    activations = outputs[0]
    input_grads = outputs[1].astype(jnp.float32)

    own_row = jnp.where(is_first, first_row, second_row)
    other_row = pair_swap(low(jnp.where(is_first, second_row, first_row)), "section")
    pair = jnp.where(
        is_first,
        jnp.concatenate([low(own_row), other_row]),
        jnp.concatenate([other_row, low(own_row)]),
    )
    if compact:
        every = gather_rows(pair, place, ring_size)
    else:
        every = lax.all_gather(pair, RING, axis=0)[::sharers]
    every = jnp.swapaxes(every, 0, 1).reshape(-1, pair.shape[1])
    bias_total = jnp.sum(every.astype(jnp.float32), axis=0)
    bias_grad = lax.dynamic_slice_in_dim(bias_total, ring_rank * bias_count, bias_count, 0)
    modulation_rows = every[:, : 6 * width]
    modulation_grad = outer_sum(silu_own, modulation_rows)
    products_back = matmul_transposed(modulation_rows, own_matrix)
    products_back = products_back + pair_swap(products_back, "section")
    _, silu_back = jax.vjp(jax.nn.silu, conditions)
    table_grad = lax.dot_general(
        selector.astype(jnp.float32),
        silu_back(products_back)[0],
        (((0,), (0,)), ((), ())),
        precision=lax.Precision.HIGHEST,
        preferred_element_type=jnp.float32,
    )
    return (
        activations[None],
        input_grads[None],
        table_grad,
        modulation_grad[None],
        att[None],
        out[None],
        up[None],
        down[None],
        bias_grad[None],
    )


def solution(mesh):
    shard = P("section", ("dp", "seq"), None)
    in_specs = (
        P(None, "dp", "seq", None),
        P(None, "dp", "seq", None),
        P(),
        P(None, "dp"),
        P(),
        shard,
        shard,
        shard,
        shard,
        shard,
        P("section", ("dp", "seq")),
    )
    out_specs = (
        P("section", None, "dp", "seq", None),
        P("section", None, "dp", "seq", None),
        P(),
        shard,
        shard,
        shard,
        shard,
        shard,
        P("section", ("dp", "seq")),
    )
    return jax.shard_map(
        per_device, mesh=mesh, in_specs=in_specs, out_specs=out_specs, check_vma=False
    )
```

```python
from functools import partial

import jax
import jax.numpy as jnp
from jax import lax
from jax.experimental import pallas as pl
from jax.experimental.pallas import tpu as pltpu
from jax.sharding import PartitionSpec as P

HEADS = 6
HEAD = 64
SCALE = HEAD ** (-0.5)
epsilon = 1e-06
RING = ("dp", "seq")
INNER = (2.0 / 3.141592653589793) ** 0.5
CUBE = 0.044715


def matmul(former, latter):
    return jnp.dot(former, latter, preferred_element_type=jnp.float32)


def matmul_transposed(former, latter):
    return lax.dot_general(
        former, latter, (((1,), (1,)), ((), ())), preferred_element_type=jnp.float32
    )


def outer_sum(former, latter):
    return lax.dot_general(
        former, latter, (((0,), (0,)), ((), ())), preferred_element_type=jnp.float32
    )


def low(values):
    return values.astype(jnp.bfloat16)


def normalize_rows(values):
    centre = jnp.mean(values, axis=-1, keepdims=True)
    centred = values - centre
    spread = jnp.mean(centred * centred, axis=-1, keepdims=True)
    factor = lax.rsqrt(spread + epsilon)
    return (centred * factor, factor)


def normalize_back(normed, factor, grad_normed):
    mean_grad = jnp.mean(grad_normed, axis=-1, keepdims=True)
    mean_cross = jnp.mean(grad_normed * normed, axis=-1, keepdims=True)
    return factor * (grad_normed - mean_grad - normed * mean_cross)


def column_sum(values):
    return jnp.sum(values.astype(jnp.float32), axis=0, keepdims=True)


def saved_shapes(layout, length):
    width, hidden = layout[:2]
    bf16, f32 = jnp.bfloat16, jnp.float32
    return [
        ((1, 6 * width), f32),
        ((length, 3 * width), bf16),
        ((length, width), bf16),
        ((length, hidden), bf16),
        ((HEADS, length, length), f32),
        ((length, hidden), f32),
        ((length, width), f32),
        ((length, width), f32),
        ((hidden, width), bf16),
    ]


def section_kernel(layout, forward, backward, after, *refs):
    width, hidden, rows, ratio, ring_size, share, bias_count = layout
    refs = list(refs)

    def take(count):
        taken = refs[:count]
        del refs[:count]
        return taken

    rank_ref, x_ref = take(2)
    if forward:
        modulation_ref, bias_ref = take(2)
    else:
        saved = take(9)
    if backward:
        (dy_ref,) = take(1)
    mine_ref, theirs_ref = take(2)
    take(after)
    if forward:
        (y_ref,) = take(1)
    if backward:
        dx_ref, dmod_ref, sums_ref, keep_ref, send_ref = take(5)
    elif forward:
        saved = take(9)
    att_w, out_w, up_w, sems, down_s, block_s = take(6)
    if forward:
        down_p, bias_s = take(2)
    if backward:
        da_s, dqkv_s, row_ref, halves, out_sems = take(5)
    if forward and backward:
        saved = take(9)
    mod_s, qkv_s, att_s, u_s, soft_s, slope_s, one_s, two_s, down_w = saved

    rank = rank_ref[0]
    split = hidden - 2 * width

    def fetches(first, second):
        moves = [
            (first.at[:, : 3 * width], att_w),
            (first.at[:, 3 * width : 4 * width], out_w),
            (first.at[:, 4 * width :], up_w.at[:, :split]),
            (second.at[:, : hidden - split], up_w.at[:, split:]),
        ]
        if forward:
            moves.append((second.at[:, hidden - split :], down_p))
        return [
            pltpu.make_async_copy(source, target, sems.at[i])
            for i, (source, target) in enumerate(moves)
        ]

    @pl.when(rank == 0)
    def _():
        for copy in fetches(mine_ref, theirs_ref):
            copy.start()

    @pl.when(rank != 0)
    def _():
        for copy in fetches(theirs_ref, mine_ref):
            copy.start()

    arrivals = fetches(mine_ref, theirs_ref)

    def part(ref, member, head):
        start = member * width + head * HEAD
        return ref[:, start : start + HEAD]

    x = x_ref[...].astype(jnp.float32)
    normed_one, factor_one = normalize_rows(x)
    if forward:
        for d in range(ring_size):
            bias_s[:, d * bias_count : (d + 1) * bias_count] = bias_ref[d : d + 1, :]
        mod_s[...] = modulation_ref[...] + bias_s[:, : 6 * width]
    shift_one, scale_one, gate_one, shift_two, scale_two, gate_two = [
        mod_s[:, i * width : (i + 1) * width] for i in range(6)
    ]
    hidden_one = low(normed_one * (1.0 + scale_one) + shift_one)
    if forward:

        def bias(a, b):
            return bias_s[:, a:b]

        at = 6 * width
        arrivals[0].wait()
        qkv_s[:, :width] = low(matmul(hidden_one, att_w[:, :width]) + bias(at, at + width))
        qkv_s[:, width : 2 * width] = low(matmul(hidden_one, att_w[:, width : 2 * width]))
        qkv_s[:, 2 * width :] = low(
            matmul(hidden_one, att_w[:, 2 * width :]) + bias(at + width, at + 2 * width)
        )
        for head in range(HEADS):
            scores = matmul_transposed(part(qkv_s, 0, head), part(qkv_s, 1, head)) * SCALE
            raised = jnp.exp(scores - jnp.max(scores, axis=-1, keepdims=True))
            soft = raised * (1.0 / jnp.sum(raised, axis=-1, keepdims=True))
            soft_s[head] = soft
            attended = matmul(low(soft), part(qkv_s, 2, head))
            att_s[:, head * HEAD : (head + 1) * HEAD] = low(attended)
        arrivals[1].wait()
        one_s[...] = matmul(att_s[...], out_w[...]) + bias(at + 2 * width, at + 3 * width)
    branch_one = one_s[...]
    middle = x + gate_one * branch_one
    normed_two, factor_two = normalize_rows(middle)
    hidden_two = low(normed_two * (1.0 + scale_two) + shift_two)
    if forward:
        arrivals[2].wait()
        arrivals[3].wait()
        at += 3 * width
        for j in range(ratio):
            cut = slice(j * width, (j + 1) * width)
            a = matmul(hidden_two, up_w[:, cut]) + bias(at + j * width, at + (j + 1) * width)
            square = a * a
            turn = jnp.tanh(INNER * (a + CUBE * (a * square)))
            half_one = 0.5 * (1.0 + turn)
            u_s[:, cut] = low(a * half_one)
            slope_s[:, cut] = half_one + (0.5 * INNER) * a * (1.0 - turn * turn) * (
                1.0 + (3.0 * CUBE) * square
            )
        arrivals[4].wait()
        block_s[...] = down_p[...].astype(jnp.float32)
        for d in range(ring_size):
            for j in range(ratio):
                down_s[(d * ratio + j) * rows : (d * ratio + j + 1) * rows, :] = block_s[
                    d * rows : (d + 1) * rows, j * width : (j + 1) * width
                ]
        down_w[...] = low(down_s[...])
        two_s[...] = matmul(u_s[...], down_w[...]) + bias(at + hidden, at + hidden + width)
        y_ref[...] = low(middle + gate_two * two_s[...])
    if not backward:
        return

    grad_out = dy_ref[...].astype(jnp.float32)
    grad_branch = low(gate_two * grad_out)
    sums_at = 6 * width
    row_ref[:, 5 * width : 6 * width] = column_sum(grad_out * two_s[...])
    row_ref[:, sums_at + 3 * width + hidden : sums_at + 4 * width + hidden] = column_sum(
        grad_branch
    )
    for j in range(ratio):
        cut = slice(j * width, (j + 1) * width)
        grad_expanded = low(slope_s[:, cut] * matmul_transposed(grad_branch, down_w[cut, :]))
        da_s[:, cut] = grad_expanded
        row_ref[:, sums_at + (3 + j) * width : sums_at + (4 + j) * width] = column_sum(
            grad_expanded
        )
    halves[0, :, 4 * width :] = low(outer_sum(hidden_two, da_s[:, :split]) * share)
    halves[1, :, : hidden - split] = low(outer_sum(hidden_two, da_s[:, split:]) * share)
    down_s[...] = outer_sum(u_s[...], grad_branch) * share
    for d in range(ring_size):
        for j in range(ratio):
            block_s[d * rows : (d + 1) * rows, j * width : (j + 1) * width] = down_s[
                (d * ratio + j) * rows : (d * ratio + j + 1) * rows, :
            ]
    halves[1, :, hidden - split :] = low(block_s[...])
    second_out = [
        pltpu.make_async_copy(halves.at[1], keep_ref, out_sems.at[1]),
        pltpu.make_async_copy(halves.at[1], send_ref, out_sems.at[1]),
    ]

    @pl.when(rank == 1)
    def _():
        second_out[0].start()

    @pl.when(rank != 1)
    def _():
        second_out[1].start()

    if not forward:
        arrivals[2].wait()
        arrivals[3].wait()
    grad_hidden_two = matmul_transposed(da_s[...], up_w[...])
    row_ref[:, 3 * width : 4 * width] = column_sum(grad_hidden_two)
    row_ref[:, 4 * width : 5 * width] = column_sum(grad_hidden_two * normed_two)
    grad_middle = grad_out + normalize_back(
        normed_two, factor_two, grad_hidden_two * (1.0 + scale_two)
    )
    row_ref[:, 2 * width : 3 * width] = column_sum(grad_middle * branch_one)
    grad_attention = low(gate_one * grad_middle)
    row_ref[:, sums_at + 2 * width : sums_at + 3 * width] = column_sum(grad_attention)
    halves[0, :, 3 * width : 4 * width] = low(outer_sum(att_s[...], grad_attention) * share)
    if not forward:
        arrivals[1].wait()
    grad_attended = low(matmul_transposed(grad_attention, out_w[...]))
    for head in range(HEADS):
        soft = soft_s[head]
        grad_head = grad_attended[:, head * HEAD : (head + 1) * HEAD]
        grad_soft = matmul_transposed(grad_head, part(qkv_s, 2, head))
        inner = jnp.sum(grad_soft * soft, axis=-1, keepdims=True)
        grad_scores = low(soft * (grad_soft - inner))
        grads = (
            matmul(grad_scores, part(qkv_s, 1, head)) * SCALE,
            outer_sum(grad_scores, part(qkv_s, 0, head)) * SCALE,
            outer_sum(low(soft), grad_head),
        )
        for member, grad in enumerate(grads):
            start = member * width + head * HEAD
            dqkv_s[:, start : start + HEAD] = low(grad)
    row_ref[:, sums_at : sums_at + width] = column_sum(dqkv_s[:, :width])
    row_ref[:, sums_at + width : sums_at + 2 * width] = column_sum(dqkv_s[:, 2 * width :])
    halves[0, :, : 3 * width] = low(outer_sum(hidden_one, dqkv_s[...]) * share)
    first_out = [
        pltpu.make_async_copy(halves.at[0], keep_ref, out_sems.at[0]),
        pltpu.make_async_copy(halves.at[0], send_ref, out_sems.at[0]),
    ]

    @pl.when(rank == 0)
    def _():
        first_out[0].start()

    @pl.when(rank != 0)
    def _():
        first_out[1].start()

    if not forward:
        arrivals[0].wait()
    grad_hidden_one = matmul_transposed(dqkv_s[...], att_w[...])
    row_ref[:, :width] = column_sum(grad_hidden_one)
    row_ref[:, width : 2 * width] = column_sum(grad_hidden_one * normed_one)
    dx_ref[...] = low(
        grad_middle
        + normalize_back(normed_one, factor_one, grad_hidden_one * (1.0 + scale_one))
    )
    row_ref[:, : 6 * width] = low(row_ref[:, : 6 * width]).astype(jnp.float32)
    dmod_ref[...] = row_ref[:, : 6 * width]
    for d in range(ring_size):
        sums_ref[d : d + 1, :] = row_ref[:, d * bias_count : (d + 1) * bias_count]
    second_out[0].wait()
    first_out[0].wait()


def run_section(layout, rank, x, halves, start=None, saved=None, dy=None, after=()):
    width, hidden, rows, ratio, ring_size, share, bias_count = layout
    length = x.shape[0]
    forward, backward = start is not None, dy is not None
    vmem = pl.BlockSpec(memory_space=pltpu.VMEM)
    hbm = pl.BlockSpec(memory_space=pl.ANY)
    bf16, f32 = jnp.bfloat16, jnp.float32
    half = 2 * width + hidden
    kept = saved_shapes(layout, length)
    operands = [rank, x, *(start if forward else saved)]
    shapes, out_specs = [], []
    scratch = [
        pltpu.VMEM((width, 3 * width), bf16),
        pltpu.VMEM((width, width), bf16),
        pltpu.VMEM((width, hidden), bf16),
        pltpu.SemaphoreType.DMA((5,)),
        pltpu.VMEM((hidden, width), f32),
        pltpu.VMEM((width, hidden), f32),
    ]
    if forward:
        shapes.append(jax.ShapeDtypeStruct((length, width), bf16))
        scratch += [
            pltpu.VMEM((width, hidden), bf16),
            pltpu.VMEM((1, bias_count * ring_size), f32),
        ]
    if backward:
        operands.append(dy)
        shapes += [
            jax.ShapeDtypeStruct((length, width), bf16),
            jax.ShapeDtypeStruct((1, 6 * width), f32),
            jax.ShapeDtypeStruct((ring_size, bias_count), f32),
            jax.ShapeDtypeStruct((width, half), bf16),
            jax.ShapeDtypeStruct((width, half), bf16),
        ]
        scratch += [
            pltpu.VMEM((length, hidden), bf16),
            pltpu.VMEM((length, 3 * width), bf16),
            pltpu.VMEM((1, 10 * width + hidden), f32),
            pltpu.VMEM((2, width, half), bf16),
            pltpu.SemaphoreType.DMA((2,)),
        ]
        if forward:
            scratch += [pltpu.VMEM(extent, kind) for extent, kind in kept]
    else:
        shapes += [jax.ShapeDtypeStruct(extent, kind) for extent, kind in kept]
    out_specs = [vmem] * len(shapes)
    if backward:
        out_specs[-2:] = [hbm, hbm]
    specs = [pl.BlockSpec(memory_space=pltpu.SMEM)] + [vmem] * (len(operands) - 1)
    specs += [hbm] * (2 + len(after))
    work = 2 * length * width * (4 * width + 2 * hidden + 2 * length)
    moved = 2 * width * (10 * width + 2 * hidden)
    return pl.pallas_call(
        partial(section_kernel, layout, forward, backward, len(after)),
        out_shape=shapes,
        in_specs=specs,
        out_specs=out_specs,
        scratch_shapes=scratch,
        compiler_params=pltpu.CompilerParams(
            vmem_limit_bytes=(36 if length <= 256 else 56) * 1024 * 1024
        ),
        cost_estimate=pl.CostEstimate(
            flops=(forward + 2 * backward) * work,
            bytes_accessed=(1 + backward) * moved,
            transcendentals=HEADS * length * length + length * hidden,
        ),
    )(*operands, *halves, *after)


def copy_all(copies):
    for copy in copies:
        copy.start()
    for copy in copies:
        copy.wait()


def pack_kernel(rank_ref, att_ref, out_ref, up_ref, down_ref, keep_ref, send_ref, sems):
    ratio, rows, width = down_ref.shape
    split = (ratio - 2) * width

    def copies(first, second):
        moves = [
            (att_ref, first.at[:, : 3 * width]),
            (out_ref, first.at[:, 3 * width : 4 * width]),
            (up_ref.at[:, :split], first.at[:, 4 * width :]),
            (up_ref.at[:, split:], second.at[:, : 2 * width]),
        ]
        for j in range(ratio):
            moves.append((down_ref.at[j], second.at[:, (2 + j) * width : (3 + j) * width]))
        return [
            pltpu.make_async_copy(source, target, sems.at[i])
            for i, (source, target) in enumerate(moves)
        ]

    @pl.when(rank_ref[0] == 0)
    def _():
        copy_all(copies(keep_ref, send_ref))

    @pl.when(rank_ref[0] != 0)
    def _():
        copy_all(copies(send_ref, keep_ref))


def stack_kernel(high, split, place_ref, *refs):
    pieces, sems = refs[:high], refs[-1]
    targets = refs[-1 - (2 if split else 1) : -1]
    copies = []
    if len(refs) > high + 1 + len(targets):
        targets = refs[high + 1 : -1]
        copies.append(pltpu.make_async_copy(refs[high], targets[-1], sems.at[high, 0]))
    for turn, piece in enumerate(pieces):
        place = lax.rem(place_ref[0] + (high - turn), high)
        parts = (piece.at[:, :split], piece.at[:, split:]) if split else (piece,)
        for i, (part, target) in enumerate(zip(parts, targets)):
            copies.append(pltpu.make_async_copy(part, target.at[place], sems.at[turn, i]))
    copy_all(copies)


def weave_kernel(split, place_ref, *refs):
    pieces, full_ref, sems = refs[:-2], refs[-2], refs[-1]
    x, y = place_ref[1], place_ref[2]
    copies = []
    for i, piece in enumerate(pieces):
        other_x, other_y = (i % 4) & 1, (i % 4) >> 1
        row = x if not other_x else 1 - x
        column = y if not other_y else 1 - y
        target = full_ref.at[:, row, column]
        if split:
            target = full_ref.at[:, row, column, :, pl.ds((i // 4) * split, split)]
        copies.append(pltpu.make_async_copy(piece, target, sems.at[i]))
    copy_all(copies)


def added(former, latter):
    return former.astype(jnp.float32) + latter.astype(jnp.float32)


def chip_sum_kernel(high, place_ref, mine, got, first_keep, first_send, second_keep, second_send):
    x, y = place_ref[1], place_ref[2]
    half = mine.shape[2]
    lanes = half // 2
    for z in range(high):
        for other in range(2):
            for target, span, chunk in (
                (first_keep, slice(0, lanes), z * 4 + x * 2 + other),
                (first_send, slice(0, lanes), z * 4 + (1 - x) * 2 + other),
                (second_keep, slice(lanes, half), z * 4 + other * 2 + y),
                (second_send, slice(lanes, half), z * 4 + other * 2 + (1 - y)),
            ):
                target[z, other] = low(added(mine[chunk, :, span], got[chunk, :, span]))


def turn_kernel(high, place_ref, *refs):
    for part, own in ((0, place_ref[2]), (1, place_ref[1])):
        kept, got = refs[2 * part : 2 * part + 2]
        keep, send = refs[4 + 2 * part : 6 + 2 * part]
        for z in range(high):
            keep[z] = low(added(kept[z, own], got[z, own]))
            send[z] = low(added(kept[z, 1 - own], got[z, 1 - own]))


def rise_kernel(high, place_ref, *refs):
    targets = refs[4:]
    lanes = refs[0].shape[2]
    for turn in range(high):
        chunk = lax.rem(place_ref[0] + turn, high)
        for part in range(2):
            kept, got = refs[2 * part : 2 * part + 2]
            total = added(kept[chunk], got[chunk])
            span = slice(part * lanes, (part + 1) * lanes)
            targets[turn][:, span] = total.astype(targets[turn].dtype)


def close_kernel(high, rank_ref, *refs):
    keep, send = refs[-2:]
    totals = []
    for section in range(2):
        pieces = refs[section * high : (section + 1) * high]
        total = pieces[0][...].astype(jnp.float32)
        for piece in pieces[1:]:
            total = total + piece[...].astype(jnp.float32)
        totals.append(total)
    first = rank_ref[0] == 0
    keep[...] = jnp.where(first, totals[0], totals[1])
    send[...] = jnp.where(first, totals[1], totals[0])


def spread_kernel(rank_ref, mine, got, att_ref, out_ref, up_ref, down_ref):
    rows, width = out_ref.shape
    split = up_ref.shape[1] - 2 * width
    first = rank_ref[0] == 0
    lower = jnp.where(first, mine[...], got[...])
    upper = jnp.where(first, got[...], mine[...])
    att_ref[...] = lower[:, : 3 * width]
    out_ref[...] = lower[:, 3 * width : 4 * width]
    up_ref[:, :split] = lower[:, 4 * width :]
    up_ref[:, split:] = upper[:, : 2 * width]
    for j in range(down_ref.shape[0] // rows):
        down_ref[j * rows : (j + 1) * rows, :] = upper[:, (2 + j) * width : (3 + j) * width]


def in_memory(kernel, shapes, operands, scratch=(), memory=pltpu.VMEM, after=(), limit=32):
    specs = [pl.BlockSpec(memory_space=pltpu.SMEM)]
    specs += [pl.BlockSpec(memory_space=memory)] * (len(operands) - 1)
    specs += [pl.BlockSpec(memory_space=pl.ANY)] * len(after)
    count = len(operands)

    def body(*refs):
        kernel(*refs[:count], *refs[count + len(after) :])

    moved = sum(shape.size * shape.dtype.itemsize for shape in shapes)
    return pl.pallas_call(
        body,
        out_shape=shapes,
        in_specs=specs,
        out_specs=[pl.BlockSpec(memory_space=pltpu.VMEM)] * len(shapes),
        scratch_shapes=list(scratch),
        compiler_params=pltpu.CompilerParams(vmem_limit_bytes=limit * 1024 * 1024),
        cost_estimate=pl.CostEstimate(flops=0, bytes_accessed=3 * moved, transcendentals=0),
    )(*operands, *after)


def pair_swap(block, axis):
    return lax.ppermute(block, axis, [(0, 1), (1, 0)])


def ring_exchange(block, size, step):
    return lax.ppermute(block, RING, [(i, step(i)) for i in range(size)])


def flip(block, size, mask):
    return ring_exchange(block, size, lambda i: i ^ mask)


def rotate(block, size, turn):
    return ring_exchange(block, size, lambda i: (i + 4 * turn) % size)


def rotations(block, size):
    return [block] + [rotate(block, size, turn) for turn in range(1, size // 4)]


def gather_along_z(shard, place, size, handed=(), after=()):
    high = size // 4
    rows, lanes = shard.shape
    return in_memory(
        partial(stack_kernel, high, lanes // 2),
        [jax.ShapeDtypeStruct((high, rows, lanes // 2), shard.dtype)] * 2
        + [jax.ShapeDtypeStruct(block.shape, block.dtype) for block in handed],
        [place, *rotations(shard, size), *handed],
        scratch=[pltpu.SemaphoreType.DMA((high + 1, 2))],
        after=after,
    )


def first_flips(first, second, size):
    return flip(first, size, 2), flip(second, size, 1)


def gather_across(first, second, first_x, second_y, place, size):
    high, rows, lanes = first.shape
    first_y, second_x = flip(first, size, 1), flip(second, size, 2)
    first_both, second_both = flip(first_x, size, 1), flip(second_y, size, 2)
    (full,) = in_memory(
        partial(weave_kernel, lanes),
        [jax.ShapeDtypeStruct((high, 2, 2, rows, 2 * lanes), first.dtype)],
        [place, first, first_x, first_y, first_both, second, second_x, second_y, second_both],
        scratch=[pltpu.SemaphoreType.DMA((8,))],
    )
    return full.reshape(size * rows, 2 * lanes)


def scatter_first(mine, got, place, size, after=()):
    rows, half = mine.shape[1:]
    shape = jax.ShapeDtypeStruct((size // 4, 2, rows, half // 2), jnp.bfloat16)
    return in_memory(
        partial(chip_sum_kernel, size // 4), [shape] * 4, [place, mine, got], after=after
    )


def scatter_flips(sorted_terms, size):
    first_keep, first_send, second_keep, second_send = sorted_terms
    return first_keep, flip(first_send, size, 2), second_keep, flip(second_send, size, 1)


def scatter_second(received, place, size, after=()):
    high, _, rows, lanes = received[0].shape
    shape = jax.ShapeDtypeStruct((high, rows, lanes), jnp.bfloat16)
    return in_memory(
        partial(turn_kernel, high), [shape] * 4, [place, *received], after=after
    )


def scatter_rest(turned, place, size):
    high, rows, lanes = turned[0].shape
    first_keep, first_send, second_keep, second_send = turned
    first_got, second_got = flip(first_send, size, 1), flip(second_send, size, 2)
    chunk = (rows, 2 * lanes)
    own, *sent = in_memory(
        partial(rise_kernel, high),
        [jax.ShapeDtypeStruct(chunk, jnp.float32)]
        + [jax.ShapeDtypeStruct(chunk, jnp.bfloat16)] * (high - 1),
        [place, first_keep, first_got, second_keep, second_got],
    )
    return [own] + [rotate(block, size, turn + 1) for turn, block in enumerate(sent)]


def scatter_sum(block, rank, size):
    half = block.shape[-1] // 2
    pieces = [block[..., :half], block[..., half:]]
    left = size
    low_bits = 0
    while left > 4:
        orders = [(0, 1), (1, 0)] if left % 4 == 0 and left >= 16 else [(0,), (0,)]
        for turn in range(len(orders[0])):
            updated = []
            for piece, order in zip(pieces, orders):
                bit = low_bits + order[turn]
                mine = (rank >> bit) & 1
                if len(order) == 2 and turn == 0:
                    shaped = piece.reshape(-1, 2, 2, *piece.shape[1:])
                    at = 2 - order[turn]
                else:
                    shaped = piece.reshape(-1, 2, *piece.shape[1:])
                    at = 1
                keep = lax.dynamic_index_in_dim(shaped, mine, at, keepdims=False)
                send = lax.dynamic_index_in_dim(shaped, 1 - mine, at, keepdims=False)
                got = ring_exchange(send, size, lambda i, bit=bit: i ^ (1 << bit))
                total = (keep.astype(jnp.float32) + got.astype(jnp.float32)).astype(jnp.bfloat16)
                updated.append(total.reshape(-1, *piece.shape[1:]))
            pieces = updated
        low_bits += len(orders[0])
        left //= 2 ** len(orders[0])
    block = jnp.concatenate(pieces, axis=-1)
    high = rank >> low_bits
    total = lax.dynamic_index_in_dim(block, high, 0, keepdims=False).astype(jnp.float32)
    stride = 1 << low_bits
    for turn in range(1, left):
        send = lax.dynamic_index_in_dim(block, (high + turn) % left, 0, keepdims=False)
        got = ring_exchange(send, size, lambda i, turn=turn: (i + turn * stride) % size)
        total = total + got.astype(jnp.float32)
    return total


def per_device(
    inputs,
    cotangent,
    time_ids,
    row_counts,
    cond_table,
    modulation_weight,
    attention_weight,
    output_weight,
    expand_weight,
    shrink_weight,
    biases,
):
    section_rank = lax.axis_index("section")
    data_rank = lax.axis_index("dp")
    seq_rank = lax.axis_index("seq")
    sections = lax.axis_size("section")
    seq_size = lax.axis_size("seq")
    ring_size = lax.axis_size("dp") * seq_size
    ring_rank = data_rank * seq_size + seq_rank
    batches, slots, tokens, width = inputs.shape
    assert batches == sections == 2 and seq_size % slots == 0
    sharers = seq_size // slots
    slot = seq_rank // sharers
    length = tokens * seq_size
    rows = attention_weight.shape[1]
    ratio = shrink_weight.shape[1] // rows
    hidden = ratio * width
    bias_count = biases.shape[1]
    half = 2 * width + hidden
    assert hidden == expand_weight.shape[2] and ratio >= 2
    table_rows = cond_table.shape[0]
    is_first = section_rank == 0
    layout = (width, hidden, rows, ratio, ring_size, 1.0 / sharers, bias_count)
    compact = ring_size in (8, 16) and seq_size == slots == 2
    rank = section_rank.astype(jnp.int32).reshape(1)
    place = jnp.stack([ring_rank >> 2, (ring_rank >> 1) & 1, ring_rank & 1]).astype(jnp.int32)

    keep, send = in_memory(
        pack_kernel,
        [jax.ShapeDtypeStruct((rows, half), jnp.bfloat16)] * 2,
        [
            rank,
            attention_weight[0],
            output_weight[0],
            expand_weight[0],
            shrink_weight[0].reshape(ratio, rows, width),
        ],
        scratch=[pltpu.SemaphoreType.DMA((4 + ratio,))],
        memory=pl.ANY,
        limit=56,
    )
    got = pair_swap(send, "section")
    first_shard = jnp.where(is_first, keep, got)
    second_shard = jnp.where(is_first, got, keep)

    live = (
        slot < lax.dynamic_index_in_dim(row_counts, section_rank, 0, keepdims=False)[0]
    ).astype(jnp.bfloat16)
    both = jnp.stack(
        [
            lax.dynamic_index_in_dim(inputs, section_rank, 0, keepdims=False),
            lax.dynamic_index_in_dim(cotangent, section_rank, 0, keepdims=False),
        ],
        axis=1,
    )

    def side_by_side(mine, got, axis):
        return jnp.where(
            seq_rank == 0,
            jnp.concatenate([mine, got], axis=axis),
            jnp.concatenate([got, mine], axis=axis),
        )

    if compact:
        mine = lax.dynamic_index_in_dim(both, seq_rank, 0, keepdims=False)
        sent = lax.dynamic_index_in_dim(both, 1 - seq_rank, 0, keepdims=False)
        both = side_by_side(mine, pair_swap(sent, "seq"), 1)
    else:
        both = lax.all_to_all(jnp.repeat(both, sharers, axis=0), "seq", 0, 0, tiled=True)
        both = jnp.swapaxes(both, 0, 1).reshape(2, length, width)
    first_input = both[0]
    last_grad = both[1] * live

    flat_ids = time_ids.reshape(-1)
    selector = (
        flat_ids[:, None] == jnp.arange(table_rows, dtype=jnp.int32)[None, :]
    ).astype(jnp.bfloat16)
    conditions = matmul(selector, cond_table)
    silu_all = jax.nn.silu(conditions).astype(jnp.bfloat16)
    silu_own = lax.dynamic_slice_in_dim(silu_all, ring_rank * rows, rows, 1)
    products = matmul(silu_own, modulation_weight[0])
    own_bias = jnp.broadcast_to(biases.astype(jnp.float32), (products.shape[0], bias_count))
    products = jnp.repeat(jnp.concatenate([products, own_bias], axis=1), sharers, axis=0)
    products = lax.all_to_all(
        products[:, None], ("section", "dp", "seq"), 0, 0, tiled=True
    ).reshape(sections, ring_size, 6 * width + bias_count)
    first_modulation, second_modulation = jnp.split(
        jnp.sum(products[:, :, : 6 * width], axis=1), 2, axis=0
    )
    first_bias, second_bias = products[0, :, 6 * width :], products[1, :, 6 * width :]

    if compact:
        *first_parts, second_shard = gather_along_z(
            first_shard, place, ring_size, handed=(second_shard,)
        )
        first_parts += first_flips(*first_parts, ring_size)
        second_parts = gather_along_z(
            second_shard, place, ring_size, after=(products, both, *first_parts[2:])
        )
        second_parts += first_flips(*second_parts, ring_size)
        first_pack = gather_across(*first_parts, place, ring_size)
        second_pack = gather_across(*second_parts, place, ring_size)
    else:
        first_pack = lax.all_gather(first_shard, RING, axis=0, tiled=True)
        second_pack = lax.all_gather(second_shard, RING, axis=0, tiled=True)
    first_halves = (first_pack, pair_swap(first_pack, "section"))
    second_halves = (second_pack, pair_swap(second_pack, "section"))
    own_matrix = lax.all_gather(modulation_weight[0], RING, axis=0, tiled=True)

    first_low, *first_saved = run_section(
        layout, rank, first_input, first_halves, (first_modulation, first_bias)
    )
    second_low, second_grad, second_dmod, second_sums, second_keep, second_send = run_section(
        layout, rank, first_low, second_halves, (second_modulation, second_bias), dy=last_grad
    )
    second_got = pair_swap(second_send, "section")

    def ring_terms(term):
        return term.reshape(ring_size, rows, half)

    early = jnp.stack([first_low * live, second_low * live, second_grad])

    def to_slots(block):
        block = block.reshape(-1, 2, tokens, width)
        mine = lax.dynamic_index_in_dim(block, seq_rank, 1, keepdims=True)
        sent = lax.dynamic_index_in_dim(block, 1 - seq_rank, 1, keepdims=True)
        return mine, pair_swap(sent, "seq")

    if compact:
        early = to_slots(early)
    first_grad, first_dmod, first_sums, first_keep, first_send = run_section(
        layout, rank, first_input, first_halves, saved=first_saved, dy=second_grad
    )
    first_got = pair_swap(first_send, "section")

    if compact:
        early_full, late = side_by_side(*early, 1), side_by_side(*to_slots(first_grad), 1)
        per_first = jnp.stack([early_full[0], late[0]])
        per_second = early_full[1:]
        mine = jnp.where(is_first, per_first, per_second)
        got = pair_swap(jnp.where(is_first, per_second, per_first), "section")
        outputs = jnp.where(is_first, jnp.stack([mine, got], 1), jnp.stack([got, mine], 1))
    else:
        pieces = jnp.stack([early[0], first_grad, early[1], early[2]])
        pieces = jnp.swapaxes(pieces.reshape(2, 2, seq_size, tokens, width), 1, 2)
        pieces = pieces.reshape(2 * seq_size, 2, tokens, width)
        pieces = lax.all_to_all(pieces, ("section", "seq"), 0, 0, tiled=True)
        pieces = pieces.reshape(batches, slots, sharers, 2, tokens, width)[:, :, 0]
        outputs = jnp.moveaxis(pieces, 2, 0)
    activations = outputs[0]
    input_grads = outputs[1].astype(jnp.float32)

    shard = jax.ShapeDtypeStruct((rows, half), jnp.float32)
    if compact:
        second_sorted = scatter_first(
            ring_terms(second_keep), ring_terms(second_got), place, ring_size
        )
        second_received = scatter_flips(second_sorted, ring_size)
        second_turned = scatter_second(second_received, place, ring_size, (early[1],))
        first_sorted = scatter_first(
            ring_terms(first_keep),
            ring_terms(first_got),
            place,
            ring_size,
            (second_sorted[0],),
        )
        first_turned = scatter_second(scatter_flips(first_sorted, ring_size), place, ring_size)
        second_pieces = scatter_rest(second_turned, place, ring_size)
        first_pieces = scatter_rest(first_turned, place, ring_size)
    else:

        def chip_sum(keep, got):
            return ring_terms(low(added(keep, got)))

        first_pieces, second_pieces = [
            [scatter_sum(chip_sum(keep, got), ring_rank, ring_size)]
            for keep, got in ((first_keep, first_got), (second_keep, second_got))
        ]
    mine, send = in_memory(
        partial(close_kernel, len(first_pieces)),
        [shard, shard],
        [rank, *first_pieces, *second_pieces],
    )
    att, out, up, down = in_memory(
        spread_kernel,
        [
            jax.ShapeDtypeStruct(extent, jnp.float32)
            for extent in (
                (rows, 3 * width),
                (rows, width),
                (rows, hidden),
                (rows * ratio, width),
            )
        ],
        [rank, mine, pair_swap(send, "section")],
    )

    rows_back = jnp.concatenate(
        [
            jnp.concatenate(
                [jnp.broadcast_to(dmod, (ring_size, 6 * width)), sums], axis=1
            )
            for dmod, sums in ((first_dmod, first_sums), (second_dmod, second_sums))
        ]
    )
    every = lax.all_to_all(rows_back[:, None], ("section", "dp", "seq"), 0, 0, tiled=True)
    every = every[::sharers, 0]
    bias_grad = jnp.sum(every[:, 6 * width :], axis=0)
    modulation_rows = low(every[:, : 6 * width])
    modulation_grad = outer_sum(silu_own, modulation_rows)
    products_back = matmul_transposed(modulation_rows, own_matrix)
    products_back = products_back + pair_swap(products_back, "section")
    _, silu_back = jax.vjp(jax.nn.silu, conditions)
    table_grad = lax.dot_general(
        selector.astype(jnp.float32),
        silu_back(products_back)[0],
        (((0,), (0,)), ((), ())),
        precision=lax.Precision.HIGHEST,
        preferred_element_type=jnp.float32,
    )
    return (
        activations[None],
        input_grads[None],
        table_grad,
        modulation_grad[None],
        att[None],
        out[None],
        up[None],
        down[None],
        bias_grad[None],
    )


def solution(mesh):
    shard = P("section", ("dp", "seq"), None)
    in_specs = (
        P(None, "dp", "seq", None),
        P(None, "dp", "seq", None),
        P(),
        P(None, "dp"),
        P(),
        shard,
        shard,
        shard,
        shard,
        shard,
        P("section", ("dp", "seq")),
    )
    out_specs = (
        P("section", None, "dp", "seq", None),
        P("section", None, "dp", "seq", None),
        P(),
        shard,
        shard,
        shard,
        shard,
        shard,
        P("section", ("dp", "seq")),
    )
    return jax.shard_map(
        per_device, mesh=mesh, in_specs=in_specs, out_specs=out_specs, check_vma=False
    )
```

```python
from functools import partial

import jax
import jax.numpy as jnp
from jax import lax
from jax.experimental import pallas as pl
from jax.experimental.pallas import tpu as pltpu
from jax.sharding import PartitionSpec as P

HEADS = 6
HEAD = 64
SCALE = HEAD ** (-0.5)
epsilon = 1e-06
RING = ("dp", "seq")
INNER = (2.0 / 3.141592653589793) ** 0.5
CUBE = 0.044715


def matmul(former, latter):
    return jnp.dot(former, latter, preferred_element_type=jnp.float32)


def matmul_transposed(former, latter):
    return lax.dot_general(
        former, latter, (((1,), (1,)), ((), ())), preferred_element_type=jnp.float32
    )


def outer_sum(former, latter):
    return lax.dot_general(
        former, latter, (((0,), (0,)), ((), ())), preferred_element_type=jnp.float32
    )


def low(values):
    return values.astype(jnp.bfloat16)


def normalize_rows(values):
    centre = jnp.mean(values, axis=-1, keepdims=True)
    centred = values - centre
    spread = jnp.mean(centred * centred, axis=-1, keepdims=True)
    factor = lax.rsqrt(spread + epsilon)
    return (centred * factor, factor)


def normalize_back(normed, factor, grad_normed):
    mean_grad = jnp.mean(grad_normed, axis=-1, keepdims=True)
    mean_cross = jnp.mean(grad_normed * normed, axis=-1, keepdims=True)
    return factor * (grad_normed - mean_grad - normed * mean_cross)


def column_sum(values):
    return jnp.sum(values.astype(jnp.float32), axis=0, keepdims=True)


def saved_shapes(layout, length):
    width, hidden = layout[:2]
    bf16, f32 = jnp.bfloat16, jnp.float32
    return [
        ((1, 6 * width), f32),
        ((length, 3 * width), bf16),
        ((length, width), bf16),
        ((length, hidden), bf16),
        ((HEADS, length, length), f32),
        ((length, hidden), f32),
        ((length, width), f32),
        ((length, width), f32),
        ((hidden, width), bf16),
    ]


def section_kernel(layout, forward, backward, after, *refs):
    width, hidden, rows, ratio, ring_size, share, bias_count = layout
    refs = list(refs)

    def take(count):
        taken = refs[:count]
        del refs[:count]
        return taken

    rank_ref, x_ref = take(2)
    if forward:
        modulation_ref, bias_ref = take(2)
    else:
        saved = take(9)
    if backward:
        (dy_ref,) = take(1)
    mine_ref, theirs_ref = take(2)
    take(after)
    if forward:
        (y_ref,) = take(1)
    if backward:
        dx_ref, dmod_ref, sums_ref, keep_ref, send_ref = take(5)
    elif forward:
        saved = take(9)
    att_w, out_w, up_w, sems, down_s, block_s = take(6)
    if forward:
        down_p, bias_s = take(2)
    if backward:
        da_s, dqkv_s, row_ref, halves, out_sems = take(5)
    if forward and backward:
        saved = take(9)
    mod_s, qkv_s, att_s, u_s, soft_s, slope_s, one_s, two_s, down_w = saved

    rank = rank_ref[0]
    split = hidden - 2 * width

    def fetches(first, second):
        moves = [
            (first.at[:, : 3 * width], att_w),
            (first.at[:, 3 * width : 4 * width], out_w),
            (first.at[:, 4 * width :], up_w.at[:, :split]),
            (second.at[:, : hidden - split], up_w.at[:, split:]),
        ]
        if forward:
            moves.append((second.at[:, hidden - split :], down_p))
        return [
            pltpu.make_async_copy(source, target, sems.at[i])
            for i, (source, target) in enumerate(moves)
        ]

    @pl.when(rank == 0)
    def _():
        for copy in fetches(mine_ref, theirs_ref):
            copy.start()

    @pl.when(rank != 0)
    def _():
        for copy in fetches(theirs_ref, mine_ref):
            copy.start()

    arrivals = fetches(mine_ref, theirs_ref)

    def part(ref, member, head):
        start = member * width + head * HEAD
        return ref[:, start : start + HEAD]

    x = x_ref[...].astype(jnp.float32)
    normed_one, factor_one = normalize_rows(x)
    if forward:
        for d in range(ring_size):
            bias_s[:, d * bias_count : (d + 1) * bias_count] = bias_ref[d : d + 1, :]
        mod_s[...] = modulation_ref[...] + bias_s[:, : 6 * width]
    shift_one, scale_one, gate_one, shift_two, scale_two, gate_two = [
        mod_s[:, i * width : (i + 1) * width] for i in range(6)
    ]
    hidden_one = low(normed_one * (1.0 + scale_one) + shift_one)
    if forward:

        def bias(a, b):
            return bias_s[:, a:b]

        at = 6 * width
        arrivals[0].wait()
        qkv_s[:, :width] = low(matmul(hidden_one, att_w[:, :width]) + bias(at, at + width))
        qkv_s[:, width : 2 * width] = low(matmul(hidden_one, att_w[:, width : 2 * width]))
        qkv_s[:, 2 * width :] = low(
            matmul(hidden_one, att_w[:, 2 * width :]) + bias(at + width, at + 2 * width)
        )
        for head in range(HEADS):
            scores = matmul_transposed(part(qkv_s, 0, head), part(qkv_s, 1, head)) * SCALE
            raised = jnp.exp(scores - jnp.max(scores, axis=-1, keepdims=True))
            soft = raised * (1.0 / jnp.sum(raised, axis=-1, keepdims=True))
            soft_s[head] = soft
            attended = matmul(low(soft), part(qkv_s, 2, head))
            att_s[:, head * HEAD : (head + 1) * HEAD] = low(attended)
        arrivals[1].wait()
        one_s[...] = matmul(att_s[...], out_w[...]) + bias(at + 2 * width, at + 3 * width)
    branch_one = one_s[...]
    middle = x + gate_one * branch_one
    normed_two, factor_two = normalize_rows(middle)
    hidden_two = low(normed_two * (1.0 + scale_two) + shift_two)
    if forward:
        arrivals[2].wait()
        arrivals[3].wait()
        at += 3 * width
        for j in range(ratio):
            cut = slice(j * width, (j + 1) * width)
            a = matmul(hidden_two, up_w[:, cut]) + bias(at + j * width, at + (j + 1) * width)
            square = a * a
            turn = jnp.tanh(INNER * (a + CUBE * (a * square)))
            half_one = 0.5 * (1.0 + turn)
            u_s[:, cut] = low(a * half_one)
            slope_s[:, cut] = half_one + (0.5 * INNER) * a * (1.0 - turn * turn) * (
                1.0 + (3.0 * CUBE) * square
            )
        arrivals[4].wait()
        block_s[...] = down_p[...].astype(jnp.float32)
        for d in range(ring_size):
            for j in range(ratio):
                down_s[(d * ratio + j) * rows : (d * ratio + j + 1) * rows, :] = block_s[
                    d * rows : (d + 1) * rows, j * width : (j + 1) * width
                ]
        down_w[...] = low(down_s[...])
        two_s[...] = matmul(u_s[...], down_w[...]) + bias(at + hidden, at + hidden + width)
        y_ref[...] = low(middle + gate_two * two_s[...])
    if not backward:
        return

    grad_out = dy_ref[...].astype(jnp.float32)
    grad_branch = low(gate_two * grad_out)
    sums_at = 6 * width
    row_ref[:, 5 * width : 6 * width] = column_sum(grad_out * two_s[...])
    row_ref[:, sums_at + 3 * width + hidden : sums_at + 4 * width + hidden] = column_sum(
        grad_branch
    )
    for j in range(ratio):
        cut = slice(j * width, (j + 1) * width)
        grad_expanded = low(slope_s[:, cut] * matmul_transposed(grad_branch, down_w[cut, :]))
        da_s[:, cut] = grad_expanded
        row_ref[:, sums_at + (3 + j) * width : sums_at + (4 + j) * width] = column_sum(
            grad_expanded
        )
    halves[0, :, 4 * width :] = low(outer_sum(hidden_two, da_s[:, :split]) * share)
    halves[1, :, : hidden - split] = low(outer_sum(hidden_two, da_s[:, split:]) * share)
    down_s[...] = outer_sum(u_s[...], grad_branch) * share
    for d in range(ring_size):
        for j in range(ratio):
            block_s[d * rows : (d + 1) * rows, j * width : (j + 1) * width] = down_s[
                (d * ratio + j) * rows : (d * ratio + j + 1) * rows, :
            ]
    halves[1, :, hidden - split :] = low(block_s[...])
    second_out = [
        pltpu.make_async_copy(halves.at[1], keep_ref, out_sems.at[1]),
        pltpu.make_async_copy(halves.at[1], send_ref, out_sems.at[1]),
    ]

    @pl.when(rank == 1)
    def _():
        second_out[0].start()

    @pl.when(rank != 1)
    def _():
        second_out[1].start()

    if not forward:
        arrivals[2].wait()
        arrivals[3].wait()
    grad_hidden_two = matmul_transposed(da_s[...], up_w[...])
    row_ref[:, 3 * width : 4 * width] = column_sum(grad_hidden_two)
    row_ref[:, 4 * width : 5 * width] = column_sum(grad_hidden_two * normed_two)
    grad_middle = grad_out + normalize_back(
        normed_two, factor_two, grad_hidden_two * (1.0 + scale_two)
    )
    row_ref[:, 2 * width : 3 * width] = column_sum(grad_middle * branch_one)
    grad_attention = low(gate_one * grad_middle)
    row_ref[:, sums_at + 2 * width : sums_at + 3 * width] = column_sum(grad_attention)
    halves[0, :, 3 * width : 4 * width] = low(outer_sum(att_s[...], grad_attention) * share)
    if not forward:
        arrivals[1].wait()
    grad_attended = low(matmul_transposed(grad_attention, out_w[...]))
    for head in range(HEADS):
        soft = soft_s[head]
        grad_head = grad_attended[:, head * HEAD : (head + 1) * HEAD]
        grad_soft = matmul_transposed(grad_head, part(qkv_s, 2, head))
        inner = jnp.sum(grad_soft * soft, axis=-1, keepdims=True)
        grad_scores = low(soft * (grad_soft - inner))
        grads = (
            matmul(grad_scores, part(qkv_s, 1, head)) * SCALE,
            outer_sum(grad_scores, part(qkv_s, 0, head)) * SCALE,
            outer_sum(low(soft), grad_head),
        )
        for member, grad in enumerate(grads):
            start = member * width + head * HEAD
            dqkv_s[:, start : start + HEAD] = low(grad)
    row_ref[:, sums_at : sums_at + width] = column_sum(dqkv_s[:, :width])
    row_ref[:, sums_at + width : sums_at + 2 * width] = column_sum(dqkv_s[:, 2 * width :])
    halves[0, :, : 3 * width] = low(outer_sum(hidden_one, dqkv_s[...]) * share)
    first_out = [
        pltpu.make_async_copy(halves.at[0], keep_ref, out_sems.at[0]),
        pltpu.make_async_copy(halves.at[0], send_ref, out_sems.at[0]),
    ]

    @pl.when(rank == 0)
    def _():
        first_out[0].start()

    @pl.when(rank != 0)
    def _():
        first_out[1].start()

    if not forward:
        arrivals[0].wait()
    grad_hidden_one = matmul_transposed(dqkv_s[...], att_w[...])
    row_ref[:, :width] = column_sum(grad_hidden_one)
    row_ref[:, width : 2 * width] = column_sum(grad_hidden_one * normed_one)
    dx_ref[...] = low(
        grad_middle
        + normalize_back(normed_one, factor_one, grad_hidden_one * (1.0 + scale_one))
    )
    row_ref[:, : 6 * width] = low(row_ref[:, : 6 * width]).astype(jnp.float32)
    dmod_ref[...] = row_ref[:, : 6 * width]
    for d in range(ring_size):
        sums_ref[d : d + 1, :] = row_ref[:, d * bias_count : (d + 1) * bias_count]
    second_out[0].wait()
    first_out[0].wait()


def run_section(layout, rank, x, halves, start=None, saved=None, dy=None, after=()):
    width, hidden, rows, ratio, ring_size, share, bias_count = layout
    length = x.shape[0]
    forward, backward = start is not None, dy is not None
    vmem = pl.BlockSpec(memory_space=pltpu.VMEM)
    hbm = pl.BlockSpec(memory_space=pl.ANY)
    bf16, f32 = jnp.bfloat16, jnp.float32
    half = 2 * width + hidden
    kept = saved_shapes(layout, length)
    operands = [rank, x, *(start if forward else saved)]
    shapes, out_specs = [], []
    scratch = [
        pltpu.VMEM((width, 3 * width), bf16),
        pltpu.VMEM((width, width), bf16),
        pltpu.VMEM((width, hidden), bf16),
        pltpu.SemaphoreType.DMA((5,)),
        pltpu.VMEM((hidden, width), f32),
        pltpu.VMEM((width, hidden), f32),
    ]
    if forward:
        shapes.append(jax.ShapeDtypeStruct((length, width), bf16))
        scratch += [
            pltpu.VMEM((width, hidden), bf16),
            pltpu.VMEM((1, bias_count * ring_size), f32),
        ]
    if backward:
        operands.append(dy)
        shapes += [
            jax.ShapeDtypeStruct((length, width), bf16),
            jax.ShapeDtypeStruct((1, 6 * width), f32),
            jax.ShapeDtypeStruct((ring_size, bias_count), f32),
            jax.ShapeDtypeStruct((width, half), bf16),
            jax.ShapeDtypeStruct((width, half), bf16),
        ]
        scratch += [
            pltpu.VMEM((length, hidden), bf16),
            pltpu.VMEM((length, 3 * width), bf16),
            pltpu.VMEM((1, 10 * width + hidden), f32),
            pltpu.VMEM((2, width, half), bf16),
            pltpu.SemaphoreType.DMA((2,)),
        ]
        if forward:
            scratch += [pltpu.VMEM(extent, kind) for extent, kind in kept]
    else:
        shapes += [jax.ShapeDtypeStruct(extent, kind) for extent, kind in kept]
    out_specs = [vmem] * len(shapes)
    if backward:
        out_specs[-2:] = [hbm, hbm]
    specs = [pl.BlockSpec(memory_space=pltpu.SMEM)] + [vmem] * (len(operands) - 1)
    specs += [hbm] * (2 + len(after))
    work = 2 * length * width * (4 * width + 2 * hidden + 2 * length)
    moved = 2 * width * (10 * width + 2 * hidden)
    return pl.pallas_call(
        partial(section_kernel, layout, forward, backward, len(after)),
        out_shape=shapes,
        in_specs=specs,
        out_specs=out_specs,
        scratch_shapes=scratch,
        compiler_params=pltpu.CompilerParams(
            vmem_limit_bytes=(36 if length <= 256 else 56) * 1024 * 1024
        ),
        cost_estimate=pl.CostEstimate(
            flops=(forward + 2 * backward) * work,
            bytes_accessed=(1 + backward) * moved,
            transcendentals=HEADS * length * length + length * hidden,
        ),
    )(*operands, *halves, *after)


def copy_all(copies):
    for copy in copies:
        copy.start()
    for copy in copies:
        copy.wait()


def pack_kernel(rank_ref, att_ref, out_ref, up_ref, down_ref, keep_ref, send_ref, sems):
    ratio, rows, width = down_ref.shape
    split = (ratio - 2) * width

    def copies(first, second):
        moves = [
            (att_ref, first.at[:, : 3 * width]),
            (out_ref, first.at[:, 3 * width : 4 * width]),
            (up_ref.at[:, :split], first.at[:, 4 * width :]),
            (up_ref.at[:, split:], second.at[:, : 2 * width]),
        ]
        for j in range(ratio):
            moves.append((down_ref.at[j], second.at[:, (2 + j) * width : (3 + j) * width]))
        return [
            pltpu.make_async_copy(source, target, sems.at[i])
            for i, (source, target) in enumerate(moves)
        ]

    @pl.when(rank_ref[0] == 0)
    def _():
        copy_all(copies(keep_ref, send_ref))

    @pl.when(rank_ref[0] != 0)
    def _():
        copy_all(copies(send_ref, keep_ref))


def stack_kernel(high, split, place_ref, *refs):
    pieces, sems = refs[:high], refs[-1]
    count = (len(refs) - high - 3) // 2
    handed, targets = refs[high : high + count], refs[high + count : -1]
    copies = [
        pltpu.make_async_copy(former, latter, sems.at[high + i, 0])
        for i, (former, latter) in enumerate(zip(handed, targets[2:]))
    ]
    for turn, piece in enumerate(pieces):
        place = lax.rem(place_ref[0] + (high - turn), high)
        parts = (piece.at[:, :split], piece.at[:, split:])
        for i, (part, target) in enumerate(zip(parts, targets)):
            copies.append(pltpu.make_async_copy(part, target.at[place], sems.at[turn, i]))
    copy_all(copies)


def weave_kernel(split, place_ref, *refs):
    pieces, full_ref, sems = refs[:-2], refs[-2], refs[-1]
    x, y = place_ref[1], place_ref[2]
    copies = []
    for i, piece in enumerate(pieces):
        other_x, other_y = (i % 4) & 1, (i % 4) >> 1
        row = x if not other_x else 1 - x
        column = y if not other_y else 1 - y
        target = full_ref.at[:, row, column, :, pl.ds((i // 4) * split, split)]
        copies.append(pltpu.make_async_copy(piece, target, sems.at[i]))
    copy_all(copies)


def added(former, latter):
    return former.astype(jnp.float32) + latter.astype(jnp.float32)


def chip_sum_kernel(high, place_ref, mine, got, *refs):
    count = (len(refs) - 4) // 2
    first_keep, first_send, second_keep, second_send = refs[count : count + 4]
    for former, latter in zip(refs[:count], refs[count + 4 :]):
        latter[...] = former[...]
    x, y = place_ref[1], place_ref[2]
    half = mine.shape[2]
    lanes = half // 2
    for z in range(high):
        for other in range(2):
            for target, span, chunk in (
                (first_keep, slice(0, lanes), z * 4 + x * 2 + other),
                (first_send, slice(0, lanes), z * 4 + (1 - x) * 2 + other),
                (second_keep, slice(lanes, half), z * 4 + other * 2 + y),
                (second_send, slice(lanes, half), z * 4 + other * 2 + (1 - y)),
            ):
                target[z, other] = low(added(mine[chunk, :, span], got[chunk, :, span]))


def turn_kernel(high, place_ref, *refs):
    for part, own in ((0, place_ref[2]), (1, place_ref[1])):
        kept, got = refs[2 * part : 2 * part + 2]
        keep, send = refs[4 + 2 * part : 6 + 2 * part]
        for z in range(high):
            keep[z] = low(added(kept[z, own], got[z, own]))
            send[z] = low(added(kept[z, 1 - own], got[z, 1 - own]))


def rise_kernel(high, place_ref, *refs):
    targets = refs[4:]
    lanes = refs[0].shape[2]
    for turn in range(high):
        chunk = lax.rem(place_ref[0] + turn, high)
        for part in range(2):
            kept, got = refs[2 * part : 2 * part + 2]
            total = added(kept[chunk], got[chunk])
            span = slice(part * lanes, (part + 1) * lanes)
            targets[turn][:, span] = total.astype(targets[turn].dtype)


def close_kernel(high, rank_ref, *refs):
    keep, send = refs[-2:]
    totals = []
    for section in range(2):
        pieces = refs[section * high : (section + 1) * high]
        total = pieces[0][...].astype(jnp.float32)
        for piece in pieces[1:]:
            total = total + piece[...].astype(jnp.float32)
        totals.append(total)
    first = rank_ref[0] == 0
    keep[...] = jnp.where(first, totals[0], totals[1])
    send[...] = jnp.where(first, totals[1], totals[0])


def spread_kernel(rank_ref, mine, got, att_ref, out_ref, up_ref, down_ref):
    rows, width = out_ref.shape
    split = up_ref.shape[1] - 2 * width
    first = rank_ref[0] == 0
    lower = jnp.where(first, mine[...], got[...])
    upper = jnp.where(first, got[...], mine[...])
    att_ref[...] = lower[:, : 3 * width]
    out_ref[...] = lower[:, 3 * width : 4 * width]
    up_ref[:, :split] = lower[:, 4 * width :]
    up_ref[:, split:] = upper[:, : 2 * width]
    for j in range(down_ref.shape[0] // rows):
        down_ref[j * rows : (j + 1) * rows, :] = upper[:, (2 + j) * width : (3 + j) * width]


def in_memory(kernel, shapes, operands, scratch=(), memory=pltpu.VMEM, after=(), limit=32):
    specs = [pl.BlockSpec(memory_space=pltpu.SMEM)]
    specs += [pl.BlockSpec(memory_space=memory)] * (len(operands) - 1)
    specs += [pl.BlockSpec(memory_space=pl.ANY)] * len(after)
    count = len(operands)

    def body(*refs):
        kernel(*refs[:count], *refs[count + len(after) :])

    moved = sum(shape.size * shape.dtype.itemsize for shape in shapes)
    return pl.pallas_call(
        body,
        out_shape=shapes,
        in_specs=specs,
        out_specs=[pl.BlockSpec(memory_space=pltpu.VMEM)] * len(shapes),
        scratch_shapes=list(scratch),
        compiler_params=pltpu.CompilerParams(vmem_limit_bytes=limit * 1024 * 1024),
        cost_estimate=pl.CostEstimate(flops=0, bytes_accessed=3 * moved, transcendentals=0),
    )(*operands, *after)


def pair_swap(block, axis):
    return lax.ppermute(block, axis, [(0, 1), (1, 0)])


def ring_exchange(block, size, step):
    return lax.ppermute(block, RING, [(i, step(i)) for i in range(size)])


def flip(block, size, mask):
    return ring_exchange(block, size, lambda i: i ^ mask)


def rotate(block, size, turn):
    return ring_exchange(block, size, lambda i: (i + 4 * turn) % size)


def rotations(block, size):
    return [block] + [rotate(block, size, turn) for turn in range(1, size // 4)]


def gather_along_z(shard, place, size, handed=(), after=()):
    high = size // 4
    rows, lanes = shard.shape
    return in_memory(
        partial(stack_kernel, high, lanes // 2),
        [jax.ShapeDtypeStruct((high, rows, lanes // 2), shard.dtype)] * 2
        + [jax.ShapeDtypeStruct(block.shape, block.dtype) for block in handed],
        [place, *rotations(shard, size), *handed],
        scratch=[pltpu.SemaphoreType.DMA((high + len(handed), 2))],
        after=after,
    )


def first_flips(first, second, size):
    return flip(first, size, 2), flip(second, size, 1)


def gather_across(first, second, first_x, second_y, place, size):
    high, rows, lanes = first.shape
    first_y, second_x = flip(first, size, 1), flip(second, size, 2)
    first_both, second_both = flip(first_x, size, 1), flip(second_y, size, 2)
    (full,) = in_memory(
        partial(weave_kernel, lanes),
        [jax.ShapeDtypeStruct((high, 2, 2, rows, 2 * lanes), first.dtype)],
        [place, first, first_x, first_y, first_both, second, second_x, second_y, second_both],
        scratch=[pltpu.SemaphoreType.DMA((8,))],
    )
    return full.reshape(size * rows, 2 * lanes)


def scatter_first(mine, got, place, size, handed=(), after=()):
    rows, half = mine.shape[1:]
    shape = jax.ShapeDtypeStruct((size // 4, 2, rows, half // 2), jnp.bfloat16)
    return in_memory(
        partial(chip_sum_kernel, size // 4),
        [shape] * 4 + [jax.ShapeDtypeStruct(block.shape, block.dtype) for block in handed],
        [place, mine, got, *handed],
        after=after,
    )


def scatter_flips(sorted_terms, size):
    first_keep, first_send, second_keep, second_send = sorted_terms
    return first_keep, flip(first_send, size, 2), second_keep, flip(second_send, size, 1)


def scatter_second(received, place, size, after=()):
    high, _, rows, lanes = received[0].shape
    shape = jax.ShapeDtypeStruct((high, rows, lanes), jnp.bfloat16)
    return in_memory(
        partial(turn_kernel, high), [shape] * 4, [place, *received], after=after
    )


def scatter_rest(turned, place, size):
    high, rows, lanes = turned[0].shape
    first_keep, first_send, second_keep, second_send = turned
    first_got, second_got = flip(first_send, size, 1), flip(second_send, size, 2)
    chunk = (rows, 2 * lanes)
    own, *sent = in_memory(
        partial(rise_kernel, high),
        [jax.ShapeDtypeStruct(chunk, jnp.float32)]
        + [jax.ShapeDtypeStruct(chunk, jnp.bfloat16)] * (high - 1),
        [place, first_keep, first_got, second_keep, second_got],
    )
    return [own] + [rotate(block, size, turn + 1) for turn, block in enumerate(sent)]


def scatter_sum(block, rank, size):
    half = block.shape[-1] // 2
    pieces = [block[..., :half], block[..., half:]]
    left = size
    low_bits = 0
    while left > 4:
        orders = [(0, 1), (1, 0)] if left % 4 == 0 and left >= 16 else [(0,), (0,)]
        for turn in range(len(orders[0])):
            updated = []
            for piece, order in zip(pieces, orders):
                bit = low_bits + order[turn]
                mine = (rank >> bit) & 1
                if len(order) == 2 and turn == 0:
                    shaped = piece.reshape(-1, 2, 2, *piece.shape[1:])
                    at = 2 - order[turn]
                else:
                    shaped = piece.reshape(-1, 2, *piece.shape[1:])
                    at = 1
                keep = lax.dynamic_index_in_dim(shaped, mine, at, keepdims=False)
                send = lax.dynamic_index_in_dim(shaped, 1 - mine, at, keepdims=False)
                got = ring_exchange(send, size, lambda i, bit=bit: i ^ (1 << bit))
                total = (keep.astype(jnp.float32) + got.astype(jnp.float32)).astype(jnp.bfloat16)
                updated.append(total.reshape(-1, *piece.shape[1:]))
            pieces = updated
        low_bits += len(orders[0])
        left //= 2 ** len(orders[0])
    block = jnp.concatenate(pieces, axis=-1)
    high = rank >> low_bits
    total = lax.dynamic_index_in_dim(block, high, 0, keepdims=False).astype(jnp.float32)
    stride = 1 << low_bits
    for turn in range(1, left):
        send = lax.dynamic_index_in_dim(block, (high + turn) % left, 0, keepdims=False)
        got = ring_exchange(send, size, lambda i, turn=turn: (i + turn * stride) % size)
        total = total + got.astype(jnp.float32)
    return total


def per_device(
    inputs,
    cotangent,
    time_ids,
    row_counts,
    cond_table,
    modulation_weight,
    attention_weight,
    output_weight,
    expand_weight,
    shrink_weight,
    biases,
):
    section_rank = lax.axis_index("section")
    data_rank = lax.axis_index("dp")
    seq_rank = lax.axis_index("seq")
    sections = lax.axis_size("section")
    seq_size = lax.axis_size("seq")
    ring_size = lax.axis_size("dp") * seq_size
    ring_rank = data_rank * seq_size + seq_rank
    batches, slots, tokens, width = inputs.shape
    assert batches == sections == 2 and seq_size % slots == 0
    sharers = seq_size // slots
    slot = seq_rank // sharers
    length = tokens * seq_size
    rows = attention_weight.shape[1]
    ratio = shrink_weight.shape[1] // rows
    hidden = ratio * width
    bias_count = biases.shape[1]
    half = 2 * width + hidden
    assert hidden == expand_weight.shape[2] and ratio >= 2
    table_rows = cond_table.shape[0]
    is_first = section_rank == 0
    layout = (width, hidden, rows, ratio, ring_size, 1.0 / sharers, bias_count)
    compact = ring_size in (8, 16) and seq_size == slots == 2
    rank = section_rank.astype(jnp.int32).reshape(1)
    place = jnp.stack([ring_rank >> 2, (ring_rank >> 1) & 1, ring_rank & 1]).astype(jnp.int32)

    keep, send = in_memory(
        pack_kernel,
        [jax.ShapeDtypeStruct((rows, half), jnp.bfloat16)] * 2,
        [
            rank,
            attention_weight[0],
            output_weight[0],
            expand_weight[0],
            shrink_weight[0].reshape(ratio, rows, width),
        ],
        scratch=[pltpu.SemaphoreType.DMA((4 + ratio,))],
        memory=pl.ANY,
        limit=56,
    )
    got = pair_swap(send, "section")
    first_shard = jnp.where(is_first, keep, got)
    second_shard = jnp.where(is_first, got, keep)

    live = (
        slot < lax.dynamic_index_in_dim(row_counts, section_rank, 0, keepdims=False)[0]
    ).astype(jnp.bfloat16)
    both = jnp.stack(
        [
            lax.dynamic_index_in_dim(inputs, section_rank, 0, keepdims=False),
            lax.dynamic_index_in_dim(cotangent, section_rank, 0, keepdims=False),
        ],
        axis=1,
    )

    def side_by_side(mine, got, axis):
        return jnp.where(
            seq_rank == 0,
            jnp.concatenate([mine, got], axis=axis),
            jnp.concatenate([got, mine], axis=axis),
        )

    if compact:
        mine = lax.dynamic_index_in_dim(both, seq_rank, 0, keepdims=False)
        sent = lax.dynamic_index_in_dim(both, 1 - seq_rank, 0, keepdims=False)
        both = side_by_side(mine, pair_swap(sent, "seq"), 1)
    else:
        both = lax.all_to_all(jnp.repeat(both, sharers, axis=0), "seq", 0, 0, tiled=True)
        both = jnp.swapaxes(both, 0, 1).reshape(2, length, width)
    first_input = both[0]
    last_grad = both[1] * live

    flat_ids = time_ids.reshape(-1)
    selector = (
        flat_ids[:, None] == jnp.arange(table_rows, dtype=jnp.int32)[None, :]
    ).astype(jnp.bfloat16)
    conditions = matmul(selector, cond_table)
    silu_all = jax.nn.silu(conditions).astype(jnp.bfloat16)
    silu_own = lax.dynamic_slice_in_dim(silu_all, ring_rank * rows, rows, 1)
    if compact:
        *first_parts, second_shard, silu_late = gather_along_z(
            first_shard, place, ring_size, handed=(second_shard, silu_own)
        )
        first_parts += first_flips(*first_parts, ring_size)
        second_parts = gather_along_z(
            second_shard, place, ring_size, after=(both, *first_parts[2:])
        )
        second_parts += first_flips(*second_parts, ring_size)
        first_pack = gather_across(*first_parts, place, ring_size)
        second_pack = gather_across(*second_parts, place, ring_size)
    else:
        silu_late = silu_own
        first_pack = lax.all_gather(first_shard, RING, axis=0, tiled=True)
        second_pack = lax.all_gather(second_shard, RING, axis=0, tiled=True)
    first_halves = (first_pack, pair_swap(first_pack, "section"))
    second_halves = (second_pack, pair_swap(second_pack, "section"))

    products = matmul(silu_late, modulation_weight[0])
    own_bias = jnp.broadcast_to(biases.astype(jnp.float32), (products.shape[0], bias_count))
    products = jnp.repeat(jnp.concatenate([products, own_bias], axis=1), sharers, axis=0)
    products = lax.all_to_all(
        products[:, None], ("section", "dp", "seq"), 0, 0, tiled=True
    ).reshape(sections, ring_size, 6 * width + bias_count)
    first_modulation, second_modulation = jnp.split(
        jnp.sum(products[:, :, : 6 * width], axis=1), 2, axis=0
    )
    first_bias, second_bias = products[0, :, 6 * width :], products[1, :, 6 * width :]


    first_low, *first_saved = run_section(
        layout, rank, first_input, first_halves, (first_modulation, first_bias)
    )
    second_low, second_grad, second_dmod, second_sums, second_keep, second_send = run_section(
        layout, rank, first_low, second_halves, (second_modulation, second_bias), dy=last_grad
    )
    second_got = pair_swap(second_send, "section")

    def ring_terms(term):
        return term.reshape(ring_size, rows, half)

    early = jnp.stack([first_low * live, second_low * live, second_grad])

    def to_slots(block):
        block = block.reshape(-1, 2, tokens, width)
        mine = lax.dynamic_index_in_dim(block, seq_rank, 1, keepdims=True)
        sent = lax.dynamic_index_in_dim(block, 1 - seq_rank, 1, keepdims=True)
        return mine, pair_swap(sent, "seq")

    if compact:
        early = to_slots(early)
    first_grad, first_dmod, first_sums, first_keep, first_send = run_section(
        layout, rank, first_input, first_halves, saved=first_saved, dy=second_grad
    )
    first_got = pair_swap(first_send, "section")

    shard = jax.ShapeDtypeStruct((rows, half), jnp.float32)
    if compact:
        second_sorted = scatter_first(
            ring_terms(second_keep),
            ring_terms(second_got),
            place,
            ring_size,
            after=(early[1],),
        )
        second_received = scatter_flips(second_sorted, ring_size)
        second_turned = scatter_second(second_received, place, ring_size)
        *first_sorted, first_grad, first_dmod, first_sums = scatter_first(
            ring_terms(first_keep),
            ring_terms(first_got),
            place,
            ring_size,
            handed=(first_grad, first_dmod, first_sums),
            after=(second_sorted[0],),
        )
        first_turned = scatter_second(scatter_flips(first_sorted, ring_size), place, ring_size)
        second_pieces = scatter_rest(second_turned, place, ring_size)
        first_pieces = scatter_rest(first_turned, place, ring_size)
    else:

        def chip_sum(keep, got):
            return ring_terms(low(added(keep, got)))

        first_pieces, second_pieces = [
            [scatter_sum(chip_sum(keep, got), ring_rank, ring_size)]
            for keep, got in ((first_keep, first_got), (second_keep, second_got))
        ]
    if compact:
        early_full, late = side_by_side(*early, 1), side_by_side(*to_slots(first_grad), 1)
        per_first = jnp.stack([early_full[0], late[0]])
        per_second = early_full[1:]
        mine = jnp.where(is_first, per_first, per_second)
        got = pair_swap(jnp.where(is_first, per_second, per_first), "section")
        outputs = jnp.where(is_first, jnp.stack([mine, got], 1), jnp.stack([got, mine], 1))
    else:
        pieces = jnp.stack([early[0], first_grad, early[1], early[2]])
        pieces = jnp.swapaxes(pieces.reshape(2, 2, seq_size, tokens, width), 1, 2)
        pieces = pieces.reshape(2 * seq_size, 2, tokens, width)
        pieces = lax.all_to_all(pieces, ("section", "seq"), 0, 0, tiled=True)
        pieces = pieces.reshape(batches, slots, sharers, 2, tokens, width)[:, :, 0]
        outputs = jnp.moveaxis(pieces, 2, 0)
    activations = outputs[0]
    input_grads = outputs[1].astype(jnp.float32)

    mine, send = in_memory(
        partial(close_kernel, len(first_pieces)),
        [shard, shard],
        [rank, *first_pieces, *second_pieces],
    )
    att, out, up, down = in_memory(
        spread_kernel,
        [
            jax.ShapeDtypeStruct(extent, jnp.float32)
            for extent in (
                (rows, 3 * width),
                (rows, width),
                (rows, hidden),
                (rows * ratio, width),
            )
        ],
        [rank, mine, pair_swap(send, "section")],
    )

    rows_back = jnp.concatenate(
        [
            jnp.concatenate(
                [jnp.broadcast_to(dmod, (ring_size, 6 * width)), sums], axis=1
            )
            for dmod, sums in ((first_dmod, first_sums), (second_dmod, second_sums))
        ]
    )
    every = lax.all_to_all(rows_back[:, None], ("section", "dp", "seq"), 0, 0, tiled=True)
    every = every[::sharers, 0]
    bias_grad = jnp.sum(every[:, 6 * width :], axis=0)
    modulation_rows = low(every[:, : 6 * width])
    modulation_grad = outer_sum(silu_own, modulation_rows)
    columns = matmul_transposed(modulation_rows, modulation_weight[0])
    columns = jnp.broadcast_to(columns.reshape(1, 1, -1), (sections * ring_size, 1, columns.size))
    columns = lax.all_to_all(columns, ("section", "dp", "seq"), 0, 0, tiled=True)
    columns = jnp.sum(columns.reshape(sections, ring_size, -1, rows), axis=0)
    products_back = jnp.swapaxes(columns, 0, 1).reshape(-1, width)
    _, silu_back = jax.vjp(jax.nn.silu, conditions)
    table_grad = lax.dot_general(
        selector.astype(jnp.float32),
        silu_back(products_back)[0],
        (((0,), (0,)), ((), ())),
        precision=lax.Precision.HIGHEST,
        preferred_element_type=jnp.float32,
    )
    return (
        activations[None],
        input_grads[None],
        table_grad,
        modulation_grad[None],
        att[None],
        out[None],
        up[None],
        down[None],
        bias_grad[None],
    )


def solution(mesh):
    shard = P("section", ("dp", "seq"), None)
    in_specs = (
        P(None, "dp", "seq", None),
        P(None, "dp", "seq", None),
        P(),
        P(None, "dp"),
        P(),
        shard,
        shard,
        shard,
        shard,
        shard,
        P("section", ("dp", "seq")),
    )
    out_specs = (
        P("section", None, "dp", "seq", None),
        P("section", None, "dp", "seq", None),
        P(),
        shard,
        shard,
        shard,
        shard,
        shard,
        P("section", ("dp", "seq")),
    )
    return jax.shard_map(
        per_device, mesh=mesh, in_specs=in_specs, out_specs=out_specs, check_vma=False
    )
```

```python
from functools import partial

import jax
import jax.numpy as jnp
from jax import lax
from jax.experimental import pallas as pl
from jax.experimental.pallas import tpu as pltpu
from jax.sharding import PartitionSpec as P

HEADS = 6
HEAD = 64
SCALE = HEAD ** (-0.5)
epsilon = 1e-06
RING = ("dp", "seq")
INNER = (2.0 / 3.141592653589793) ** 0.5
CUBE = 0.044715


def matmul(former, latter):
    return jnp.dot(former, latter, preferred_element_type=jnp.float32)


def matmul_transposed(former, latter):
    return lax.dot_general(
        former, latter, (((1,), (1,)), ((), ())), preferred_element_type=jnp.float32
    )


def outer_sum(former, latter):
    return lax.dot_general(
        former, latter, (((0,), (0,)), ((), ())), preferred_element_type=jnp.float32
    )


def low(values):
    return values.astype(jnp.bfloat16)


def normalize_rows(values):
    centre = jnp.mean(values, axis=-1, keepdims=True)
    centred = values - centre
    spread = jnp.mean(centred * centred, axis=-1, keepdims=True)
    factor = lax.rsqrt(spread + epsilon)
    return (centred * factor, factor)


def normalize_back(normed, factor, grad_normed):
    mean_grad = jnp.mean(grad_normed, axis=-1, keepdims=True)
    mean_cross = jnp.mean(grad_normed * normed, axis=-1, keepdims=True)
    return factor * (grad_normed - mean_grad - normed * mean_cross)


def column_sum(values):
    return jnp.sum(values.astype(jnp.float32), axis=0, keepdims=True)


def saved_shapes(layout, length):
    width, hidden = layout[:2]
    bf16, f32 = jnp.bfloat16, jnp.float32
    return [
        ((1, 6 * width), f32),
        ((length, 3 * width), bf16),
        ((length, width), bf16),
        ((length, hidden), bf16),
        ((HEADS, length, length), f32),
        ((length, hidden), f32),
        ((length, width), f32),
        ((length, width), f32),
        ((hidden, width), bf16),
    ]


def section_kernel(layout, forward, backward, after, *refs):
    width, hidden, rows, ratio, ring_size, share, bias_count = layout
    refs = list(refs)

    def take(count):
        taken = refs[:count]
        del refs[:count]
        return taken

    rank_ref, x_ref = take(2)
    if forward:
        modulation_ref, bias_ref = take(2)
    else:
        saved = take(9)
    if backward:
        (dy_ref,) = take(1)
    mine_ref, theirs_ref = take(2)
    take(after)
    if forward:
        (y_ref,) = take(1)
    if backward:
        dx_ref, dmod_ref, sums_ref, keep_ref, send_ref = take(5)
    elif forward:
        saved = take(9)
    att_w, out_w, up_w, sems, down_s, block_s = take(6)
    if forward:
        down_p, bias_s = take(2)
    if backward:
        da_s, dqkv_s, row_ref, halves, out_sems = take(5)
    if forward and backward:
        saved = take(9)
    mod_s, qkv_s, att_s, u_s, soft_s, slope_s, one_s, two_s, down_w = saved

    rank = rank_ref[0]
    split = hidden - 2 * width

    def fetches(first, second):
        moves = [
            (first.at[:, : 3 * width], att_w),
            (first.at[:, 3 * width : 4 * width], out_w),
            (first.at[:, 4 * width :], up_w.at[:, :split]),
            (second.at[:, : hidden - split], up_w.at[:, split:]),
        ]
        if forward:
            moves.append((second.at[:, hidden - split :], down_p))
        return [
            pltpu.make_async_copy(source, target, sems.at[i])
            for i, (source, target) in enumerate(moves)
        ]

    @pl.when(rank == 0)
    def _():
        for copy in fetches(mine_ref, theirs_ref):
            copy.start()

    @pl.when(rank != 0)
    def _():
        for copy in fetches(theirs_ref, mine_ref):
            copy.start()

    arrivals = fetches(mine_ref, theirs_ref)

    def part(ref, member, head):
        start = member * width + head * HEAD
        return ref[:, start : start + HEAD]

    x = x_ref[...].astype(jnp.float32)
    normed_one, factor_one = normalize_rows(x)
    if forward:
        for d in range(ring_size):
            bias_s[:, d * bias_count : (d + 1) * bias_count] = bias_ref[d : d + 1, :]
        mod_s[...] = modulation_ref[...] + bias_s[:, : 6 * width]
    shift_one, scale_one, gate_one, shift_two, scale_two, gate_two = [
        mod_s[:, i * width : (i + 1) * width] for i in range(6)
    ]
    hidden_one = low(normed_one * (1.0 + scale_one) + shift_one)
    if forward:

        def bias(a, b):
            return bias_s[:, a:b]

        at = 6 * width
        arrivals[0].wait()
        qkv_s[:, :width] = low(matmul(hidden_one, att_w[:, :width]) + bias(at, at + width))
        qkv_s[:, width : 2 * width] = low(matmul(hidden_one, att_w[:, width : 2 * width]))
        qkv_s[:, 2 * width :] = low(
            matmul(hidden_one, att_w[:, 2 * width :]) + bias(at + width, at + 2 * width)
        )
        for head in range(HEADS):
            scores = matmul_transposed(part(qkv_s, 0, head), part(qkv_s, 1, head)) * SCALE
            raised = jnp.exp(scores - jnp.max(scores, axis=-1, keepdims=True))
            soft = raised * (1.0 / jnp.sum(raised, axis=-1, keepdims=True))
            soft_s[head] = soft
            attended = matmul(low(soft), part(qkv_s, 2, head))
            att_s[:, head * HEAD : (head + 1) * HEAD] = low(attended)
        arrivals[1].wait()
        one_s[...] = matmul(att_s[...], out_w[...]) + bias(at + 2 * width, at + 3 * width)
    branch_one = one_s[...]
    middle = x + gate_one * branch_one
    normed_two, factor_two = normalize_rows(middle)
    hidden_two = low(normed_two * (1.0 + scale_two) + shift_two)
    if forward:
        arrivals[2].wait()
        arrivals[3].wait()
        at += 3 * width
        for j in range(ratio):
            cut = slice(j * width, (j + 1) * width)
            a = matmul(hidden_two, up_w[:, cut]) + bias(at + j * width, at + (j + 1) * width)
            square = a * a
            turn = jnp.tanh(INNER * (a + CUBE * (a * square)))
            half_one = 0.5 * (1.0 + turn)
            u_s[:, cut] = low(a * half_one)
            slope_s[:, cut] = half_one + (0.5 * INNER) * a * (1.0 - turn * turn) * (
                1.0 + (3.0 * CUBE) * square
            )
        arrivals[4].wait()
        block_s[...] = down_p[...].astype(jnp.float32)
        for d in range(ring_size):
            for j in range(ratio):
                down_s[(d * ratio + j) * rows : (d * ratio + j + 1) * rows, :] = block_s[
                    d * rows : (d + 1) * rows, j * width : (j + 1) * width
                ]
        down_w[...] = low(down_s[...])
        two_s[...] = matmul(u_s[...], down_w[...]) + bias(at + hidden, at + hidden + width)
        y_ref[...] = low(middle + gate_two * two_s[...])
    if not backward:
        return

    grad_out = dy_ref[...].astype(jnp.float32)
    grad_branch = low(gate_two * grad_out)
    sums_at = 6 * width
    row_ref[:, 5 * width : 6 * width] = column_sum(grad_out * two_s[...])
    row_ref[:, sums_at + 3 * width + hidden : sums_at + 4 * width + hidden] = column_sum(
        grad_branch
    )
    for j in range(ratio):
        cut = slice(j * width, (j + 1) * width)
        grad_expanded = low(slope_s[:, cut] * matmul_transposed(grad_branch, down_w[cut, :]))
        da_s[:, cut] = grad_expanded
        row_ref[:, sums_at + (3 + j) * width : sums_at + (4 + j) * width] = column_sum(
            grad_expanded
        )
    halves[0, :, 4 * width :] = low(outer_sum(hidden_two, da_s[:, :split]) * share)
    halves[1, :, : hidden - split] = low(outer_sum(hidden_two, da_s[:, split:]) * share)
    down_s[...] = outer_sum(u_s[...], grad_branch) * share
    for d in range(ring_size):
        for j in range(ratio):
            block_s[d * rows : (d + 1) * rows, j * width : (j + 1) * width] = down_s[
                (d * ratio + j) * rows : (d * ratio + j + 1) * rows, :
            ]
    halves[1, :, hidden - split :] = low(block_s[...])
    second_out = [
        pltpu.make_async_copy(halves.at[1], keep_ref, out_sems.at[1]),
        pltpu.make_async_copy(halves.at[1], send_ref, out_sems.at[1]),
    ]

    @pl.when(rank == 1)
    def _():
        second_out[0].start()

    @pl.when(rank != 1)
    def _():
        second_out[1].start()

    if not forward:
        arrivals[2].wait()
        arrivals[3].wait()
    grad_hidden_two = matmul_transposed(da_s[...], up_w[...])
    row_ref[:, 3 * width : 4 * width] = column_sum(grad_hidden_two)
    row_ref[:, 4 * width : 5 * width] = column_sum(grad_hidden_two * normed_two)
    grad_middle = grad_out + normalize_back(
        normed_two, factor_two, grad_hidden_two * (1.0 + scale_two)
    )
    row_ref[:, 2 * width : 3 * width] = column_sum(grad_middle * branch_one)
    grad_attention = low(gate_one * grad_middle)
    row_ref[:, sums_at + 2 * width : sums_at + 3 * width] = column_sum(grad_attention)
    halves[0, :, 3 * width : 4 * width] = low(outer_sum(att_s[...], grad_attention) * share)
    if not forward:
        arrivals[1].wait()
    grad_attended = low(matmul_transposed(grad_attention, out_w[...]))
    for head in range(HEADS):
        soft = soft_s[head]
        grad_head = grad_attended[:, head * HEAD : (head + 1) * HEAD]
        grad_soft = matmul_transposed(grad_head, part(qkv_s, 2, head))
        inner = jnp.sum(grad_soft * soft, axis=-1, keepdims=True)
        grad_scores = low(soft * (grad_soft - inner))
        grads = (
            matmul(grad_scores, part(qkv_s, 1, head)) * SCALE,
            outer_sum(grad_scores, part(qkv_s, 0, head)) * SCALE,
            outer_sum(low(soft), grad_head),
        )
        for member, grad in enumerate(grads):
            start = member * width + head * HEAD
            dqkv_s[:, start : start + HEAD] = low(grad)
    row_ref[:, sums_at : sums_at + width] = column_sum(dqkv_s[:, :width])
    row_ref[:, sums_at + width : sums_at + 2 * width] = column_sum(dqkv_s[:, 2 * width :])
    halves[0, :, : 3 * width] = low(outer_sum(hidden_one, dqkv_s[...]) * share)
    first_out = [
        pltpu.make_async_copy(halves.at[0], keep_ref, out_sems.at[0]),
        pltpu.make_async_copy(halves.at[0], send_ref, out_sems.at[0]),
    ]

    @pl.when(rank == 0)
    def _():
        first_out[0].start()

    @pl.when(rank != 0)
    def _():
        first_out[1].start()

    if not forward:
        arrivals[0].wait()
    grad_hidden_one = matmul_transposed(dqkv_s[...], att_w[...])
    row_ref[:, :width] = column_sum(grad_hidden_one)
    row_ref[:, width : 2 * width] = column_sum(grad_hidden_one * normed_one)
    dx_ref[...] = low(
        grad_middle
        + normalize_back(normed_one, factor_one, grad_hidden_one * (1.0 + scale_one))
    )
    row_ref[:, : 6 * width] = low(row_ref[:, : 6 * width]).astype(jnp.float32)
    dmod_ref[...] = row_ref[:, : 6 * width]
    for d in range(ring_size):
        sums_ref[d : d + 1, :] = row_ref[:, d * bias_count : (d + 1) * bias_count]
    second_out[0].wait()
    first_out[0].wait()


def run_section(layout, rank, x, halves, start=None, saved=None, dy=None, after=()):
    width, hidden, rows, ratio, ring_size, share, bias_count = layout
    length = x.shape[0]
    forward, backward = start is not None, dy is not None
    vmem = pl.BlockSpec(memory_space=pltpu.VMEM)
    hbm = pl.BlockSpec(memory_space=pl.ANY)
    bf16, f32 = jnp.bfloat16, jnp.float32
    half = 2 * width + hidden
    kept = saved_shapes(layout, length)
    operands = [rank, x, *(start if forward else saved)]
    shapes, out_specs = [], []
    scratch = [
        pltpu.VMEM((width, 3 * width), bf16),
        pltpu.VMEM((width, width), bf16),
        pltpu.VMEM((width, hidden), bf16),
        pltpu.SemaphoreType.DMA((5,)),
        pltpu.VMEM((hidden, width), f32),
        pltpu.VMEM((width, hidden), f32),
    ]
    if forward:
        shapes.append(jax.ShapeDtypeStruct((length, width), bf16))
        scratch += [
            pltpu.VMEM((width, hidden), bf16),
            pltpu.VMEM((1, bias_count * ring_size), f32),
        ]
    if backward:
        operands.append(dy)
        shapes += [
            jax.ShapeDtypeStruct((length, width), bf16),
            jax.ShapeDtypeStruct((1, 6 * width), f32),
            jax.ShapeDtypeStruct((ring_size, bias_count), f32),
            jax.ShapeDtypeStruct((width, half), bf16),
            jax.ShapeDtypeStruct((width, half), bf16),
        ]
        scratch += [
            pltpu.VMEM((length, hidden), bf16),
            pltpu.VMEM((length, 3 * width), bf16),
            pltpu.VMEM((1, 10 * width + hidden), f32),
            pltpu.VMEM((2, width, half), bf16),
            pltpu.SemaphoreType.DMA((2,)),
        ]
        if forward:
            scratch += [pltpu.VMEM(extent, kind) for extent, kind in kept]
    else:
        shapes += [jax.ShapeDtypeStruct(extent, kind) for extent, kind in kept]
    out_specs = [vmem] * len(shapes)
    if backward:
        out_specs[-2:] = [hbm, hbm]
    specs = [pl.BlockSpec(memory_space=pltpu.SMEM)] + [vmem] * (len(operands) - 1)
    specs += [hbm] * (2 + len(after))
    work = 2 * length * width * (4 * width + 2 * hidden + 2 * length)
    moved = 2 * width * (10 * width + 2 * hidden)
    return pl.pallas_call(
        partial(section_kernel, layout, forward, backward, len(after)),
        out_shape=shapes,
        in_specs=specs,
        out_specs=out_specs,
        scratch_shapes=scratch,
        compiler_params=pltpu.CompilerParams(
            vmem_limit_bytes=(26 if length <= 256 else 56) * 1024 * 1024
        ),
        cost_estimate=pl.CostEstimate(
            flops=(forward + 2 * backward) * work,
            bytes_accessed=(1 + backward) * moved,
            transcendentals=HEADS * length * length + length * hidden,
        ),
    )(*operands, *halves, *after)


def copy_all(copies):
    for copy in copies:
        copy.start()
    for copy in copies:
        copy.wait()


def pack_kernel(rank_ref, att_ref, out_ref, up_ref, down_ref, keep_ref, send_ref, sems):
    ratio, rows, width = down_ref.shape
    split = (ratio - 2) * width

    def copies(first, second):
        moves = [
            (att_ref, first.at[:, : 3 * width]),
            (out_ref, first.at[:, 3 * width : 4 * width]),
            (up_ref.at[:, :split], first.at[:, 4 * width :]),
            (up_ref.at[:, split:], second.at[:, : 2 * width]),
        ]
        for j in range(ratio):
            moves.append((down_ref.at[j], second.at[:, (2 + j) * width : (3 + j) * width]))
        return [
            pltpu.make_async_copy(source, target, sems.at[i])
            for i, (source, target) in enumerate(moves)
        ]

    @pl.when(rank_ref[0] == 0)
    def _():
        copy_all(copies(keep_ref, send_ref))

    @pl.when(rank_ref[0] != 0)
    def _():
        copy_all(copies(send_ref, keep_ref))


def stack_kernel(high, place_ref, *refs):
    pieces, sems = refs[:high], refs[-1]
    count = (len(refs) - high - 2) // 2
    handed, block = refs[high : high + count], refs[high + count]
    lanes = block.shape[3]
    copies = [
        pltpu.make_async_copy(former, latter, sems.at[high + i, 0])
        for i, (former, latter) in enumerate(zip(handed, refs[high + count + 1 : -1]))
    ]
    for turn, piece in enumerate(pieces):
        place = lax.rem(place_ref[0] + (high - turn), high)
        for part in range(2):
            source = piece.at[:, pl.ds(part * lanes, lanes)]
            copies.append(
                pltpu.make_async_copy(source, block.at[part, place], sems.at[turn, part])
            )
    copy_all(copies)


def weave_kernel(place_ref, own, from_x, from_y, first_both, second_both, full_ref, sems):
    x, y = place_ref[1], place_ref[2]
    lanes = own.shape[3]
    moves = []
    for part, both in ((0, first_both), (1, second_both)):
        for source, row, column in (
            (own.at[part], x, y),
            (from_x.at[part], 1 - x, y),
            (from_y.at[part], x, 1 - y),
            (both, 1 - x, 1 - y),
        ):
            moves.append((source, full_ref.at[:, row, column, :, pl.ds(part * lanes, lanes)]))
    copy_all(
        [
            pltpu.make_async_copy(source, target, sems.at[i])
            for i, (source, target) in enumerate(moves)
        ]
    )


def added(former, latter):
    return former.astype(jnp.float32) + latter.astype(jnp.float32)


def chip_sum_kernel(rank_ref, mine, got, total):
    total[...] = low(added(mine[...], got[...]))


def sort_kernel(high, place_ref, *refs):
    count = (len(refs) - 7) // 2
    mine, got, done = refs[:3]
    handed = refs[3 : 3 + count]
    first_keep, first_send, second_keep, second_send = refs[3 + count : 7 + count]
    x, y = place_ref[1], place_ref[2]
    half = mine.shape[2]
    lanes = half // 2
    for z in range(high):
        for other in range(2):
            for target, span, chunk in (
                (first_send, slice(0, lanes), z * 4 + (1 - x) * 2 + other),
                (second_send, slice(lanes, half), z * 4 + other * 2 + (1 - y)),
                (first_keep, slice(0, lanes), z * 4 + x * 2 + other),
                (second_keep, slice(lanes, half), z * 4 + other * 2 + y),
            ):
                target[z, other, 0] = low(added(mine[chunk, :, span], got[chunk, :, span]))
                target[z, other, 1] = done[chunk, :, span]
    for former, latter in zip(handed, refs[7 + count :]):
        latter[...] = former[...]


def turn_kernel(high, place_ref, *refs):
    refs[-1][...] = refs[4][...]
    for part, own in ((0, place_ref[2]), (1, place_ref[1])):
        kept, got = refs[2 * part : 2 * part + 2]
        keep, send = refs[5 + 2 * part : 7 + 2 * part]
        for z in range(high):
            keep[z] = low(added(kept[z, own], got[z, own]))
            send[z] = low(added(kept[z, 1 - own], got[z, 1 - own]))


def rise_kernel(high, place_ref, *refs):
    targets = refs[4:]
    lanes = refs[0].shape[3]
    for turn in range(high):
        chunk = lax.rem(place_ref[0] + turn, high)
        for part in range(2):
            kept, got = refs[2 * part : 2 * part + 2]
            total = added(kept[chunk], got[chunk])
            span = slice(part * lanes, (part + 1) * lanes)
            targets[turn][:, :, span] = total.astype(targets[turn].dtype)


def close_kernel(rank_ref, *refs):
    pieces, (keep, send) = refs[:-2], refs[-2:]
    own = rank_ref[0]
    for target, section in ((keep, own), (send, 1 - own)):
        total = pieces[0][section].astype(jnp.float32)
        for piece in pieces[1:]:
            total = total + piece[section].astype(jnp.float32)
        target[...] = total


def spread_kernel(rank_ref, mine, got, att_ref, out_ref, up_ref, down_ref):
    rows, width = out_ref.shape
    split = up_ref.shape[1] - 2 * width
    first = rank_ref[0] == 0
    lower = jnp.where(first, mine[...], got[...])
    upper = jnp.where(first, got[...], mine[...])
    att_ref[...] = lower[:, : 3 * width]
    out_ref[...] = lower[:, 3 * width : 4 * width]
    up_ref[:, :split] = lower[:, 4 * width :]
    up_ref[:, split:] = upper[:, : 2 * width]
    for j in range(down_ref.shape[0] // rows):
        down_ref[j * rows : (j + 1) * rows, :] = upper[:, (2 + j) * width : (3 + j) * width]


def in_memory(kernel, shapes, operands, scratch=(), memory=pltpu.VMEM, after=(), limit=32):
    specs = [pl.BlockSpec(memory_space=pltpu.SMEM)]
    specs += [pl.BlockSpec(memory_space=memory)] * (len(operands) - 1)
    specs += [pl.BlockSpec(memory_space=pl.ANY)] * len(after)
    count = len(operands)

    def body(*refs):
        kernel(*refs[:count], *refs[count + len(after) :])

    moved = sum(shape.size * shape.dtype.itemsize for shape in shapes)
    return pl.pallas_call(
        body,
        out_shape=shapes,
        in_specs=specs,
        out_specs=[pl.BlockSpec(memory_space=pltpu.VMEM)] * len(shapes),
        scratch_shapes=list(scratch),
        compiler_params=pltpu.CompilerParams(vmem_limit_bytes=limit * 1024 * 1024),
        cost_estimate=pl.CostEstimate(flops=0, bytes_accessed=3 * moved, transcendentals=0),
    )(*operands, *after)


def pair_swap(block, axis):
    return lax.ppermute(block, axis, [(0, 1), (1, 0)])


def ring_exchange(block, size, step):
    return lax.ppermute(block, RING, [(i, step(i)) for i in range(size)])


def flip(block, size, mask):
    return ring_exchange(block, size, lambda i: i ^ mask)


def rotate(block, size, turn):
    return ring_exchange(block, size, lambda i: (i + 4 * turn) % size)


def rotations(block, size):
    return [block] + [rotate(block, size, turn) for turn in range(1, size // 4)]


def gather_along_z(shard, place, size, handed=(), after=()):
    high = size // 4
    rows, lanes = shard.shape
    return in_memory(
        partial(stack_kernel, high),
        [jax.ShapeDtypeStruct((2, high, rows, lanes // 2), shard.dtype)]
        + [jax.ShapeDtypeStruct(block.shape, block.dtype) for block in handed],
        [place, *rotations(shard, size), *handed],
        scratch=[pltpu.SemaphoreType.DMA((high + len(handed), 2))],
        after=after,
    )


def gather_across(block, from_x, from_y, place, size):
    _, high, rows, lanes = block.shape
    first_both, second_both = flip(from_x[0], size, 1), flip(from_y[1], size, 2)
    (full,) = in_memory(
        weave_kernel,
        [jax.ShapeDtypeStruct((high, 2, 2, rows, 2 * lanes), block.dtype)],
        [place, block, from_x, from_y, first_both, second_both],
        scratch=[pltpu.SemaphoreType.DMA((8,))],
    )
    return full.reshape(size * rows, 2 * lanes)


def scatter_along(terms, place, size, handed, later):
    high = size // 4
    rows, half = terms[0].shape[1:]
    lanes = half // 2
    low_type = jnp.bfloat16
    first_keep, first_send, second_keep, second_send, *handed = in_memory(
        partial(sort_kernel, high),
        [jax.ShapeDtypeStruct((high, 2, 2, rows, lanes), low_type)] * 4
        + [jax.ShapeDtypeStruct(block.shape, block.dtype) for block in handed],
        [place, *terms, *handed],
    )
    first_got, second_got = flip(first_send, size, 2), flip(second_send, size, 1)
    first_keep, first_send, second_keep, second_send, later = in_memory(
        partial(turn_kernel, high),
        [jax.ShapeDtypeStruct((high, 2, rows, lanes), low_type)] * 4
        + [jax.ShapeDtypeStruct(later.shape, later.dtype)],
        [place, first_keep, first_got, second_keep, second_got, later],
    )
    first_got, second_got = flip(first_send, size, 1), flip(second_send, size, 2)
    own, *sent = in_memory(
        partial(rise_kernel, high),
        [
            jax.ShapeDtypeStruct((2, rows, half), kind)
            for kind in (jnp.float32, *[low_type] * (high - 1))
        ],
        [place, first_keep, first_got, second_keep, second_got],
    )
    received = [rotate(block, size, turn + 1) for turn, block in enumerate(sent)]
    return [own, *received], handed, later


def scatter_sum(block, rank, size):
    half = block.shape[-1] // 2
    pieces = [block[..., :half], block[..., half:]]
    left = size
    low_bits = 0
    while left > 4:
        orders = [(0, 1), (1, 0)] if left % 4 == 0 and left >= 16 else [(0,), (0,)]
        for turn in range(len(orders[0])):
            updated = []
            for piece, order in zip(pieces, orders):
                bit = low_bits + order[turn]
                mine = (rank >> bit) & 1
                if len(order) == 2 and turn == 0:
                    shaped = piece.reshape(-1, 2, 2, *piece.shape[1:])
                    at = 2 - order[turn]
                else:
                    shaped = piece.reshape(-1, 2, *piece.shape[1:])
                    at = 1
                keep = lax.dynamic_index_in_dim(shaped, mine, at, keepdims=False)
                send = lax.dynamic_index_in_dim(shaped, 1 - mine, at, keepdims=False)
                got = ring_exchange(send, size, lambda i, bit=bit: i ^ (1 << bit))
                total = (keep.astype(jnp.float32) + got.astype(jnp.float32)).astype(jnp.bfloat16)
                updated.append(total.reshape(-1, *piece.shape[1:]))
            pieces = updated
        low_bits += len(orders[0])
        left //= 2 ** len(orders[0])
    block = jnp.concatenate(pieces, axis=-1)
    high = rank >> low_bits
    total = lax.dynamic_index_in_dim(block, high, 0, keepdims=False).astype(jnp.float32)
    stride = 1 << low_bits
    for turn in range(1, left):
        send = lax.dynamic_index_in_dim(block, (high + turn) % left, 0, keepdims=False)
        got = ring_exchange(send, size, lambda i, turn=turn: (i + turn * stride) % size)
        total = total + got.astype(jnp.float32)
    return total


def per_device(
    inputs,
    cotangent,
    time_ids,
    row_counts,
    cond_table,
    modulation_weight,
    attention_weight,
    output_weight,
    expand_weight,
    shrink_weight,
    biases,
):
    section_rank = lax.axis_index("section")
    data_rank = lax.axis_index("dp")
    seq_rank = lax.axis_index("seq")
    sections = lax.axis_size("section")
    seq_size = lax.axis_size("seq")
    ring_size = lax.axis_size("dp") * seq_size
    ring_rank = data_rank * seq_size + seq_rank
    batches, slots, tokens, width = inputs.shape
    assert batches == sections == 2 and seq_size % slots == 0
    sharers = seq_size // slots
    slot = seq_rank // sharers
    length = tokens * seq_size
    rows = attention_weight.shape[1]
    ratio = shrink_weight.shape[1] // rows
    hidden = ratio * width
    bias_count = biases.shape[1]
    half = 2 * width + hidden
    assert hidden == expand_weight.shape[2] and ratio >= 2
    table_rows = cond_table.shape[0]
    is_first = section_rank == 0
    layout = (width, hidden, rows, ratio, ring_size, 1.0 / sharers, bias_count)
    compact = ring_size in (8, 16) and seq_size == slots == 2
    rank = section_rank.astype(jnp.int32).reshape(1)
    place = jnp.stack([ring_rank >> 2, (ring_rank >> 1) & 1, ring_rank & 1]).astype(jnp.int32)

    keep, send = in_memory(
        pack_kernel,
        [jax.ShapeDtypeStruct((rows, half), jnp.bfloat16)] * 2,
        [
            rank,
            attention_weight[0],
            output_weight[0],
            expand_weight[0],
            shrink_weight[0].reshape(ratio, rows, width),
        ],
        scratch=[pltpu.SemaphoreType.DMA((4 + ratio,))],
        memory=pl.ANY,
        limit=56,
    )
    got = pair_swap(send, "section")
    first_shard = jnp.where(is_first, keep, got)
    second_shard = jnp.where(is_first, got, keep)

    live = (
        slot < lax.dynamic_index_in_dim(row_counts, section_rank, 0, keepdims=False)[0]
    ).astype(jnp.bfloat16)
    both = jnp.stack(
        [
            lax.dynamic_index_in_dim(inputs, section_rank, 0, keepdims=False),
            lax.dynamic_index_in_dim(cotangent, section_rank, 0, keepdims=False),
        ],
        axis=1,
    )

    def side_by_side(mine, got, axis):
        return jnp.where(
            seq_rank == 0,
            jnp.concatenate([mine, got], axis=axis),
            jnp.concatenate([got, mine], axis=axis),
        )

    if compact:
        mine = lax.dynamic_index_in_dim(both, seq_rank, 0, keepdims=False)
        sent = lax.dynamic_index_in_dim(both, 1 - seq_rank, 0, keepdims=False)
        both = side_by_side(mine, pair_swap(sent, "seq"), 1)
    else:
        both = lax.all_to_all(jnp.repeat(both, sharers, axis=0), "seq", 0, 0, tiled=True)
        both = jnp.swapaxes(both, 0, 1).reshape(2, length, width)
    first_input = both[0]
    last_grad = both[1] * live

    flat_ids = time_ids.reshape(-1)
    selector = (
        flat_ids[:, None] == jnp.arange(table_rows, dtype=jnp.int32)[None, :]
    ).astype(jnp.bfloat16)
    conditions = matmul(selector, cond_table)
    silu_all = jax.nn.silu(conditions).astype(jnp.bfloat16)
    silu_own = lax.dynamic_slice_in_dim(silu_all, ring_rank * rows, rows, 1)
    if compact:
        first_block, second_shard, silu_late = gather_along_z(
            first_shard, place, ring_size, handed=(second_shard, silu_own)
        )
        first_blocks = (first_block, flip(first_block, ring_size, 2), flip(first_block, ring_size, 1))
    else:
        silu_late = silu_own

    products = matmul(silu_late, modulation_weight[0])
    own_bias = jnp.broadcast_to(biases.astype(jnp.float32), (products.shape[0], bias_count))
    products = jnp.repeat(jnp.concatenate([products, own_bias], axis=1), sharers, axis=0)
    products = lax.all_to_all(
        products[:, None], ("section", "dp", "seq"), 0, 0, tiled=True
    ).reshape(sections, ring_size, 6 * width + bias_count)
    first_modulation, second_modulation = jnp.split(
        jnp.sum(products[:, :, : 6 * width], axis=1), 2, axis=0
    )
    first_bias, second_bias = products[0, :, 6 * width :], products[1, :, 6 * width :]


    if compact:
        (second_block,) = gather_along_z(
            second_shard, place, ring_size, after=(products, both, *first_blocks[1:])
        )
        second_blocks = (
            second_block,
            flip(second_block, ring_size, 2),
            flip(second_block, ring_size, 1),
        )
        first_pack = gather_across(*first_blocks, place, ring_size)
        second_pack = gather_across(*second_blocks, place, ring_size)
    else:
        first_pack = lax.all_gather(first_shard, RING, axis=0, tiled=True)
        second_pack = lax.all_gather(second_shard, RING, axis=0, tiled=True)
    first_halves = (first_pack, pair_swap(first_pack, "section"))
    second_halves = (second_pack, pair_swap(second_pack, "section"))

    first_low, *first_saved = run_section(
        layout, rank, first_input, first_halves, (first_modulation, first_bias)
    )
    second_low, *second_saved = run_section(
        layout, rank, first_low, second_halves, (second_modulation, second_bias)
    )

    def to_slots(block):
        block = block.reshape(-1, 2, tokens, width)
        mine = lax.dynamic_index_in_dim(block, seq_rank, 1, keepdims=True)
        sent = lax.dynamic_index_in_dim(block, 1 - seq_rank, 1, keepdims=True)
        return mine, pair_swap(sent, "seq")

    early = jnp.stack([first_low * live, second_low * live])
    after = ()
    if compact:
        early = to_slots(early)
        after = (early[1],)
    second_grad, second_dmod, second_sums, second_keep, second_send = run_section(
        layout, rank, first_low, second_halves, saved=second_saved, dy=last_grad
    )
    second_got = pair_swap(second_send, "section")
    first_grad, first_dmod, first_sums, first_keep, first_send = run_section(
        layout, rank, first_input, first_halves, saved=first_saved, dy=second_grad, after=after
    )
    first_got = pair_swap(first_send, "section")

    def ring_terms(term):
        return term.reshape(ring_size, rows, half)

    shard = jax.ShapeDtypeStruct((rows, half), jnp.float32)
    if compact:
        second_term = ring_terms(second_keep)
        (second_total,) = in_memory(
            chip_sum_kernel,
            [jax.ShapeDtypeStruct(second_term.shape, second_term.dtype)],
            [rank, second_term, ring_terms(second_got)],
        )
        pieces, (first_dmod, first_sums), first_grad = scatter_along(
            [ring_terms(first_keep), ring_terms(first_got), second_total],
            place,
            ring_size,
            (first_dmod, first_sums),
            first_grad,
        )
    else:

        def chip_sum(keep, got):
            return ring_terms(low(added(keep, got)))

        pieces = [
            jnp.stack(
                [
                    scatter_sum(chip_sum(keep, got), ring_rank, ring_size)
                    for keep, got in ((first_keep, first_got), (second_keep, second_got))
                ]
            )
        ]
    if compact:
        late = to_slots(jnp.stack([first_grad, second_grad]))
        per_section = jnp.stack([side_by_side(*early, 1), side_by_side(*late, 1)], axis=1)
        per_first, per_second = per_section
        mine = jnp.where(is_first, per_first, per_second)
        got = pair_swap(jnp.where(is_first, per_second, per_first), "section")
        outputs = jnp.where(is_first, jnp.stack([mine, got], 1), jnp.stack([got, mine], 1))
    else:
        blocks = jnp.stack([early[0], first_grad, early[1], second_grad])
        blocks = jnp.swapaxes(blocks.reshape(2, 2, seq_size, tokens, width), 1, 2)
        blocks = blocks.reshape(2 * seq_size, 2, tokens, width)
        blocks = lax.all_to_all(blocks, ("section", "seq"), 0, 0, tiled=True)
        blocks = blocks.reshape(batches, slots, sharers, 2, tokens, width)[:, :, 0]
        outputs = jnp.moveaxis(blocks, 2, 0)
    activations = outputs[0]
    input_grads = outputs[1].astype(jnp.float32)

    mine, send = in_memory(close_kernel, [shard, shard], [rank, *pieces])
    att, out, up, down = in_memory(
        spread_kernel,
        [
            jax.ShapeDtypeStruct(extent, jnp.float32)
            for extent in (
                (rows, 3 * width),
                (rows, width),
                (rows, hidden),
                (rows * ratio, width),
            )
        ],
        [rank, mine, pair_swap(send, "section")],
    )

    rows_back = jnp.concatenate(
        [
            jnp.concatenate(
                [jnp.broadcast_to(dmod, (ring_size, 6 * width)), sums], axis=1
            )
            for dmod, sums in ((first_dmod, first_sums), (second_dmod, second_sums))
        ]
    )
    every = lax.all_to_all(rows_back[:, None], ("section", "dp", "seq"), 0, 0, tiled=True)
    every = every[::sharers, 0]
    bias_grad = jnp.sum(every[:, 6 * width :], axis=0)
    modulation_rows = low(every[:, : 6 * width])
    modulation_grad = outer_sum(silu_own, modulation_rows)
    columns = matmul_transposed(modulation_rows, modulation_weight[0])
    columns = jnp.broadcast_to(columns.reshape(1, 1, -1), (sections * ring_size, 1, columns.size))
    columns = lax.all_to_all(columns, ("section", "dp", "seq"), 0, 0, tiled=True)
    columns = jnp.sum(columns.reshape(sections, ring_size, -1, rows), axis=0)
    products_back = jnp.swapaxes(columns, 0, 1).reshape(-1, width)
    _, silu_back = jax.vjp(jax.nn.silu, conditions)
    table_grad = lax.dot_general(
        selector.astype(jnp.float32),
        silu_back(products_back)[0],
        (((0,), (0,)), ((), ())),
        precision=lax.Precision.HIGHEST,
        preferred_element_type=jnp.float32,
    )
    return (
        activations[None],
        input_grads[None],
        table_grad,
        modulation_grad[None],
        att[None],
        out[None],
        up[None],
        down[None],
        bias_grad[None],
    )


def solution(mesh):
    shard = P("section", ("dp", "seq"), None)
    in_specs = (
        P(None, "dp", "seq", None),
        P(None, "dp", "seq", None),
        P(),
        P(None, "dp"),
        P(),
        shard,
        shard,
        shard,
        shard,
        shard,
        P("section", ("dp", "seq")),
    )
    out_specs = (
        P("section", None, "dp", "seq", None),
        P("section", None, "dp", "seq", None),
        P(),
        shard,
        shard,
        shard,
        shard,
        shard,
        P("section", ("dp", "seq")),
    )
    return jax.shard_map(
        per_device, mesh=mesh, in_specs=in_specs, out_specs=out_specs, check_vma=False
    )
```

```python
from functools import partial

import jax
import jax.numpy as jnp
from jax import lax
from jax.experimental import pallas as pl
from jax.experimental.pallas import tpu as pltpu
from jax.sharding import PartitionSpec as P

HEADS = 6
HEAD = 64
SCALE = HEAD ** (-0.5)
epsilon = 1e-06
RING = ("dp", "seq")
INNER = (2.0 / 3.141592653589793) ** 0.5
CUBE = 0.044715


def matmul(former, latter):
    return jnp.dot(former, latter, preferred_element_type=jnp.float32)


def matmul_transposed(former, latter):
    return lax.dot_general(
        former, latter, (((1,), (1,)), ((), ())), preferred_element_type=jnp.float32
    )


def outer_sum(former, latter):
    return lax.dot_general(
        former, latter, (((0,), (0,)), ((), ())), preferred_element_type=jnp.float32
    )


def low(values):
    return values.astype(jnp.bfloat16)


def normalize_rows(values):
    centre = jnp.mean(values, axis=-1, keepdims=True)
    centred = values - centre
    spread = jnp.mean(centred * centred, axis=-1, keepdims=True)
    factor = lax.rsqrt(spread + epsilon)
    return (centred * factor, factor)


def normalize_back(normed, factor, grad_normed):
    mean_grad = jnp.mean(grad_normed, axis=-1, keepdims=True)
    mean_cross = jnp.mean(grad_normed * normed, axis=-1, keepdims=True)
    return factor * (grad_normed - mean_grad - normed * mean_cross)


def column_sum(values):
    return jnp.sum(values.astype(jnp.float32), axis=0, keepdims=True)


def saved_shapes(layout, length):
    width, hidden = layout[:2]
    bf16, f32 = jnp.bfloat16, jnp.float32
    return [
        ((1, 6 * width), f32),
        ((length, 3 * width), bf16),
        ((length, width), bf16),
        ((length, hidden), bf16),
        ((HEADS, length, length), f32),
        ((length, hidden), f32),
        ((length, width), f32),
        ((length, width), f32),
        ((hidden, width), bf16),
    ]


def section_kernel(layout, forward, backward, after, *refs):
    width, hidden, rows, ratio, ring_size, share, bias_count = layout
    refs = list(refs)

    def take(count):
        taken = refs[:count]
        del refs[:count]
        return taken

    rank_ref, x_ref = take(2)
    if forward:
        modulation_ref, bias_ref = take(2)
    else:
        saved = take(9)
    if backward:
        (dy_ref,) = take(1)
    mine_ref, theirs_ref = take(2)
    take(after)
    if forward:
        (y_ref,) = take(1)
    if backward:
        dx_ref, dmod_ref, sums_ref, keep_ref, send_ref = take(5)
    elif forward:
        saved = take(9)
    att_w, out_w, up_w, sems, down_s, block_s = take(6)
    if forward:
        down_p, bias_s = take(2)
    if backward:
        da_s, dqkv_s, row_ref, halves, out_sems = take(5)
    if forward and backward:
        saved = take(9)
    mod_s, qkv_s, att_s, u_s, soft_s, slope_s, one_s, two_s, down_w = saved

    rank = rank_ref[0]
    split = hidden - 2 * width

    def fetches(first, second):
        moves = [
            (first.at[:, : 3 * width], att_w),
            (first.at[:, 3 * width : 4 * width], out_w),
            (first.at[:, 4 * width :], up_w.at[:, :split]),
            (second.at[:, : hidden - split], up_w.at[:, split:]),
        ]
        if forward:
            moves.append((second.at[:, hidden - split :], down_p))
        return [
            pltpu.make_async_copy(source, target, sems.at[i])
            for i, (source, target) in enumerate(moves)
        ]

    @pl.when(rank == 0)
    def _():
        for copy in fetches(mine_ref, theirs_ref):
            copy.start()

    @pl.when(rank != 0)
    def _():
        for copy in fetches(theirs_ref, mine_ref):
            copy.start()

    arrivals = fetches(mine_ref, theirs_ref)

    def part(ref, member, head):
        start = member * width + head * HEAD
        return ref[:, start : start + HEAD]

    x = x_ref[...].astype(jnp.float32)
    normed_one, factor_one = normalize_rows(x)
    if forward:
        for d in range(ring_size):
            bias_s[:, d * bias_count : (d + 1) * bias_count] = bias_ref[d : d + 1, :]
        mod_s[...] = modulation_ref[...] + bias_s[:, : 6 * width]
    shift_one, scale_one, gate_one, shift_two, scale_two, gate_two = [
        mod_s[:, i * width : (i + 1) * width] for i in range(6)
    ]
    hidden_one = low(normed_one * (1.0 + scale_one) + shift_one)
    if forward:

        def bias(a, b):
            return bias_s[:, a:b]

        at = 6 * width
        arrivals[0].wait()
        qkv_s[:, :width] = low(matmul(hidden_one, att_w[:, :width]) + bias(at, at + width))
        qkv_s[:, width : 2 * width] = low(matmul(hidden_one, att_w[:, width : 2 * width]))
        qkv_s[:, 2 * width :] = low(
            matmul(hidden_one, att_w[:, 2 * width :]) + bias(at + width, at + 2 * width)
        )
        for head in range(HEADS):
            scores = matmul_transposed(part(qkv_s, 0, head), part(qkv_s, 1, head)) * SCALE
            raised = jnp.exp(scores - jnp.max(scores, axis=-1, keepdims=True))
            soft = raised * (1.0 / jnp.sum(raised, axis=-1, keepdims=True))
            soft_s[head] = soft
            attended = matmul(low(soft), part(qkv_s, 2, head))
            att_s[:, head * HEAD : (head + 1) * HEAD] = low(attended)
        arrivals[1].wait()
        one_s[...] = matmul(att_s[...], out_w[...]) + bias(at + 2 * width, at + 3 * width)
    branch_one = one_s[...]
    middle = x + gate_one * branch_one
    normed_two, factor_two = normalize_rows(middle)
    hidden_two = low(normed_two * (1.0 + scale_two) + shift_two)
    if forward:
        arrivals[2].wait()
        arrivals[3].wait()
        at += 3 * width
        for j in range(ratio):
            cut = slice(j * width, (j + 1) * width)
            a = matmul(hidden_two, up_w[:, cut]) + bias(at + j * width, at + (j + 1) * width)
            square = a * a
            turn = jnp.tanh(INNER * (a + CUBE * (a * square)))
            half_one = 0.5 * (1.0 + turn)
            u_s[:, cut] = low(a * half_one)
            slope_s[:, cut] = half_one + (0.5 * INNER) * a * (1.0 - turn * turn) * (
                1.0 + (3.0 * CUBE) * square
            )
        arrivals[4].wait()
        block_s[...] = down_p[...].astype(jnp.float32)
        for d in range(ring_size):
            for j in range(ratio):
                down_s[(d * ratio + j) * rows : (d * ratio + j + 1) * rows, :] = block_s[
                    d * rows : (d + 1) * rows, j * width : (j + 1) * width
                ]
        down_w[...] = low(down_s[...])
        two_s[...] = matmul(u_s[...], down_w[...]) + bias(at + hidden, at + hidden + width)
        y_ref[...] = low(middle + gate_two * two_s[...])
    if not backward:
        return

    grad_out = dy_ref[...].astype(jnp.float32)
    grad_branch = low(gate_two * grad_out)
    sums_at = 6 * width
    row_ref[:, 5 * width : 6 * width] = column_sum(grad_out * two_s[...])
    row_ref[:, sums_at + 3 * width + hidden : sums_at + 4 * width + hidden] = column_sum(
        grad_branch
    )
    for j in range(ratio):
        cut = slice(j * width, (j + 1) * width)
        grad_expanded = low(slope_s[:, cut] * matmul_transposed(grad_branch, down_w[cut, :]))
        da_s[:, cut] = grad_expanded
        row_ref[:, sums_at + (3 + j) * width : sums_at + (4 + j) * width] = column_sum(
            grad_expanded
        )
    halves[0, :, 4 * width :] = low(outer_sum(hidden_two, da_s[:, :split]) * share)
    halves[1, :, : hidden - split] = low(outer_sum(hidden_two, da_s[:, split:]) * share)
    down_s[...] = outer_sum(u_s[...], grad_branch) * share
    for d in range(ring_size):
        for j in range(ratio):
            block_s[d * rows : (d + 1) * rows, j * width : (j + 1) * width] = down_s[
                (d * ratio + j) * rows : (d * ratio + j + 1) * rows, :
            ]
    halves[1, :, hidden - split :] = low(block_s[...])
    second_out = [
        pltpu.make_async_copy(halves.at[1], keep_ref, out_sems.at[1]),
        pltpu.make_async_copy(halves.at[1], send_ref, out_sems.at[1]),
    ]

    @pl.when(rank == 1)
    def _():
        second_out[0].start()

    @pl.when(rank != 1)
    def _():
        second_out[1].start()

    if not forward:
        arrivals[2].wait()
        arrivals[3].wait()
    grad_hidden_two = matmul_transposed(da_s[...], up_w[...])
    row_ref[:, 3 * width : 4 * width] = column_sum(grad_hidden_two)
    row_ref[:, 4 * width : 5 * width] = column_sum(grad_hidden_two * normed_two)
    grad_middle = grad_out + normalize_back(
        normed_two, factor_two, grad_hidden_two * (1.0 + scale_two)
    )
    row_ref[:, 2 * width : 3 * width] = column_sum(grad_middle * branch_one)
    grad_attention = low(gate_one * grad_middle)
    row_ref[:, sums_at + 2 * width : sums_at + 3 * width] = column_sum(grad_attention)
    halves[0, :, 3 * width : 4 * width] = low(outer_sum(att_s[...], grad_attention) * share)
    if not forward:
        arrivals[1].wait()
    grad_attended = low(matmul_transposed(grad_attention, out_w[...]))
    for head in range(HEADS):
        soft = soft_s[head]
        grad_head = grad_attended[:, head * HEAD : (head + 1) * HEAD]
        grad_soft = matmul_transposed(grad_head, part(qkv_s, 2, head))
        inner = jnp.sum(grad_soft * soft, axis=-1, keepdims=True)
        grad_scores = low(soft * (grad_soft - inner))
        grads = (
            matmul(grad_scores, part(qkv_s, 1, head)) * SCALE,
            outer_sum(grad_scores, part(qkv_s, 0, head)) * SCALE,
            outer_sum(low(soft), grad_head),
        )
        for member, grad in enumerate(grads):
            start = member * width + head * HEAD
            dqkv_s[:, start : start + HEAD] = low(grad)
    row_ref[:, sums_at : sums_at + width] = column_sum(dqkv_s[:, :width])
    row_ref[:, sums_at + width : sums_at + 2 * width] = column_sum(dqkv_s[:, 2 * width :])
    halves[0, :, : 3 * width] = low(outer_sum(hidden_one, dqkv_s[...]) * share)
    first_out = [
        pltpu.make_async_copy(halves.at[0], keep_ref, out_sems.at[0]),
        pltpu.make_async_copy(halves.at[0], send_ref, out_sems.at[0]),
    ]

    @pl.when(rank == 0)
    def _():
        first_out[0].start()

    @pl.when(rank != 0)
    def _():
        first_out[1].start()

    if not forward:
        arrivals[0].wait()
    grad_hidden_one = matmul_transposed(dqkv_s[...], att_w[...])
    row_ref[:, :width] = column_sum(grad_hidden_one)
    row_ref[:, width : 2 * width] = column_sum(grad_hidden_one * normed_one)
    dx_ref[...] = low(
        grad_middle
        + normalize_back(normed_one, factor_one, grad_hidden_one * (1.0 + scale_one))
    )
    row_ref[:, : 6 * width] = low(row_ref[:, : 6 * width]).astype(jnp.float32)
    dmod_ref[...] = row_ref[:, : 6 * width]
    for d in range(ring_size):
        sums_ref[d : d + 1, :] = row_ref[:, d * bias_count : (d + 1) * bias_count]
    second_out[0].wait()
    first_out[0].wait()


def run_section(layout, rank, x, halves, start=None, saved=None, dy=None, after=()):
    width, hidden, rows, ratio, ring_size, share, bias_count = layout
    length = x.shape[0]
    forward, backward = start is not None, dy is not None
    vmem = pl.BlockSpec(memory_space=pltpu.VMEM)
    hbm = pl.BlockSpec(memory_space=pl.ANY)
    bf16, f32 = jnp.bfloat16, jnp.float32
    half = 2 * width + hidden
    kept = saved_shapes(layout, length)
    operands = [rank, x, *(start if forward else saved)]
    shapes, out_specs = [], []
    scratch = [
        pltpu.VMEM((width, 3 * width), bf16),
        pltpu.VMEM((width, width), bf16),
        pltpu.VMEM((width, hidden), bf16),
        pltpu.SemaphoreType.DMA((5,)),
        pltpu.VMEM((hidden, width), f32),
        pltpu.VMEM((width, hidden), f32),
    ]
    if forward:
        shapes.append(jax.ShapeDtypeStruct((length, width), bf16))
        scratch += [
            pltpu.VMEM((width, hidden), bf16),
            pltpu.VMEM((1, bias_count * ring_size), f32),
        ]
    if backward:
        operands.append(dy)
        shapes += [
            jax.ShapeDtypeStruct((length, width), bf16),
            jax.ShapeDtypeStruct((1, 6 * width), f32),
            jax.ShapeDtypeStruct((ring_size, bias_count), f32),
            jax.ShapeDtypeStruct((width, half), bf16),
            jax.ShapeDtypeStruct((width, half), bf16),
        ]
        scratch += [
            pltpu.VMEM((length, hidden), bf16),
            pltpu.VMEM((length, 3 * width), bf16),
            pltpu.VMEM((1, 10 * width + hidden), f32),
            pltpu.VMEM((2, width, half), bf16),
            pltpu.SemaphoreType.DMA((2,)),
        ]
        if forward:
            scratch += [pltpu.VMEM(extent, kind) for extent, kind in kept]
    else:
        shapes += [jax.ShapeDtypeStruct(extent, kind) for extent, kind in kept]
    out_specs = [vmem] * len(shapes)
    if backward:
        out_specs[-2:] = [hbm, hbm]
    specs = [pl.BlockSpec(memory_space=pltpu.SMEM)] + [vmem] * (len(operands) - 1)
    specs += [hbm] * (2 + len(after))
    work = 2 * length * width * (4 * width + 2 * hidden + 2 * length)
    moved = 2 * width * (10 * width + 2 * hidden)
    return pl.pallas_call(
        partial(section_kernel, layout, forward, backward, len(after)),
        out_shape=shapes,
        in_specs=specs,
        out_specs=out_specs,
        scratch_shapes=scratch,
        compiler_params=pltpu.CompilerParams(
            vmem_limit_bytes=(56 if length > 256 else 26 if forward and backward else 22)
            * 1024
            * 1024
        ),
        cost_estimate=pl.CostEstimate(
            flops=(forward + 2 * backward) * work,
            bytes_accessed=(1 + backward) * moved,
            transcendentals=HEADS * length * length + length * hidden,
        ),
    )(*operands, *halves, *after)


def copy_all(copies):
    for copy in copies:
        copy.start()
    for copy in copies:
        copy.wait()


def pack_kernel(rank_ref, att_ref, out_ref, up_ref, down_ref, keep_ref, send_ref, sems):
    ratio, rows, width = down_ref.shape
    split = (ratio - 2) * width

    def copies(first, second):
        moves = [
            (att_ref, first.at[:, : 3 * width]),
            (out_ref, first.at[:, 3 * width : 4 * width]),
            (up_ref.at[:, :split], first.at[:, 4 * width :]),
            (up_ref.at[:, split:], second.at[:, : 2 * width]),
        ]
        for j in range(ratio):
            moves.append((down_ref.at[j], second.at[:, (2 + j) * width : (3 + j) * width]))
        return [
            pltpu.make_async_copy(source, target, sems.at[i])
            for i, (source, target) in enumerate(moves)
        ]

    @pl.when(rank_ref[0] == 0)
    def _():
        copy_all(copies(keep_ref, send_ref))

    @pl.when(rank_ref[0] != 0)
    def _():
        copy_all(copies(send_ref, keep_ref))


def stack_kernel(high, split, place_ref, *refs):
    pieces, sems = refs[:high], refs[-1]
    count = (len(refs) - high - 3) // 2
    handed, targets = refs[high : high + count], refs[high + count : -1]
    copies = [
        pltpu.make_async_copy(former, latter, sems.at[high + i, 0])
        for i, (former, latter) in enumerate(zip(handed, targets[2:]))
    ]
    for turn, piece in enumerate(pieces):
        place = lax.rem(place_ref[0] + (high - turn), high)
        parts = (piece.at[:, :split], piece.at[:, split:])
        for i, (part, target) in enumerate(zip(parts, targets)):
            copies.append(pltpu.make_async_copy(part, target.at[place], sems.at[turn, i]))
    copy_all(copies)


def weave_kernel(split, place_ref, *refs):
    pieces, full_ref, sems = refs[:-2], refs[-2], refs[-1]
    x, y = place_ref[1], place_ref[2]
    copies = []
    for i, piece in enumerate(pieces):
        other_x, other_y = (i % 4) & 1, (i % 4) >> 1
        row = x if not other_x else 1 - x
        column = y if not other_y else 1 - y
        target = full_ref.at[:, row, column, :, pl.ds((i // 4) * split, split)]
        copies.append(pltpu.make_async_copy(piece, target, sems.at[i]))
    copy_all(copies)


def added(former, latter):
    return former.astype(jnp.float32) + latter.astype(jnp.float32)


def chip_sum_kernel(high, place_ref, mine, got, *refs):
    count = (len(refs) - 4) // 2
    first_keep, first_send, second_keep, second_send = refs[count : count + 4]
    for former, latter in zip(refs[:count], refs[count + 4 :]):
        latter[...] = former[...]
    x, y = place_ref[1], place_ref[2]
    half = mine.shape[2]
    lanes = half // 2
    for z in range(high):
        for other in range(2):
            for target, span, chunk in (
                (first_keep, slice(0, lanes), z * 4 + x * 2 + other),
                (first_send, slice(0, lanes), z * 4 + (1 - x) * 2 + other),
                (second_keep, slice(lanes, half), z * 4 + other * 2 + y),
                (second_send, slice(lanes, half), z * 4 + other * 2 + (1 - y)),
            ):
                target[z, other] = low(added(mine[chunk, :, span], got[chunk, :, span]))


def turn_kernel(high, place_ref, *refs):
    count = (len(refs) - 8) // 2
    for former, latter in zip(refs[4 : 4 + count], refs[8 + count :]):
        latter[...] = former[...]
    for part, own in ((0, place_ref[2]), (1, place_ref[1])):
        kept, got = refs[2 * part : 2 * part + 2]
        keep, send = refs[4 + count + 2 * part : 6 + count + 2 * part]
        for z in range(high):
            keep[z] = low(added(kept[z, own], got[z, own]))
            send[z] = low(added(kept[z, 1 - own], got[z, 1 - own]))


def rise_kernel(high, place_ref, *refs):
    targets = refs[4:]
    lanes = refs[0].shape[2]
    for turn in range(high):
        chunk = lax.rem(place_ref[0] + turn, high)
        for part in range(2):
            kept, got = refs[2 * part : 2 * part + 2]
            total = added(kept[chunk], got[chunk])
            span = slice(part * lanes, (part + 1) * lanes)
            targets[turn][:, span] = total.astype(targets[turn].dtype)


def close_kernel(high, rank_ref, *refs):
    keep, send = refs[-2:]
    totals = []
    for section in range(2):
        pieces = refs[section * high : (section + 1) * high]
        total = pieces[0][...].astype(jnp.float32)
        for piece in pieces[1:]:
            total = total + piece[...].astype(jnp.float32)
        totals.append(total)
    first = rank_ref[0] == 0
    keep[...] = jnp.where(first, totals[0], totals[1])
    send[...] = jnp.where(first, totals[1], totals[0])


def spread_kernel(rank_ref, mine, got, att_ref, out_ref, up_ref, down_ref):
    rows, width = out_ref.shape
    split = up_ref.shape[1] - 2 * width
    first = rank_ref[0] == 0
    lower = jnp.where(first, mine[...], got[...])
    upper = jnp.where(first, got[...], mine[...])
    att_ref[...] = lower[:, : 3 * width]
    out_ref[...] = lower[:, 3 * width : 4 * width]
    up_ref[:, :split] = lower[:, 4 * width :]
    up_ref[:, split:] = upper[:, : 2 * width]
    for j in range(down_ref.shape[0] // rows):
        down_ref[j * rows : (j + 1) * rows, :] = upper[:, (2 + j) * width : (3 + j) * width]


def in_memory(kernel, shapes, operands, scratch=(), memory=pltpu.VMEM, after=(), limit=16):
    specs = [pl.BlockSpec(memory_space=pltpu.SMEM)]
    specs += [pl.BlockSpec(memory_space=memory)] * (len(operands) - 1)
    specs += [pl.BlockSpec(memory_space=pl.ANY)] * len(after)
    count = len(operands)

    def body(*refs):
        kernel(*refs[:count], *refs[count + len(after) :])

    moved = sum(shape.size * shape.dtype.itemsize for shape in shapes)
    return pl.pallas_call(
        body,
        out_shape=shapes,
        in_specs=specs,
        out_specs=[pl.BlockSpec(memory_space=pltpu.VMEM)] * len(shapes),
        scratch_shapes=list(scratch),
        compiler_params=pltpu.CompilerParams(vmem_limit_bytes=limit * 1024 * 1024),
        cost_estimate=pl.CostEstimate(flops=0, bytes_accessed=3 * moved, transcendentals=0),
    )(*operands, *after)


def pair_swap(block, axis):
    return lax.ppermute(block, axis, [(0, 1), (1, 0)])


def ring_exchange(block, size, step):
    return lax.ppermute(block, RING, [(i, step(i)) for i in range(size)])


def flip(block, size, mask):
    return ring_exchange(block, size, lambda i: i ^ mask)


def rotate(block, size, turn):
    return ring_exchange(block, size, lambda i: (i + 4 * turn) % size)


def rotations(block, size):
    return [block] + [rotate(block, size, turn) for turn in range(1, size // 4)]


def gather_along_z(shard, place, size, handed=(), after=()):
    high = size // 4
    rows, lanes = shard.shape
    return in_memory(
        partial(stack_kernel, high, lanes // 2),
        [jax.ShapeDtypeStruct((high, rows, lanes // 2), shard.dtype)] * 2
        + [jax.ShapeDtypeStruct(block.shape, block.dtype) for block in handed],
        [place, *rotations(shard, size), *handed],
        scratch=[pltpu.SemaphoreType.DMA((high + len(handed), 2))],
        after=after,
    )


def first_flips(first, second, size):
    return flip(first, size, 2), flip(second, size, 1)


def gather_across(first, second, first_x, second_y, place, size):
    high, rows, lanes = first.shape
    first_y, second_x = flip(first, size, 1), flip(second, size, 2)
    first_both, second_both = flip(first_x, size, 1), flip(second_y, size, 2)
    (full,) = in_memory(
        partial(weave_kernel, lanes),
        [jax.ShapeDtypeStruct((high, 2, 2, rows, 2 * lanes), first.dtype)],
        [place, first, first_x, first_y, first_both, second, second_x, second_y, second_both],
        scratch=[pltpu.SemaphoreType.DMA((8,))],
    )
    return full.reshape(size * rows, 2 * lanes)


def scatter_first(mine, got, place, size, handed=(), after=()):
    rows, half = mine.shape[1:]
    shape = jax.ShapeDtypeStruct((size // 4, 2, rows, half // 2), jnp.bfloat16)
    return in_memory(
        partial(chip_sum_kernel, size // 4),
        [shape] * 4 + [jax.ShapeDtypeStruct(block.shape, block.dtype) for block in handed],
        [place, mine, got, *handed],
        after=after,
    )


def scatter_flips(sorted_terms, size):
    first_keep, first_send, second_keep, second_send = sorted_terms
    return first_keep, flip(first_send, size, 2), second_keep, flip(second_send, size, 1)


def scatter_second(received, place, size, handed=(), after=()):
    high, _, rows, lanes = received[0].shape
    shape = jax.ShapeDtypeStruct((high, rows, lanes), jnp.bfloat16)
    first_keep, first_send, second_keep, second_send, *handed = in_memory(
        partial(turn_kernel, high),
        [shape] * 4 + [jax.ShapeDtypeStruct(block.shape, block.dtype) for block in handed],
        [place, *received, *handed],
        after=after,
    )
    turned = (first_keep, flip(first_send, size, 1), second_keep, flip(second_send, size, 2))
    return turned, handed


def scatter_third(turned, place, size, after=()):
    high, rows, lanes = turned[0].shape
    chunk = (rows, 2 * lanes)
    return in_memory(
        partial(rise_kernel, high),
        [jax.ShapeDtypeStruct(chunk, jnp.float32)]
        + [jax.ShapeDtypeStruct(chunk, jnp.bfloat16)] * (high - 1),
        [place, *turned],
        after=after,
    )


def scatter_along_z(pieces, size):
    own, *sent = pieces
    return [own] + [rotate(block, size, turn + 1) for turn, block in enumerate(sent)]


def scatter_sum(block, rank, size):
    half = block.shape[-1] // 2
    pieces = [block[..., :half], block[..., half:]]
    left = size
    low_bits = 0
    while left > 4:
        orders = [(0, 1), (1, 0)] if left % 4 == 0 and left >= 16 else [(0,), (0,)]
        for turn in range(len(orders[0])):
            updated = []
            for piece, order in zip(pieces, orders):
                bit = low_bits + order[turn]
                mine = (rank >> bit) & 1
                if len(order) == 2 and turn == 0:
                    shaped = piece.reshape(-1, 2, 2, *piece.shape[1:])
                    at = 2 - order[turn]
                else:
                    shaped = piece.reshape(-1, 2, *piece.shape[1:])
                    at = 1
                keep = lax.dynamic_index_in_dim(shaped, mine, at, keepdims=False)
                send = lax.dynamic_index_in_dim(shaped, 1 - mine, at, keepdims=False)
                got = ring_exchange(send, size, lambda i, bit=bit: i ^ (1 << bit))
                total = (keep.astype(jnp.float32) + got.astype(jnp.float32)).astype(jnp.bfloat16)
                updated.append(total.reshape(-1, *piece.shape[1:]))
            pieces = updated
        low_bits += len(orders[0])
        left //= 2 ** len(orders[0])
    block = jnp.concatenate(pieces, axis=-1)
    high = rank >> low_bits
    total = lax.dynamic_index_in_dim(block, high, 0, keepdims=False).astype(jnp.float32)
    stride = 1 << low_bits
    for turn in range(1, left):
        send = lax.dynamic_index_in_dim(block, (high + turn) % left, 0, keepdims=False)
        got = ring_exchange(send, size, lambda i, turn=turn: (i + turn * stride) % size)
        total = total + got.astype(jnp.float32)
    return total


def per_device(
    inputs,
    cotangent,
    time_ids,
    row_counts,
    cond_table,
    modulation_weight,
    attention_weight,
    output_weight,
    expand_weight,
    shrink_weight,
    biases,
):
    section_rank = lax.axis_index("section")
    data_rank = lax.axis_index("dp")
    seq_rank = lax.axis_index("seq")
    sections = lax.axis_size("section")
    seq_size = lax.axis_size("seq")
    ring_size = lax.axis_size("dp") * seq_size
    ring_rank = data_rank * seq_size + seq_rank
    batches, slots, tokens, width = inputs.shape
    assert batches == sections == 2 and seq_size % slots == 0
    sharers = seq_size // slots
    slot = seq_rank // sharers
    length = tokens * seq_size
    rows = attention_weight.shape[1]
    ratio = shrink_weight.shape[1] // rows
    hidden = ratio * width
    bias_count = biases.shape[1]
    half = 2 * width + hidden
    assert hidden == expand_weight.shape[2] and ratio >= 2
    table_rows = cond_table.shape[0]
    is_first = section_rank == 0
    layout = (width, hidden, rows, ratio, ring_size, 1.0 / sharers, bias_count)
    compact = ring_size in (8, 16) and seq_size == slots == 2
    rank = section_rank.astype(jnp.int32).reshape(1)
    place = jnp.stack([ring_rank >> 2, (ring_rank >> 1) & 1, ring_rank & 1]).astype(jnp.int32)

    keep, send = in_memory(
        pack_kernel,
        [jax.ShapeDtypeStruct((rows, half), jnp.bfloat16)] * 2,
        [
            rank,
            attention_weight[0],
            output_weight[0],
            expand_weight[0],
            shrink_weight[0].reshape(ratio, rows, width),
        ],
        scratch=[pltpu.SemaphoreType.DMA((4 + ratio,))],
        memory=pl.ANY,
        limit=56,
    )
    got = pair_swap(send, "section")
    first_shard = jnp.where(is_first, keep, got)
    second_shard = jnp.where(is_first, got, keep)

    live = (
        slot < lax.dynamic_index_in_dim(row_counts, section_rank, 0, keepdims=False)[0]
    ).astype(jnp.bfloat16)
    both = jnp.stack(
        [
            lax.dynamic_index_in_dim(inputs, section_rank, 0, keepdims=False),
            lax.dynamic_index_in_dim(cotangent, section_rank, 0, keepdims=False),
        ],
        axis=1,
    )

    def side_by_side(mine, got, axis):
        return jnp.where(
            seq_rank == 0,
            jnp.concatenate([mine, got], axis=axis),
            jnp.concatenate([got, mine], axis=axis),
        )

    if compact:
        mine = lax.dynamic_index_in_dim(both, seq_rank, 0, keepdims=False)
        sent = lax.dynamic_index_in_dim(both, 1 - seq_rank, 0, keepdims=False)
        both = side_by_side(mine, pair_swap(sent, "seq"), 1)
    else:
        both = lax.all_to_all(jnp.repeat(both, sharers, axis=0), "seq", 0, 0, tiled=True)
        both = jnp.swapaxes(both, 0, 1).reshape(2, length, width)
    first_input = both[0]
    last_grad = both[1] * live

    flat_ids = time_ids.reshape(-1)
    selector = (
        flat_ids[:, None] == jnp.arange(table_rows, dtype=jnp.int32)[None, :]
    ).astype(jnp.bfloat16)
    conditions = matmul(selector, cond_table)
    silu_all = jax.nn.silu(conditions).astype(jnp.bfloat16)
    silu_own = lax.dynamic_slice_in_dim(silu_all, ring_rank * rows, rows, 1)
    if compact:
        *first_parts, second_shard, silu_late = gather_along_z(
            first_shard, place, ring_size, handed=(second_shard, silu_own)
        )
        first_parts += first_flips(*first_parts, ring_size)
    else:
        silu_late = silu_own

    products = matmul(silu_late, modulation_weight[0])
    own_bias = jnp.broadcast_to(biases.astype(jnp.float32), (products.shape[0], bias_count))
    products = jnp.repeat(jnp.concatenate([products, own_bias], axis=1), sharers, axis=0)
    products = lax.all_to_all(
        products[:, None], ("section", "dp", "seq"), 0, 0, tiled=True
    ).reshape(sections, ring_size, 6 * width + bias_count)
    first_modulation, second_modulation = jnp.split(
        jnp.sum(products[:, :, : 6 * width], axis=1), 2, axis=0
    )
    first_bias, second_bias = products[0, :, 6 * width :], products[1, :, 6 * width :]

    if compact:
        second_parts = gather_along_z(
            second_shard, place, ring_size, after=(products, both, *first_parts[2:])
        )
        second_parts += first_flips(*second_parts, ring_size)
        first_pack = gather_across(*first_parts, place, ring_size)
        second_pack = gather_across(*second_parts, place, ring_size)
    else:
        first_pack = lax.all_gather(first_shard, RING, axis=0, tiled=True)
        second_pack = lax.all_gather(second_shard, RING, axis=0, tiled=True)
    first_halves = (first_pack, pair_swap(first_pack, "section"))
    second_halves = (second_pack, pair_swap(second_pack, "section"))

    first_low, *first_saved = run_section(
        layout, rank, first_input, first_halves, (first_modulation, first_bias)
    )
    second_low, second_grad, second_dmod, second_sums, second_keep, second_send = run_section(
        layout, rank, first_low, second_halves, (second_modulation, second_bias), dy=last_grad
    )
    second_got = pair_swap(second_send, "section")

    def ring_terms(term):
        return term.reshape(ring_size, rows, half)

    first_grad, first_dmod, first_sums, first_keep, first_send = run_section(
        layout, rank, first_input, first_halves, saved=first_saved, dy=second_grad
    )
    first_got = pair_swap(first_send, "section")

    shard = jax.ShapeDtypeStruct((rows, half), jnp.float32)
    if compact:
        second_sorted = scatter_first(
            ring_terms(second_keep), ring_terms(second_got), place, ring_size
        )
        second_received = scatter_flips(second_sorted, ring_size)
        *first_sorted, first_dmod, first_sums = scatter_first(
            ring_terms(first_keep),
            ring_terms(first_got),
            place,
            ring_size,
            handed=(first_dmod, first_sums),
            after=(second_sorted[0],),
        )
        first_received = scatter_flips(first_sorted, ring_size)
        second_turned, _ = scatter_second(second_received, place, ring_size)
        second_sent = scatter_third(second_turned, place, ring_size)
        second_pieces = scatter_along_z(second_sent, ring_size)
        first_turned, (first_grad,) = scatter_second(
            first_received, place, ring_size, handed=(first_grad,), after=(second_sent[0],)
        )
        first_sent = scatter_third(first_turned, place, ring_size, tuple(second_pieces[1:]))
        first_pieces = scatter_along_z(first_sent, ring_size)
    else:

        def chip_sum(keep, got):
            return ring_terms(low(added(keep, got)))

        first_pieces, second_pieces = [
            [scatter_sum(chip_sum(keep, got), ring_rank, ring_size)]
            for keep, got in ((first_keep, first_got), (second_keep, second_got))
        ]
    outputs_ready = (first_low * live, second_low * live)
    if compact:
        block = jnp.stack([outputs_ready[0], first_grad, outputs_ready[1], second_grad])
        block = block.reshape(4, 2, tokens, width)
        mine = lax.dynamic_index_in_dim(block, seq_rank, 1, keepdims=True)
        sent = lax.dynamic_index_in_dim(block, 1 - seq_rank, 1, keepdims=True)
        block = side_by_side(mine, pair_swap(sent, "seq"), 1)
        per_first, per_second = block[:2], block[2:]
        mine = jnp.where(is_first, per_first, per_second)
        got = pair_swap(jnp.where(is_first, per_second, per_first), "section")
        outputs = jnp.where(is_first, jnp.stack([mine, got], 1), jnp.stack([got, mine], 1))
    else:
        pieces = jnp.stack([outputs_ready[0], first_grad, outputs_ready[1], second_grad])
        pieces = jnp.swapaxes(pieces.reshape(2, 2, seq_size, tokens, width), 1, 2)
        pieces = pieces.reshape(2 * seq_size, 2, tokens, width)
        pieces = lax.all_to_all(pieces, ("section", "seq"), 0, 0, tiled=True)
        pieces = pieces.reshape(batches, slots, sharers, 2, tokens, width)[:, :, 0]
        outputs = jnp.moveaxis(pieces, 2, 0)
    activations = outputs[0]
    input_grads = outputs[1].astype(jnp.float32)

    mine, send = in_memory(
        partial(close_kernel, len(first_pieces)),
        [shard, shard],
        [rank, *first_pieces, *second_pieces],
    )
    att, out, up, down = in_memory(
        spread_kernel,
        [
            jax.ShapeDtypeStruct(extent, jnp.float32)
            for extent in (
                (rows, 3 * width),
                (rows, width),
                (rows, hidden),
                (rows * ratio, width),
            )
        ],
        [rank, mine, pair_swap(send, "section")],
    )

    rows_back = jnp.concatenate(
        [
            jnp.concatenate(
                [jnp.broadcast_to(dmod, (ring_size, 6 * width)), sums], axis=1
            )
            for dmod, sums in ((first_dmod, first_sums), (second_dmod, second_sums))
        ]
    )
    every = lax.all_to_all(rows_back[:, None], ("section", "dp", "seq"), 0, 0, tiled=True)
    every = every[::sharers, 0]
    bias_grad = jnp.sum(every[:, 6 * width :], axis=0)
    modulation_rows = low(every[:, : 6 * width])
    modulation_grad = outer_sum(silu_own, modulation_rows)
    columns = matmul_transposed(modulation_rows, modulation_weight[0])
    columns = jnp.broadcast_to(columns.reshape(1, 1, -1), (sections * ring_size, 1, columns.size))
    columns = lax.all_to_all(columns, ("section", "dp", "seq"), 0, 0, tiled=True)
    columns = jnp.sum(columns.reshape(sections, ring_size, -1, rows), axis=0)
    products_back = jnp.swapaxes(columns, 0, 1).reshape(-1, width)
    _, silu_back = jax.vjp(jax.nn.silu, conditions)
    table_grad = lax.dot_general(
        selector.astype(jnp.float32),
        silu_back(products_back)[0],
        (((0,), (0,)), ((), ())),
        precision=lax.Precision.HIGHEST,
        preferred_element_type=jnp.float32,
    )
    return (
        activations[None],
        input_grads[None],
        table_grad,
        modulation_grad[None],
        att[None],
        out[None],
        up[None],
        down[None],
        bias_grad[None],
    )


def solution(mesh):
    shard = P("section", ("dp", "seq"), None)
    in_specs = (
        P(None, "dp", "seq", None),
        P(None, "dp", "seq", None),
        P(),
        P(None, "dp"),
        P(),
        shard,
        shard,
        shard,
        shard,
        shard,
        P("section", ("dp", "seq")),
    )
    out_specs = (
        P("section", None, "dp", "seq", None),
        P("section", None, "dp", "seq", None),
        P(),
        shard,
        shard,
        shard,
        shard,
        shard,
        P("section", ("dp", "seq")),
    )
    return jax.shard_map(
        per_device, mesh=mesh, in_specs=in_specs, out_specs=out_specs, check_vma=False
    )
```

```python
from functools import partial

import jax
import jax.numpy as jnp
from jax import lax
from jax.experimental import pallas as pl
from jax.experimental.pallas import tpu as pltpu
from jax.sharding import PartitionSpec as P

HEADS = 6
HEAD = 64
SCALE = HEAD ** (-0.5)
epsilon = 1e-06
RING = ("dp", "seq")
INNER = (2.0 / 3.141592653589793) ** 0.5
CUBE = 0.044715


def matmul(former, latter):
    return jnp.dot(former, latter, preferred_element_type=jnp.float32)


def matmul_transposed(former, latter):
    return lax.dot_general(
        former, latter, (((1,), (1,)), ((), ())), preferred_element_type=jnp.float32
    )


def outer_sum(former, latter):
    return lax.dot_general(
        former, latter, (((0,), (0,)), ((), ())), preferred_element_type=jnp.float32
    )


def low(values):
    return values.astype(jnp.bfloat16)


def normalize_rows(values):
    centre = jnp.mean(values, axis=-1, keepdims=True)
    centred = values - centre
    spread = jnp.mean(centred * centred, axis=-1, keepdims=True)
    factor = lax.rsqrt(spread + epsilon)
    return (centred * factor, factor)


def normalize_back(normed, factor, grad_normed):
    mean_grad = jnp.mean(grad_normed, axis=-1, keepdims=True)
    mean_cross = jnp.mean(grad_normed * normed, axis=-1, keepdims=True)
    return factor * (grad_normed - mean_grad - normed * mean_cross)


def column_sum(values):
    return jnp.sum(values.astype(jnp.float32), axis=0, keepdims=True)


def saved_shapes(layout, length):
    width, hidden = layout[:2]
    bf16, f32 = jnp.bfloat16, jnp.float32
    return [
        ((1, 6 * width), f32),
        ((length, 3 * width), bf16),
        ((length, width), bf16),
        ((length, hidden), bf16),
        ((HEADS, length, length), f32),
        ((length, hidden), f32),
        ((length, width), f32),
        ((length, width), f32),
        ((hidden, width), bf16),
    ]


def section_kernel(layout, forward, backward, after, *refs):
    width, hidden, rows, ratio, ring_size, share, bias_count = layout
    refs = list(refs)

    def take(count):
        taken = refs[:count]
        del refs[:count]
        return taken

    rank_ref, x_ref = take(2)
    if forward:
        modulation_ref, bias_ref = take(2)
    else:
        saved = take(9)
    if backward:
        (dy_ref,) = take(1)
    mine_ref, theirs_ref = take(2)
    take(after)
    if forward:
        (y_ref,) = take(1)
    if backward:
        dx_ref, dmod_ref, sums_ref, keep_ref, send_ref = take(5)
    elif forward:
        saved = take(9)
    att_w, out_w, up_w, sems, down_s, block_s = take(6)
    if forward:
        down_p, bias_s = take(2)
    if backward:
        da_s, dqkv_s, row_ref, halves, out_sems = take(5)
    if forward and backward:
        saved = take(9)
    mod_s, qkv_s, att_s, u_s, soft_s, slope_s, one_s, two_s, down_w = saved

    rank = rank_ref[0]
    split = hidden - 2 * width

    def fetches(first, second):
        moves = [
            (first.at[:, : 3 * width], att_w),
            (first.at[:, 3 * width : 4 * width], out_w),
            (first.at[:, 4 * width :], up_w.at[:, :split]),
            (second.at[:, : hidden - split], up_w.at[:, split:]),
        ]
        if forward:
            moves.append((second.at[:, hidden - split :], down_p))
        return [
            pltpu.make_async_copy(source, target, sems.at[i])
            for i, (source, target) in enumerate(moves)
        ]

    @pl.when(rank == 0)
    def _():
        for copy in fetches(mine_ref, theirs_ref):
            copy.start()

    @pl.when(rank != 0)
    def _():
        for copy in fetches(theirs_ref, mine_ref):
            copy.start()

    arrivals = fetches(mine_ref, theirs_ref)

    def part(ref, member, head):
        start = member * width + head * HEAD
        return ref[:, start : start + HEAD]

    x = x_ref[...].astype(jnp.float32)
    normed_one, factor_one = normalize_rows(x)
    if forward:
        for d in range(ring_size):
            bias_s[:, d * bias_count : (d + 1) * bias_count] = bias_ref[d : d + 1, :]
        mod_s[...] = modulation_ref[...] + bias_s[:, : 6 * width]
    shift_one, scale_one, gate_one, shift_two, scale_two, gate_two = [
        mod_s[:, i * width : (i + 1) * width] for i in range(6)
    ]
    hidden_one = low(normed_one * (1.0 + scale_one) + shift_one)
    if forward:

        def bias(a, b):
            return bias_s[:, a:b]

        at = 6 * width
        arrivals[0].wait()
        qkv_s[:, :width] = low(matmul(hidden_one, att_w[:, :width]) + bias(at, at + width))
        qkv_s[:, width : 2 * width] = low(matmul(hidden_one, att_w[:, width : 2 * width]))
        qkv_s[:, 2 * width :] = low(
            matmul(hidden_one, att_w[:, 2 * width :]) + bias(at + width, at + 2 * width)
        )
        for head in range(HEADS):
            scores = matmul_transposed(part(qkv_s, 0, head), part(qkv_s, 1, head)) * SCALE
            raised = jnp.exp(scores - jnp.max(scores, axis=-1, keepdims=True))
            soft = raised * (1.0 / jnp.sum(raised, axis=-1, keepdims=True))
            soft_s[head] = soft
            attended = matmul(low(soft), part(qkv_s, 2, head))
            att_s[:, head * HEAD : (head + 1) * HEAD] = low(attended)
        arrivals[1].wait()
        one_s[...] = matmul(att_s[...], out_w[...]) + bias(at + 2 * width, at + 3 * width)
    branch_one = one_s[...]
    middle = x + gate_one * branch_one
    normed_two, factor_two = normalize_rows(middle)
    hidden_two = low(normed_two * (1.0 + scale_two) + shift_two)
    if forward:
        arrivals[2].wait()
        arrivals[3].wait()
        at += 3 * width
        for j in range(ratio):
            cut = slice(j * width, (j + 1) * width)
            a = matmul(hidden_two, up_w[:, cut]) + bias(at + j * width, at + (j + 1) * width)
            square = a * a
            turn = jnp.tanh(INNER * (a + CUBE * (a * square)))
            half_one = 0.5 * (1.0 + turn)
            u_s[:, cut] = low(a * half_one)
            slope_s[:, cut] = half_one + (0.5 * INNER) * a * (1.0 - turn * turn) * (
                1.0 + (3.0 * CUBE) * square
            )
        arrivals[4].wait()
        block_s[...] = down_p[...].astype(jnp.float32)
        for d in range(ring_size):
            for j in range(ratio):
                down_s[(d * ratio + j) * rows : (d * ratio + j + 1) * rows, :] = block_s[
                    d * rows : (d + 1) * rows, j * width : (j + 1) * width
                ]
        down_w[...] = low(down_s[...])
        two_s[...] = matmul(u_s[...], down_w[...]) + bias(at + hidden, at + hidden + width)
        y_ref[...] = low(middle + gate_two * two_s[...])
    if not backward:
        return

    grad_out = dy_ref[...].astype(jnp.float32)
    grad_branch = low(gate_two * grad_out)
    sums_at = 6 * width
    row_ref[:, 5 * width : 6 * width] = column_sum(grad_out * two_s[...])
    row_ref[:, sums_at + 3 * width + hidden : sums_at + 4 * width + hidden] = column_sum(
        grad_branch
    )
    for j in range(ratio):
        cut = slice(j * width, (j + 1) * width)
        grad_expanded = low(slope_s[:, cut] * matmul_transposed(grad_branch, down_w[cut, :]))
        da_s[:, cut] = grad_expanded
        row_ref[:, sums_at + (3 + j) * width : sums_at + (4 + j) * width] = column_sum(
            grad_expanded
        )
    halves[0, :, 4 * width :] = low(outer_sum(hidden_two, da_s[:, :split]) * share)
    halves[1, :, : hidden - split] = low(outer_sum(hidden_two, da_s[:, split:]) * share)
    down_s[...] = outer_sum(u_s[...], grad_branch) * share
    for d in range(ring_size):
        for j in range(ratio):
            block_s[d * rows : (d + 1) * rows, j * width : (j + 1) * width] = down_s[
                (d * ratio + j) * rows : (d * ratio + j + 1) * rows, :
            ]
    halves[1, :, hidden - split :] = low(block_s[...])
    second_out = [
        pltpu.make_async_copy(halves.at[1], keep_ref, out_sems.at[1]),
        pltpu.make_async_copy(halves.at[1], send_ref, out_sems.at[1]),
    ]

    @pl.when(rank == 1)
    def _():
        second_out[0].start()

    @pl.when(rank != 1)
    def _():
        second_out[1].start()

    if not forward:
        arrivals[2].wait()
        arrivals[3].wait()
    grad_hidden_two = matmul_transposed(da_s[...], up_w[...])
    row_ref[:, 3 * width : 4 * width] = column_sum(grad_hidden_two)
    row_ref[:, 4 * width : 5 * width] = column_sum(grad_hidden_two * normed_two)
    grad_middle = grad_out + normalize_back(
        normed_two, factor_two, grad_hidden_two * (1.0 + scale_two)
    )
    row_ref[:, 2 * width : 3 * width] = column_sum(grad_middle * branch_one)
    grad_attention = low(gate_one * grad_middle)
    row_ref[:, sums_at + 2 * width : sums_at + 3 * width] = column_sum(grad_attention)
    halves[0, :, 3 * width : 4 * width] = low(outer_sum(att_s[...], grad_attention) * share)
    if not forward:
        arrivals[1].wait()
    grad_attended = low(matmul_transposed(grad_attention, out_w[...]))
    for head in range(HEADS):
        soft = soft_s[head]
        grad_head = grad_attended[:, head * HEAD : (head + 1) * HEAD]
        grad_soft = matmul_transposed(grad_head, part(qkv_s, 2, head))
        inner = jnp.sum(grad_soft * soft, axis=-1, keepdims=True)
        grad_scores = low(soft * (grad_soft - inner))
        grads = (
            matmul(grad_scores, part(qkv_s, 1, head)) * SCALE,
            outer_sum(grad_scores, part(qkv_s, 0, head)) * SCALE,
            outer_sum(low(soft), grad_head),
        )
        for member, grad in enumerate(grads):
            start = member * width + head * HEAD
            dqkv_s[:, start : start + HEAD] = low(grad)
    row_ref[:, sums_at : sums_at + width] = column_sum(dqkv_s[:, :width])
    row_ref[:, sums_at + width : sums_at + 2 * width] = column_sum(dqkv_s[:, 2 * width :])
    halves[0, :, : 3 * width] = low(outer_sum(hidden_one, dqkv_s[...]) * share)
    first_out = [
        pltpu.make_async_copy(halves.at[0], keep_ref, out_sems.at[0]),
        pltpu.make_async_copy(halves.at[0], send_ref, out_sems.at[0]),
    ]

    @pl.when(rank == 0)
    def _():
        first_out[0].start()

    @pl.when(rank != 0)
    def _():
        first_out[1].start()

    if not forward:
        arrivals[0].wait()
    grad_hidden_one = matmul_transposed(dqkv_s[...], att_w[...])
    row_ref[:, :width] = column_sum(grad_hidden_one)
    row_ref[:, width : 2 * width] = column_sum(grad_hidden_one * normed_one)
    dx_ref[...] = low(
        grad_middle
        + normalize_back(normed_one, factor_one, grad_hidden_one * (1.0 + scale_one))
    )
    row_ref[:, : 6 * width] = low(row_ref[:, : 6 * width]).astype(jnp.float32)
    dmod_ref[...] = row_ref[:, : 6 * width]
    for d in range(ring_size):
        sums_ref[d : d + 1, :] = row_ref[:, d * bias_count : (d + 1) * bias_count]
    second_out[0].wait()
    first_out[0].wait()


def run_section(layout, rank, x, halves, start=None, saved=None, dy=None, after=()):
    width, hidden, rows, ratio, ring_size, share, bias_count = layout
    length = x.shape[0]
    forward, backward = start is not None, dy is not None
    vmem = pl.BlockSpec(memory_space=pltpu.VMEM)
    hbm = pl.BlockSpec(memory_space=pl.ANY)
    bf16, f32 = jnp.bfloat16, jnp.float32
    half = 2 * width + hidden
    kept = saved_shapes(layout, length)
    operands = [rank, x, *(start if forward else saved)]
    shapes, out_specs = [], []
    scratch = [
        pltpu.VMEM((width, 3 * width), bf16),
        pltpu.VMEM((width, width), bf16),
        pltpu.VMEM((width, hidden), bf16),
        pltpu.SemaphoreType.DMA((5,)),
        pltpu.VMEM((hidden, width), f32),
        pltpu.VMEM((width, hidden), f32),
    ]
    if forward:
        shapes.append(jax.ShapeDtypeStruct((length, width), bf16))
        scratch += [
            pltpu.VMEM((width, hidden), bf16),
            pltpu.VMEM((1, bias_count * ring_size), f32),
        ]
    if backward:
        operands.append(dy)
        shapes += [
            jax.ShapeDtypeStruct((length, width), bf16),
            jax.ShapeDtypeStruct((1, 6 * width), f32),
            jax.ShapeDtypeStruct((ring_size, bias_count), f32),
            jax.ShapeDtypeStruct((width, half), bf16),
            jax.ShapeDtypeStruct((width, half), bf16),
        ]
        scratch += [
            pltpu.VMEM((length, hidden), bf16),
            pltpu.VMEM((length, 3 * width), bf16),
            pltpu.VMEM((1, 10 * width + hidden), f32),
            pltpu.VMEM((2, width, half), bf16),
            pltpu.SemaphoreType.DMA((2,)),
        ]
        if forward:
            scratch += [pltpu.VMEM(extent, kind) for extent, kind in kept]
    else:
        shapes += [jax.ShapeDtypeStruct(extent, kind) for extent, kind in kept]
    out_specs = [vmem] * len(shapes)
    if backward:
        out_specs[-2:] = [hbm, hbm]
    specs = [pl.BlockSpec(memory_space=pltpu.SMEM)] + [vmem] * (len(operands) - 1)
    specs += [hbm] * (2 + len(after))
    work = 2 * length * width * (4 * width + 2 * hidden + 2 * length)
    moved = 2 * width * (10 * width + 2 * hidden)
    return pl.pallas_call(
        partial(section_kernel, layout, forward, backward, len(after)),
        out_shape=shapes,
        in_specs=specs,
        out_specs=out_specs,
        scratch_shapes=scratch,
        compiler_params=pltpu.CompilerParams(
            vmem_limit_bytes=(56 if length > 256 else 26 if forward and backward else 22)
            * 1024
            * 1024
        ),
        cost_estimate=pl.CostEstimate(
            flops=(forward + 2 * backward) * work,
            bytes_accessed=(1 + backward) * moved,
            transcendentals=HEADS * length * length + length * hidden,
        ),
    )(*operands, *halves, *after)


def copy_all(copies):
    for copy in copies:
        copy.start()
    for copy in copies:
        copy.wait()


def pack_kernel(rank_ref, att_ref, out_ref, up_ref, down_ref, keep_ref, send_ref, sems):
    ratio, rows, width = down_ref.shape
    split = (ratio - 2) * width

    def copies(first, second):
        moves = [
            (att_ref, first.at[:, : 3 * width]),
            (out_ref, first.at[:, 3 * width : 4 * width]),
            (up_ref.at[:, :split], first.at[:, 4 * width :]),
            (up_ref.at[:, split:], second.at[:, : 2 * width]),
        ]
        for j in range(ratio):
            moves.append((down_ref.at[j], second.at[:, (2 + j) * width : (3 + j) * width]))
        return [
            pltpu.make_async_copy(source, target, sems.at[i])
            for i, (source, target) in enumerate(moves)
        ]

    @pl.when(rank_ref[0] == 0)
    def _():
        copy_all(copies(keep_ref, send_ref))

    @pl.when(rank_ref[0] != 0)
    def _():
        copy_all(copies(send_ref, keep_ref))


def stack_kernel(high, split, place_ref, *refs):
    pieces, sems = refs[:high], refs[-1]
    count = (len(refs) - high - 3) // 2
    handed, targets = refs[high : high + count], refs[high + count : -1]
    copies = [
        pltpu.make_async_copy(former, latter, sems.at[high + i, 0])
        for i, (former, latter) in enumerate(zip(handed, targets[2:]))
    ]
    for turn, piece in enumerate(pieces):
        place = lax.rem(place_ref[0] + (high - turn), high)
        parts = (piece.at[:, :split], piece.at[:, split:])
        for i, (part, target) in enumerate(zip(parts, targets)):
            copies.append(pltpu.make_async_copy(part, target.at[place], sems.at[turn, i]))
    copy_all(copies)


def weave_kernel(split, place_ref, *refs):
    pieces, full_ref, sems = refs[:-2], refs[-2], refs[-1]
    x, y = place_ref[1], place_ref[2]
    copies = []
    for i, piece in enumerate(pieces):
        other_x, other_y = (i % 4) & 1, (i % 4) >> 1
        row = x if not other_x else 1 - x
        column = y if not other_y else 1 - y
        target = full_ref.at[:, row, column, :, pl.ds((i // 4) * split, split)]
        copies.append(pltpu.make_async_copy(piece, target, sems.at[i]))
    copy_all(copies)


def added(former, latter):
    return former.astype(jnp.float32) + latter.astype(jnp.float32)


def chip_sum_kernel(high, place_ref, mine, got, *refs):
    count = (len(refs) - 4) // 2
    first_keep, first_send, second_keep, second_send = refs[count : count + 4]
    for former, latter in zip(refs[:count], refs[count + 4 :]):
        latter[...] = former[...]
    x, y = place_ref[1], place_ref[2]
    half = mine.shape[2]
    lanes = half // 2
    for z in range(high):
        for other in range(2):
            for target, span, chunk in (
                (first_keep, slice(0, lanes), z * 4 + x * 2 + other),
                (first_send, slice(0, lanes), z * 4 + (1 - x) * 2 + other),
                (second_keep, slice(lanes, half), z * 4 + other * 2 + y),
                (second_send, slice(lanes, half), z * 4 + other * 2 + (1 - y)),
            ):
                target[z, other] = low(added(mine[chunk, :, span], got[chunk, :, span]))


def turn_kernel(high, place_ref, *refs):
    count = (len(refs) - 8) // 2
    for former, latter in zip(refs[4 : 4 + count], refs[8 + count :]):
        latter[...] = former[...]
    for part, own in ((0, place_ref[2]), (1, place_ref[1])):
        kept, got = refs[2 * part : 2 * part + 2]
        keep, send = refs[4 + count + 2 * part : 6 + count + 2 * part]
        for z in range(high):
            keep[z] = low(added(kept[z, own], got[z, own]))
            send[z] = low(added(kept[z, 1 - own], got[z, 1 - own]))


def rise_kernel(high, place_ref, *refs):
    count = (len(refs) - 4 - high) // 2
    for former, latter in zip(refs[4 : 4 + count], refs[4 + count + high :]):
        latter[...] = former[...]
    targets = refs[4 + count :]
    lanes = refs[0].shape[2]
    for turn in range(high):
        chunk = lax.rem(place_ref[0] + turn, high)
        for part in range(2):
            kept, got = refs[2 * part : 2 * part + 2]
            total = added(kept[chunk], got[chunk])
            span = slice(part * lanes, (part + 1) * lanes)
            targets[turn][:, span] = total.astype(targets[turn].dtype)


def close_kernel(high, rank_ref, *refs):
    keep, send = refs[-2:]
    totals = []
    for section in range(2):
        pieces = refs[section * high : (section + 1) * high]
        total = pieces[0][...].astype(jnp.float32)
        for piece in pieces[1:]:
            total = total + piece[...].astype(jnp.float32)
        totals.append(total)
    first = rank_ref[0] == 0
    keep[...] = jnp.where(first, totals[0], totals[1])
    send[...] = jnp.where(first, totals[1], totals[0])


def spread_kernel(rank_ref, mine, got, att_ref, out_ref, up_ref, down_ref):
    rows, width = out_ref.shape
    split = up_ref.shape[1] - 2 * width
    first = rank_ref[0] == 0
    lower = jnp.where(first, mine[...], got[...])
    upper = jnp.where(first, got[...], mine[...])
    att_ref[...] = lower[:, : 3 * width]
    out_ref[...] = lower[:, 3 * width : 4 * width]
    up_ref[:, :split] = lower[:, 4 * width :]
    up_ref[:, split:] = upper[:, : 2 * width]
    for j in range(down_ref.shape[0] // rows):
        down_ref[j * rows : (j + 1) * rows, :] = upper[:, (2 + j) * width : (3 + j) * width]


def in_memory(kernel, shapes, operands, scratch=(), memory=pltpu.VMEM, after=(), limit=16):
    specs = [pl.BlockSpec(memory_space=pltpu.SMEM)]
    specs += [pl.BlockSpec(memory_space=memory)] * (len(operands) - 1)
    specs += [pl.BlockSpec(memory_space=pl.ANY)] * len(after)
    count = len(operands)

    def body(*refs):
        kernel(*refs[:count], *refs[count + len(after) :])

    moved = sum(shape.size * shape.dtype.itemsize for shape in shapes)
    return pl.pallas_call(
        body,
        out_shape=shapes,
        in_specs=specs,
        out_specs=[pl.BlockSpec(memory_space=pltpu.VMEM)] * len(shapes),
        scratch_shapes=list(scratch),
        compiler_params=pltpu.CompilerParams(vmem_limit_bytes=limit * 1024 * 1024),
        cost_estimate=pl.CostEstimate(flops=0, bytes_accessed=3 * moved, transcendentals=0),
    )(*operands, *after)


def pair_swap(block, axis):
    return lax.ppermute(block, axis, [(0, 1), (1, 0)])


def ring_exchange(block, size, step):
    return lax.ppermute(block, RING, [(i, step(i)) for i in range(size)])


def flip(block, size, mask):
    return ring_exchange(block, size, lambda i: i ^ mask)


def rotate(block, size, turn):
    return ring_exchange(block, size, lambda i: (i + 4 * turn) % size)


def rotations(block, size):
    return [block] + [rotate(block, size, turn) for turn in range(1, size // 4)]


def gather_along_z(shard, place, size, handed=(), after=()):
    high = size // 4
    rows, lanes = shard.shape
    return in_memory(
        partial(stack_kernel, high, lanes // 2),
        [jax.ShapeDtypeStruct((high, rows, lanes // 2), shard.dtype)] * 2
        + [jax.ShapeDtypeStruct(block.shape, block.dtype) for block in handed],
        [place, *rotations(shard, size), *handed],
        scratch=[pltpu.SemaphoreType.DMA((high + len(handed), 2))],
        after=after,
    )


def first_flips(first, second, size):
    return flip(first, size, 2), flip(second, size, 1)


def gather_across(first, second, first_x, second_y, place, size, after=()):
    high, rows, lanes = first.shape
    first_y, second_x = flip(first, size, 1), flip(second, size, 2)
    first_both, second_both = flip(first_x, size, 1), flip(second_y, size, 2)
    (full,) = in_memory(
        partial(weave_kernel, lanes),
        [jax.ShapeDtypeStruct((high, 2, 2, rows, 2 * lanes), first.dtype)],
        [place, first, first_x, first_y, first_both, second, second_x, second_y, second_both],
        scratch=[pltpu.SemaphoreType.DMA((8,))],
        after=after,
    )
    return full.reshape(size * rows, 2 * lanes)


def scatter_first(mine, got, place, size, handed=(), after=()):
    rows, half = mine.shape[1:]
    shape = jax.ShapeDtypeStruct((size // 4, 2, rows, half // 2), jnp.bfloat16)
    return in_memory(
        partial(chip_sum_kernel, size // 4),
        [shape] * 4 + [jax.ShapeDtypeStruct(block.shape, block.dtype) for block in handed],
        [place, mine, got, *handed],
        after=after,
    )


def scatter_flips(sorted_terms, size):
    first_keep, first_send, second_keep, second_send = sorted_terms
    return first_keep, flip(first_send, size, 2), second_keep, flip(second_send, size, 1)


def scatter_second(received, place, size, handed=(), after=()):
    high, _, rows, lanes = received[0].shape
    shape = jax.ShapeDtypeStruct((high, rows, lanes), jnp.bfloat16)
    first_keep, first_send, second_keep, second_send, *handed = in_memory(
        partial(turn_kernel, high),
        [shape] * 4 + [jax.ShapeDtypeStruct(block.shape, block.dtype) for block in handed],
        [place, *received, *handed],
        after=after,
    )
    turned = (first_keep, flip(first_send, size, 1), second_keep, flip(second_send, size, 2))
    return turned, handed


def scatter_third(turned, place, size, handed=(), after=()):
    high, rows, lanes = turned[0].shape
    chunk = (rows, 2 * lanes)
    return in_memory(
        partial(rise_kernel, high),
        [jax.ShapeDtypeStruct(chunk, jnp.float32)]
        + [jax.ShapeDtypeStruct(chunk, jnp.bfloat16)] * (high - 1)
        + [jax.ShapeDtypeStruct(block.shape, block.dtype) for block in handed],
        [place, *turned, *handed],
        after=after,
    )


def scatter_along_z(pieces, size):
    own, *sent = pieces
    return [own] + [rotate(block, size, turn + 1) for turn, block in enumerate(sent)]


def scatter_sum(block, rank, size):
    half = block.shape[-1] // 2
    pieces = [block[..., :half], block[..., half:]]
    left = size
    low_bits = 0
    while left > 4:
        orders = [(0, 1), (1, 0)] if left % 4 == 0 and left >= 16 else [(0,), (0,)]
        for turn in range(len(orders[0])):
            updated = []
            for piece, order in zip(pieces, orders):
                bit = low_bits + order[turn]
                mine = (rank >> bit) & 1
                if len(order) == 2 and turn == 0:
                    shaped = piece.reshape(-1, 2, 2, *piece.shape[1:])
                    at = 2 - order[turn]
                else:
                    shaped = piece.reshape(-1, 2, *piece.shape[1:])
                    at = 1
                keep = lax.dynamic_index_in_dim(shaped, mine, at, keepdims=False)
                send = lax.dynamic_index_in_dim(shaped, 1 - mine, at, keepdims=False)
                got = ring_exchange(send, size, lambda i, bit=bit: i ^ (1 << bit))
                total = (keep.astype(jnp.float32) + got.astype(jnp.float32)).astype(jnp.bfloat16)
                updated.append(total.reshape(-1, *piece.shape[1:]))
            pieces = updated
        low_bits += len(orders[0])
        left //= 2 ** len(orders[0])
    block = jnp.concatenate(pieces, axis=-1)
    high = rank >> low_bits
    total = lax.dynamic_index_in_dim(block, high, 0, keepdims=False).astype(jnp.float32)
    stride = 1 << low_bits
    for turn in range(1, left):
        send = lax.dynamic_index_in_dim(block, (high + turn) % left, 0, keepdims=False)
        got = ring_exchange(send, size, lambda i, turn=turn: (i + turn * stride) % size)
        total = total + got.astype(jnp.float32)
    return total


def per_device(
    inputs,
    cotangent,
    time_ids,
    row_counts,
    cond_table,
    modulation_weight,
    attention_weight,
    output_weight,
    expand_weight,
    shrink_weight,
    biases,
):
    section_rank = lax.axis_index("section")
    data_rank = lax.axis_index("dp")
    seq_rank = lax.axis_index("seq")
    sections = lax.axis_size("section")
    seq_size = lax.axis_size("seq")
    ring_size = lax.axis_size("dp") * seq_size
    ring_rank = data_rank * seq_size + seq_rank
    batches, slots, tokens, width = inputs.shape
    assert batches == sections == 2 and seq_size % slots == 0
    sharers = seq_size // slots
    slot = seq_rank // sharers
    length = tokens * seq_size
    rows = attention_weight.shape[1]
    ratio = shrink_weight.shape[1] // rows
    hidden = ratio * width
    bias_count = biases.shape[1]
    half = 2 * width + hidden
    assert hidden == expand_weight.shape[2] and ratio >= 2
    table_rows = cond_table.shape[0]
    is_first = section_rank == 0
    layout = (width, hidden, rows, ratio, ring_size, 1.0 / sharers, bias_count)
    compact = ring_size in (8, 16) and seq_size == slots == 2
    rank = section_rank.astype(jnp.int32).reshape(1)
    place = jnp.stack([ring_rank >> 2, (ring_rank >> 1) & 1, ring_rank & 1]).astype(jnp.int32)

    keep, send = in_memory(
        pack_kernel,
        [jax.ShapeDtypeStruct((rows, half), jnp.bfloat16)] * 2,
        [
            rank,
            attention_weight[0],
            output_weight[0],
            expand_weight[0],
            shrink_weight[0].reshape(ratio, rows, width),
        ],
        scratch=[pltpu.SemaphoreType.DMA((4 + ratio,))],
        memory=pl.ANY,
        limit=56,
    )
    got = pair_swap(send, "section")
    first_shard = jnp.where(is_first, keep, got)
    second_shard = jnp.where(is_first, got, keep)

    live = (
        slot < lax.dynamic_index_in_dim(row_counts, section_rank, 0, keepdims=False)[0]
    ).astype(jnp.bfloat16)
    both = jnp.stack(
        [
            lax.dynamic_index_in_dim(inputs, section_rank, 0, keepdims=False),
            lax.dynamic_index_in_dim(cotangent, section_rank, 0, keepdims=False),
        ],
        axis=1,
    )

    def side_by_side(mine, got, axis):
        return jnp.where(
            seq_rank == 0,
            jnp.concatenate([mine, got], axis=axis),
            jnp.concatenate([got, mine], axis=axis),
        )

    if compact:
        mine = lax.dynamic_index_in_dim(both, seq_rank, 0, keepdims=False)
        sent = lax.dynamic_index_in_dim(both, 1 - seq_rank, 0, keepdims=False)
        both = side_by_side(mine, pair_swap(sent, "seq"), 1)
    else:
        both = lax.all_to_all(jnp.repeat(both, sharers, axis=0), "seq", 0, 0, tiled=True)
        both = jnp.swapaxes(both, 0, 1).reshape(2, length, width)
    first_input = both[0]
    last_grad = both[1] * live

    flat_ids = time_ids.reshape(-1)
    selector = (
        flat_ids[:, None] == jnp.arange(table_rows, dtype=jnp.int32)[None, :]
    ).astype(jnp.bfloat16)
    conditions = matmul(selector, cond_table)
    silu_all = jax.nn.silu(conditions).astype(jnp.bfloat16)
    silu_own = lax.dynamic_slice_in_dim(silu_all, ring_rank * rows, rows, 1)
    if compact:
        *first_parts, second_shard = gather_along_z(
            first_shard, place, ring_size, handed=(second_shard,)
        )
        first_parts += first_flips(*first_parts, ring_size)
        *second_parts, silu_late = gather_along_z(
            second_shard, place, ring_size, handed=(silu_own,), after=(both, *first_parts[2:])
        )
        second_parts += first_flips(*second_parts, ring_size)
    else:
        silu_late = silu_own

    products = matmul(silu_late, modulation_weight[0])
    own_bias = jnp.broadcast_to(biases.astype(jnp.float32), (products.shape[0], bias_count))
    products = jnp.repeat(jnp.concatenate([products, own_bias], axis=1), sharers, axis=0)
    products = lax.all_to_all(
        products[:, None], ("section", "dp", "seq"), 0, 0, tiled=True
    ).reshape(sections, ring_size, 6 * width + bias_count)
    first_modulation, second_modulation = jnp.split(
        jnp.sum(products[:, :, : 6 * width], axis=1), 2, axis=0
    )
    first_bias, second_bias = products[0, :, 6 * width :], products[1, :, 6 * width :]

    if compact:
        first_pack = gather_across(*first_parts, place, ring_size, after=(products,))
        second_pack = gather_across(*second_parts, place, ring_size)
    else:
        first_pack = lax.all_gather(first_shard, RING, axis=0, tiled=True)
        second_pack = lax.all_gather(second_shard, RING, axis=0, tiled=True)
    first_halves = (first_pack, pair_swap(first_pack, "section"))
    second_halves = (second_pack, pair_swap(second_pack, "section"))

    first_low, *first_saved = run_section(
        layout, rank, first_input, first_halves, (first_modulation, first_bias)
    )
    second_low, second_grad, second_dmod, second_sums, second_keep, second_send = run_section(
        layout, rank, first_low, second_halves, (second_modulation, second_bias), dy=last_grad
    )
    second_got = pair_swap(second_send, "section")

    def ring_terms(term):
        return term.reshape(ring_size, rows, half)

    first_grad, first_dmod, first_sums, first_keep, first_send = run_section(
        layout, rank, first_input, first_halves, saved=first_saved, dy=second_grad
    )
    first_got = pair_swap(first_send, "section")

    shard = jax.ShapeDtypeStruct((rows, half), jnp.float32)
    if compact:
        second_sorted = scatter_first(
            ring_terms(second_keep), ring_terms(second_got), place, ring_size
        )
        second_received = scatter_flips(second_sorted, ring_size)
        first_sorted = scatter_first(
            ring_terms(first_keep),
            ring_terms(first_got),
            place,
            ring_size,
            after=(second_sorted[0],),
        )
        first_received = scatter_flips(first_sorted, ring_size)
        second_turned, (first_dmod, first_sums) = scatter_second(
            second_received, place, ring_size, handed=(first_dmod, first_sums)
        )
        second_sent = scatter_third(second_turned, place, ring_size)
        second_pieces = scatter_along_z(second_sent, ring_size)
        first_turned, (first_grad,) = scatter_second(
            first_received, place, ring_size, handed=(first_grad,), after=(second_sent[0],)
        )

    rows_back = jnp.concatenate(
        [
            jnp.concatenate(
                [jnp.broadcast_to(dmod, (ring_size, 6 * width)), sums], axis=1
            )
            for dmod, sums in ((first_dmod, first_sums), (second_dmod, second_sums))
        ]
    )
    every = lax.all_to_all(rows_back[:, None], ("section", "dp", "seq"), 0, 0, tiled=True)
    every = every[::sharers, 0]
    bias_grad = jnp.sum(every[:, 6 * width :], axis=0)
    modulation_rows = low(every[:, : 6 * width])
    modulation_grad = outer_sum(silu_own, modulation_rows)
    columns = matmul_transposed(modulation_rows, modulation_weight[0])

    if compact:
        *first_sent, columns = scatter_third(
            first_turned, place, ring_size, handed=(columns,), after=tuple(second_pieces[1:])
        )
        first_pieces = scatter_along_z(first_sent, ring_size)
    else:

        def chip_sum(keep, got):
            return ring_terms(low(added(keep, got)))

        first_pieces, second_pieces = [
            [scatter_sum(chip_sum(keep, got), ring_rank, ring_size)]
            for keep, got in ((first_keep, first_got), (second_keep, second_got))
        ]
    outputs_ready = (first_low * live, second_low * live)
    if compact:
        block = jnp.stack([outputs_ready[0], first_grad, outputs_ready[1], second_grad])
        block = block.reshape(4, 2, tokens, width)
        mine = lax.dynamic_index_in_dim(block, seq_rank, 1, keepdims=True)
        sent = lax.dynamic_index_in_dim(block, 1 - seq_rank, 1, keepdims=True)
        block = side_by_side(mine, pair_swap(sent, "seq"), 1)
        per_first, per_second = block[:2], block[2:]
        mine = jnp.where(is_first, per_first, per_second)
        got = pair_swap(jnp.where(is_first, per_second, per_first), "section")
        outputs = jnp.where(is_first, jnp.stack([mine, got], 1), jnp.stack([got, mine], 1))
    else:
        pieces = jnp.stack([outputs_ready[0], first_grad, outputs_ready[1], second_grad])
        pieces = jnp.swapaxes(pieces.reshape(2, 2, seq_size, tokens, width), 1, 2)
        pieces = pieces.reshape(2 * seq_size, 2, tokens, width)
        pieces = lax.all_to_all(pieces, ("section", "seq"), 0, 0, tiled=True)
        pieces = pieces.reshape(batches, slots, sharers, 2, tokens, width)[:, :, 0]
        outputs = jnp.moveaxis(pieces, 2, 0)
    activations = outputs[0]
    input_grads = outputs[1].astype(jnp.float32)

    mine, send = in_memory(
        partial(close_kernel, len(first_pieces)),
        [shard, shard],
        [rank, *first_pieces, *second_pieces],
    )
    att, out, up, down = in_memory(
        spread_kernel,
        [
            jax.ShapeDtypeStruct(extent, jnp.float32)
            for extent in (
                (rows, 3 * width),
                (rows, width),
                (rows, hidden),
                (rows * ratio, width),
            )
        ],
        [rank, mine, pair_swap(send, "section")],
    )

    columns = jnp.broadcast_to(columns.reshape(1, 1, -1), (sections * ring_size, 1, columns.size))
    columns = lax.all_to_all(columns, ("section", "dp", "seq"), 0, 0, tiled=True)
    columns = jnp.sum(columns.reshape(sections, ring_size, -1, rows), axis=0)
    products_back = jnp.swapaxes(columns, 0, 1).reshape(-1, width)
    _, silu_back = jax.vjp(jax.nn.silu, conditions)
    table_grad = lax.dot_general(
        selector.astype(jnp.float32),
        silu_back(products_back)[0],
        (((0,), (0,)), ((), ())),
        precision=lax.Precision.HIGHEST,
        preferred_element_type=jnp.float32,
    )
    return (
        activations[None],
        input_grads[None],
        table_grad,
        modulation_grad[None],
        att[None],
        out[None],
        up[None],
        down[None],
        bias_grad[None],
    )


def solution(mesh):
    shard = P("section", ("dp", "seq"), None)
    in_specs = (
        P(None, "dp", "seq", None),
        P(None, "dp", "seq", None),
        P(),
        P(None, "dp"),
        P(),
        shard,
        shard,
        shard,
        shard,
        shard,
        P("section", ("dp", "seq")),
    )
    out_specs = (
        P("section", None, "dp", "seq", None),
        P("section", None, "dp", "seq", None),
        P(),
        shard,
        shard,
        shard,
        shard,
        shard,
        P("section", ("dp", "seq")),
    )
    return jax.shard_map(
        per_device, mesh=mesh, in_specs=in_specs, out_specs=out_specs, check_vma=False
    )
```

```python
from functools import partial

import jax
import jax.numpy as jnp
from jax import lax
from jax.experimental import pallas as pl
from jax.experimental.pallas import tpu as pltpu
from jax.sharding import PartitionSpec as P

HEADS = 6
HEAD = 64
SCALE = HEAD ** (-0.5)
epsilon = 1e-06
RING = ("dp", "seq")
INNER = (2.0 / 3.141592653589793) ** 0.5
CUBE = 0.044715


def matmul(former, latter):
    return jnp.dot(former, latter, preferred_element_type=jnp.float32)


def matmul_transposed(former, latter):
    return lax.dot_general(
        former, latter, (((1,), (1,)), ((), ())), preferred_element_type=jnp.float32
    )


def outer_sum(former, latter):
    return lax.dot_general(
        former, latter, (((0,), (0,)), ((), ())), preferred_element_type=jnp.float32
    )


def low(values):
    return values.astype(jnp.bfloat16)


def normalize_rows(values):
    centre = jnp.mean(values, axis=-1, keepdims=True)
    centred = values - centre
    spread = jnp.mean(centred * centred, axis=-1, keepdims=True)
    factor = lax.rsqrt(spread + epsilon)
    return (centred * factor, factor)


def normalize_back(normed, factor, grad_normed):
    mean_grad = jnp.mean(grad_normed, axis=-1, keepdims=True)
    mean_cross = jnp.mean(grad_normed * normed, axis=-1, keepdims=True)
    return factor * (grad_normed - mean_grad - normed * mean_cross)


def column_sum(values):
    return jnp.sum(values.astype(jnp.float32), axis=0, keepdims=True)


def saved_shapes(layout, length):
    width, hidden = layout[:2]
    bf16, f32 = jnp.bfloat16, jnp.float32
    return [
        ((1, 6 * width), f32),
        ((length, 3 * width), bf16),
        ((length, width), bf16),
        ((length, hidden), bf16),
        ((HEADS, length, length), f32),
        ((length, hidden), f32),
        ((length, width), f32),
        ((length, width), f32),
        ((hidden, width), bf16),
    ]


def section_kernel(layout, forward, backward, after, *refs):
    width, hidden, rows, ratio, ring_size, share, bias_count = layout
    refs = list(refs)

    def take(count):
        taken = refs[:count]
        del refs[:count]
        return taken

    rank_ref, x_ref = take(2)
    if forward:
        modulation_ref, bias_ref = take(2)
    else:
        saved = take(9)
    if backward:
        (dy_ref,) = take(1)
    mine_ref, theirs_ref = take(2)
    take(after)
    if forward:
        (y_ref,) = take(1)
    if backward:
        dx_ref, dmod_ref, sums_ref, keep_ref, send_ref = take(5)
    elif forward:
        saved = take(9)
    att_w, out_w, up_w, sems, down_s, block_s = take(6)
    if forward:
        down_p, bias_s = take(2)
    if backward:
        da_s, dqkv_s, row_ref, halves, out_sems = take(5)
    if forward and backward:
        saved = take(9)
    mod_s, qkv_s, att_s, u_s, soft_s, slope_s, one_s, two_s, down_w = saved

    rank = rank_ref[0]
    split = hidden - 2 * width

    def fetches(first, second):
        moves = [
            (first.at[:, : 3 * width], att_w),
            (first.at[:, 3 * width : 4 * width], out_w),
            (first.at[:, 4 * width :], up_w.at[:, :split]),
            (second.at[:, : hidden - split], up_w.at[:, split:]),
        ]
        if forward:
            moves.append((second.at[:, hidden - split :], down_p))
        return [
            pltpu.make_async_copy(source, target, sems.at[i])
            for i, (source, target) in enumerate(moves)
        ]

    @pl.when(rank == 0)
    def _():
        for copy in fetches(mine_ref, theirs_ref):
            copy.start()

    @pl.when(rank != 0)
    def _():
        for copy in fetches(theirs_ref, mine_ref):
            copy.start()

    arrivals = fetches(mine_ref, theirs_ref)

    def part(ref, member, head):
        start = member * width + head * HEAD
        return ref[:, start : start + HEAD]

    x = x_ref[...].astype(jnp.float32)
    normed_one, factor_one = normalize_rows(x)
    if forward:
        for d in range(ring_size):
            bias_s[:, d * bias_count : (d + 1) * bias_count] = bias_ref[d : d + 1, :]
        mod_s[...] = modulation_ref[...] + bias_s[:, : 6 * width]
    shift_one, scale_one, gate_one, shift_two, scale_two, gate_two = [
        mod_s[:, i * width : (i + 1) * width] for i in range(6)
    ]
    hidden_one = low(normed_one * (1.0 + scale_one) + shift_one)
    if forward:

        def bias(a, b):
            return bias_s[:, a:b]

        at = 6 * width
        arrivals[0].wait()
        qkv_s[:, :width] = low(matmul(hidden_one, att_w[:, :width]) + bias(at, at + width))
        qkv_s[:, width : 2 * width] = low(matmul(hidden_one, att_w[:, width : 2 * width]))
        qkv_s[:, 2 * width :] = low(
            matmul(hidden_one, att_w[:, 2 * width :]) + bias(at + width, at + 2 * width)
        )
        for head in range(HEADS):
            scores = matmul_transposed(part(qkv_s, 0, head), part(qkv_s, 1, head)) * SCALE
            raised = jnp.exp(scores - jnp.max(scores, axis=-1, keepdims=True))
            soft = raised * (1.0 / jnp.sum(raised, axis=-1, keepdims=True))
            soft_s[head] = soft
            attended = matmul(low(soft), part(qkv_s, 2, head))
            att_s[:, head * HEAD : (head + 1) * HEAD] = low(attended)
        arrivals[1].wait()
        one_s[...] = matmul(att_s[...], out_w[...]) + bias(at + 2 * width, at + 3 * width)
    branch_one = one_s[...]
    middle = x + gate_one * branch_one
    normed_two, factor_two = normalize_rows(middle)
    hidden_two = low(normed_two * (1.0 + scale_two) + shift_two)
    if forward:
        arrivals[2].wait()
        arrivals[3].wait()
        at += 3 * width
        for j in range(ratio):
            cut = slice(j * width, (j + 1) * width)
            a = matmul(hidden_two, up_w[:, cut]) + bias(at + j * width, at + (j + 1) * width)
            square = a * a
            turn = jnp.tanh(INNER * (a + CUBE * (a * square)))
            half_one = 0.5 * (1.0 + turn)
            u_s[:, cut] = low(a * half_one)
            slope_s[:, cut] = half_one + (0.5 * INNER) * a * (1.0 - turn * turn) * (
                1.0 + (3.0 * CUBE) * square
            )
        arrivals[4].wait()
        block_s[...] = down_p[...].astype(jnp.float32)
        for d in range(ring_size):
            for j in range(ratio):
                down_s[(d * ratio + j) * rows : (d * ratio + j + 1) * rows, :] = block_s[
                    d * rows : (d + 1) * rows, j * width : (j + 1) * width
                ]
        down_w[...] = low(down_s[...])
        two_s[...] = matmul(u_s[...], down_w[...]) + bias(at + hidden, at + hidden + width)
        y_ref[...] = low(middle + gate_two * two_s[...])
    if not backward:
        return

    grad_out = dy_ref[...].astype(jnp.float32)
    grad_branch = low(gate_two * grad_out)
    sums_at = 6 * width
    row_ref[:, 5 * width : 6 * width] = column_sum(grad_out * two_s[...])
    row_ref[:, sums_at + 3 * width + hidden : sums_at + 4 * width + hidden] = column_sum(
        grad_branch
    )
    for j in range(ratio):
        cut = slice(j * width, (j + 1) * width)
        grad_expanded = low(slope_s[:, cut] * matmul_transposed(grad_branch, down_w[cut, :]))
        da_s[:, cut] = grad_expanded
        row_ref[:, sums_at + (3 + j) * width : sums_at + (4 + j) * width] = column_sum(
            grad_expanded
        )
    halves[0, :, 4 * width :] = low(outer_sum(hidden_two, da_s[:, :split]) * share)
    halves[1, :, : hidden - split] = low(outer_sum(hidden_two, da_s[:, split:]) * share)
    down_s[...] = outer_sum(u_s[...], grad_branch) * share
    for d in range(ring_size):
        for j in range(ratio):
            block_s[d * rows : (d + 1) * rows, j * width : (j + 1) * width] = down_s[
                (d * ratio + j) * rows : (d * ratio + j + 1) * rows, :
            ]
    halves[1, :, hidden - split :] = low(block_s[...])
    second_out = [
        pltpu.make_async_copy(halves.at[1], keep_ref, out_sems.at[1]),
        pltpu.make_async_copy(halves.at[1], send_ref, out_sems.at[1]),
    ]

    @pl.when(rank == 1)
    def _():
        second_out[0].start()

    @pl.when(rank != 1)
    def _():
        second_out[1].start()

    if not forward:
        arrivals[2].wait()
        arrivals[3].wait()
    grad_hidden_two = matmul_transposed(da_s[...], up_w[...])
    row_ref[:, 3 * width : 4 * width] = column_sum(grad_hidden_two)
    row_ref[:, 4 * width : 5 * width] = column_sum(grad_hidden_two * normed_two)
    grad_middle = grad_out + normalize_back(
        normed_two, factor_two, grad_hidden_two * (1.0 + scale_two)
    )
    row_ref[:, 2 * width : 3 * width] = column_sum(grad_middle * branch_one)
    grad_attention = low(gate_one * grad_middle)
    row_ref[:, sums_at + 2 * width : sums_at + 3 * width] = column_sum(grad_attention)
    halves[0, :, 3 * width : 4 * width] = low(outer_sum(att_s[...], grad_attention) * share)
    if not forward:
        arrivals[1].wait()
    grad_attended = low(matmul_transposed(grad_attention, out_w[...]))
    for head in range(HEADS):
        soft = soft_s[head]
        grad_head = grad_attended[:, head * HEAD : (head + 1) * HEAD]
        grad_soft = matmul_transposed(grad_head, part(qkv_s, 2, head))
        inner = jnp.sum(grad_soft * soft, axis=-1, keepdims=True)
        grad_scores = low(soft * (grad_soft - inner))
        grads = (
            matmul(grad_scores, part(qkv_s, 1, head)) * SCALE,
            outer_sum(grad_scores, part(qkv_s, 0, head)) * SCALE,
            outer_sum(low(soft), grad_head),
        )
        for member, grad in enumerate(grads):
            start = member * width + head * HEAD
            dqkv_s[:, start : start + HEAD] = low(grad)
    row_ref[:, sums_at : sums_at + width] = column_sum(dqkv_s[:, :width])
    row_ref[:, sums_at + width : sums_at + 2 * width] = column_sum(dqkv_s[:, 2 * width :])
    halves[0, :, : 3 * width] = low(outer_sum(hidden_one, dqkv_s[...]) * share)
    first_out = [
        pltpu.make_async_copy(halves.at[0], keep_ref, out_sems.at[0]),
        pltpu.make_async_copy(halves.at[0], send_ref, out_sems.at[0]),
    ]

    @pl.when(rank == 0)
    def _():
        first_out[0].start()

    @pl.when(rank != 0)
    def _():
        first_out[1].start()

    if not forward:
        arrivals[0].wait()
    grad_hidden_one = matmul_transposed(dqkv_s[...], att_w[...])
    row_ref[:, :width] = column_sum(grad_hidden_one)
    row_ref[:, width : 2 * width] = column_sum(grad_hidden_one * normed_one)
    dx_ref[...] = low(
        grad_middle
        + normalize_back(normed_one, factor_one, grad_hidden_one * (1.0 + scale_one))
    )
    row_ref[:, : 6 * width] = low(row_ref[:, : 6 * width]).astype(jnp.float32)
    dmod_ref[...] = row_ref[:, : 6 * width]
    for d in range(ring_size):
        sums_ref[d : d + 1, :] = row_ref[:, d * bias_count : (d + 1) * bias_count]
    second_out[0].wait()
    first_out[0].wait()


def run_section(layout, rank, x, halves, start=None, saved=None, dy=None, after=()):
    width, hidden, rows, ratio, ring_size, share, bias_count = layout
    length = x.shape[0]
    forward, backward = start is not None, dy is not None
    vmem = pl.BlockSpec(memory_space=pltpu.VMEM)
    hbm = pl.BlockSpec(memory_space=pl.ANY)
    bf16, f32 = jnp.bfloat16, jnp.float32
    half = 2 * width + hidden
    kept = saved_shapes(layout, length)
    operands = [rank, x, *(start if forward else saved)]
    shapes, out_specs = [], []
    scratch = [
        pltpu.VMEM((width, 3 * width), bf16),
        pltpu.VMEM((width, width), bf16),
        pltpu.VMEM((width, hidden), bf16),
        pltpu.SemaphoreType.DMA((5,)),
        pltpu.VMEM((hidden, width), f32),
        pltpu.VMEM((width, hidden), f32),
    ]
    if forward:
        shapes.append(jax.ShapeDtypeStruct((length, width), bf16))
        scratch += [
            pltpu.VMEM((width, hidden), bf16),
            pltpu.VMEM((1, bias_count * ring_size), f32),
        ]
    if backward:
        operands.append(dy)
        shapes += [
            jax.ShapeDtypeStruct((length, width), bf16),
            jax.ShapeDtypeStruct((1, 6 * width), f32),
            jax.ShapeDtypeStruct((ring_size, bias_count), f32),
            jax.ShapeDtypeStruct((width, half), bf16),
            jax.ShapeDtypeStruct((width, half), bf16),
        ]
        scratch += [
            pltpu.VMEM((length, hidden), bf16),
            pltpu.VMEM((length, 3 * width), bf16),
            pltpu.VMEM((1, 10 * width + hidden), f32),
            pltpu.VMEM((2, width, half), bf16),
            pltpu.SemaphoreType.DMA((2,)),
        ]
        if forward:
            scratch += [pltpu.VMEM(extent, kind) for extent, kind in kept]
    else:
        shapes += [jax.ShapeDtypeStruct(extent, kind) for extent, kind in kept]
    out_specs = [vmem] * len(shapes)
    if backward:
        out_specs[-2:] = [hbm, hbm]
    specs = [pl.BlockSpec(memory_space=pltpu.SMEM)] + [vmem] * (len(operands) - 1)
    specs += [hbm] * (2 + len(after))
    work = 2 * length * width * (4 * width + 2 * hidden + 2 * length)
    moved = 2 * width * (10 * width + 2 * hidden)
    return pl.pallas_call(
        partial(section_kernel, layout, forward, backward, len(after)),
        out_shape=shapes,
        in_specs=specs,
        out_specs=out_specs,
        scratch_shapes=scratch,
        compiler_params=pltpu.CompilerParams(
            vmem_limit_bytes=(56 if length > 256 else 26 if forward and backward else 22)
            * 1024
            * 1024
        ),
        cost_estimate=pl.CostEstimate(
            flops=(forward + 2 * backward) * work,
            bytes_accessed=(1 + backward) * moved,
            transcendentals=HEADS * length * length + length * hidden,
        ),
    )(*operands, *halves, *after)


def copy_all(copies):
    for copy in copies:
        copy.start()
    for copy in copies:
        copy.wait()


def pack_kernel(rank_ref, att_ref, out_ref, up_ref, down_ref, keep_ref, send_ref, sems):
    ratio, rows, width = down_ref.shape
    split = (ratio - 2) * width

    def copies(first, second):
        moves = [
            (att_ref, first.at[:, : 3 * width]),
            (out_ref, first.at[:, 3 * width : 4 * width]),
            (up_ref.at[:, :split], first.at[:, 4 * width :]),
            (up_ref.at[:, split:], second.at[:, : 2 * width]),
        ]
        for j in range(ratio):
            moves.append((down_ref.at[j], second.at[:, (2 + j) * width : (3 + j) * width]))
        return [
            pltpu.make_async_copy(source, target, sems.at[i])
            for i, (source, target) in enumerate(moves)
        ]

    @pl.when(rank_ref[0] == 0)
    def _():
        copy_all(copies(keep_ref, send_ref))

    @pl.when(rank_ref[0] != 0)
    def _():
        copy_all(copies(send_ref, keep_ref))


def stack_kernel(high, split, place_ref, *refs):
    pieces, sems = refs[:high], refs[-1]
    count = (len(refs) - high - 3) // 2
    handed, targets = refs[high : high + count], refs[high + count : -1]
    copies = [
        pltpu.make_async_copy(former, latter, sems.at[high + i, 0])
        for i, (former, latter) in enumerate(zip(handed, targets[2:]))
    ]
    for turn, piece in enumerate(pieces):
        place = lax.rem(place_ref[0] + (high - turn), high)
        parts = (piece.at[:, :split], piece.at[:, split:])
        for i, (part, target) in enumerate(zip(parts, targets)):
            copies.append(pltpu.make_async_copy(part, target.at[place], sems.at[turn, i]))
    copy_all(copies)


def weave_kernel(split, place_ref, *refs):
    pieces, full_ref, sems = refs[:-2], refs[-2], refs[-1]
    x, y = place_ref[1], place_ref[2]
    copies = []
    for i, piece in enumerate(pieces):
        other_x, other_y = (i % 4) & 1, (i % 4) >> 1
        row = x if not other_x else 1 - x
        column = y if not other_y else 1 - y
        target = full_ref.at[:, row, column, :, pl.ds((i // 4) * split, split)]
        copies.append(pltpu.make_async_copy(piece, target, sems.at[i]))
    copy_all(copies)


def added(former, latter):
    return former.astype(jnp.float32) + latter.astype(jnp.float32)


def chip_sum_kernel(high, place_ref, mine, got, *refs):
    count = (len(refs) - 4) // 2
    first_keep, first_send, second_keep, second_send = refs[count : count + 4]
    for former, latter in zip(refs[:count], refs[count + 4 :]):
        latter[...] = former[...]
    x, y = place_ref[1], place_ref[2]
    half = mine.shape[2]
    lanes = half // 2
    for z in range(high):
        for other in range(2):
            for target, span, chunk in (
                (first_keep, slice(0, lanes), z * 4 + x * 2 + other),
                (first_send, slice(0, lanes), z * 4 + (1 - x) * 2 + other),
                (second_keep, slice(lanes, half), z * 4 + other * 2 + y),
                (second_send, slice(lanes, half), z * 4 + other * 2 + (1 - y)),
            ):
                target[z, other] = low(added(mine[chunk, :, span], got[chunk, :, span]))


def turn_kernel(high, place_ref, *refs):
    count = (len(refs) - 8) // 2
    for former, latter in zip(refs[4 : 4 + count], refs[8 + count :]):
        latter[...] = former[...]
    for part, own in ((0, place_ref[2]), (1, place_ref[1])):
        kept, got = refs[2 * part : 2 * part + 2]
        keep, send = refs[4 + count + 2 * part : 6 + count + 2 * part]
        for z in range(high):
            keep[z] = low(added(kept[z, own], got[z, own]))
            send[z] = low(added(kept[z, 1 - own], got[z, 1 - own]))


def rise_kernel(high, place_ref, *refs):
    targets = refs[4:]
    lanes = refs[0].shape[2]
    for turn in range(high):
        chunk = lax.rem(place_ref[0] + turn, high)
        for part in range(2):
            kept, got = refs[2 * part : 2 * part + 2]
            total = added(kept[chunk], got[chunk])
            span = slice(part * lanes, (part + 1) * lanes)
            targets[turn][:, span] = total.astype(targets[turn].dtype)


def close_kernel(high, rank_ref, *refs):
    keep, send = refs[-2:]
    totals = []
    for section in range(2):
        pieces = refs[section * high : (section + 1) * high]
        total = pieces[0][...].astype(jnp.float32)
        for piece in pieces[1:]:
            total = total + piece[...].astype(jnp.float32)
        totals.append(total)
    first = rank_ref[0] == 0
    keep[...] = jnp.where(first, totals[0], totals[1])
    send[...] = jnp.where(first, totals[1], totals[0])


def spread_kernel(rank_ref, mine, got, att_ref, out_ref, up_ref, down_ref):
    rows, width = out_ref.shape
    split = up_ref.shape[1] - 2 * width
    first = rank_ref[0] == 0
    lower = jnp.where(first, mine[...], got[...])
    upper = jnp.where(first, got[...], mine[...])
    att_ref[...] = lower[:, : 3 * width]
    out_ref[...] = lower[:, 3 * width : 4 * width]
    up_ref[:, :split] = lower[:, 4 * width :]
    up_ref[:, split:] = upper[:, : 2 * width]
    for j in range(down_ref.shape[0] // rows):
        down_ref[j * rows : (j + 1) * rows, :] = upper[:, (2 + j) * width : (3 + j) * width]


def in_memory(kernel, shapes, operands, scratch=(), memory=pltpu.VMEM, after=(), limit=16):
    specs = [pl.BlockSpec(memory_space=pltpu.SMEM)]
    specs += [pl.BlockSpec(memory_space=memory)] * (len(operands) - 1)
    specs += [pl.BlockSpec(memory_space=pl.ANY)] * len(after)
    count = len(operands)

    def body(*refs):
        kernel(*refs[:count], *refs[count + len(after) :])

    moved = sum(shape.size * shape.dtype.itemsize for shape in shapes)
    return pl.pallas_call(
        body,
        out_shape=shapes,
        in_specs=specs,
        out_specs=[pl.BlockSpec(memory_space=pltpu.VMEM)] * len(shapes),
        scratch_shapes=list(scratch),
        compiler_params=pltpu.CompilerParams(vmem_limit_bytes=limit * 1024 * 1024),
        cost_estimate=pl.CostEstimate(flops=0, bytes_accessed=3 * moved, transcendentals=0),
    )(*operands, *after)


def hand_kernel(rank_ref, former, latter):
    latter[...] = former[...]


def hand_on(rank, block, after):
    shape = jax.ShapeDtypeStruct(block.shape, block.dtype)
    return in_memory(hand_kernel, [shape], [rank, block], after=after)[0]


def pair_swap(block, axis):
    return lax.ppermute(block, axis, [(0, 1), (1, 0)])


def ring_exchange(block, size, step):
    return lax.ppermute(block, RING, [(i, step(i)) for i in range(size)])


def flip(block, size, mask):
    return ring_exchange(block, size, lambda i: i ^ mask)


def rotate(block, size, turn):
    return ring_exchange(block, size, lambda i: (i + 4 * turn) % size)


def rotations(block, size):
    return [block] + [rotate(block, size, turn) for turn in range(1, size // 4)]


def gather_along_z(shards, place, handed=(), after=()):
    high = len(shards)
    rows, lanes = shards[0].shape
    return in_memory(
        partial(stack_kernel, high, lanes // 2),
        [jax.ShapeDtypeStruct((high, rows, lanes // 2), shards[0].dtype)] * 2
        + [jax.ShapeDtypeStruct(block.shape, block.dtype) for block in handed],
        [place, *shards, *handed],
        scratch=[pltpu.SemaphoreType.DMA((high + len(handed), 2))],
        memory=pl.ANY,
        after=after,
    )


def first_flips(first, second, size):
    return flip(first, size, 2), flip(second, size, 1)


def gather_across(first, second, first_x, second_y, place, size):
    high, rows, lanes = first.shape
    first_y, second_x = flip(first, size, 1), flip(second, size, 2)
    first_both, second_both = flip(first_x, size, 1), flip(second_y, size, 2)
    (full,) = in_memory(
        partial(weave_kernel, lanes),
        [jax.ShapeDtypeStruct((high, 2, 2, rows, 2 * lanes), first.dtype)],
        [place, first, first_x, first_y, first_both, second, second_x, second_y, second_both],
        scratch=[pltpu.SemaphoreType.DMA((8,))],
        memory=pl.ANY,
    )
    return full.reshape(size * rows, 2 * lanes)


def scatter_first(mine, got, place, size, handed=(), after=()):
    rows, half = mine.shape[1:]
    shape = jax.ShapeDtypeStruct((size // 4, 2, rows, half // 2), jnp.bfloat16)
    return in_memory(
        partial(chip_sum_kernel, size // 4),
        [shape] * 4 + [jax.ShapeDtypeStruct(block.shape, block.dtype) for block in handed],
        [place, mine, got, *handed],
        after=after,
    )


def scatter_flips(sorted_terms, size):
    first_keep, first_send, second_keep, second_send = sorted_terms
    return first_keep, flip(first_send, size, 2), second_keep, flip(second_send, size, 1)


def scatter_second(received, place, size, handed=(), after=()):
    high, _, rows, lanes = received[0].shape
    shape = jax.ShapeDtypeStruct((high, rows, lanes), jnp.bfloat16)
    first_keep, first_send, second_keep, second_send, *handed = in_memory(
        partial(turn_kernel, high),
        [shape] * 4 + [jax.ShapeDtypeStruct(block.shape, block.dtype) for block in handed],
        [place, *received, *handed],
        after=after,
    )
    turned = (first_keep, flip(first_send, size, 1), second_keep, flip(second_send, size, 2))
    return turned, handed


def scatter_third(turned, place, size, after=()):
    high, rows, lanes = turned[0].shape
    chunk = (rows, 2 * lanes)
    return in_memory(
        partial(rise_kernel, high),
        [jax.ShapeDtypeStruct(chunk, jnp.float32)]
        + [jax.ShapeDtypeStruct(chunk, jnp.bfloat16)] * (high - 1),
        [place, *turned],
        after=after,
    )


def scatter_along_z(pieces, size):
    own, *sent = pieces
    return [own] + [rotate(block, size, turn + 1) for turn, block in enumerate(sent)]


def scatter_sum(block, rank, size):
    half = block.shape[-1] // 2
    pieces = [block[..., :half], block[..., half:]]
    left = size
    low_bits = 0
    while left > 4:
        orders = [(0, 1), (1, 0)] if left % 4 == 0 and left >= 16 else [(0,), (0,)]
        for turn in range(len(orders[0])):
            updated = []
            for piece, order in zip(pieces, orders):
                bit = low_bits + order[turn]
                mine = (rank >> bit) & 1
                if len(order) == 2 and turn == 0:
                    shaped = piece.reshape(-1, 2, 2, *piece.shape[1:])
                    at = 2 - order[turn]
                else:
                    shaped = piece.reshape(-1, 2, *piece.shape[1:])
                    at = 1
                keep = lax.dynamic_index_in_dim(shaped, mine, at, keepdims=False)
                send = lax.dynamic_index_in_dim(shaped, 1 - mine, at, keepdims=False)
                got = ring_exchange(send, size, lambda i, bit=bit: i ^ (1 << bit))
                total = (keep.astype(jnp.float32) + got.astype(jnp.float32)).astype(jnp.bfloat16)
                updated.append(total.reshape(-1, *piece.shape[1:]))
            pieces = updated
        low_bits += len(orders[0])
        left //= 2 ** len(orders[0])
    block = jnp.concatenate(pieces, axis=-1)
    high = rank >> low_bits
    total = lax.dynamic_index_in_dim(block, high, 0, keepdims=False).astype(jnp.float32)
    stride = 1 << low_bits
    for turn in range(1, left):
        send = lax.dynamic_index_in_dim(block, (high + turn) % left, 0, keepdims=False)
        got = ring_exchange(send, size, lambda i, turn=turn: (i + turn * stride) % size)
        total = total + got.astype(jnp.float32)
    return total


def per_device(
    inputs,
    cotangent,
    time_ids,
    row_counts,
    cond_table,
    modulation_weight,
    attention_weight,
    output_weight,
    expand_weight,
    shrink_weight,
    biases,
):
    section_rank = lax.axis_index("section")
    data_rank = lax.axis_index("dp")
    seq_rank = lax.axis_index("seq")
    sections = lax.axis_size("section")
    seq_size = lax.axis_size("seq")
    ring_size = lax.axis_size("dp") * seq_size
    ring_rank = data_rank * seq_size + seq_rank
    batches, slots, tokens, width = inputs.shape
    assert batches == sections == 2 and seq_size % slots == 0
    sharers = seq_size // slots
    slot = seq_rank // sharers
    length = tokens * seq_size
    rows = attention_weight.shape[1]
    ratio = shrink_weight.shape[1] // rows
    hidden = ratio * width
    bias_count = biases.shape[1]
    half = 2 * width + hidden
    assert hidden == expand_weight.shape[2] and ratio >= 2
    table_rows = cond_table.shape[0]
    is_first = section_rank == 0
    layout = (width, hidden, rows, ratio, ring_size, 1.0 / sharers, bias_count)
    compact = ring_size in (8, 16) and seq_size == slots == 2
    rank = section_rank.astype(jnp.int32).reshape(1)
    place = jnp.stack([ring_rank >> 2, (ring_rank >> 1) & 1, ring_rank & 1]).astype(jnp.int32)

    keep, send = in_memory(
        pack_kernel,
        [jax.ShapeDtypeStruct((rows, half), jnp.bfloat16)] * 2,
        [
            rank,
            attention_weight[0],
            output_weight[0],
            expand_weight[0],
            shrink_weight[0].reshape(ratio, rows, width),
        ],
        scratch=[pltpu.SemaphoreType.DMA((4 + ratio,))],
        memory=pl.ANY,
        limit=56,
    )
    got = pair_swap(send, "section")
    first_shard = jnp.where(is_first, keep, got)
    second_shard = jnp.where(is_first, got, keep)

    live = (
        slot < lax.dynamic_index_in_dim(row_counts, section_rank, 0, keepdims=False)[0]
    ).astype(jnp.bfloat16)
    both = jnp.stack(
        [
            lax.dynamic_index_in_dim(inputs, section_rank, 0, keepdims=False),
            lax.dynamic_index_in_dim(cotangent, section_rank, 0, keepdims=False),
        ],
        axis=1,
    )

    def side_by_side(mine, got, axis):
        return jnp.where(
            seq_rank == 0,
            jnp.concatenate([mine, got], axis=axis),
            jnp.concatenate([got, mine], axis=axis),
        )

    if compact:
        mine = lax.dynamic_index_in_dim(both, seq_rank, 0, keepdims=False)
        sent = lax.dynamic_index_in_dim(both, 1 - seq_rank, 0, keepdims=False)
        both = side_by_side(mine, pair_swap(sent, "seq"), 1)
    else:
        both = lax.all_to_all(jnp.repeat(both, sharers, axis=0), "seq", 0, 0, tiled=True)
        both = jnp.swapaxes(both, 0, 1).reshape(2, length, width)
    first_input = both[0]
    last_grad = both[1] * live

    flat_ids = time_ids.reshape(-1)
    selector = (
        flat_ids[:, None] == jnp.arange(table_rows, dtype=jnp.int32)[None, :]
    ).astype(jnp.bfloat16)
    conditions = matmul(selector, cond_table)
    silu_all = jax.nn.silu(conditions).astype(jnp.bfloat16)
    silu_own = lax.dynamic_slice_in_dim(silu_all, ring_rank * rows, rows, 1)
    if compact:
        first_shards = rotations(first_shard, ring_size)
        silu_late = hand_on(rank, silu_own, (first_shards[1],))
        *first_parts, second_shard = gather_along_z(first_shards, place, handed=(second_shard,))
        first_parts += first_flips(*first_parts, ring_size)
    else:
        silu_late = silu_own

    products = matmul(silu_late, modulation_weight[0])
    own_bias = jnp.broadcast_to(biases.astype(jnp.float32), (products.shape[0], bias_count))
    products = jnp.repeat(jnp.concatenate([products, own_bias], axis=1), sharers, axis=0)
    products = lax.all_to_all(
        products[:, None], ("section", "dp", "seq"), 0, 0, tiled=True
    ).reshape(sections, ring_size, 6 * width + bias_count)
    first_modulation, second_modulation = jnp.split(
        jnp.sum(products[:, :, : 6 * width], axis=1), 2, axis=0
    )
    first_bias, second_bias = products[0, :, 6 * width :], products[1, :, 6 * width :]

    if compact:
        second_parts = gather_along_z(
            rotations(second_shard, ring_size), place, after=(products, both, *first_parts[2:])
        )
        second_parts += first_flips(*second_parts, ring_size)
        first_pack = gather_across(*first_parts, place, ring_size)
        second_pack = gather_across(*second_parts, place, ring_size)
    else:
        first_pack = lax.all_gather(first_shard, RING, axis=0, tiled=True)
        second_pack = lax.all_gather(second_shard, RING, axis=0, tiled=True)
    first_halves = (first_pack, pair_swap(first_pack, "section"))
    second_halves = (second_pack, pair_swap(second_pack, "section"))

    first_low, *first_saved = run_section(
        layout, rank, first_input, first_halves, (first_modulation, first_bias)
    )
    second_low, second_grad, second_dmod, second_sums, second_keep, second_send = run_section(
        layout, rank, first_low, second_halves, (second_modulation, second_bias), dy=last_grad
    )
    second_got = pair_swap(second_send, "section")

    def ring_terms(term):
        return term.reshape(ring_size, rows, half)

    first_grad, first_dmod, first_sums, first_keep, first_send = run_section(
        layout, rank, first_input, first_halves, saved=first_saved, dy=second_grad
    )
    first_got = pair_swap(first_send, "section")

    shard = jax.ShapeDtypeStruct((rows, half), jnp.float32)
    if compact:
        second_sorted = scatter_first(
            ring_terms(second_keep), ring_terms(second_got), place, ring_size
        )
        second_received = scatter_flips(second_sorted, ring_size)
        *first_sorted, first_dmod, first_sums = scatter_first(
            ring_terms(first_keep),
            ring_terms(first_got),
            place,
            ring_size,
            handed=(first_dmod, first_sums),
            after=(second_sorted[0],),
        )
        first_received = scatter_flips(first_sorted, ring_size)
        second_turned, _ = scatter_second(second_received, place, ring_size)
        second_sent = scatter_third(second_turned, place, ring_size)
        second_pieces = scatter_along_z(second_sent, ring_size)
        first_turned, (first_grad,) = scatter_second(
            first_received, place, ring_size, handed=(first_grad,), after=(second_sent[0],)
        )
        first_sent = scatter_third(first_turned, place, ring_size, tuple(second_pieces[1:]))
        first_pieces = scatter_along_z(first_sent, ring_size)
    else:

        def chip_sum(keep, got):
            return ring_terms(low(added(keep, got)))

        first_pieces, second_pieces = [
            [scatter_sum(chip_sum(keep, got), ring_rank, ring_size)]
            for keep, got in ((first_keep, first_got), (second_keep, second_got))
        ]
    rows_back = jnp.concatenate(
        [
            jnp.concatenate(
                [jnp.broadcast_to(dmod, (ring_size, 6 * width)), sums], axis=1
            )
            for dmod, sums in ((first_dmod, first_sums), (second_dmod, second_sums))
        ]
    )
    every = lax.all_to_all(rows_back[:, None], ("section", "dp", "seq"), 0, 0, tiled=True)
    every = every[::sharers, 0]
    bias_grad = jnp.sum(every[:, 6 * width :], axis=0)
    modulation_rows = low(every[:, : 6 * width])
    modulation_grad = outer_sum(silu_own, modulation_rows)
    columns = matmul_transposed(modulation_rows, modulation_weight[0])
    if compact:
        columns = hand_on(rank, columns, (second_pieces[1],))
    columns = jnp.broadcast_to(columns.reshape(1, 1, -1), (sections * ring_size, 1, columns.size))
    columns = lax.all_to_all(columns, ("section", "dp", "seq"), 0, 0, tiled=True)

    outputs_ready = (first_low * live, second_low * live)
    if compact:
        block = jnp.stack([outputs_ready[0], first_grad, outputs_ready[1], second_grad])
        block = block.reshape(4, 2, tokens, width)
        mine = lax.dynamic_index_in_dim(block, seq_rank, 1, keepdims=True)
        sent = lax.dynamic_index_in_dim(block, 1 - seq_rank, 1, keepdims=True)
        block = side_by_side(mine, pair_swap(sent, "seq"), 1)
        per_first, per_second = block[:2], block[2:]
        mine = jnp.where(is_first, per_first, per_second)
        got = pair_swap(jnp.where(is_first, per_second, per_first), "section")
        outputs = jnp.where(is_first, jnp.stack([mine, got], 1), jnp.stack([got, mine], 1))
    else:
        pieces = jnp.stack([outputs_ready[0], first_grad, outputs_ready[1], second_grad])
        pieces = jnp.swapaxes(pieces.reshape(2, 2, seq_size, tokens, width), 1, 2)
        pieces = pieces.reshape(2 * seq_size, 2, tokens, width)
        pieces = lax.all_to_all(pieces, ("section", "seq"), 0, 0, tiled=True)
        pieces = pieces.reshape(batches, slots, sharers, 2, tokens, width)[:, :, 0]
        outputs = jnp.moveaxis(pieces, 2, 0)
    activations = outputs[0]
    input_grads = outputs[1].astype(jnp.float32)

    mine, send = in_memory(
        partial(close_kernel, len(first_pieces)),
        [shard, shard],
        [rank, *first_pieces, *second_pieces],
        after=(columns,),
    )
    att, out, up, down = in_memory(
        spread_kernel,
        [
            jax.ShapeDtypeStruct(extent, jnp.float32)
            for extent in (
                (rows, 3 * width),
                (rows, width),
                (rows, hidden),
                (rows * ratio, width),
            )
        ],
        [rank, mine, pair_swap(send, "section")],
    )

    columns = jnp.sum(columns.reshape(sections, ring_size, -1, rows), axis=0)
    products_back = jnp.swapaxes(columns, 0, 1).reshape(-1, width)
    _, silu_back = jax.vjp(jax.nn.silu, conditions)
    table_grad = lax.dot_general(
        selector.astype(jnp.float32),
        silu_back(products_back)[0],
        (((0,), (0,)), ((), ())),
        precision=lax.Precision.HIGHEST,
        preferred_element_type=jnp.float32,
    )
    return (
        activations[None],
        input_grads[None],
        table_grad,
        modulation_grad[None],
        att[None],
        out[None],
        up[None],
        down[None],
        bias_grad[None],
    )


def solution(mesh):
    shard = P("section", ("dp", "seq"), None)
    in_specs = (
        P(None, "dp", "seq", None),
        P(None, "dp", "seq", None),
        P(),
        P(None, "dp"),
        P(),
        shard,
        shard,
        shard,
        shard,
        shard,
        P("section", ("dp", "seq")),
    )
    out_specs = (
        P("section", None, "dp", "seq", None),
        P("section", None, "dp", "seq", None),
        P(),
        shard,
        shard,
        shard,
        shard,
        shard,
        P("section", ("dp", "seq")),
    )
    return jax.shard_map(
        per_device, mesh=mesh, in_specs=in_specs, out_specs=out_specs, check_vma=False
    )
```

```python
from functools import partial

import jax
import jax.numpy as jnp
from jax import lax
from jax.experimental import pallas as pl
from jax.experimental.pallas import tpu as pltpu
from jax.sharding import PartitionSpec as P

HEADS = 6
HEAD = 64
SCALE = HEAD ** (-0.5)
epsilon = 1e-06
RING = ("dp", "seq")
INNER = (2.0 / 3.141592653589793) ** 0.5
CUBE = 0.044715


def matmul(former, latter):
    return jnp.dot(former, latter, preferred_element_type=jnp.float32)


def matmul_transposed(former, latter):
    return lax.dot_general(
        former, latter, (((1,), (1,)), ((), ())), preferred_element_type=jnp.float32
    )


def outer_sum(former, latter):
    return lax.dot_general(
        former, latter, (((0,), (0,)), ((), ())), preferred_element_type=jnp.float32
    )


def low(values):
    return values.astype(jnp.bfloat16)


def normalize_rows(values):
    centre = jnp.mean(values, axis=-1, keepdims=True)
    centred = values - centre
    spread = jnp.mean(centred * centred, axis=-1, keepdims=True)
    factor = lax.rsqrt(spread + epsilon)
    return (centred * factor, factor)


def normalize_back(normed, factor, grad_normed):
    mean_grad = jnp.mean(grad_normed, axis=-1, keepdims=True)
    mean_cross = jnp.mean(grad_normed * normed, axis=-1, keepdims=True)
    return factor * (grad_normed - mean_grad - normed * mean_cross)


def column_sum(values):
    return jnp.sum(values.astype(jnp.float32), axis=0, keepdims=True)


def saved_shapes(layout, length):
    width, hidden = layout[:2]
    bf16, f32 = jnp.bfloat16, jnp.float32
    return [
        ((1, 6 * width), f32),
        ((length, 3 * width), bf16),
        ((length, width), bf16),
        ((length, hidden), bf16),
        ((HEADS, length, length), f32),
        ((length, hidden), f32),
        ((length, width), f32),
        ((length, width), f32),
        ((hidden, width), bf16),
    ]


def section_kernel(layout, forward, backward, after, *refs):
    width, hidden, rows, ratio, ring_size, share, bias_count = layout
    refs = list(refs)

    def take(count):
        taken = refs[:count]
        del refs[:count]
        return taken

    rank_ref, x_ref = take(2)
    if forward:
        modulation_ref, bias_ref = take(2)
    else:
        saved = take(9)
    if backward:
        (dy_ref,) = take(1)
    mine_ref, theirs_ref = take(2)
    take(after)
    if forward:
        (y_ref,) = take(1)
    if backward:
        dx_ref, dmod_ref, sums_ref, keep_ref, send_ref = take(5)
    elif forward:
        saved = take(9)
    att_w, out_w, up_w, sems, down_s, block_s = take(6)
    if forward:
        down_p, bias_s = take(2)
    if backward:
        da_s, dqkv_s, row_ref, halves, out_sems = take(5)
    if forward and backward:
        saved = take(9)
    mod_s, qkv_s, att_s, u_s, soft_s, slope_s, one_s, two_s, down_w = saved

    rank = rank_ref[0]
    split = hidden - 2 * width

    def fetches(first, second):
        moves = [
            (first.at[:, : 3 * width], att_w),
            (first.at[:, 3 * width : 4 * width], out_w),
            (first.at[:, 4 * width :], up_w.at[:, :split]),
            (second.at[:, : hidden - split], up_w.at[:, split:]),
        ]
        if forward:
            moves.append((second.at[:, hidden - split :], down_p))
        return [
            pltpu.make_async_copy(source, target, sems.at[i])
            for i, (source, target) in enumerate(moves)
        ]

    @pl.when(rank == 0)
    def _():
        for copy in fetches(mine_ref, theirs_ref):
            copy.start()

    @pl.when(rank != 0)
    def _():
        for copy in fetches(theirs_ref, mine_ref):
            copy.start()

    arrivals = fetches(mine_ref, theirs_ref)

    def part(ref, member, head):
        start = member * width + head * HEAD
        return ref[:, start : start + HEAD]

    x = x_ref[...].astype(jnp.float32)
    normed_one, factor_one = normalize_rows(x)
    if forward:
        for d in range(ring_size):
            bias_s[:, d * bias_count : (d + 1) * bias_count] = bias_ref[d : d + 1, :]
        mod_s[...] = modulation_ref[...] + bias_s[:, : 6 * width]
    shift_one, scale_one, gate_one, shift_two, scale_two, gate_two = [
        mod_s[:, i * width : (i + 1) * width] for i in range(6)
    ]
    hidden_one = low(normed_one * (1.0 + scale_one) + shift_one)
    if forward:

        def bias(a, b):
            return bias_s[:, a:b]

        at = 6 * width
        arrivals[0].wait()
        qkv_s[:, :width] = low(matmul(hidden_one, att_w[:, :width]) + bias(at, at + width))
        qkv_s[:, width : 2 * width] = low(matmul(hidden_one, att_w[:, width : 2 * width]))
        qkv_s[:, 2 * width :] = low(
            matmul(hidden_one, att_w[:, 2 * width :]) + bias(at + width, at + 2 * width)
        )
        for head in range(HEADS):
            scores = matmul_transposed(part(qkv_s, 0, head), part(qkv_s, 1, head)) * SCALE
            raised = jnp.exp(scores - jnp.max(scores, axis=-1, keepdims=True))
            soft = raised * (1.0 / jnp.sum(raised, axis=-1, keepdims=True))
            soft_s[head] = soft
            attended = matmul(low(soft), part(qkv_s, 2, head))
            att_s[:, head * HEAD : (head + 1) * HEAD] = low(attended)
        arrivals[1].wait()
        one_s[...] = matmul(att_s[...], out_w[...]) + bias(at + 2 * width, at + 3 * width)
    branch_one = one_s[...]
    middle = x + gate_one * branch_one
    normed_two, factor_two = normalize_rows(middle)
    hidden_two = low(normed_two * (1.0 + scale_two) + shift_two)
    if forward:
        arrivals[2].wait()
        arrivals[3].wait()
        at += 3 * width
        for j in range(ratio):
            cut = slice(j * width, (j + 1) * width)
            a = matmul(hidden_two, up_w[:, cut]) + bias(at + j * width, at + (j + 1) * width)
            square = a * a
            turn = jnp.tanh(INNER * (a + CUBE * (a * square)))
            half_one = 0.5 * (1.0 + turn)
            u_s[:, cut] = low(a * half_one)
            slope_s[:, cut] = half_one + (0.5 * INNER) * a * (1.0 - turn * turn) * (
                1.0 + (3.0 * CUBE) * square
            )
        arrivals[4].wait()
        block_s[...] = down_p[...].astype(jnp.float32)
        for d in range(ring_size):
            for j in range(ratio):
                down_s[(d * ratio + j) * rows : (d * ratio + j + 1) * rows, :] = block_s[
                    d * rows : (d + 1) * rows, j * width : (j + 1) * width
                ]
        down_w[...] = low(down_s[...])
        two_s[...] = matmul(u_s[...], down_w[...]) + bias(at + hidden, at + hidden + width)
        y_ref[...] = low(middle + gate_two * two_s[...])
    if not backward:
        return

    grad_out = dy_ref[...].astype(jnp.float32)
    grad_branch = low(gate_two * grad_out)
    sums_at = 6 * width
    row_ref[:, 5 * width : 6 * width] = column_sum(grad_out * two_s[...])
    row_ref[:, sums_at + 3 * width + hidden : sums_at + 4 * width + hidden] = column_sum(
        grad_branch
    )
    for j in range(ratio):
        cut = slice(j * width, (j + 1) * width)
        grad_expanded = low(slope_s[:, cut] * matmul_transposed(grad_branch, down_w[cut, :]))
        da_s[:, cut] = grad_expanded
        row_ref[:, sums_at + (3 + j) * width : sums_at + (4 + j) * width] = column_sum(
            grad_expanded
        )
    halves[0, :, 4 * width :] = low(outer_sum(hidden_two, da_s[:, :split]) * share)
    halves[1, :, : hidden - split] = low(outer_sum(hidden_two, da_s[:, split:]) * share)
    down_s[...] = outer_sum(u_s[...], grad_branch) * share
    for d in range(ring_size):
        for j in range(ratio):
            block_s[d * rows : (d + 1) * rows, j * width : (j + 1) * width] = down_s[
                (d * ratio + j) * rows : (d * ratio + j + 1) * rows, :
            ]
    halves[1, :, hidden - split :] = low(block_s[...])
    second_out = [
        pltpu.make_async_copy(halves.at[1], keep_ref, out_sems.at[1]),
        pltpu.make_async_copy(halves.at[1], send_ref, out_sems.at[1]),
    ]

    @pl.when(rank == 1)
    def _():
        second_out[0].start()

    @pl.when(rank != 1)
    def _():
        second_out[1].start()

    if not forward:
        arrivals[2].wait()
        arrivals[3].wait()
    grad_hidden_two = matmul_transposed(da_s[...], up_w[...])
    row_ref[:, 3 * width : 4 * width] = column_sum(grad_hidden_two)
    row_ref[:, 4 * width : 5 * width] = column_sum(grad_hidden_two * normed_two)
    grad_middle = grad_out + normalize_back(
        normed_two, factor_two, grad_hidden_two * (1.0 + scale_two)
    )
    row_ref[:, 2 * width : 3 * width] = column_sum(grad_middle * branch_one)
    grad_attention = low(gate_one * grad_middle)
    row_ref[:, sums_at + 2 * width : sums_at + 3 * width] = column_sum(grad_attention)
    halves[0, :, 3 * width : 4 * width] = low(outer_sum(att_s[...], grad_attention) * share)
    if not forward:
        arrivals[1].wait()
    grad_attended = low(matmul_transposed(grad_attention, out_w[...]))
    for head in range(HEADS):
        soft = soft_s[head]
        grad_head = grad_attended[:, head * HEAD : (head + 1) * HEAD]
        grad_soft = matmul_transposed(grad_head, part(qkv_s, 2, head))
        inner = jnp.sum(grad_soft * soft, axis=-1, keepdims=True)
        grad_scores = low(soft * (grad_soft - inner))
        grads = (
            matmul(grad_scores, part(qkv_s, 1, head)) * SCALE,
            outer_sum(grad_scores, part(qkv_s, 0, head)) * SCALE,
            outer_sum(low(soft), grad_head),
        )
        for member, grad in enumerate(grads):
            start = member * width + head * HEAD
            dqkv_s[:, start : start + HEAD] = low(grad)
    row_ref[:, sums_at : sums_at + width] = column_sum(dqkv_s[:, :width])
    row_ref[:, sums_at + width : sums_at + 2 * width] = column_sum(dqkv_s[:, 2 * width :])
    halves[0, :, : 3 * width] = low(outer_sum(hidden_one, dqkv_s[...]) * share)
    first_out = [
        pltpu.make_async_copy(halves.at[0], keep_ref, out_sems.at[0]),
        pltpu.make_async_copy(halves.at[0], send_ref, out_sems.at[0]),
    ]

    @pl.when(rank == 0)
    def _():
        first_out[0].start()

    @pl.when(rank != 0)
    def _():
        first_out[1].start()

    if not forward:
        arrivals[0].wait()
    grad_hidden_one = matmul_transposed(dqkv_s[...], att_w[...])
    row_ref[:, :width] = column_sum(grad_hidden_one)
    row_ref[:, width : 2 * width] = column_sum(grad_hidden_one * normed_one)
    dx_ref[...] = low(
        grad_middle
        + normalize_back(normed_one, factor_one, grad_hidden_one * (1.0 + scale_one))
    )
    row_ref[:, : 6 * width] = low(row_ref[:, : 6 * width]).astype(jnp.float32)
    dmod_ref[...] = row_ref[:, : 6 * width]
    for d in range(ring_size):
        sums_ref[d : d + 1, :] = row_ref[:, d * bias_count : (d + 1) * bias_count]
    second_out[0].wait()
    first_out[0].wait()


def run_section(layout, rank, x, halves, start=None, saved=None, dy=None, after=()):
    width, hidden, rows, ratio, ring_size, share, bias_count = layout
    length = x.shape[0]
    forward, backward = start is not None, dy is not None
    vmem = pl.BlockSpec(memory_space=pltpu.VMEM)
    hbm = pl.BlockSpec(memory_space=pl.ANY)
    bf16, f32 = jnp.bfloat16, jnp.float32
    half = 2 * width + hidden
    kept = saved_shapes(layout, length)
    operands = [rank, x, *(start if forward else saved)]
    shapes, out_specs = [], []
    scratch = [
        pltpu.VMEM((width, 3 * width), bf16),
        pltpu.VMEM((width, width), bf16),
        pltpu.VMEM((width, hidden), bf16),
        pltpu.SemaphoreType.DMA((5,)),
        pltpu.VMEM((hidden, width), f32),
        pltpu.VMEM((width, hidden), f32),
    ]
    if forward:
        shapes.append(jax.ShapeDtypeStruct((length, width), bf16))
        scratch += [
            pltpu.VMEM((width, hidden), bf16),
            pltpu.VMEM((1, bias_count * ring_size), f32),
        ]
    if backward:
        operands.append(dy)
        shapes += [
            jax.ShapeDtypeStruct((length, width), bf16),
            jax.ShapeDtypeStruct((1, 6 * width), f32),
            jax.ShapeDtypeStruct((ring_size, bias_count), f32),
            jax.ShapeDtypeStruct((width, half), bf16),
            jax.ShapeDtypeStruct((width, half), bf16),
        ]
        scratch += [
            pltpu.VMEM((length, hidden), bf16),
            pltpu.VMEM((length, 3 * width), bf16),
            pltpu.VMEM((1, 10 * width + hidden), f32),
            pltpu.VMEM((2, width, half), bf16),
            pltpu.SemaphoreType.DMA((2,)),
        ]
        if forward:
            scratch += [pltpu.VMEM(extent, kind) for extent, kind in kept]
    else:
        shapes += [jax.ShapeDtypeStruct(extent, kind) for extent, kind in kept]
    out_specs = [vmem] * len(shapes)
    if backward:
        out_specs[-2:] = [hbm, hbm]
    specs = [pl.BlockSpec(memory_space=pltpu.SMEM)] + [vmem] * (len(operands) - 1)
    specs += [hbm] * (2 + len(after))
    work = 2 * length * width * (4 * width + 2 * hidden + 2 * length)
    moved = 2 * width * (10 * width + 2 * hidden)
    return pl.pallas_call(
        partial(section_kernel, layout, forward, backward, len(after)),
        out_shape=shapes,
        in_specs=specs,
        out_specs=out_specs,
        scratch_shapes=scratch,
        compiler_params=pltpu.CompilerParams(
            vmem_limit_bytes=(56 if length > 256 else 36 if forward and backward else 36)
            * 1024
            * 1024
        ),
        cost_estimate=pl.CostEstimate(
            flops=(forward + 2 * backward) * work,
            bytes_accessed=(1 + backward) * moved,
            transcendentals=HEADS * length * length + length * hidden,
        ),
    )(*operands, *halves, *after)


def copy_all(copies):
    for copy in copies:
        copy.start()
    for copy in copies:
        copy.wait()


def pack_kernel(rank_ref, att_ref, out_ref, up_ref, down_ref, keep_ref, send_ref, sems):
    ratio, rows, width = down_ref.shape
    split = (ratio - 2) * width

    def copies(first, second):
        moves = [
            (att_ref, first.at[:, : 3 * width]),
            (out_ref, first.at[:, 3 * width : 4 * width]),
            (up_ref.at[:, :split], first.at[:, 4 * width :]),
            (up_ref.at[:, split:], second.at[:, : 2 * width]),
        ]
        for j in range(ratio):
            moves.append((down_ref.at[j], second.at[:, (2 + j) * width : (3 + j) * width]))
        return [
            pltpu.make_async_copy(source, target, sems.at[i])
            for i, (source, target) in enumerate(moves)
        ]

    @pl.when(rank_ref[0] == 0)
    def _():
        copy_all(copies(keep_ref, send_ref))

    @pl.when(rank_ref[0] != 0)
    def _():
        copy_all(copies(send_ref, keep_ref))


def stack_kernel(high, split, place_ref, *refs):
    pieces, sems = refs[:high], refs[-1]
    count = (len(refs) - high - 3) // 2
    handed, targets = refs[high : high + count], refs[high + count : -1]
    copies = [
        pltpu.make_async_copy(former, latter, sems.at[high + i, 0])
        for i, (former, latter) in enumerate(zip(handed, targets[2:]))
    ]
    for turn, piece in enumerate(pieces):
        place = lax.rem(place_ref[0] + (high - turn), high)
        parts = (piece.at[:, :split], piece.at[:, split:])
        for i, (part, target) in enumerate(zip(parts, targets)):
            copies.append(pltpu.make_async_copy(part, target.at[place], sems.at[turn, i]))
    copy_all(copies)


def weave_kernel(split, place_ref, *refs):
    pieces, full_ref, sems = refs[:-2], refs[-2], refs[-1]
    x, y = place_ref[1], place_ref[2]
    copies = []
    for i, piece in enumerate(pieces):
        other_x, other_y = (i % 4) & 1, (i % 4) >> 1
        row = x if not other_x else 1 - x
        column = y if not other_y else 1 - y
        target = full_ref.at[:, row, column, :, pl.ds((i // 4) * split, split)]
        copies.append(pltpu.make_async_copy(piece, target, sems.at[i]))
    copy_all(copies)


def added(former, latter):
    return former.astype(jnp.float32) + latter.astype(jnp.float32)


def chip_sum_kernel(high, place_ref, mine, got, *refs):
    count = (len(refs) - 4) // 2
    first_keep, first_send, second_keep, second_send = refs[count : count + 4]
    for former, latter in zip(refs[:count], refs[count + 4 :]):
        latter[...] = former[...]
    x, y = place_ref[1], place_ref[2]
    half = mine.shape[2]
    lanes = half // 2
    for z in range(high):
        for other in range(2):
            for target, span, chunk in (
                (first_keep, slice(0, lanes), z * 4 + x * 2 + other),
                (first_send, slice(0, lanes), z * 4 + (1 - x) * 2 + other),
                (second_keep, slice(lanes, half), z * 4 + other * 2 + y),
                (second_send, slice(lanes, half), z * 4 + other * 2 + (1 - y)),
            ):
                target[z, other] = low(added(mine[chunk, :, span], got[chunk, :, span]))


def turn_kernel(high, place_ref, *refs):
    count = (len(refs) - 8) // 2
    for former, latter in zip(refs[4 : 4 + count], refs[8 + count :]):
        latter[...] = former[...]
    for part, own in ((0, place_ref[2]), (1, place_ref[1])):
        kept, got = refs[2 * part : 2 * part + 2]
        keep, send = refs[4 + count + 2 * part : 6 + count + 2 * part]
        for z in range(high):
            keep[z] = low(added(kept[z, own], got[z, own]))
            send[z] = low(added(kept[z, 1 - own], got[z, 1 - own]))


def rise_kernel(high, place_ref, *refs):
    count = (len(refs) - 4 - high) // 2
    for former, latter in zip(refs[4 : 4 + count], refs[4 + count + high :]):
        latter[...] = former[...]
    targets = refs[4 + count :]
    lanes = refs[0].shape[2]
    for turn in range(high):
        chunk = lax.rem(place_ref[0] + turn, high)
        for part in range(2):
            kept, got = refs[2 * part : 2 * part + 2]
            total = added(kept[chunk], got[chunk])
            span = slice(part * lanes, (part + 1) * lanes)
            targets[turn][:, span] = total.astype(targets[turn].dtype)


def close_kernel(high, rank_ref, *refs):
    keep, send = refs[-2:]
    totals = []
    for section in range(2):
        pieces = refs[section * high : (section + 1) * high]
        total = pieces[0][...].astype(jnp.float32)
        for piece in pieces[1:]:
            total = total + piece[...].astype(jnp.float32)
        totals.append(total)
    first = rank_ref[0] == 0
    keep[...] = jnp.where(first, totals[0], totals[1])
    send[...] = jnp.where(first, totals[1], totals[0])


def spread_kernel(rank_ref, mine, got, att_ref, out_ref, up_ref, down_ref):
    rows, width = out_ref.shape
    split = up_ref.shape[1] - 2 * width
    first = rank_ref[0] == 0
    lower = jnp.where(first, mine[...], got[...])
    upper = jnp.where(first, got[...], mine[...])
    att_ref[...] = lower[:, : 3 * width]
    out_ref[...] = lower[:, 3 * width : 4 * width]
    up_ref[:, :split] = lower[:, 4 * width :]
    up_ref[:, split:] = upper[:, : 2 * width]
    for j in range(down_ref.shape[0] // rows):
        down_ref[j * rows : (j + 1) * rows, :] = upper[:, (2 + j) * width : (3 + j) * width]


def in_memory(kernel, shapes, operands, scratch=(), memory=pltpu.VMEM, after=(), limit=32):
    specs = [pl.BlockSpec(memory_space=pltpu.SMEM)]
    specs += [pl.BlockSpec(memory_space=memory)] * (len(operands) - 1)
    specs += [pl.BlockSpec(memory_space=pl.ANY)] * len(after)
    count = len(operands)

    def body(*refs):
        kernel(*refs[:count], *refs[count + len(after) :])

    moved = sum(shape.size * shape.dtype.itemsize for shape in shapes)
    return pl.pallas_call(
        body,
        out_shape=shapes,
        in_specs=specs,
        out_specs=[pl.BlockSpec(memory_space=pltpu.VMEM)] * len(shapes),
        scratch_shapes=list(scratch),
        compiler_params=pltpu.CompilerParams(vmem_limit_bytes=limit * 1024 * 1024),
        cost_estimate=pl.CostEstimate(flops=0, bytes_accessed=3 * moved, transcendentals=0),
    )(*operands, *after)


def pair_swap(block, axis):
    return lax.ppermute(block, axis, [(0, 1), (1, 0)])


def ring_exchange(block, size, step):
    return lax.ppermute(block, RING, [(i, step(i)) for i in range(size)])


def flip(block, size, mask):
    return ring_exchange(block, size, lambda i: i ^ mask)


def rotate(block, size, turn):
    return ring_exchange(block, size, lambda i: (i + 4 * turn) % size)


def rotations(block, size):
    return [block] + [rotate(block, size, turn) for turn in range(1, size // 4)]


def gather_along_z(shard, place, size, handed=(), after=()):
    high = size // 4
    rows, lanes = shard.shape
    return in_memory(
        partial(stack_kernel, high, lanes // 2),
        [jax.ShapeDtypeStruct((high, rows, lanes // 2), shard.dtype)] * 2
        + [jax.ShapeDtypeStruct(block.shape, block.dtype) for block in handed],
        [place, *rotations(shard, size), *handed],
        scratch=[pltpu.SemaphoreType.DMA((high + len(handed), 2))],
        after=after,
    )


def first_flips(first, second, size):
    return flip(first, size, 2), flip(second, size, 1)


def gather_across(first, second, first_x, second_y, place, size):
    high, rows, lanes = first.shape
    first_y, second_x = flip(first, size, 1), flip(second, size, 2)
    first_both, second_both = flip(first_x, size, 1), flip(second_y, size, 2)
    (full,) = in_memory(
        partial(weave_kernel, lanes),
        [jax.ShapeDtypeStruct((high, 2, 2, rows, 2 * lanes), first.dtype)],
        [place, first, first_x, first_y, first_both, second, second_x, second_y, second_both],
        scratch=[pltpu.SemaphoreType.DMA((8,))],
    )
    return full.reshape(size * rows, 2 * lanes)


def scatter_first(mine, got, place, size, handed=(), after=()):
    rows, half = mine.shape[1:]
    shape = jax.ShapeDtypeStruct((size // 4, 2, rows, half // 2), jnp.bfloat16)
    return in_memory(
        partial(chip_sum_kernel, size // 4),
        [shape] * 4 + [jax.ShapeDtypeStruct(block.shape, block.dtype) for block in handed],
        [place, mine, got, *handed],
        after=after,
    )


def scatter_flips(sorted_terms, size):
    first_keep, first_send, second_keep, second_send = sorted_terms
    return first_keep, flip(first_send, size, 2), second_keep, flip(second_send, size, 1)


def scatter_second(received, place, size, handed=(), after=()):
    high, _, rows, lanes = received[0].shape
    shape = jax.ShapeDtypeStruct((high, rows, lanes), jnp.bfloat16)
    first_keep, first_send, second_keep, second_send, *handed = in_memory(
        partial(turn_kernel, high),
        [shape] * 4 + [jax.ShapeDtypeStruct(block.shape, block.dtype) for block in handed],
        [place, *received, *handed],
        after=after,
    )
    turned = (first_keep, flip(first_send, size, 1), second_keep, flip(second_send, size, 2))
    return turned, handed


def scatter_third(turned, place, size, handed=(), after=()):
    high, rows, lanes = turned[0].shape
    chunk = (rows, 2 * lanes)
    return in_memory(
        partial(rise_kernel, high),
        [jax.ShapeDtypeStruct(chunk, jnp.float32)]
        + [jax.ShapeDtypeStruct(chunk, jnp.bfloat16)] * (high - 1)
        + [jax.ShapeDtypeStruct(block.shape, block.dtype) for block in handed],
        [place, *turned, *handed],
        after=after,
    )


def scatter_along_z(pieces, size):
    own, *sent = pieces
    return [own] + [rotate(block, size, turn + 1) for turn, block in enumerate(sent)]


def scatter_sum(block, rank, size):
    half = block.shape[-1] // 2
    pieces = [block[..., :half], block[..., half:]]
    left = size
    low_bits = 0
    while left > 4:
        orders = [(0, 1), (1, 0)] if left % 4 == 0 and left >= 16 else [(0,), (0,)]
        for turn in range(len(orders[0])):
            updated = []
            for piece, order in zip(pieces, orders):
                bit = low_bits + order[turn]
                mine = (rank >> bit) & 1
                if len(order) == 2 and turn == 0:
                    shaped = piece.reshape(-1, 2, 2, *piece.shape[1:])
                    at = 2 - order[turn]
                else:
                    shaped = piece.reshape(-1, 2, *piece.shape[1:])
                    at = 1
                keep = lax.dynamic_index_in_dim(shaped, mine, at, keepdims=False)
                send = lax.dynamic_index_in_dim(shaped, 1 - mine, at, keepdims=False)
                got = ring_exchange(send, size, lambda i, bit=bit: i ^ (1 << bit))
                total = (keep.astype(jnp.float32) + got.astype(jnp.float32)).astype(jnp.bfloat16)
                updated.append(total.reshape(-1, *piece.shape[1:]))
            pieces = updated
        low_bits += len(orders[0])
        left //= 2 ** len(orders[0])
    block = jnp.concatenate(pieces, axis=-1)
    high = rank >> low_bits
    total = lax.dynamic_index_in_dim(block, high, 0, keepdims=False).astype(jnp.float32)
    stride = 1 << low_bits
    for turn in range(1, left):
        send = lax.dynamic_index_in_dim(block, (high + turn) % left, 0, keepdims=False)
        got = ring_exchange(send, size, lambda i, turn=turn: (i + turn * stride) % size)
        total = total + got.astype(jnp.float32)
    return total


def per_device(
    inputs,
    cotangent,
    time_ids,
    row_counts,
    cond_table,
    modulation_weight,
    attention_weight,
    output_weight,
    expand_weight,
    shrink_weight,
    biases,
):
    section_rank = lax.axis_index("section")
    data_rank = lax.axis_index("dp")
    seq_rank = lax.axis_index("seq")
    sections = lax.axis_size("section")
    seq_size = lax.axis_size("seq")
    ring_size = lax.axis_size("dp") * seq_size
    ring_rank = data_rank * seq_size + seq_rank
    batches, slots, tokens, width = inputs.shape
    assert batches == sections == 2 and seq_size % slots == 0
    sharers = seq_size // slots
    slot = seq_rank // sharers
    length = tokens * seq_size
    rows = attention_weight.shape[1]
    ratio = shrink_weight.shape[1] // rows
    hidden = ratio * width
    bias_count = biases.shape[1]
    half = 2 * width + hidden
    assert hidden == expand_weight.shape[2] and ratio >= 2
    table_rows = cond_table.shape[0]
    is_first = section_rank == 0
    layout = (width, hidden, rows, ratio, ring_size, 1.0 / sharers, bias_count)
    compact = ring_size in (8, 16) and seq_size == slots == 2
    rank = section_rank.astype(jnp.int32).reshape(1)
    place = jnp.stack([ring_rank >> 2, (ring_rank >> 1) & 1, ring_rank & 1]).astype(jnp.int32)

    keep, send = in_memory(
        pack_kernel,
        [jax.ShapeDtypeStruct((rows, half), jnp.bfloat16)] * 2,
        [
            rank,
            attention_weight[0],
            output_weight[0],
            expand_weight[0],
            shrink_weight[0].reshape(ratio, rows, width),
        ],
        scratch=[pltpu.SemaphoreType.DMA((4 + ratio,))],
        memory=pl.ANY,
        limit=56,
    )
    got = pair_swap(send, "section")
    first_shard = jnp.where(is_first, keep, got)
    second_shard = jnp.where(is_first, got, keep)

    live = (
        slot < lax.dynamic_index_in_dim(row_counts, section_rank, 0, keepdims=False)[0]
    ).astype(jnp.bfloat16)
    both = jnp.stack(
        [
            lax.dynamic_index_in_dim(inputs, section_rank, 0, keepdims=False),
            lax.dynamic_index_in_dim(cotangent, section_rank, 0, keepdims=False),
        ],
        axis=1,
    )

    def side_by_side(mine, got, axis):
        return jnp.where(
            seq_rank == 0,
            jnp.concatenate([mine, got], axis=axis),
            jnp.concatenate([got, mine], axis=axis),
        )

    if compact:
        mine = lax.dynamic_index_in_dim(both, seq_rank, 0, keepdims=False)
        sent = lax.dynamic_index_in_dim(both, 1 - seq_rank, 0, keepdims=False)
        both = side_by_side(mine, pair_swap(sent, "seq"), 1)
    else:
        both = lax.all_to_all(jnp.repeat(both, sharers, axis=0), "seq", 0, 0, tiled=True)
        both = jnp.swapaxes(both, 0, 1).reshape(2, length, width)
    first_input = both[0]
    last_grad = both[1] * live

    flat_ids = time_ids.reshape(-1)
    selector = (
        flat_ids[:, None] == jnp.arange(table_rows, dtype=jnp.int32)[None, :]
    ).astype(jnp.bfloat16)
    conditions = matmul(selector, cond_table)
    silu_all = jax.nn.silu(conditions).astype(jnp.bfloat16)
    silu_own = lax.dynamic_slice_in_dim(silu_all, ring_rank * rows, rows, 1)
    if compact:
        *first_parts, second_shard, silu_late = gather_along_z(
            first_shard, place, ring_size, handed=(second_shard, silu_own)
        )
        first_parts += first_flips(*first_parts, ring_size)
    else:
        silu_late = silu_own

    products = matmul(silu_late, modulation_weight[0])
    own_bias = jnp.broadcast_to(biases.astype(jnp.float32), (products.shape[0], bias_count))
    products = jnp.repeat(jnp.concatenate([products, own_bias], axis=1), sharers, axis=0)
    products = lax.all_to_all(
        products[:, None], ("section", "dp", "seq"), 0, 0, tiled=True
    ).reshape(sections, ring_size, 6 * width + bias_count)
    first_modulation, second_modulation = jnp.split(
        jnp.sum(products[:, :, : 6 * width], axis=1), 2, axis=0
    )
    first_bias, second_bias = products[0, :, 6 * width :], products[1, :, 6 * width :]

    if compact:
        second_parts = gather_along_z(
            second_shard, place, ring_size, after=(both, *first_parts[2:])
        )
        second_parts += first_flips(*second_parts, ring_size)
        first_pack = gather_across(*first_parts, place, ring_size)
        second_pack = gather_across(*second_parts, place, ring_size)
    else:
        first_pack = lax.all_gather(first_shard, RING, axis=0, tiled=True)
        second_pack = lax.all_gather(second_shard, RING, axis=0, tiled=True)
    first_halves = (first_pack, pair_swap(first_pack, "section"))
    second_halves = (second_pack, pair_swap(second_pack, "section"))

    first_low, *first_saved = run_section(
        layout, rank, first_input, first_halves, (first_modulation, first_bias)
    )
    second_low, second_grad, second_dmod, second_sums, second_keep, second_send = run_section(
        layout, rank, first_low, second_halves, (second_modulation, second_bias), dy=last_grad
    )
    second_got = pair_swap(second_send, "section")

    def ring_terms(term):
        return term.reshape(ring_size, rows, half)

    first_grad, first_dmod, first_sums, first_keep, first_send = run_section(
        layout, rank, first_input, first_halves, saved=first_saved, dy=second_grad
    )
    first_got = pair_swap(first_send, "section")

    shard = jax.ShapeDtypeStruct((rows, half), jnp.float32)
    if compact:
        second_sorted = scatter_first(
            ring_terms(second_keep), ring_terms(second_got), place, ring_size
        )
        second_received = scatter_flips(second_sorted, ring_size)
        *first_sorted, first_dmod, first_sums = scatter_first(
            ring_terms(first_keep),
            ring_terms(first_got),
            place,
            ring_size,
            handed=(first_dmod, first_sums),
            after=(second_sorted[0],),
        )
        first_received = scatter_flips(first_sorted, ring_size)
        second_turned, _ = scatter_second(second_received, place, ring_size)
        first_turned, (first_grad,) = scatter_second(
            first_received, place, ring_size, handed=(first_grad,), after=(second_turned[0],)
        )
        second_sent = scatter_third(second_turned, place, ring_size, after=(first_turned[0],))
        second_pieces = scatter_along_z(second_sent, ring_size)

    rows_back = jnp.concatenate(
        [
            jnp.concatenate(
                [jnp.broadcast_to(dmod, (ring_size, 6 * width)), sums], axis=1
            )
            for dmod, sums in ((first_dmod, first_sums), (second_dmod, second_sums))
        ]
    )
    every = lax.all_to_all(rows_back[:, None], ("section", "dp", "seq"), 0, 0, tiled=True)
    every = every[::sharers, 0]
    bias_grad = jnp.sum(every[:, 6 * width :], axis=0)
    modulation_rows = low(every[:, : 6 * width])
    modulation_grad = outer_sum(silu_own, modulation_rows)
    columns = matmul_transposed(modulation_rows, modulation_weight[0])

    if compact:
        *first_sent, columns = scatter_third(
            first_turned, place, ring_size, handed=(columns,), after=(second_sent[0],)
        )
        first_pieces = scatter_along_z(first_sent, ring_size)
    else:

        def chip_sum(keep, got):
            return ring_terms(low(added(keep, got)))

        first_pieces, second_pieces = [
            [scatter_sum(chip_sum(keep, got), ring_rank, ring_size)]
            for keep, got in ((first_keep, first_got), (second_keep, second_got))
        ]
    outputs_ready = (first_low * live, second_low * live)
    if compact:
        block = jnp.stack([outputs_ready[0], first_grad, outputs_ready[1], second_grad])
        block = block.reshape(4, 2, tokens, width)
        mine = lax.dynamic_index_in_dim(block, seq_rank, 1, keepdims=True)
        sent = lax.dynamic_index_in_dim(block, 1 - seq_rank, 1, keepdims=True)
        block = side_by_side(mine, pair_swap(sent, "seq"), 1)
        per_first, per_second = block[:2], block[2:]
        mine = jnp.where(is_first, per_first, per_second)
        got = pair_swap(jnp.where(is_first, per_second, per_first), "section")
        outputs = jnp.where(is_first, jnp.stack([mine, got], 1), jnp.stack([got, mine], 1))
    else:
        pieces = jnp.stack([outputs_ready[0], first_grad, outputs_ready[1], second_grad])
        pieces = jnp.swapaxes(pieces.reshape(2, 2, seq_size, tokens, width), 1, 2)
        pieces = pieces.reshape(2 * seq_size, 2, tokens, width)
        pieces = lax.all_to_all(pieces, ("section", "seq"), 0, 0, tiled=True)
        pieces = pieces.reshape(batches, slots, sharers, 2, tokens, width)[:, :, 0]
        outputs = jnp.moveaxis(pieces, 2, 0)
    activations = outputs[0]
    input_grads = outputs[1].astype(jnp.float32)

    mine, send = in_memory(
        partial(close_kernel, len(first_pieces)),
        [shard, shard],
        [rank, *first_pieces, *second_pieces],
    )
    att, out, up, down = in_memory(
        spread_kernel,
        [
            jax.ShapeDtypeStruct(extent, jnp.float32)
            for extent in (
                (rows, 3 * width),
                (rows, width),
                (rows, hidden),
                (rows * ratio, width),
            )
        ],
        [rank, mine, pair_swap(send, "section")],
    )

    columns = jnp.broadcast_to(columns.reshape(1, 1, -1), (sections * ring_size, 1, columns.size))
    columns = lax.all_to_all(columns, ("section", "dp", "seq"), 0, 0, tiled=True)
    columns = jnp.sum(columns.reshape(sections, ring_size, -1, rows), axis=0)
    products_back = jnp.swapaxes(columns, 0, 1).reshape(-1, width)
    _, silu_back = jax.vjp(jax.nn.silu, conditions)
    table_grad = lax.dot_general(
        selector.astype(jnp.float32),
        silu_back(products_back)[0],
        (((0,), (0,)), ((), ())),
        precision=lax.Precision.HIGHEST,
        preferred_element_type=jnp.float32,
    )
    return (
        activations[None],
        input_grads[None],
        table_grad,
        modulation_grad[None],
        att[None],
        out[None],
        up[None],
        down[None],
        bias_grad[None],
    )


def solution(mesh):
    shard = P("section", ("dp", "seq"), None)
    in_specs = (
        P(None, "dp", "seq", None),
        P(None, "dp", "seq", None),
        P(),
        P(None, "dp"),
        P(),
        shard,
        shard,
        shard,
        shard,
        shard,
        P("section", ("dp", "seq")),
    )
    out_specs = (
        P("section", None, "dp", "seq", None),
        P("section", None, "dp", "seq", None),
        P(),
        shard,
        shard,
        shard,
        shard,
        shard,
        P("section", ("dp", "seq")),
    )
    return jax.shard_map(
        per_device, mesh=mesh, in_specs=in_specs, out_specs=out_specs, check_vma=False
    )
```

```python
from functools import partial

import jax
import jax.numpy as jnp
from jax import lax
from jax.experimental import pallas as pl
from jax.experimental.pallas import tpu as pltpu
from jax.sharding import PartitionSpec as P

HEADS = 6
HEAD = 64
SCALE = HEAD ** (-0.5)
epsilon = 1e-06
RING = ("dp", "seq")
INNER = (2.0 / 3.141592653589793) ** 0.5
CUBE = 0.044715


def matmul(former, latter):
    return jnp.dot(former, latter, preferred_element_type=jnp.float32)


def matmul_transposed(former, latter):
    return lax.dot_general(
        former, latter, (((1,), (1,)), ((), ())), preferred_element_type=jnp.float32
    )


def outer_sum(former, latter):
    return lax.dot_general(
        former, latter, (((0,), (0,)), ((), ())), preferred_element_type=jnp.float32
    )


def low(values):
    return values.astype(jnp.bfloat16)


def normalize_rows(values):
    centre = jnp.mean(values, axis=-1, keepdims=True)
    centred = values - centre
    spread = jnp.mean(centred * centred, axis=-1, keepdims=True)
    factor = lax.rsqrt(spread + epsilon)
    return (centred * factor, factor)


def normalize_back(normed, factor, grad_normed):
    mean_grad = jnp.mean(grad_normed, axis=-1, keepdims=True)
    mean_cross = jnp.mean(grad_normed * normed, axis=-1, keepdims=True)
    return factor * (grad_normed - mean_grad - normed * mean_cross)


def column_sum(values):
    return jnp.sum(values.astype(jnp.float32), axis=0, keepdims=True)


def saved_shapes(layout, length):
    width, hidden = layout[:2]
    bf16, f32 = jnp.bfloat16, jnp.float32
    return [
        ((1, 6 * width), f32),
        ((length, 3 * width), bf16),
        ((length, width), bf16),
        ((length, hidden), bf16),
        ((HEADS, length, length), f32),
        ((length, hidden), f32),
        ((length, width), f32),
        ((length, width), f32),
        ((hidden, width), bf16),
    ]


def section_kernel(layout, forward, backward, after, *refs):
    width, hidden, rows, ratio, ring_size, share, bias_count = layout
    refs = list(refs)

    def take(count):
        taken = refs[:count]
        del refs[:count]
        return taken

    rank_ref, x_ref = take(2)
    if forward:
        modulation_ref, bias_ref = take(2)
    else:
        saved = take(9)
    if backward:
        (dy_ref,) = take(1)
    mine_ref, theirs_ref = take(2)
    take(after)
    if forward:
        (y_ref,) = take(1)
    if backward:
        dx_ref, dmod_ref, sums_ref, keep_ref, send_ref = take(5)
    elif forward:
        saved = take(9)
    att_w, out_w, up_w, sems, down_s, block_s = take(6)
    if forward:
        down_p, bias_s = take(2)
    if backward:
        da_s, dqkv_s, row_ref, halves, out_sems = take(5)
    if forward and backward:
        saved = take(9)
    mod_s, qkv_s, att_s, u_s, soft_s, slope_s, one_s, two_s, down_w = saved

    rank = rank_ref[0]
    split = hidden - 2 * width

    def fetches(first, second):
        moves = [
            (first.at[:, : 3 * width], att_w),
            (first.at[:, 3 * width : 4 * width], out_w),
            (first.at[:, 4 * width :], up_w.at[:, :split]),
            (second.at[:, : hidden - split], up_w.at[:, split:]),
        ]
        if forward:
            moves.append((second.at[:, hidden - split :], down_p))
        return [
            pltpu.make_async_copy(source, target, sems.at[i])
            for i, (source, target) in enumerate(moves)
        ]

    @pl.when(rank == 0)
    def _():
        for copy in fetches(mine_ref, theirs_ref):
            copy.start()

    @pl.when(rank != 0)
    def _():
        for copy in fetches(theirs_ref, mine_ref):
            copy.start()

    arrivals = fetches(mine_ref, theirs_ref)

    def part(ref, member, head):
        start = member * width + head * HEAD
        return ref[:, start : start + HEAD]

    x = x_ref[...].astype(jnp.float32)
    normed_one, factor_one = normalize_rows(x)
    if forward:
        for d in range(ring_size):
            bias_s[:, d * bias_count : (d + 1) * bias_count] = bias_ref[d : d + 1, :]
        mod_s[...] = modulation_ref[...] + bias_s[:, : 6 * width]
    shift_one, scale_one, gate_one, shift_two, scale_two, gate_two = [
        mod_s[:, i * width : (i + 1) * width] for i in range(6)
    ]
    hidden_one = low(normed_one * (1.0 + scale_one) + shift_one)
    if forward:

        def bias(a, b):
            return bias_s[:, a:b]

        at = 6 * width
        arrivals[0].wait()
        qkv_s[:, :width] = low(matmul(hidden_one, att_w[:, :width]) + bias(at, at + width))
        qkv_s[:, width : 2 * width] = low(matmul(hidden_one, att_w[:, width : 2 * width]))
        qkv_s[:, 2 * width :] = low(
            matmul(hidden_one, att_w[:, 2 * width :]) + bias(at + width, at + 2 * width)
        )
        for head in range(HEADS):
            scores = matmul_transposed(part(qkv_s, 0, head), part(qkv_s, 1, head)) * SCALE
            raised = jnp.exp(scores - jnp.max(scores, axis=-1, keepdims=True))
            soft = raised * (1.0 / jnp.sum(raised, axis=-1, keepdims=True))
            soft_s[head] = soft
            attended = matmul(low(soft), part(qkv_s, 2, head))
            att_s[:, head * HEAD : (head + 1) * HEAD] = low(attended)
        arrivals[1].wait()
        one_s[...] = matmul(att_s[...], out_w[...]) + bias(at + 2 * width, at + 3 * width)
    branch_one = one_s[...]
    middle = x + gate_one * branch_one
    normed_two, factor_two = normalize_rows(middle)
    hidden_two = low(normed_two * (1.0 + scale_two) + shift_two)
    if forward:
        arrivals[2].wait()
        arrivals[3].wait()
        at += 3 * width
        for j in range(ratio):
            cut = slice(j * width, (j + 1) * width)
            a = matmul(hidden_two, up_w[:, cut]) + bias(at + j * width, at + (j + 1) * width)
            square = a * a
            turn = jnp.tanh(INNER * (a + CUBE * (a * square)))
            half_one = 0.5 * (1.0 + turn)
            u_s[:, cut] = low(a * half_one)
            slope_s[:, cut] = half_one + (0.5 * INNER) * a * (1.0 - turn * turn) * (
                1.0 + (3.0 * CUBE) * square
            )
        arrivals[4].wait()
        block_s[...] = down_p[...].astype(jnp.float32)
        for d in range(ring_size):
            for j in range(ratio):
                down_s[(d * ratio + j) * rows : (d * ratio + j + 1) * rows, :] = block_s[
                    d * rows : (d + 1) * rows, j * width : (j + 1) * width
                ]
        down_w[...] = low(down_s[...])
        two_s[...] = matmul(u_s[...], down_w[...]) + bias(at + hidden, at + hidden + width)
        y_ref[...] = low(middle + gate_two * two_s[...])
    if not backward:
        return

    grad_out = dy_ref[...].astype(jnp.float32)
    grad_branch = low(gate_two * grad_out)
    sums_at = 6 * width
    row_ref[:, 5 * width : 6 * width] = column_sum(grad_out * two_s[...])
    row_ref[:, sums_at + 3 * width + hidden : sums_at + 4 * width + hidden] = column_sum(
        grad_branch
    )
    for j in range(ratio):
        cut = slice(j * width, (j + 1) * width)
        grad_expanded = low(slope_s[:, cut] * matmul_transposed(grad_branch, down_w[cut, :]))
        da_s[:, cut] = grad_expanded
        row_ref[:, sums_at + (3 + j) * width : sums_at + (4 + j) * width] = column_sum(
            grad_expanded
        )
    halves[0, :, 4 * width :] = low(outer_sum(hidden_two, da_s[:, :split]) * share)
    halves[1, :, : hidden - split] = low(outer_sum(hidden_two, da_s[:, split:]) * share)
    down_s[...] = outer_sum(u_s[...], grad_branch) * share
    for d in range(ring_size):
        for j in range(ratio):
            block_s[d * rows : (d + 1) * rows, j * width : (j + 1) * width] = down_s[
                (d * ratio + j) * rows : (d * ratio + j + 1) * rows, :
            ]
    halves[1, :, hidden - split :] = low(block_s[...])
    second_out = [
        pltpu.make_async_copy(halves.at[1], keep_ref, out_sems.at[1]),
        pltpu.make_async_copy(halves.at[1], send_ref, out_sems.at[1]),
    ]

    @pl.when(rank == 1)
    def _():
        second_out[0].start()

    @pl.when(rank != 1)
    def _():
        second_out[1].start()

    if not forward:
        arrivals[2].wait()
        arrivals[3].wait()
    grad_hidden_two = matmul_transposed(da_s[...], up_w[...])
    row_ref[:, 3 * width : 4 * width] = column_sum(grad_hidden_two)
    row_ref[:, 4 * width : 5 * width] = column_sum(grad_hidden_two * normed_two)
    grad_middle = grad_out + normalize_back(
        normed_two, factor_two, grad_hidden_two * (1.0 + scale_two)
    )
    row_ref[:, 2 * width : 3 * width] = column_sum(grad_middle * branch_one)
    grad_attention = low(gate_one * grad_middle)
    row_ref[:, sums_at + 2 * width : sums_at + 3 * width] = column_sum(grad_attention)
    halves[0, :, 3 * width : 4 * width] = low(outer_sum(att_s[...], grad_attention) * share)
    if not forward:
        arrivals[1].wait()
    grad_attended = low(matmul_transposed(grad_attention, out_w[...]))
    for head in range(HEADS):
        soft = soft_s[head]
        grad_head = grad_attended[:, head * HEAD : (head + 1) * HEAD]
        grad_soft = matmul_transposed(grad_head, part(qkv_s, 2, head))
        inner = jnp.sum(grad_soft * soft, axis=-1, keepdims=True)
        grad_scores = low(soft * (grad_soft - inner))
        grads = (
            matmul(grad_scores, part(qkv_s, 1, head)) * SCALE,
            outer_sum(grad_scores, part(qkv_s, 0, head)) * SCALE,
            outer_sum(low(soft), grad_head),
        )
        for member, grad in enumerate(grads):
            start = member * width + head * HEAD
            dqkv_s[:, start : start + HEAD] = low(grad)
    row_ref[:, sums_at : sums_at + width] = column_sum(dqkv_s[:, :width])
    row_ref[:, sums_at + width : sums_at + 2 * width] = column_sum(dqkv_s[:, 2 * width :])
    halves[0, :, : 3 * width] = low(outer_sum(hidden_one, dqkv_s[...]) * share)
    first_out = [
        pltpu.make_async_copy(halves.at[0], keep_ref, out_sems.at[0]),
        pltpu.make_async_copy(halves.at[0], send_ref, out_sems.at[0]),
    ]

    @pl.when(rank == 0)
    def _():
        first_out[0].start()

    @pl.when(rank != 0)
    def _():
        first_out[1].start()

    if not forward:
        arrivals[0].wait()
    grad_hidden_one = matmul_transposed(dqkv_s[...], att_w[...])
    row_ref[:, :width] = column_sum(grad_hidden_one)
    row_ref[:, width : 2 * width] = column_sum(grad_hidden_one * normed_one)
    dx_ref[...] = low(
        grad_middle
        + normalize_back(normed_one, factor_one, grad_hidden_one * (1.0 + scale_one))
    )
    row_ref[:, : 6 * width] = low(row_ref[:, : 6 * width]).astype(jnp.float32)
    dmod_ref[...] = row_ref[:, : 6 * width]
    for d in range(ring_size):
        sums_ref[d : d + 1, :] = row_ref[:, d * bias_count : (d + 1) * bias_count]
    second_out[0].wait()
    first_out[0].wait()


def run_section(layout, rank, x, halves, start=None, saved=None, dy=None, after=()):
    width, hidden, rows, ratio, ring_size, share, bias_count = layout
    length = x.shape[0]
    forward, backward = start is not None, dy is not None
    vmem = pl.BlockSpec(memory_space=pltpu.VMEM)
    hbm = pl.BlockSpec(memory_space=pl.ANY)
    bf16, f32 = jnp.bfloat16, jnp.float32
    half = 2 * width + hidden
    kept = saved_shapes(layout, length)
    operands = [rank, x, *(start if forward else saved)]
    shapes, out_specs = [], []
    scratch = [
        pltpu.VMEM((width, 3 * width), bf16),
        pltpu.VMEM((width, width), bf16),
        pltpu.VMEM((width, hidden), bf16),
        pltpu.SemaphoreType.DMA((5,)),
        pltpu.VMEM((hidden, width), f32),
        pltpu.VMEM((width, hidden), f32),
    ]
    if forward:
        shapes.append(jax.ShapeDtypeStruct((length, width), bf16))
        scratch += [
            pltpu.VMEM((width, hidden), bf16),
            pltpu.VMEM((1, bias_count * ring_size), f32),
        ]
    if backward:
        operands.append(dy)
        shapes += [
            jax.ShapeDtypeStruct((length, width), bf16),
            jax.ShapeDtypeStruct((1, 6 * width), f32),
            jax.ShapeDtypeStruct((ring_size, bias_count), f32),
            jax.ShapeDtypeStruct((width, half), bf16),
            jax.ShapeDtypeStruct((width, half), bf16),
        ]
        scratch += [
            pltpu.VMEM((length, hidden), bf16),
            pltpu.VMEM((length, 3 * width), bf16),
            pltpu.VMEM((1, 10 * width + hidden), f32),
            pltpu.VMEM((2, width, half), bf16),
            pltpu.SemaphoreType.DMA((2,)),
        ]
        if forward:
            scratch += [pltpu.VMEM(extent, kind) for extent, kind in kept]
    else:
        shapes += [jax.ShapeDtypeStruct(extent, kind) for extent, kind in kept]
    out_specs = [vmem] * len(shapes)
    if backward:
        out_specs[-2:] = [hbm, hbm]
    specs = [pl.BlockSpec(memory_space=pltpu.SMEM)] + [vmem] * (len(operands) - 1)
    specs += [hbm] * (2 + len(after))
    work = 2 * length * width * (4 * width + 2 * hidden + 2 * length)
    moved = 2 * width * (10 * width + 2 * hidden)
    return pl.pallas_call(
        partial(section_kernel, layout, forward, backward, len(after)),
        out_shape=shapes,
        in_specs=specs,
        out_specs=out_specs,
        scratch_shapes=scratch,
        compiler_params=pltpu.CompilerParams(
            vmem_limit_bytes=(56 if length > 256 else 26 if forward and backward else 22)
            * 1024
            * 1024
        ),
        cost_estimate=pl.CostEstimate(
            flops=(forward + 2 * backward) * work,
            bytes_accessed=(1 + backward) * moved,
            transcendentals=HEADS * length * length + length * hidden,
        ),
    )(*operands, *halves, *after)


def copy_all(copies):
    for copy in copies:
        copy.start()
    for copy in copies:
        copy.wait()


def pack_kernel(rank_ref, att_ref, out_ref, up_ref, down_ref, keep_ref, send_ref, sems):
    ratio, rows, width = down_ref.shape
    split = (ratio - 2) * width

    def copies(first, second):
        moves = [
            (att_ref, first.at[:, : 3 * width]),
            (out_ref, first.at[:, 3 * width : 4 * width]),
            (up_ref.at[:, :split], first.at[:, 4 * width :]),
            (up_ref.at[:, split:], second.at[:, : 2 * width]),
        ]
        for j in range(ratio):
            moves.append((down_ref.at[j], second.at[:, (2 + j) * width : (3 + j) * width]))
        return [
            pltpu.make_async_copy(source, target, sems.at[i])
            for i, (source, target) in enumerate(moves)
        ]

    @pl.when(rank_ref[0] == 0)
    def _():
        copy_all(copies(keep_ref, send_ref))

    @pl.when(rank_ref[0] != 0)
    def _():
        copy_all(copies(send_ref, keep_ref))


def stack_kernel(high, split, place_ref, *refs):
    pieces, sems = refs[:high], refs[-1]
    count = (len(refs) - high - 3) // 2
    handed, targets = refs[high : high + count], refs[high + count : -1]
    copies = [
        pltpu.make_async_copy(former, latter, sems.at[high + i, 0])
        for i, (former, latter) in enumerate(zip(handed, targets[2:]))
    ]
    for turn, piece in enumerate(pieces):
        place = lax.rem(place_ref[0] + (high - turn), high)
        parts = (piece.at[:, :split], piece.at[:, split:])
        for i, (part, target) in enumerate(zip(parts, targets)):
            copies.append(pltpu.make_async_copy(part, target.at[place], sems.at[turn, i]))
    copy_all(copies)


def weave_kernel(split, place_ref, *refs):
    pieces, full_ref, sems = refs[:-2], refs[-2], refs[-1]
    x, y = place_ref[1], place_ref[2]
    copies = []
    for i, piece in enumerate(pieces):
        other_x, other_y = (i % 4) & 1, (i % 4) >> 1
        row = x if not other_x else 1 - x
        column = y if not other_y else 1 - y
        target = full_ref.at[:, row, column, :, pl.ds((i // 4) * split, split)]
        copies.append(pltpu.make_async_copy(piece, target, sems.at[i]))
    copy_all(copies)


def added(former, latter):
    return former.astype(jnp.float32) + latter.astype(jnp.float32)


def chip_sum_kernel(high, place_ref, mine, got, *refs):
    count = (len(refs) - 4) // 2
    first_keep, first_send, second_keep, second_send = refs[count : count + 4]
    for former, latter in zip(refs[:count], refs[count + 4 :]):
        latter[...] = former[...]
    x, y = place_ref[1], place_ref[2]
    half = mine.shape[2]
    lanes = half // 2
    for z in range(high):
        for other in range(2):
            for target, span, chunk in (
                (first_keep, slice(0, lanes), z * 4 + x * 2 + other),
                (first_send, slice(0, lanes), z * 4 + (1 - x) * 2 + other),
                (second_keep, slice(lanes, half), z * 4 + other * 2 + y),
                (second_send, slice(lanes, half), z * 4 + other * 2 + (1 - y)),
            ):
                target[z, other] = low(added(mine[chunk, :, span], got[chunk, :, span]))


def turn_kernel(high, place_ref, *refs):
    count = (len(refs) - 8) // 2
    for former, latter in zip(refs[4 : 4 + count], refs[8 + count :]):
        latter[...] = former[...]
    for part, own in ((0, place_ref[2]), (1, place_ref[1])):
        kept, got = refs[2 * part : 2 * part + 2]
        keep, send = refs[4 + count + 2 * part : 6 + count + 2 * part]
        for z in range(high):
            keep[z] = low(added(kept[z, own], got[z, own]))
            send[z] = low(added(kept[z, 1 - own], got[z, 1 - own]))


def rise_kernel(high, place_ref, *refs):
    targets = refs[4:]
    lanes = refs[0].shape[2]
    for turn in range(high):
        chunk = lax.rem(place_ref[0] + turn, high)
        for part in range(2):
            kept, got = refs[2 * part : 2 * part + 2]
            total = added(kept[chunk], got[chunk])
            span = slice(part * lanes, (part + 1) * lanes)
            targets[turn][:, span] = total.astype(targets[turn].dtype)


def close_kernel(high, rank_ref, *refs):
    keep, send = refs[-2:]
    totals = []
    for section in range(2):
        pieces = refs[section * high : (section + 1) * high]
        total = pieces[0][...].astype(jnp.float32)
        for piece in pieces[1:]:
            total = total + piece[...].astype(jnp.float32)
        totals.append(total)
    first = rank_ref[0] == 0
    keep[...] = jnp.where(first, totals[0], totals[1])
    send[...] = jnp.where(first, totals[1], totals[0])


def spread_kernel(rank_ref, mine, got, att_ref, out_ref, up_ref, down_ref):
    rows, width = out_ref.shape
    split = up_ref.shape[1] - 2 * width
    first = rank_ref[0] == 0
    lower = jnp.where(first, mine[...], got[...])
    upper = jnp.where(first, got[...], mine[...])
    att_ref[...] = lower[:, : 3 * width]
    out_ref[...] = lower[:, 3 * width : 4 * width]
    up_ref[:, :split] = lower[:, 4 * width :]
    up_ref[:, split:] = upper[:, : 2 * width]
    for j in range(down_ref.shape[0] // rows):
        down_ref[j * rows : (j + 1) * rows, :] = upper[:, (2 + j) * width : (3 + j) * width]


def in_memory(kernel, shapes, operands, scratch=(), memory=pltpu.VMEM, after=(), limit=16):
    specs = [pl.BlockSpec(memory_space=pltpu.SMEM)]
    specs += [pl.BlockSpec(memory_space=memory)] * (len(operands) - 1)
    specs += [pl.BlockSpec(memory_space=pl.ANY)] * len(after)
    count = len(operands)

    def body(*refs):
        kernel(*refs[:count], *refs[count + len(after) :])

    moved = sum(shape.size * shape.dtype.itemsize for shape in shapes)
    return pl.pallas_call(
        body,
        out_shape=shapes,
        in_specs=specs,
        out_specs=[pl.BlockSpec(memory_space=pltpu.VMEM)] * len(shapes),
        scratch_shapes=list(scratch),
        compiler_params=pltpu.CompilerParams(vmem_limit_bytes=limit * 1024 * 1024),
        cost_estimate=pl.CostEstimate(flops=0, bytes_accessed=3 * moved, transcendentals=0),
    )(*operands, *after)


def hand_kernel(rank_ref, former, latter):
    latter[...] = former[...]


def hand_on(rank, block, after):
    shape = jax.ShapeDtypeStruct(block.shape, block.dtype)
    return in_memory(hand_kernel, [shape], [rank, block], after=after)[0]


def pair_swap(block, axis):
    return lax.ppermute(block, axis, [(0, 1), (1, 0)])


def ring_exchange(block, size, step):
    return lax.ppermute(block, RING, [(i, step(i)) for i in range(size)])


def flip(block, size, mask):
    return ring_exchange(block, size, lambda i: i ^ mask)


def rotate(block, size, turn):
    return ring_exchange(block, size, lambda i: (i + 4 * turn) % size)


def rotations(block, size):
    return [block] + [rotate(block, size, turn) for turn in range(1, size // 4)]


def gather_along_z(shards, place, handed=(), after=()):
    high = len(shards)
    rows, lanes = shards[0].shape
    return in_memory(
        partial(stack_kernel, high, lanes // 2),
        [jax.ShapeDtypeStruct((high, rows, lanes // 2), shards[0].dtype)] * 2
        + [jax.ShapeDtypeStruct(block.shape, block.dtype) for block in handed],
        [place, *shards, *handed],
        scratch=[pltpu.SemaphoreType.DMA((high + len(handed), 2))],
        after=after,
        limit=32,
    )


def first_flips(first, second, size):
    return flip(first, size, 2), flip(second, size, 1)


def gather_across(first, second, first_x, second_y, place, size):
    high, rows, lanes = first.shape
    first_y, second_x = flip(first, size, 1), flip(second, size, 2)
    first_both, second_both = flip(first_x, size, 1), flip(second_y, size, 2)
    (full,) = in_memory(
        partial(weave_kernel, lanes),
        [jax.ShapeDtypeStruct((high, 2, 2, rows, 2 * lanes), first.dtype)],
        [place, first, first_x, first_y, first_both, second, second_x, second_y, second_both],
        scratch=[pltpu.SemaphoreType.DMA((8,))],
        limit=32,
    )
    return full.reshape(size * rows, 2 * lanes)


def scatter_first(mine, got, place, size, handed=(), after=()):
    rows, half = mine.shape[1:]
    shape = jax.ShapeDtypeStruct((size // 4, 2, rows, half // 2), jnp.bfloat16)
    return in_memory(
        partial(chip_sum_kernel, size // 4),
        [shape] * 4 + [jax.ShapeDtypeStruct(block.shape, block.dtype) for block in handed],
        [place, mine, got, *handed],
        after=after,
    )


def scatter_flips(sorted_terms, size):
    first_keep, first_send, second_keep, second_send = sorted_terms
    return first_keep, flip(first_send, size, 2), second_keep, flip(second_send, size, 1)


def scatter_second(received, place, size, handed=(), after=()):
    high, _, rows, lanes = received[0].shape
    shape = jax.ShapeDtypeStruct((high, rows, lanes), jnp.bfloat16)
    first_keep, first_send, second_keep, second_send, *handed = in_memory(
        partial(turn_kernel, high),
        [shape] * 4 + [jax.ShapeDtypeStruct(block.shape, block.dtype) for block in handed],
        [place, *received, *handed],
        after=after,
    )
    turned = (first_keep, flip(first_send, size, 1), second_keep, flip(second_send, size, 2))
    return turned, handed


def scatter_third(turned, place, size, after=()):
    high, rows, lanes = turned[0].shape
    chunk = (rows, 2 * lanes)
    return in_memory(
        partial(rise_kernel, high),
        [jax.ShapeDtypeStruct(chunk, jnp.float32)]
        + [jax.ShapeDtypeStruct(chunk, jnp.bfloat16)] * (high - 1),
        [place, *turned],
        after=after,
    )


def scatter_along_z(pieces, size):
    own, *sent = pieces
    return [own] + [rotate(block, size, turn + 1) for turn, block in enumerate(sent)]


def scatter_sum(block, rank, size):
    half = block.shape[-1] // 2
    pieces = [block[..., :half], block[..., half:]]
    left = size
    low_bits = 0
    while left > 4:
        orders = [(0, 1), (1, 0)] if left % 4 == 0 and left >= 16 else [(0,), (0,)]
        for turn in range(len(orders[0])):
            updated = []
            for piece, order in zip(pieces, orders):
                bit = low_bits + order[turn]
                mine = (rank >> bit) & 1
                if len(order) == 2 and turn == 0:
                    shaped = piece.reshape(-1, 2, 2, *piece.shape[1:])
                    at = 2 - order[turn]
                else:
                    shaped = piece.reshape(-1, 2, *piece.shape[1:])
                    at = 1
                keep = lax.dynamic_index_in_dim(shaped, mine, at, keepdims=False)
                send = lax.dynamic_index_in_dim(shaped, 1 - mine, at, keepdims=False)
                got = ring_exchange(send, size, lambda i, bit=bit: i ^ (1 << bit))
                total = (keep.astype(jnp.float32) + got.astype(jnp.float32)).astype(jnp.bfloat16)
                updated.append(total.reshape(-1, *piece.shape[1:]))
            pieces = updated
        low_bits += len(orders[0])
        left //= 2 ** len(orders[0])
    block = jnp.concatenate(pieces, axis=-1)
    high = rank >> low_bits
    total = lax.dynamic_index_in_dim(block, high, 0, keepdims=False).astype(jnp.float32)
    stride = 1 << low_bits
    for turn in range(1, left):
        send = lax.dynamic_index_in_dim(block, (high + turn) % left, 0, keepdims=False)
        got = ring_exchange(send, size, lambda i, turn=turn: (i + turn * stride) % size)
        total = total + got.astype(jnp.float32)
    return total


def per_device(
    inputs,
    cotangent,
    time_ids,
    row_counts,
    cond_table,
    modulation_weight,
    attention_weight,
    output_weight,
    expand_weight,
    shrink_weight,
    biases,
):
    section_rank = lax.axis_index("section")
    data_rank = lax.axis_index("dp")
    seq_rank = lax.axis_index("seq")
    sections = lax.axis_size("section")
    seq_size = lax.axis_size("seq")
    ring_size = lax.axis_size("dp") * seq_size
    ring_rank = data_rank * seq_size + seq_rank
    batches, slots, tokens, width = inputs.shape
    assert batches == sections == 2 and seq_size % slots == 0
    sharers = seq_size // slots
    slot = seq_rank // sharers
    length = tokens * seq_size
    rows = attention_weight.shape[1]
    ratio = shrink_weight.shape[1] // rows
    hidden = ratio * width
    bias_count = biases.shape[1]
    half = 2 * width + hidden
    assert hidden == expand_weight.shape[2] and ratio >= 2
    table_rows = cond_table.shape[0]
    is_first = section_rank == 0
    layout = (width, hidden, rows, ratio, ring_size, 1.0 / sharers, bias_count)
    compact = ring_size in (8, 16) and seq_size == slots == 2
    rank = section_rank.astype(jnp.int32).reshape(1)
    place = jnp.stack([ring_rank >> 2, (ring_rank >> 1) & 1, ring_rank & 1]).astype(jnp.int32)

    keep, send = in_memory(
        pack_kernel,
        [jax.ShapeDtypeStruct((rows, half), jnp.bfloat16)] * 2,
        [
            rank,
            attention_weight[0],
            output_weight[0],
            expand_weight[0],
            shrink_weight[0].reshape(ratio, rows, width),
        ],
        scratch=[pltpu.SemaphoreType.DMA((4 + ratio,))],
        memory=pl.ANY,
        limit=56,
    )
    got = pair_swap(send, "section")
    first_shard = jnp.where(is_first, keep, got)
    second_shard = jnp.where(is_first, got, keep)

    live = (
        slot < lax.dynamic_index_in_dim(row_counts, section_rank, 0, keepdims=False)[0]
    ).astype(jnp.bfloat16)
    both = jnp.stack(
        [
            lax.dynamic_index_in_dim(inputs, section_rank, 0, keepdims=False),
            lax.dynamic_index_in_dim(cotangent, section_rank, 0, keepdims=False),
        ],
        axis=1,
    )

    def side_by_side(mine, got, axis):
        return jnp.where(
            seq_rank == 0,
            jnp.concatenate([mine, got], axis=axis),
            jnp.concatenate([got, mine], axis=axis),
        )

    if compact:
        mine = lax.dynamic_index_in_dim(both, seq_rank, 0, keepdims=False)
        sent = lax.dynamic_index_in_dim(both, 1 - seq_rank, 0, keepdims=False)
        both = side_by_side(mine, pair_swap(sent, "seq"), 1)
    else:
        both = lax.all_to_all(jnp.repeat(both, sharers, axis=0), "seq", 0, 0, tiled=True)
        both = jnp.swapaxes(both, 0, 1).reshape(2, length, width)
    first_input = both[0]
    last_grad = both[1] * live

    flat_ids = time_ids.reshape(-1)
    selector = (
        flat_ids[:, None] == jnp.arange(table_rows, dtype=jnp.int32)[None, :]
    ).astype(jnp.bfloat16)
    conditions = matmul(selector, cond_table)
    silu_all = jax.nn.silu(conditions).astype(jnp.bfloat16)
    silu_own = lax.dynamic_slice_in_dim(silu_all, ring_rank * rows, rows, 1)
    if compact:
        first_shards = rotations(first_shard, ring_size)
        *first_parts, second_shard, silu_late = gather_along_z(
            first_shards, place, handed=(second_shard, silu_own)
        )
        first_parts += first_flips(*first_parts, ring_size)
    else:
        silu_late = silu_own

    products = matmul(silu_late, modulation_weight[0])
    own_bias = jnp.broadcast_to(biases.astype(jnp.float32), (products.shape[0], bias_count))
    products = jnp.repeat(jnp.concatenate([products, own_bias], axis=1), sharers, axis=0)
    products = lax.all_to_all(
        products[:, None], ("section", "dp", "seq"), 0, 0, tiled=True
    ).reshape(sections, ring_size, 6 * width + bias_count)
    first_modulation, second_modulation = jnp.split(
        jnp.sum(products[:, :, : 6 * width], axis=1), 2, axis=0
    )
    first_bias, second_bias = products[0, :, 6 * width :], products[1, :, 6 * width :]

    if compact:
        second_parts = gather_along_z(
            rotations(second_shard, ring_size), place, after=(both, *first_parts[2:])
        )
        second_parts += first_flips(*second_parts, ring_size)
        first_pack = gather_across(*first_parts, place, ring_size)
        second_pack = gather_across(*second_parts, place, ring_size)
    else:
        first_pack = lax.all_gather(first_shard, RING, axis=0, tiled=True)
        second_pack = lax.all_gather(second_shard, RING, axis=0, tiled=True)
    first_halves = (first_pack, pair_swap(first_pack, "section"))
    second_halves = (second_pack, pair_swap(second_pack, "section"))

    first_low, *first_saved = run_section(
        layout, rank, first_input, first_halves, (first_modulation, first_bias)
    )
    second_low, second_grad, second_dmod, second_sums, second_keep, second_send = run_section(
        layout, rank, first_low, second_halves, (second_modulation, second_bias), dy=last_grad
    )
    second_got = pair_swap(second_send, "section")

    def ring_terms(term):
        return term.reshape(ring_size, rows, half)

    first_grad, first_dmod, first_sums, first_keep, first_send = run_section(
        layout, rank, first_input, first_halves, saved=first_saved, dy=second_grad
    )
    first_got = pair_swap(first_send, "section")

    shard = jax.ShapeDtypeStruct((rows, half), jnp.float32)
    if compact:
        second_sorted = scatter_first(
            ring_terms(second_keep), ring_terms(second_got), place, ring_size
        )
        second_received = scatter_flips(second_sorted, ring_size)
        *first_sorted, first_dmod, first_sums = scatter_first(
            ring_terms(first_keep),
            ring_terms(first_got),
            place,
            ring_size,
            handed=(first_dmod, first_sums),
            after=(second_sorted[0],),
        )
        first_received = scatter_flips(first_sorted, ring_size)
        second_turned, _ = scatter_second(second_received, place, ring_size)
        second_sent = scatter_third(second_turned, place, ring_size)
        second_pieces = scatter_along_z(second_sent, ring_size)
        first_turned, (first_grad,) = scatter_second(
            first_received, place, ring_size, handed=(first_grad,), after=(second_sent[0],)
        )
        first_sent = scatter_third(first_turned, place, ring_size, tuple(second_pieces[1:]))
        first_pieces = scatter_along_z(first_sent, ring_size)
    else:

        def chip_sum(keep, got):
            return ring_terms(low(added(keep, got)))

        first_pieces, second_pieces = [
            [scatter_sum(chip_sum(keep, got), ring_rank, ring_size)]
            for keep, got in ((first_keep, first_got), (second_keep, second_got))
        ]
    rows_back = jnp.concatenate(
        [
            jnp.concatenate(
                [jnp.broadcast_to(dmod, (ring_size, 6 * width)), sums], axis=1
            )
            for dmod, sums in ((first_dmod, first_sums), (second_dmod, second_sums))
        ]
    )
    every = lax.all_to_all(rows_back[:, None], ("section", "dp", "seq"), 0, 0, tiled=True)
    every = every[::sharers, 0]
    bias_grad = jnp.sum(every[:, 6 * width :], axis=0)
    modulation_rows = low(every[:, : 6 * width])
    modulation_grad = outer_sum(silu_own, modulation_rows)
    columns = matmul_transposed(modulation_rows, modulation_weight[0])
    if compact:
        columns = hand_on(rank, columns, (second_pieces[1],))
    columns = jnp.broadcast_to(columns.reshape(1, 1, -1), (sections * ring_size, 1, columns.size))
    columns = lax.all_to_all(columns, ("section", "dp", "seq"), 0, 0, tiled=True)

    outputs_ready = (first_low * live, second_low * live)
    if compact:
        block = jnp.stack([outputs_ready[0], first_grad, outputs_ready[1], second_grad])
        block = block.reshape(4, 2, tokens, width)
        mine = lax.dynamic_index_in_dim(block, seq_rank, 1, keepdims=True)
        sent = lax.dynamic_index_in_dim(block, 1 - seq_rank, 1, keepdims=True)
        block = side_by_side(mine, pair_swap(sent, "seq"), 1)
        per_first, per_second = block[:2], block[2:]
        mine = jnp.where(is_first, per_first, per_second)
        got = pair_swap(jnp.where(is_first, per_second, per_first), "section")
        outputs = jnp.where(is_first, jnp.stack([mine, got], 1), jnp.stack([got, mine], 1))
    else:
        pieces = jnp.stack([outputs_ready[0], first_grad, outputs_ready[1], second_grad])
        pieces = jnp.swapaxes(pieces.reshape(2, 2, seq_size, tokens, width), 1, 2)
        pieces = pieces.reshape(2 * seq_size, 2, tokens, width)
        pieces = lax.all_to_all(pieces, ("section", "seq"), 0, 0, tiled=True)
        pieces = pieces.reshape(batches, slots, sharers, 2, tokens, width)[:, :, 0]
        outputs = jnp.moveaxis(pieces, 2, 0)
    activations = outputs[0]
    input_grads = outputs[1].astype(jnp.float32)

    mine, send = in_memory(
        partial(close_kernel, len(first_pieces)),
        [shard, shard],
        [rank, *first_pieces, *second_pieces],
        after=(columns,),
    )
    att, out, up, down = in_memory(
        spread_kernel,
        [
            jax.ShapeDtypeStruct(extent, jnp.float32)
            for extent in (
                (rows, 3 * width),
                (rows, width),
                (rows, hidden),
                (rows * ratio, width),
            )
        ],
        [rank, mine, pair_swap(send, "section")],
    )

    columns = jnp.sum(columns.reshape(sections, ring_size, -1, rows), axis=0)
    products_back = jnp.swapaxes(columns, 0, 1).reshape(-1, width)
    _, silu_back = jax.vjp(jax.nn.silu, conditions)
    table_grad = lax.dot_general(
        selector.astype(jnp.float32),
        silu_back(products_back)[0],
        (((0,), (0,)), ((), ())),
        precision=lax.Precision.HIGHEST,
        preferred_element_type=jnp.float32,
    )
    return (
        activations[None],
        input_grads[None],
        table_grad,
        modulation_grad[None],
        att[None],
        out[None],
        up[None],
        down[None],
        bias_grad[None],
    )


def solution(mesh):
    shard = P("section", ("dp", "seq"), None)
    in_specs = (
        P(None, "dp", "seq", None),
        P(None, "dp", "seq", None),
        P(),
        P(None, "dp"),
        P(),
        shard,
        shard,
        shard,
        shard,
        shard,
        P("section", ("dp", "seq")),
    )
    out_specs = (
        P("section", None, "dp", "seq", None),
        P("section", None, "dp", "seq", None),
        P(),
        shard,
        shard,
        shard,
        shard,
        shard,
        P("section", ("dp", "seq")),
    )
    return jax.shard_map(
        per_device, mesh=mesh, in_specs=in_specs, out_specs=out_specs, check_vma=False
    )
```

```python
from functools import partial

import jax
import jax.numpy as jnp
from jax import lax
from jax.experimental import pallas as pl
from jax.experimental.pallas import tpu as pltpu
from jax.sharding import PartitionSpec as P

HEADS = 6
HEAD = 64
SCALE = HEAD ** (-0.5)
epsilon = 1e-06
RING = ("dp", "seq")
INNER = (2.0 / 3.141592653589793) ** 0.5
CUBE = 0.044715


def matmul(former, latter):
    return jnp.dot(former, latter, preferred_element_type=jnp.float32)


def matmul_transposed(former, latter):
    return lax.dot_general(
        former, latter, (((1,), (1,)), ((), ())), preferred_element_type=jnp.float32
    )


def outer_sum(former, latter):
    return lax.dot_general(
        former, latter, (((0,), (0,)), ((), ())), preferred_element_type=jnp.float32
    )


def low(values):
    return values.astype(jnp.bfloat16)


def normalize_rows(values):
    centre = jnp.mean(values, axis=-1, keepdims=True)
    centred = values - centre
    spread = jnp.mean(centred * centred, axis=-1, keepdims=True)
    factor = lax.rsqrt(spread + epsilon)
    return (centred * factor, factor)


def normalize_back(normed, factor, grad_normed):
    mean_grad = jnp.mean(grad_normed, axis=-1, keepdims=True)
    mean_cross = jnp.mean(grad_normed * normed, axis=-1, keepdims=True)
    return factor * (grad_normed - mean_grad - normed * mean_cross)


def column_sum(values):
    return jnp.sum(values.astype(jnp.float32), axis=0, keepdims=True)


def saved_shapes(layout, length):
    width, hidden = layout[:2]
    bf16, f32 = jnp.bfloat16, jnp.float32
    return [
        ((1, 6 * width), f32),
        ((length, 3 * width), bf16),
        ((length, width), bf16),
        ((length, hidden), bf16),
        ((HEADS, length, length), f32),
        ((length, hidden), f32),
        ((length, width), f32),
        ((length, width), f32),
        ((hidden, width), bf16),
    ]


def section_kernel(layout, forward, backward, after, *refs):
    width, hidden, rows, ratio, ring_size, share, bias_count = layout
    refs = list(refs)

    def take(count):
        taken = refs[:count]
        del refs[:count]
        return taken

    rank_ref, x_ref = take(2)
    if forward:
        modulation_ref, bias_ref = take(2)
    else:
        saved = take(9)
    if backward:
        (dy_ref,) = take(1)
    mine_ref, theirs_ref = take(2)
    take(after)
    if forward:
        (y_ref,) = take(1)
    if backward:
        dx_ref, dmod_ref, sums_ref, keep_ref, send_ref = take(5)
    elif forward:
        saved = take(9)
    att_w, out_w, up_w, sems, down_s, block_s = take(6)
    if forward:
        down_p, bias_s = take(2)
    if backward:
        da_s, dqkv_s, row_ref, halves, out_sems = take(5)
    if forward and backward:
        saved = take(9)
    mod_s, qkv_s, att_s, u_s, soft_s, slope_s, one_s, two_s, down_w = saved

    rank = rank_ref[0]
    split = hidden - 2 * width

    def fetches(first, second):
        moves = [
            (first.at[:, : 3 * width], att_w),
            (first.at[:, 3 * width : 4 * width], out_w),
            (first.at[:, 4 * width :], up_w.at[:, :split]),
            (second.at[:, : hidden - split], up_w.at[:, split:]),
        ]
        if forward:
            moves.append((second.at[:, hidden - split :], down_p))
        return [
            pltpu.make_async_copy(source, target, sems.at[i])
            for i, (source, target) in enumerate(moves)
        ]

    @pl.when(rank == 0)
    def _():
        for copy in fetches(mine_ref, theirs_ref):
            copy.start()

    @pl.when(rank != 0)
    def _():
        for copy in fetches(theirs_ref, mine_ref):
            copy.start()

    arrivals = fetches(mine_ref, theirs_ref)

    def part(ref, member, head):
        start = member * width + head * HEAD
        return ref[:, start : start + HEAD]

    x = x_ref[...].astype(jnp.float32)
    normed_one, factor_one = normalize_rows(x)
    if forward:
        for d in range(ring_size):
            bias_s[:, d * bias_count : (d + 1) * bias_count] = bias_ref[d : d + 1, :]
        mod_s[...] = modulation_ref[...] + bias_s[:, : 6 * width]
    shift_one, scale_one, gate_one, shift_two, scale_two, gate_two = [
        mod_s[:, i * width : (i + 1) * width] for i in range(6)
    ]
    hidden_one = low(normed_one * (1.0 + scale_one) + shift_one)
    if forward:

        def bias(a, b):
            return bias_s[:, a:b]

        at = 6 * width
        arrivals[0].wait()
        qkv_s[:, :width] = low(matmul(hidden_one, att_w[:, :width]) + bias(at, at + width))
        qkv_s[:, width : 2 * width] = low(matmul(hidden_one, att_w[:, width : 2 * width]))
        qkv_s[:, 2 * width :] = low(
            matmul(hidden_one, att_w[:, 2 * width :]) + bias(at + width, at + 2 * width)
        )
        for head in range(HEADS):
            scores = matmul_transposed(part(qkv_s, 0, head), part(qkv_s, 1, head)) * SCALE
            raised = jnp.exp(scores - jnp.max(scores, axis=-1, keepdims=True))
            soft = raised * (1.0 / jnp.sum(raised, axis=-1, keepdims=True))
            soft_s[head] = soft
            attended = matmul(low(soft), part(qkv_s, 2, head))
            att_s[:, head * HEAD : (head + 1) * HEAD] = low(attended)
        arrivals[1].wait()
        one_s[...] = matmul(att_s[...], out_w[...]) + bias(at + 2 * width, at + 3 * width)
    branch_one = one_s[...]
    middle = x + gate_one * branch_one
    normed_two, factor_two = normalize_rows(middle)
    hidden_two = low(normed_two * (1.0 + scale_two) + shift_two)
    if forward:
        arrivals[2].wait()
        arrivals[3].wait()
        at += 3 * width
        for j in range(ratio):
            cut = slice(j * width, (j + 1) * width)
            a = matmul(hidden_two, up_w[:, cut]) + bias(at + j * width, at + (j + 1) * width)
            square = a * a
            turn = jnp.tanh(INNER * (a + CUBE * (a * square)))
            half_one = 0.5 * (1.0 + turn)
            u_s[:, cut] = low(a * half_one)
            slope_s[:, cut] = half_one + (0.5 * INNER) * a * (1.0 - turn * turn) * (
                1.0 + (3.0 * CUBE) * square
            )
        arrivals[4].wait()
        block_s[...] = down_p[...].astype(jnp.float32)
        for d in range(ring_size):
            for j in range(ratio):
                down_s[(d * ratio + j) * rows : (d * ratio + j + 1) * rows, :] = block_s[
                    d * rows : (d + 1) * rows, j * width : (j + 1) * width
                ]
        down_w[...] = low(down_s[...])
        two_s[...] = matmul(u_s[...], down_w[...]) + bias(at + hidden, at + hidden + width)
        y_ref[...] = low(middle + gate_two * two_s[...])
    if not backward:
        return

    grad_out = dy_ref[...].astype(jnp.float32)
    grad_branch = low(gate_two * grad_out)
    sums_at = 6 * width
    row_ref[:, 5 * width : 6 * width] = column_sum(grad_out * two_s[...])
    row_ref[:, sums_at + 3 * width + hidden : sums_at + 4 * width + hidden] = column_sum(
        grad_branch
    )
    for j in range(ratio):
        cut = slice(j * width, (j + 1) * width)
        grad_expanded = low(slope_s[:, cut] * matmul_transposed(grad_branch, down_w[cut, :]))
        da_s[:, cut] = grad_expanded
        row_ref[:, sums_at + (3 + j) * width : sums_at + (4 + j) * width] = column_sum(
            grad_expanded
        )
    halves[0, :, 4 * width :] = low(outer_sum(hidden_two, da_s[:, :split]) * share)
    halves[1, :, : hidden - split] = low(outer_sum(hidden_two, da_s[:, split:]) * share)
    down_s[...] = outer_sum(u_s[...], grad_branch) * share
    for d in range(ring_size):
        for j in range(ratio):
            block_s[d * rows : (d + 1) * rows, j * width : (j + 1) * width] = down_s[
                (d * ratio + j) * rows : (d * ratio + j + 1) * rows, :
            ]
    halves[1, :, hidden - split :] = low(block_s[...])
    second_out = [
        pltpu.make_async_copy(halves.at[1], keep_ref, out_sems.at[1]),
        pltpu.make_async_copy(halves.at[1], send_ref, out_sems.at[1]),
    ]

    @pl.when(rank == 1)
    def _():
        second_out[0].start()

    @pl.when(rank != 1)
    def _():
        second_out[1].start()

    if not forward:
        arrivals[2].wait()
        arrivals[3].wait()
    grad_hidden_two = matmul_transposed(da_s[...], up_w[...])
    row_ref[:, 3 * width : 4 * width] = column_sum(grad_hidden_two)
    row_ref[:, 4 * width : 5 * width] = column_sum(grad_hidden_two * normed_two)
    grad_middle = grad_out + normalize_back(
        normed_two, factor_two, grad_hidden_two * (1.0 + scale_two)
    )
    row_ref[:, 2 * width : 3 * width] = column_sum(grad_middle * branch_one)
    grad_attention = low(gate_one * grad_middle)
    row_ref[:, sums_at + 2 * width : sums_at + 3 * width] = column_sum(grad_attention)
    halves[0, :, 3 * width : 4 * width] = low(outer_sum(att_s[...], grad_attention) * share)
    if not forward:
        arrivals[1].wait()
    grad_attended = low(matmul_transposed(grad_attention, out_w[...]))
    for head in range(HEADS):
        soft = soft_s[head]
        grad_head = grad_attended[:, head * HEAD : (head + 1) * HEAD]
        grad_soft = matmul_transposed(grad_head, part(qkv_s, 2, head))
        inner = jnp.sum(grad_soft * soft, axis=-1, keepdims=True)
        grad_scores = low(soft * (grad_soft - inner))
        grads = (
            matmul(grad_scores, part(qkv_s, 1, head)) * SCALE,
            outer_sum(grad_scores, part(qkv_s, 0, head)) * SCALE,
            outer_sum(low(soft), grad_head),
        )
        for member, grad in enumerate(grads):
            start = member * width + head * HEAD
            dqkv_s[:, start : start + HEAD] = low(grad)
    row_ref[:, sums_at : sums_at + width] = column_sum(dqkv_s[:, :width])
    row_ref[:, sums_at + width : sums_at + 2 * width] = column_sum(dqkv_s[:, 2 * width :])
    halves[0, :, : 3 * width] = low(outer_sum(hidden_one, dqkv_s[...]) * share)
    first_out = [
        pltpu.make_async_copy(halves.at[0], keep_ref, out_sems.at[0]),
        pltpu.make_async_copy(halves.at[0], send_ref, out_sems.at[0]),
    ]

    @pl.when(rank == 0)
    def _():
        first_out[0].start()

    @pl.when(rank != 0)
    def _():
        first_out[1].start()

    if not forward:
        arrivals[0].wait()
    grad_hidden_one = matmul_transposed(dqkv_s[...], att_w[...])
    row_ref[:, :width] = column_sum(grad_hidden_one)
    row_ref[:, width : 2 * width] = column_sum(grad_hidden_one * normed_one)
    dx_ref[...] = low(
        grad_middle
        + normalize_back(normed_one, factor_one, grad_hidden_one * (1.0 + scale_one))
    )
    row_ref[:, : 6 * width] = low(row_ref[:, : 6 * width]).astype(jnp.float32)
    dmod_ref[...] = row_ref[:, : 6 * width]
    for d in range(ring_size):
        sums_ref[d : d + 1, :] = row_ref[:, d * bias_count : (d + 1) * bias_count]
    second_out[0].wait()
    first_out[0].wait()


def run_section(layout, rank, x, halves, start=None, saved=None, dy=None, after=()):
    width, hidden, rows, ratio, ring_size, share, bias_count = layout
    length = x.shape[0]
    forward, backward = start is not None, dy is not None
    vmem = pl.BlockSpec(memory_space=pltpu.VMEM)
    hbm = pl.BlockSpec(memory_space=pl.ANY)
    bf16, f32 = jnp.bfloat16, jnp.float32
    half = 2 * width + hidden
    kept = saved_shapes(layout, length)
    operands = [rank, x, *(start if forward else saved)]
    shapes, out_specs = [], []
    scratch = [
        pltpu.VMEM((width, 3 * width), bf16),
        pltpu.VMEM((width, width), bf16),
        pltpu.VMEM((width, hidden), bf16),
        pltpu.SemaphoreType.DMA((5,)),
        pltpu.VMEM((hidden, width), f32),
        pltpu.VMEM((width, hidden), f32),
    ]
    if forward:
        shapes.append(jax.ShapeDtypeStruct((length, width), bf16))
        scratch += [
            pltpu.VMEM((width, hidden), bf16),
            pltpu.VMEM((1, bias_count * ring_size), f32),
        ]
    if backward:
        operands.append(dy)
        shapes += [
            jax.ShapeDtypeStruct((length, width), bf16),
            jax.ShapeDtypeStruct((1, 6 * width), f32),
            jax.ShapeDtypeStruct((ring_size, bias_count), f32),
            jax.ShapeDtypeStruct((width, half), bf16),
            jax.ShapeDtypeStruct((width, half), bf16),
        ]
        scratch += [
            pltpu.VMEM((length, hidden), bf16),
            pltpu.VMEM((length, 3 * width), bf16),
            pltpu.VMEM((1, 10 * width + hidden), f32),
            pltpu.VMEM((2, width, half), bf16),
            pltpu.SemaphoreType.DMA((2,)),
        ]
        if forward:
            scratch += [pltpu.VMEM(extent, kind) for extent, kind in kept]
    else:
        shapes += [jax.ShapeDtypeStruct(extent, kind) for extent, kind in kept]
    out_specs = [vmem] * len(shapes)
    if backward:
        out_specs[-2:] = [hbm, hbm]
    specs = [pl.BlockSpec(memory_space=pltpu.SMEM)] + [vmem] * (len(operands) - 1)
    specs += [hbm] * (2 + len(after))
    work = 2 * length * width * (4 * width + 2 * hidden + 2 * length)
    moved = 2 * width * (10 * width + 2 * hidden)
    return pl.pallas_call(
        partial(section_kernel, layout, forward, backward, len(after)),
        out_shape=shapes,
        in_specs=specs,
        out_specs=out_specs,
        scratch_shapes=scratch,
        compiler_params=pltpu.CompilerParams(
            vmem_limit_bytes=(56 if length > 256 else 26 if forward and backward else 22)
            * 1024
            * 1024
        ),
        cost_estimate=pl.CostEstimate(
            flops=(forward + 2 * backward) * work,
            bytes_accessed=(1 + backward) * moved,
            transcendentals=HEADS * length * length + length * hidden,
        ),
    )(*operands, *halves, *after)


def copy_all(copies):
    for copy in copies:
        copy.start()
    for copy in copies:
        copy.wait()


def pack_kernel(rank_ref, att_ref, out_ref, up_ref, down_ref, keep_ref, send_ref, sems):
    ratio, rows, width = down_ref.shape
    split = (ratio - 2) * width

    def copies(first, second):
        moves = [
            (att_ref, first.at[:, : 3 * width]),
            (out_ref, first.at[:, 3 * width : 4 * width]),
            (up_ref.at[:, :split], first.at[:, 4 * width :]),
            (up_ref.at[:, split:], second.at[:, : 2 * width]),
        ]
        for j in range(ratio):
            moves.append((down_ref.at[j], second.at[:, (2 + j) * width : (3 + j) * width]))
        return [
            pltpu.make_async_copy(source, target, sems.at[i])
            for i, (source, target) in enumerate(moves)
        ]

    @pl.when(rank_ref[0] == 0)
    def _():
        copy_all(copies(keep_ref, send_ref))

    @pl.when(rank_ref[0] != 0)
    def _():
        copy_all(copies(send_ref, keep_ref))


def stack_kernel(high, split, place_ref, *refs):
    pieces, sems = refs[:high], refs[-1]
    count = (len(refs) - high - 3) // 2
    handed, targets = refs[high : high + count], refs[high + count : -1]
    copies = [
        pltpu.make_async_copy(former, latter, sems.at[high + i, 0])
        for i, (former, latter) in enumerate(zip(handed, targets[2:]))
    ]
    for turn, piece in enumerate(pieces):
        place = lax.rem(place_ref[0] + (high - turn), high)
        parts = (piece.at[:, :split], piece.at[:, split:])
        for i, (part, target) in enumerate(zip(parts, targets)):
            copies.append(pltpu.make_async_copy(part, target.at[place], sems.at[turn, i]))
    copy_all(copies)


def weave_kernel(split, place_ref, *refs):
    pieces, full_ref, sems = refs[:-2], refs[-2], refs[-1]
    x, y = place_ref[1], place_ref[2]
    copies = []
    for i, piece in enumerate(pieces):
        other_x, other_y = (i % 4) & 1, (i % 4) >> 1
        row = x if not other_x else 1 - x
        column = y if not other_y else 1 - y
        target = full_ref.at[:, row, column, :, pl.ds((i // 4) * split, split)]
        copies.append(pltpu.make_async_copy(piece, target, sems.at[i]))
    copy_all(copies)


def added(former, latter):
    return former.astype(jnp.float32) + latter.astype(jnp.float32)


def chip_sum_kernel(high, place_ref, mine, got, *refs):
    count = (len(refs) - 4) // 2
    first_keep, first_send, second_keep, second_send = refs[count : count + 4]
    for former, latter in zip(refs[:count], refs[count + 4 :]):
        latter[...] = former[...]
    x, y = place_ref[1], place_ref[2]
    half = mine.shape[2]
    lanes = half // 2
    for z in range(high):
        for other in range(2):
            for target, span, chunk in (
                (first_keep, slice(0, lanes), z * 4 + x * 2 + other),
                (first_send, slice(0, lanes), z * 4 + (1 - x) * 2 + other),
                (second_keep, slice(lanes, half), z * 4 + other * 2 + y),
                (second_send, slice(lanes, half), z * 4 + other * 2 + (1 - y)),
            ):
                target[z, other] = low(added(mine[chunk, :, span], got[chunk, :, span]))


def turn_kernel(high, place_ref, *refs):
    count = (len(refs) - 8) // 2
    for former, latter in zip(refs[4 : 4 + count], refs[8 + count :]):
        latter[...] = former[...]
    for part, own in ((0, place_ref[2]), (1, place_ref[1])):
        kept, got = refs[2 * part : 2 * part + 2]
        keep, send = refs[4 + count + 2 * part : 6 + count + 2 * part]
        for z in range(high):
            keep[z] = low(added(kept[z, own], got[z, own]))
            send[z] = low(added(kept[z, 1 - own], got[z, 1 - own]))


def rise_kernel(high, place_ref, *refs):
    targets = refs[4:]
    lanes = refs[0].shape[2]
    for turn in range(high):
        chunk = lax.rem(place_ref[0] + turn, high)
        for part in range(2):
            kept, got = refs[2 * part : 2 * part + 2]
            total = added(kept[chunk], got[chunk])
            span = slice(part * lanes, (part + 1) * lanes)
            targets[turn][:, span] = total.astype(targets[turn].dtype)


def close_kernel(high, rank_ref, *refs):
    keep, send = refs[-2:]
    totals = []
    for section in range(2):
        pieces = refs[section * high : (section + 1) * high]
        total = pieces[0][...].astype(jnp.float32)
        for piece in pieces[1:]:
            total = total + piece[...].astype(jnp.float32)
        totals.append(total)
    first = rank_ref[0] == 0
    keep[...] = jnp.where(first, totals[0], totals[1])
    send[...] = jnp.where(first, totals[1], totals[0])


def spread_kernel(rank_ref, mine, got, att_ref, out_ref, up_ref, down_ref):
    rows, width = out_ref.shape
    split = up_ref.shape[1] - 2 * width
    first = rank_ref[0] == 0
    lower = jnp.where(first, mine[...], got[...])
    upper = jnp.where(first, got[...], mine[...])
    att_ref[...] = lower[:, : 3 * width]
    out_ref[...] = lower[:, 3 * width : 4 * width]
    up_ref[:, :split] = lower[:, 4 * width :]
    up_ref[:, split:] = upper[:, : 2 * width]
    for j in range(down_ref.shape[0] // rows):
        down_ref[j * rows : (j + 1) * rows, :] = upper[:, (2 + j) * width : (3 + j) * width]


def in_memory(kernel, shapes, operands, scratch=(), memory=pltpu.VMEM, after=(), limit=16):
    specs = [pl.BlockSpec(memory_space=pltpu.SMEM)]
    specs += [pl.BlockSpec(memory_space=memory)] * (len(operands) - 1)
    specs += [pl.BlockSpec(memory_space=pl.ANY)] * len(after)
    count = len(operands)

    def body(*refs):
        kernel(*refs[:count], *refs[count + len(after) :])

    moved = sum(shape.size * shape.dtype.itemsize for shape in shapes)
    return pl.pallas_call(
        body,
        out_shape=shapes,
        in_specs=specs,
        out_specs=[pl.BlockSpec(memory_space=pltpu.VMEM)] * len(shapes),
        scratch_shapes=list(scratch),
        compiler_params=pltpu.CompilerParams(vmem_limit_bytes=limit * 1024 * 1024),
        cost_estimate=pl.CostEstimate(flops=0, bytes_accessed=3 * moved, transcendentals=0),
    )(*operands, *after)


def hand_kernel(rank_ref, former, latter):
    latter[...] = former[...]


def hand_on(rank, block, after):
    shape = jax.ShapeDtypeStruct(block.shape, block.dtype)
    return in_memory(hand_kernel, [shape], [rank, block], after=after)[0]


def pair_swap(block, axis):
    return lax.ppermute(block, axis, [(0, 1), (1, 0)])


def ring_exchange(block, size, step):
    return lax.ppermute(block, RING, [(i, step(i)) for i in range(size)])


def flip(block, size, mask):
    return ring_exchange(block, size, lambda i: i ^ mask)


def rotate(block, size, turn):
    return ring_exchange(block, size, lambda i: (i + 4 * turn) % size)


def rotations(block, size):
    return [block] + [rotate(block, size, turn) for turn in range(1, size // 4)]


def gather_along_z(shards, place, handed=(), after=()):
    high = len(shards)
    rows, lanes = shards[0].shape
    return in_memory(
        partial(stack_kernel, high, lanes // 2),
        [jax.ShapeDtypeStruct((high, rows, lanes // 2), shards[0].dtype)] * 2
        + [jax.ShapeDtypeStruct(block.shape, block.dtype) for block in handed],
        [place, *shards, *handed],
        scratch=[pltpu.SemaphoreType.DMA((high + len(handed), 2))],
        after=after,
        limit=32,
    )


def first_flips(first, second, size):
    return flip(first, size, 2), flip(second, size, 1)


def gather_across(first, second, first_x, second_y, place, size, after=()):
    high, rows, lanes = first.shape
    first_y, second_x = flip(first, size, 1), flip(second, size, 2)
    first_both, second_both = flip(first_x, size, 1), flip(second_y, size, 2)
    (full,) = in_memory(
        partial(weave_kernel, lanes),
        [jax.ShapeDtypeStruct((high, 2, 2, rows, 2 * lanes), first.dtype)],
        [place, first, first_x, first_y, first_both, second, second_x, second_y, second_both],
        scratch=[pltpu.SemaphoreType.DMA((8,))],
        after=after,
        limit=32,
    )
    return full.reshape(size * rows, 2 * lanes)


def scatter_first(mine, got, place, size, handed=(), after=()):
    rows, half = mine.shape[1:]
    shape = jax.ShapeDtypeStruct((size // 4, 2, rows, half // 2), jnp.bfloat16)
    return in_memory(
        partial(chip_sum_kernel, size // 4),
        [shape] * 4 + [jax.ShapeDtypeStruct(block.shape, block.dtype) for block in handed],
        [place, mine, got, *handed],
        after=after,
    )


def scatter_flips(sorted_terms, size):
    first_keep, first_send, second_keep, second_send = sorted_terms
    return first_keep, flip(first_send, size, 2), second_keep, flip(second_send, size, 1)


def scatter_second(received, place, size, handed=(), after=()):
    high, _, rows, lanes = received[0].shape
    shape = jax.ShapeDtypeStruct((high, rows, lanes), jnp.bfloat16)
    first_keep, first_send, second_keep, second_send, *handed = in_memory(
        partial(turn_kernel, high),
        [shape] * 4 + [jax.ShapeDtypeStruct(block.shape, block.dtype) for block in handed],
        [place, *received, *handed],
        after=after,
    )
    turned = (first_keep, flip(first_send, size, 1), second_keep, flip(second_send, size, 2))
    return turned, handed


def scatter_third(turned, place, size, after=()):
    high, rows, lanes = turned[0].shape
    chunk = (rows, 2 * lanes)
    return in_memory(
        partial(rise_kernel, high),
        [jax.ShapeDtypeStruct(chunk, jnp.float32)]
        + [jax.ShapeDtypeStruct(chunk, jnp.bfloat16)] * (high - 1),
        [place, *turned],
        after=after,
    )


def scatter_along_z(pieces, size):
    own, *sent = pieces
    return [own] + [rotate(block, size, turn + 1) for turn, block in enumerate(sent)]


def scatter_sum(block, rank, size):
    half = block.shape[-1] // 2
    pieces = [block[..., :half], block[..., half:]]
    left = size
    low_bits = 0
    while left > 4:
        orders = [(0, 1), (1, 0)] if left % 4 == 0 and left >= 16 else [(0,), (0,)]
        for turn in range(len(orders[0])):
            updated = []
            for piece, order in zip(pieces, orders):
                bit = low_bits + order[turn]
                mine = (rank >> bit) & 1
                if len(order) == 2 and turn == 0:
                    shaped = piece.reshape(-1, 2, 2, *piece.shape[1:])
                    at = 2 - order[turn]
                else:
                    shaped = piece.reshape(-1, 2, *piece.shape[1:])
                    at = 1
                keep = lax.dynamic_index_in_dim(shaped, mine, at, keepdims=False)
                send = lax.dynamic_index_in_dim(shaped, 1 - mine, at, keepdims=False)
                got = ring_exchange(send, size, lambda i, bit=bit: i ^ (1 << bit))
                total = (keep.astype(jnp.float32) + got.astype(jnp.float32)).astype(jnp.bfloat16)
                updated.append(total.reshape(-1, *piece.shape[1:]))
            pieces = updated
        low_bits += len(orders[0])
        left //= 2 ** len(orders[0])
    block = jnp.concatenate(pieces, axis=-1)
    high = rank >> low_bits
    total = lax.dynamic_index_in_dim(block, high, 0, keepdims=False).astype(jnp.float32)
    stride = 1 << low_bits
    for turn in range(1, left):
        send = lax.dynamic_index_in_dim(block, (high + turn) % left, 0, keepdims=False)
        got = ring_exchange(send, size, lambda i, turn=turn: (i + turn * stride) % size)
        total = total + got.astype(jnp.float32)
    return total


def per_device(
    inputs,
    cotangent,
    time_ids,
    row_counts,
    cond_table,
    modulation_weight,
    attention_weight,
    output_weight,
    expand_weight,
    shrink_weight,
    biases,
):
    section_rank = lax.axis_index("section")
    data_rank = lax.axis_index("dp")
    seq_rank = lax.axis_index("seq")
    sections = lax.axis_size("section")
    seq_size = lax.axis_size("seq")
    ring_size = lax.axis_size("dp") * seq_size
    ring_rank = data_rank * seq_size + seq_rank
    batches, slots, tokens, width = inputs.shape
    assert batches == sections == 2 and seq_size % slots == 0
    sharers = seq_size // slots
    slot = seq_rank // sharers
    length = tokens * seq_size
    rows = attention_weight.shape[1]
    ratio = shrink_weight.shape[1] // rows
    hidden = ratio * width
    bias_count = biases.shape[1]
    half = 2 * width + hidden
    assert hidden == expand_weight.shape[2] and ratio >= 2
    table_rows = cond_table.shape[0]
    is_first = section_rank == 0
    layout = (width, hidden, rows, ratio, ring_size, 1.0 / sharers, bias_count)
    compact = ring_size in (8, 16) and seq_size == slots == 2
    rank = section_rank.astype(jnp.int32).reshape(1)
    place = jnp.stack([ring_rank >> 2, (ring_rank >> 1) & 1, ring_rank & 1]).astype(jnp.int32)

    keep, send = in_memory(
        pack_kernel,
        [jax.ShapeDtypeStruct((rows, half), jnp.bfloat16)] * 2,
        [
            rank,
            attention_weight[0],
            output_weight[0],
            expand_weight[0],
            shrink_weight[0].reshape(ratio, rows, width),
        ],
        scratch=[pltpu.SemaphoreType.DMA((4 + ratio,))],
        memory=pl.ANY,
        limit=56,
    )
    got = pair_swap(send, "section")
    first_shard = jnp.where(is_first, keep, got)
    second_shard = jnp.where(is_first, got, keep)

    live = (
        slot < lax.dynamic_index_in_dim(row_counts, section_rank, 0, keepdims=False)[0]
    ).astype(jnp.bfloat16)
    both = jnp.stack(
        [
            lax.dynamic_index_in_dim(inputs, section_rank, 0, keepdims=False),
            lax.dynamic_index_in_dim(cotangent, section_rank, 0, keepdims=False),
        ],
        axis=1,
    )

    def side_by_side(mine, got, axis):
        return jnp.where(
            seq_rank == 0,
            jnp.concatenate([mine, got], axis=axis),
            jnp.concatenate([got, mine], axis=axis),
        )

    if compact:
        mine = lax.dynamic_index_in_dim(both, seq_rank, 0, keepdims=False)
        sent = lax.dynamic_index_in_dim(both, 1 - seq_rank, 0, keepdims=False)
        both = side_by_side(mine, pair_swap(sent, "seq"), 1)
    else:
        both = lax.all_to_all(jnp.repeat(both, sharers, axis=0), "seq", 0, 0, tiled=True)
        both = jnp.swapaxes(both, 0, 1).reshape(2, length, width)
    first_input = both[0]
    last_grad = both[1] * live

    flat_ids = time_ids.reshape(-1)
    selector = (
        flat_ids[:, None] == jnp.arange(table_rows, dtype=jnp.int32)[None, :]
    ).astype(jnp.bfloat16)
    conditions = matmul(selector, cond_table)
    silu_all = jax.nn.silu(conditions).astype(jnp.bfloat16)
    silu_own = lax.dynamic_slice_in_dim(silu_all, ring_rank * rows, rows, 1)
    if compact:
        *first_parts, second_shard = gather_along_z(
            rotations(first_shard, ring_size), place, handed=(second_shard,)
        )
        first_parts += first_flips(*first_parts, ring_size)
        *second_parts, silu_late = gather_along_z(
            rotations(second_shard, ring_size),
            place,
            handed=(silu_own,),
            after=(both, *first_parts[2:]),
        )
        second_parts += first_flips(*second_parts, ring_size)
    else:
        silu_late = silu_own

    products = matmul(silu_late, modulation_weight[0])
    own_bias = jnp.broadcast_to(biases.astype(jnp.float32), (products.shape[0], bias_count))
    products = jnp.repeat(jnp.concatenate([products, own_bias], axis=1), sharers, axis=0)
    products = lax.all_to_all(
        products[:, None], ("section", "dp", "seq"), 0, 0, tiled=True
    ).reshape(sections, ring_size, 6 * width + bias_count)
    first_modulation, second_modulation = jnp.split(
        jnp.sum(products[:, :, : 6 * width], axis=1), 2, axis=0
    )
    first_bias, second_bias = products[0, :, 6 * width :], products[1, :, 6 * width :]

    if compact:
        first_pack = gather_across(*first_parts, place, ring_size)
        second_pack = gather_across(*second_parts, place, ring_size, after=(products,))
    else:
        first_pack = lax.all_gather(first_shard, RING, axis=0, tiled=True)
        second_pack = lax.all_gather(second_shard, RING, axis=0, tiled=True)
    first_halves = (first_pack, pair_swap(first_pack, "section"))
    second_halves = (second_pack, pair_swap(second_pack, "section"))

    first_low, *first_saved = run_section(
        layout, rank, first_input, first_halves, (first_modulation, first_bias)
    )
    second_low, second_grad, second_dmod, second_sums, second_keep, second_send = run_section(
        layout, rank, first_low, second_halves, (second_modulation, second_bias), dy=last_grad
    )
    second_got = pair_swap(second_send, "section")

    def ring_terms(term):
        return term.reshape(ring_size, rows, half)

    first_grad, first_dmod, first_sums, first_keep, first_send = run_section(
        layout, rank, first_input, first_halves, saved=first_saved, dy=second_grad
    )
    first_got = pair_swap(first_send, "section")

    shard = jax.ShapeDtypeStruct((rows, half), jnp.float32)
    if compact:
        second_sorted = scatter_first(
            ring_terms(second_keep), ring_terms(second_got), place, ring_size
        )
        second_received = scatter_flips(second_sorted, ring_size)
        *first_sorted, first_dmod, first_sums = scatter_first(
            ring_terms(first_keep),
            ring_terms(first_got),
            place,
            ring_size,
            handed=(first_dmod, first_sums),
            after=(second_sorted[0],),
        )
        first_received = scatter_flips(first_sorted, ring_size)
        second_turned, _ = scatter_second(second_received, place, ring_size)
        second_sent = scatter_third(second_turned, place, ring_size)
        second_pieces = scatter_along_z(second_sent, ring_size)
        first_turned, (first_grad,) = scatter_second(
            first_received, place, ring_size, handed=(first_grad,), after=(second_sent[0],)
        )
        first_sent = scatter_third(first_turned, place, ring_size, tuple(second_pieces[1:]))
        first_pieces = scatter_along_z(first_sent, ring_size)
    else:

        def chip_sum(keep, got):
            return ring_terms(low(added(keep, got)))

        first_pieces, second_pieces = [
            [scatter_sum(chip_sum(keep, got), ring_rank, ring_size)]
            for keep, got in ((first_keep, first_got), (second_keep, second_got))
        ]
    rows_back = jnp.concatenate(
        [
            jnp.concatenate(
                [jnp.broadcast_to(dmod, (ring_size, 6 * width)), sums], axis=1
            )
            for dmod, sums in ((first_dmod, first_sums), (second_dmod, second_sums))
        ]
    )
    every = lax.all_to_all(rows_back[:, None], ("section", "dp", "seq"), 0, 0, tiled=True)
    every = every[::sharers, 0]
    bias_grad = jnp.sum(every[:, 6 * width :], axis=0)
    modulation_rows = low(every[:, : 6 * width])
    modulation_grad = outer_sum(silu_own, modulation_rows)
    columns = matmul_transposed(modulation_rows, modulation_weight[0])
    if compact:
        columns = hand_on(rank, columns, (second_pieces[1],))
    columns = jnp.broadcast_to(columns.reshape(1, 1, -1), (sections * ring_size, 1, columns.size))
    columns = lax.all_to_all(columns, ("section", "dp", "seq"), 0, 0, tiled=True)

    outputs_ready = (first_low * live, second_low * live)
    if compact:
        block = jnp.stack([outputs_ready[0], first_grad, outputs_ready[1], second_grad])
        block = block.reshape(4, 2, tokens, width)
        mine = lax.dynamic_index_in_dim(block, seq_rank, 1, keepdims=True)
        sent = lax.dynamic_index_in_dim(block, 1 - seq_rank, 1, keepdims=True)
        block = side_by_side(mine, pair_swap(sent, "seq"), 1)
        per_first, per_second = block[:2], block[2:]
        mine = jnp.where(is_first, per_first, per_second)
        got = pair_swap(jnp.where(is_first, per_second, per_first), "section")
        outputs = jnp.where(is_first, jnp.stack([mine, got], 1), jnp.stack([got, mine], 1))
    else:
        pieces = jnp.stack([outputs_ready[0], first_grad, outputs_ready[1], second_grad])
        pieces = jnp.swapaxes(pieces.reshape(2, 2, seq_size, tokens, width), 1, 2)
        pieces = pieces.reshape(2 * seq_size, 2, tokens, width)
        pieces = lax.all_to_all(pieces, ("section", "seq"), 0, 0, tiled=True)
        pieces = pieces.reshape(batches, slots, sharers, 2, tokens, width)[:, :, 0]
        outputs = jnp.moveaxis(pieces, 2, 0)
    activations = outputs[0]
    input_grads = outputs[1].astype(jnp.float32)

    mine, send = in_memory(
        partial(close_kernel, len(first_pieces)),
        [shard, shard],
        [rank, *first_pieces, *second_pieces],
        after=(columns, outputs),
    )
    att, out, up, down = in_memory(
        spread_kernel,
        [
            jax.ShapeDtypeStruct(extent, jnp.float32)
            for extent in (
                (rows, 3 * width),
                (rows, width),
                (rows, hidden),
                (rows * ratio, width),
            )
        ],
        [rank, mine, pair_swap(send, "section")],
    )

    columns = jnp.sum(columns.reshape(sections, ring_size, -1, rows), axis=0)
    products_back = jnp.swapaxes(columns, 0, 1).reshape(-1, width)
    _, silu_back = jax.vjp(jax.nn.silu, conditions)
    table_grad = lax.dot_general(
        selector.astype(jnp.float32),
        silu_back(products_back)[0],
        (((0,), (0,)), ((), ())),
        precision=lax.Precision.HIGHEST,
        preferred_element_type=jnp.float32,
    )
    return (
        activations[None],
        input_grads[None],
        table_grad,
        modulation_grad[None],
        att[None],
        out[None],
        up[None],
        down[None],
        bias_grad[None],
    )


def solution(mesh):
    shard = P("section", ("dp", "seq"), None)
    in_specs = (
        P(None, "dp", "seq", None),
        P(None, "dp", "seq", None),
        P(),
        P(None, "dp"),
        P(),
        shard,
        shard,
        shard,
        shard,
        shard,
        P("section", ("dp", "seq")),
    )
    out_specs = (
        P("section", None, "dp", "seq", None),
        P("section", None, "dp", "seq", None),
        P(),
        shard,
        shard,
        shard,
        shard,
        shard,
        P("section", ("dp", "seq")),
    )
    return jax.shard_map(
        per_device, mesh=mesh, in_specs=in_specs, out_specs=out_specs, check_vma=False
    )
```

```python
from functools import partial

import jax
import jax.numpy as jnp
from jax import lax
from jax.experimental import pallas as pl
from jax.experimental.pallas import tpu as pltpu
from jax.sharding import PartitionSpec as P

HEADS = 6
HEAD = 64
SCALE = HEAD ** (-0.5)
epsilon = 1e-06
RING = ("dp", "seq")
INNER = (2.0 / 3.141592653589793) ** 0.5
CUBE = 0.044715


def matmul(former, latter):
    return jnp.dot(former, latter, preferred_element_type=jnp.float32)


def matmul_transposed(former, latter):
    return lax.dot_general(
        former, latter, (((1,), (1,)), ((), ())), preferred_element_type=jnp.float32
    )


def outer_sum(former, latter):
    return lax.dot_general(
        former, latter, (((0,), (0,)), ((), ())), preferred_element_type=jnp.float32
    )


def low(values):
    return values.astype(jnp.bfloat16)


def normalize_rows(values):
    centre = jnp.mean(values, axis=-1, keepdims=True)
    centred = values - centre
    spread = jnp.mean(centred * centred, axis=-1, keepdims=True)
    factor = lax.rsqrt(spread + epsilon)
    return (centred * factor, factor)


def normalize_back(normed, factor, grad_normed):
    mean_grad = jnp.mean(grad_normed, axis=-1, keepdims=True)
    mean_cross = jnp.mean(grad_normed * normed, axis=-1, keepdims=True)
    return factor * (grad_normed - mean_grad - normed * mean_cross)


def column_sum(values):
    return jnp.sum(values.astype(jnp.float32), axis=0, keepdims=True)


def saved_shapes(layout, length):
    width, hidden = layout[:2]
    bf16, f32 = jnp.bfloat16, jnp.float32
    return [
        ((1, 6 * width), f32),
        ((length, 3 * width), bf16),
        ((length, width), bf16),
        ((length, hidden), bf16),
        ((HEADS, length, length), f32),
        ((length, hidden), f32),
        ((length, width), f32),
        ((length, width), f32),
        ((hidden, width), bf16),
    ]


def section_kernel(layout, forward, backward, after, *refs):
    width, hidden, rows, ratio, ring_size, share, bias_count = layout
    refs = list(refs)

    def take(count):
        taken = refs[:count]
        del refs[:count]
        return taken

    rank_ref, x_ref = take(2)
    if forward:
        modulation_ref, bias_ref = take(2)
    else:
        saved = take(9)
    if backward:
        (dy_ref,) = take(1)
    mine_ref, theirs_ref = take(2)
    take(after)
    if forward:
        (y_ref,) = take(1)
    if backward:
        dx_ref, dmod_ref, sums_ref, keep_ref, send_ref = take(5)
    elif forward:
        saved = take(9)
    att_w, out_w, up_w, sems, down_s, block_s = take(6)
    if forward:
        down_p, bias_s = take(2)
    if backward:
        da_s, dqkv_s, row_ref, halves, out_sems = take(5)
    if forward and backward:
        saved = take(9)
    mod_s, qkv_s, att_s, u_s, soft_s, slope_s, one_s, two_s, down_w = saved

    rank = rank_ref[0]
    split = hidden - 2 * width

    def fetches(first, second):
        moves = [
            (first.at[:, : 3 * width], att_w),
            (first.at[:, 3 * width : 4 * width], out_w),
            (first.at[:, 4 * width :], up_w.at[:, :split]),
            (second.at[:, : hidden - split], up_w.at[:, split:]),
        ]
        if forward:
            moves.append((second.at[:, hidden - split :], down_p))
        return [
            pltpu.make_async_copy(source, target, sems.at[i])
            for i, (source, target) in enumerate(moves)
        ]

    @pl.when(rank == 0)
    def _():
        for copy in fetches(mine_ref, theirs_ref):
            copy.start()

    @pl.when(rank != 0)
    def _():
        for copy in fetches(theirs_ref, mine_ref):
            copy.start()

    arrivals = fetches(mine_ref, theirs_ref)

    def part(ref, member, head):
        start = member * width + head * HEAD
        return ref[:, start : start + HEAD]

    x = x_ref[...].astype(jnp.float32)
    normed_one, factor_one = normalize_rows(x)
    if forward:
        for d in range(ring_size):
            bias_s[:, d * bias_count : (d + 1) * bias_count] = bias_ref[d : d + 1, :]
        mod_s[...] = modulation_ref[...] + bias_s[:, : 6 * width]
    shift_one, scale_one, gate_one, shift_two, scale_two, gate_two = [
        mod_s[:, i * width : (i + 1) * width] for i in range(6)
    ]
    hidden_one = low(normed_one * (1.0 + scale_one) + shift_one)
    if forward:

        def bias(a, b):
            return bias_s[:, a:b]

        at = 6 * width
        arrivals[0].wait()
        queries = low(matmul(hidden_one, att_w[:, :width]) + bias(at, at + width))
        qkv_s[:, :width] = low(queries.astype(jnp.float32) * SCALE)
        qkv_s[:, width : 2 * width] = low(matmul(hidden_one, att_w[:, width : 2 * width]))
        qkv_s[:, 2 * width :] = low(
            matmul(hidden_one, att_w[:, 2 * width :]) + bias(at + width, at + 2 * width)
        )
        for head in range(HEADS):
            scores = matmul_transposed(part(qkv_s, 0, head), part(qkv_s, 1, head))
            raised = jnp.exp(scores - jnp.max(scores, axis=-1, keepdims=True))
            soft = raised * (1.0 / jnp.sum(raised, axis=-1, keepdims=True))
            soft_s[head] = soft
            attended = matmul(low(soft), part(qkv_s, 2, head))
            att_s[:, head * HEAD : (head + 1) * HEAD] = low(attended)
        arrivals[1].wait()
        one_s[...] = matmul(att_s[...], out_w[...]) + bias(at + 2 * width, at + 3 * width)
    branch_one = one_s[...]
    middle = x + gate_one * branch_one
    normed_two, factor_two = normalize_rows(middle)
    hidden_two = low(normed_two * (1.0 + scale_two) + shift_two)
    if forward:
        arrivals[2].wait()
        arrivals[3].wait()
        at += 3 * width
        for j in range(ratio):
            cut = slice(j * width, (j + 1) * width)
            a = matmul(hidden_two, up_w[:, cut]) + bias(at + j * width, at + (j + 1) * width)
            square = a * a
            turn = jnp.tanh(INNER * (a + CUBE * (a * square)))
            half_one = 0.5 * (1.0 + turn)
            u_s[:, cut] = low(a * half_one)
            slope_s[:, cut] = half_one + (0.5 * INNER) * a * (1.0 - turn * turn) * (
                1.0 + (3.0 * CUBE) * square
            )
        arrivals[4].wait()
        packed = down_p[...].astype(jnp.float32)
        for d in range(ring_size):
            for j in range(ratio):
                down_s[(d * ratio + j) * rows : (d * ratio + j + 1) * rows, :] = packed[
                    d * rows : (d + 1) * rows, j * width : (j + 1) * width
                ]
        down_w[...] = low(down_s[...])
        two_s[...] = matmul(u_s[...], down_w[...]) + bias(at + hidden, at + hidden + width)
        y_ref[...] = low(middle + gate_two * two_s[...])
    if not backward:
        return

    grad_out = dy_ref[...].astype(jnp.float32)
    grad_branch = low(gate_two * grad_out)
    sums_at = 6 * width
    row_ref[:, 5 * width : 6 * width] = column_sum(grad_out * two_s[...])
    row_ref[:, sums_at + 3 * width + hidden : sums_at + 4 * width + hidden] = column_sum(
        grad_branch
    )
    for j in range(ratio):
        cut = slice(j * width, (j + 1) * width)
        grad_expanded = low(slope_s[:, cut] * matmul_transposed(grad_branch, down_w[cut, :]))
        da_s[:, cut] = grad_expanded
        row_ref[:, sums_at + (3 + j) * width : sums_at + (4 + j) * width] = column_sum(
            grad_expanded
        )
    halves[0, :, 4 * width :] = low(outer_sum(hidden_two, da_s[:, :split]) * share)
    halves[1, :, : hidden - split] = low(outer_sum(hidden_two, da_s[:, split:]) * share)
    down_grad = outer_sum(u_s[...], grad_branch) * share
    for d in range(ring_size):
        for j in range(ratio):
            block_s[d * rows : (d + 1) * rows, j * width : (j + 1) * width] = down_grad[
                (d * ratio + j) * rows : (d * ratio + j + 1) * rows, :
            ]
    halves[1, :, hidden - split :] = low(block_s[...])
    second_out = [
        pltpu.make_async_copy(halves.at[1], keep_ref, out_sems.at[1]),
        pltpu.make_async_copy(halves.at[1], send_ref, out_sems.at[1]),
    ]

    @pl.when(rank == 1)
    def _():
        second_out[0].start()

    @pl.when(rank != 1)
    def _():
        second_out[1].start()

    if not forward:
        arrivals[2].wait()
        arrivals[3].wait()
    grad_hidden_two = matmul_transposed(da_s[...], up_w[...])
    row_ref[:, 3 * width : 4 * width] = column_sum(grad_hidden_two)
    row_ref[:, 4 * width : 5 * width] = column_sum(grad_hidden_two * normed_two)
    grad_middle = grad_out + normalize_back(
        normed_two, factor_two, grad_hidden_two * (1.0 + scale_two)
    )
    row_ref[:, 2 * width : 3 * width] = column_sum(grad_middle * branch_one)
    grad_attention = low(gate_one * grad_middle)
    row_ref[:, sums_at + 2 * width : sums_at + 3 * width] = column_sum(grad_attention)
    halves[0, :, 3 * width : 4 * width] = low(outer_sum(att_s[...], grad_attention) * share)
    if not forward:
        arrivals[1].wait()
    grad_attended = low(matmul_transposed(grad_attention, out_w[...]))
    for head in range(HEADS):
        soft = soft_s[head]
        grad_head = grad_attended[:, head * HEAD : (head + 1) * HEAD]
        grad_soft = matmul_transposed(grad_head, part(qkv_s, 2, head))
        inner = jnp.sum(grad_soft * soft, axis=-1, keepdims=True)
        grad_scores = low(soft * (grad_soft - inner))
        grads = (
            matmul(grad_scores, part(qkv_s, 1, head)) * SCALE,
            outer_sum(grad_scores, part(qkv_s, 0, head)),
            outer_sum(low(soft), grad_head),
        )
        for member, grad in enumerate(grads):
            start = member * width + head * HEAD
            dqkv_s[:, start : start + HEAD] = low(grad)
    row_ref[:, sums_at : sums_at + width] = column_sum(dqkv_s[:, :width])
    row_ref[:, sums_at + width : sums_at + 2 * width] = column_sum(dqkv_s[:, 2 * width :])
    halves[0, :, : 3 * width] = low(outer_sum(hidden_one, dqkv_s[...]) * share)
    first_out = [
        pltpu.make_async_copy(halves.at[0], keep_ref, out_sems.at[0]),
        pltpu.make_async_copy(halves.at[0], send_ref, out_sems.at[0]),
    ]

    @pl.when(rank == 0)
    def _():
        first_out[0].start()

    @pl.when(rank != 0)
    def _():
        first_out[1].start()

    if not forward:
        arrivals[0].wait()
    grad_hidden_one = matmul_transposed(dqkv_s[...], att_w[...])
    row_ref[:, :width] = column_sum(grad_hidden_one)
    row_ref[:, width : 2 * width] = column_sum(grad_hidden_one * normed_one)
    dx_ref[...] = low(
        grad_middle
        + normalize_back(normed_one, factor_one, grad_hidden_one * (1.0 + scale_one))
    )
    row_ref[:, : 6 * width] = low(row_ref[:, : 6 * width]).astype(jnp.float32)
    dmod_ref[...] = row_ref[:, : 6 * width]
    for d in range(ring_size):
        sums_ref[d : d + 1, :] = row_ref[:, d * bias_count : (d + 1) * bias_count]
    second_out[0].wait()
    first_out[0].wait()


def run_section(layout, rank, x, halves, start=None, saved=None, dy=None, after=()):
    width, hidden, rows, ratio, ring_size, share, bias_count = layout
    length = x.shape[0]
    forward, backward = start is not None, dy is not None
    vmem = pl.BlockSpec(memory_space=pltpu.VMEM)
    hbm = pl.BlockSpec(memory_space=pl.ANY)
    bf16, f32 = jnp.bfloat16, jnp.float32
    half = 2 * width + hidden
    kept = saved_shapes(layout, length)
    operands = [rank, x, *(start if forward else saved)]
    shapes, out_specs = [], []
    scratch = [
        pltpu.VMEM((width, 3 * width), bf16),
        pltpu.VMEM((width, width), bf16),
        pltpu.VMEM((width, hidden), bf16),
        pltpu.SemaphoreType.DMA((5,)),
        pltpu.VMEM((hidden, width), f32),
        pltpu.VMEM((width, hidden), f32),
    ]
    if forward:
        shapes.append(jax.ShapeDtypeStruct((length, width), bf16))
        scratch += [
            pltpu.VMEM((width, hidden), bf16),
            pltpu.VMEM((1, bias_count * ring_size), f32),
        ]
    if backward:
        operands.append(dy)
        shapes += [
            jax.ShapeDtypeStruct((length, width), bf16),
            jax.ShapeDtypeStruct((1, 6 * width), f32),
            jax.ShapeDtypeStruct((ring_size, bias_count), f32),
            jax.ShapeDtypeStruct((width, half), bf16),
            jax.ShapeDtypeStruct((width, half), bf16),
        ]
        scratch += [
            pltpu.VMEM((length, hidden), bf16),
            pltpu.VMEM((length, 3 * width), bf16),
            pltpu.VMEM((1, 10 * width + hidden), f32),
            pltpu.VMEM((2, width, half), bf16),
            pltpu.SemaphoreType.DMA((2,)),
        ]
        if forward:
            scratch += [pltpu.VMEM(extent, kind) for extent, kind in kept]
    else:
        shapes += [jax.ShapeDtypeStruct(extent, kind) for extent, kind in kept]
    out_specs = [vmem] * len(shapes)
    if backward:
        out_specs[-2:] = [hbm, hbm]
    specs = [pl.BlockSpec(memory_space=pltpu.SMEM)] + [vmem] * (len(operands) - 1)
    specs += [hbm] * (2 + len(after))
    work = 2 * length * width * (4 * width + 2 * hidden + 2 * length)
    moved = 2 * width * (10 * width + 2 * hidden)
    return pl.pallas_call(
        partial(section_kernel, layout, forward, backward, len(after)),
        out_shape=shapes,
        in_specs=specs,
        out_specs=out_specs,
        scratch_shapes=scratch,
        compiler_params=pltpu.CompilerParams(
            vmem_limit_bytes=(56 if length > 256 else 26 if forward and backward else 22)
            * 1024
            * 1024
        ),
        cost_estimate=pl.CostEstimate(
            flops=(forward + 2 * backward) * work,
            bytes_accessed=(1 + backward) * moved,
            transcendentals=HEADS * length * length + length * hidden,
        ),
    )(*operands, *halves, *after)


def copy_all(copies):
    for copy in copies:
        copy.start()
    for copy in copies:
        copy.wait()


def pack_kernel(rank_ref, att_ref, out_ref, up_ref, down_ref, keep_ref, send_ref, sems):
    ratio, rows, width = down_ref.shape
    split = (ratio - 2) * width

    def copies(first, second):
        moves = [
            (att_ref, first.at[:, : 3 * width]),
            (out_ref, first.at[:, 3 * width : 4 * width]),
            (up_ref.at[:, :split], first.at[:, 4 * width :]),
            (up_ref.at[:, split:], second.at[:, : 2 * width]),
        ]
        for j in range(ratio):
            moves.append((down_ref.at[j], second.at[:, (2 + j) * width : (3 + j) * width]))
        return [
            pltpu.make_async_copy(source, target, sems.at[i])
            for i, (source, target) in enumerate(moves)
        ]

    @pl.when(rank_ref[0] == 0)
    def _():
        copy_all(copies(keep_ref, send_ref))

    @pl.when(rank_ref[0] != 0)
    def _():
        copy_all(copies(send_ref, keep_ref))


def stack_kernel(high, split, place_ref, *refs):
    pieces, sems = refs[:high], refs[-1]
    count = (len(refs) - high - 3) // 2
    handed, targets = refs[high : high + count], refs[high + count : -1]
    copies = [
        pltpu.make_async_copy(former, latter, sems.at[high + i, 0])
        for i, (former, latter) in enumerate(zip(handed, targets[2:]))
    ]
    for turn, piece in enumerate(pieces):
        place = lax.rem(place_ref[0] + (high - turn), high)
        parts = (piece.at[:, :split], piece.at[:, split:])
        for i, (part, target) in enumerate(zip(parts, targets)):
            copies.append(pltpu.make_async_copy(part, target.at[place], sems.at[turn, i]))
    copy_all(copies)


def weave_kernel(split, place_ref, *refs):
    pieces, full_ref, sems = refs[:-2], refs[-2], refs[-1]
    x, y = place_ref[1], place_ref[2]
    copies = []
    for i, piece in enumerate(pieces):
        other_x, other_y = (i % 4) & 1, (i % 4) >> 1
        row = x if not other_x else 1 - x
        column = y if not other_y else 1 - y
        target = full_ref.at[:, row, column, :, pl.ds((i // 4) * split, split)]
        copies.append(pltpu.make_async_copy(piece, target, sems.at[i]))
    copy_all(copies)


def added(former, latter):
    return former.astype(jnp.float32) + latter.astype(jnp.float32)


def chip_sum_kernel(high, place_ref, mine, got, *refs):
    count = (len(refs) - 4) // 2
    first_keep, first_send, second_keep, second_send = refs[count : count + 4]
    for former, latter in zip(refs[:count], refs[count + 4 :]):
        latter[...] = former[...]
    x, y = place_ref[1], place_ref[2]
    half = mine.shape[2]
    lanes = half // 2
    for z in range(high):
        for other in range(2):
            for target, span, chunk in (
                (first_keep, slice(0, lanes), z * 4 + x * 2 + other),
                (first_send, slice(0, lanes), z * 4 + (1 - x) * 2 + other),
                (second_keep, slice(lanes, half), z * 4 + other * 2 + y),
                (second_send, slice(lanes, half), z * 4 + other * 2 + (1 - y)),
            ):
                target[z, other] = low(added(mine[chunk, :, span], got[chunk, :, span]))


def turn_kernel(high, place_ref, *refs):
    count = (len(refs) - 8) // 2
    for former, latter in zip(refs[4 : 4 + count], refs[8 + count :]):
        latter[...] = former[...]
    for part, own in ((0, place_ref[2]), (1, place_ref[1])):
        kept, got = refs[2 * part : 2 * part + 2]
        keep, send = refs[4 + count + 2 * part : 6 + count + 2 * part]
        for z in range(high):
            keep[z] = low(added(kept[z, own], got[z, own]))
            send[z] = low(added(kept[z, 1 - own], got[z, 1 - own]))


def rise_kernel(high, place_ref, *refs):
    targets = refs[4:]
    lanes = refs[0].shape[2]
    for turn in range(high):
        chunk = lax.rem(place_ref[0] + turn, high)
        for part in range(2):
            kept, got = refs[2 * part : 2 * part + 2]
            total = added(kept[chunk], got[chunk])
            span = slice(part * lanes, (part + 1) * lanes)
            targets[turn][:, span] = total.astype(targets[turn].dtype)


def close_kernel(high, rank_ref, *refs):
    keep, send = refs[-2:]
    totals = []
    for section in range(2):
        pieces = refs[section * high : (section + 1) * high]
        total = pieces[0][...].astype(jnp.float32)
        for piece in pieces[1:]:
            total = total + piece[...].astype(jnp.float32)
        totals.append(total)
    first = rank_ref[0] == 0
    keep[...] = jnp.where(first, totals[0], totals[1])
    send[...] = jnp.where(first, totals[1], totals[0])


def spread_kernel(rank_ref, mine, got, att_ref, out_ref, up_ref, down_ref):
    rows, width = out_ref.shape
    split = up_ref.shape[1] - 2 * width
    first = rank_ref[0] == 0
    lower = jnp.where(first, mine[...], got[...])
    upper = jnp.where(first, got[...], mine[...])
    att_ref[...] = lower[:, : 3 * width]
    out_ref[...] = lower[:, 3 * width : 4 * width]
    up_ref[:, :split] = lower[:, 4 * width :]
    up_ref[:, split:] = upper[:, : 2 * width]
    for j in range(down_ref.shape[0] // rows):
        down_ref[j * rows : (j + 1) * rows, :] = upper[:, (2 + j) * width : (3 + j) * width]


def in_memory(kernel, shapes, operands, scratch=(), memory=pltpu.VMEM, after=(), limit=16):
    specs = [pl.BlockSpec(memory_space=pltpu.SMEM)]
    specs += [pl.BlockSpec(memory_space=memory)] * (len(operands) - 1)
    specs += [pl.BlockSpec(memory_space=pl.ANY)] * len(after)
    count = len(operands)

    def body(*refs):
        kernel(*refs[:count], *refs[count + len(after) :])

    moved = sum(shape.size * shape.dtype.itemsize for shape in shapes)
    return pl.pallas_call(
        body,
        out_shape=shapes,
        in_specs=specs,
        out_specs=[pl.BlockSpec(memory_space=pltpu.VMEM)] * len(shapes),
        scratch_shapes=list(scratch),
        compiler_params=pltpu.CompilerParams(vmem_limit_bytes=limit * 1024 * 1024),
        cost_estimate=pl.CostEstimate(flops=0, bytes_accessed=3 * moved, transcendentals=0),
    )(*operands, *after)


def hand_kernel(rank_ref, former, latter):
    latter[...] = former[...]


def hand_on(rank, block, after):
    shape = jax.ShapeDtypeStruct(block.shape, block.dtype)
    return in_memory(hand_kernel, [shape], [rank, block], after=after)[0]


def pair_swap(block, axis):
    return lax.ppermute(block, axis, [(0, 1), (1, 0)])


def ring_exchange(block, size, step):
    return lax.ppermute(block, RING, [(i, step(i)) for i in range(size)])


def flip(block, size, mask):
    return ring_exchange(block, size, lambda i: i ^ mask)


def rotate(block, size, turn):
    return ring_exchange(block, size, lambda i: (i + 4 * turn) % size)


def rotations(block, size):
    return [block] + [rotate(block, size, turn) for turn in range(1, size // 4)]


def gather_along_z(shards, place, handed=(), after=()):
    high = len(shards)
    rows, lanes = shards[0].shape
    return in_memory(
        partial(stack_kernel, high, lanes // 2),
        [jax.ShapeDtypeStruct((high, rows, lanes // 2), shards[0].dtype)] * 2
        + [jax.ShapeDtypeStruct(block.shape, block.dtype) for block in handed],
        [place, *shards, *handed],
        scratch=[pltpu.SemaphoreType.DMA((high + len(handed), 2))],
        after=after,
        limit=32,
    )


def first_flips(first, second, size):
    return flip(first, size, 2), flip(second, size, 1)


def gather_across(first, second, first_x, second_y, place, size):
    high, rows, lanes = first.shape
    first_y, second_x = flip(first, size, 1), flip(second, size, 2)
    first_both, second_both = flip(first_x, size, 1), flip(second_y, size, 2)
    (full,) = in_memory(
        partial(weave_kernel, lanes),
        [jax.ShapeDtypeStruct((high, 2, 2, rows, 2 * lanes), first.dtype)],
        [place, first, first_x, first_y, first_both, second, second_x, second_y, second_both],
        scratch=[pltpu.SemaphoreType.DMA((8,))],
        limit=32,
    )
    return full.reshape(size * rows, 2 * lanes)


def scatter_first(mine, got, place, size, handed=(), after=()):
    rows, half = mine.shape[1:]
    shape = jax.ShapeDtypeStruct((size // 4, 2, rows, half // 2), jnp.bfloat16)
    return in_memory(
        partial(chip_sum_kernel, size // 4),
        [shape] * 4 + [jax.ShapeDtypeStruct(block.shape, block.dtype) for block in handed],
        [place, mine, got, *handed],
        after=after,
    )


def scatter_flips(sorted_terms, size):
    first_keep, first_send, second_keep, second_send = sorted_terms
    return first_keep, flip(first_send, size, 2), second_keep, flip(second_send, size, 1)


def scatter_second(received, place, size, handed=(), after=()):
    high, _, rows, lanes = received[0].shape
    shape = jax.ShapeDtypeStruct((high, rows, lanes), jnp.bfloat16)
    first_keep, first_send, second_keep, second_send, *handed = in_memory(
        partial(turn_kernel, high),
        [shape] * 4 + [jax.ShapeDtypeStruct(block.shape, block.dtype) for block in handed],
        [place, *received, *handed],
        after=after,
    )
    turned = (first_keep, flip(first_send, size, 1), second_keep, flip(second_send, size, 2))
    return turned, handed


def scatter_third(turned, place, size, after=()):
    high, rows, lanes = turned[0].shape
    chunk = (rows, 2 * lanes)
    return in_memory(
        partial(rise_kernel, high),
        [jax.ShapeDtypeStruct(chunk, jnp.float32)]
        + [jax.ShapeDtypeStruct(chunk, jnp.bfloat16)] * (high - 1),
        [place, *turned],
        after=after,
    )


def scatter_along_z(pieces, size):
    own, *sent = pieces
    return [own] + [rotate(block, size, turn + 1) for turn, block in enumerate(sent)]


def scatter_sum(block, rank, size):
    half = block.shape[-1] // 2
    pieces = [block[..., :half], block[..., half:]]
    left = size
    low_bits = 0
    while left > 4:
        orders = [(0, 1), (1, 0)] if left % 4 == 0 and left >= 16 else [(0,), (0,)]
        for turn in range(len(orders[0])):
            updated = []
            for piece, order in zip(pieces, orders):
                bit = low_bits + order[turn]
                mine = (rank >> bit) & 1
                if len(order) == 2 and turn == 0:
                    shaped = piece.reshape(-1, 2, 2, *piece.shape[1:])
                    at = 2 - order[turn]
                else:
                    shaped = piece.reshape(-1, 2, *piece.shape[1:])
                    at = 1
                keep = lax.dynamic_index_in_dim(shaped, mine, at, keepdims=False)
                send = lax.dynamic_index_in_dim(shaped, 1 - mine, at, keepdims=False)
                got = ring_exchange(send, size, lambda i, bit=bit: i ^ (1 << bit))
                total = (keep.astype(jnp.float32) + got.astype(jnp.float32)).astype(jnp.bfloat16)
                updated.append(total.reshape(-1, *piece.shape[1:]))
            pieces = updated
        low_bits += len(orders[0])
        left //= 2 ** len(orders[0])
    block = jnp.concatenate(pieces, axis=-1)
    high = rank >> low_bits
    total = lax.dynamic_index_in_dim(block, high, 0, keepdims=False).astype(jnp.float32)
    stride = 1 << low_bits
    for turn in range(1, left):
        send = lax.dynamic_index_in_dim(block, (high + turn) % left, 0, keepdims=False)
        got = ring_exchange(send, size, lambda i, turn=turn: (i + turn * stride) % size)
        total = total + got.astype(jnp.float32)
    return total


def per_device(
    inputs,
    cotangent,
    time_ids,
    row_counts,
    cond_table,
    modulation_weight,
    attention_weight,
    output_weight,
    expand_weight,
    shrink_weight,
    biases,
):
    section_rank = lax.axis_index("section")
    data_rank = lax.axis_index("dp")
    seq_rank = lax.axis_index("seq")
    sections = lax.axis_size("section")
    seq_size = lax.axis_size("seq")
    ring_size = lax.axis_size("dp") * seq_size
    ring_rank = data_rank * seq_size + seq_rank
    batches, slots, tokens, width = inputs.shape
    assert batches == sections == 2 and seq_size % slots == 0
    sharers = seq_size // slots
    slot = seq_rank // sharers
    length = tokens * seq_size
    rows = attention_weight.shape[1]
    ratio = shrink_weight.shape[1] // rows
    hidden = ratio * width
    bias_count = biases.shape[1]
    half = 2 * width + hidden
    assert hidden == expand_weight.shape[2] and ratio >= 2
    table_rows = cond_table.shape[0]
    is_first = section_rank == 0
    layout = (width, hidden, rows, ratio, ring_size, 1.0 / sharers, bias_count)
    compact = ring_size in (8, 16) and seq_size == slots == 2
    rank = section_rank.astype(jnp.int32).reshape(1)
    place = jnp.stack([ring_rank >> 2, (ring_rank >> 1) & 1, ring_rank & 1]).astype(jnp.int32)

    keep, send = in_memory(
        pack_kernel,
        [jax.ShapeDtypeStruct((rows, half), jnp.bfloat16)] * 2,
        [
            rank,
            attention_weight[0],
            output_weight[0],
            expand_weight[0],
            shrink_weight[0].reshape(ratio, rows, width),
        ],
        scratch=[pltpu.SemaphoreType.DMA((4 + ratio,))],
        memory=pl.ANY,
        limit=56,
    )
    got = pair_swap(send, "section")
    first_shard = jnp.where(is_first, keep, got)
    second_shard = jnp.where(is_first, got, keep)

    live = (
        slot < lax.dynamic_index_in_dim(row_counts, section_rank, 0, keepdims=False)[0]
    ).astype(jnp.bfloat16)
    both = jnp.stack(
        [
            lax.dynamic_index_in_dim(inputs, section_rank, 0, keepdims=False),
            lax.dynamic_index_in_dim(cotangent, section_rank, 0, keepdims=False),
        ],
        axis=1,
    )

    def side_by_side(mine, got, axis):
        return jnp.where(
            seq_rank == 0,
            jnp.concatenate([mine, got], axis=axis),
            jnp.concatenate([got, mine], axis=axis),
        )

    if compact:
        mine = lax.dynamic_index_in_dim(both, seq_rank, 0, keepdims=False)
        sent = lax.dynamic_index_in_dim(both, 1 - seq_rank, 0, keepdims=False)
        both = side_by_side(mine, pair_swap(sent, "seq"), 1)
    else:
        both = lax.all_to_all(jnp.repeat(both, sharers, axis=0), "seq", 0, 0, tiled=True)
        both = jnp.swapaxes(both, 0, 1).reshape(2, length, width)
    first_input = both[0]
    last_grad = both[1] * live

    flat_ids = time_ids.reshape(-1)
    selector = (
        flat_ids[:, None] == jnp.arange(table_rows, dtype=jnp.int32)[None, :]
    ).astype(jnp.bfloat16)
    conditions = matmul(selector, cond_table)
    silu_all = jax.nn.silu(conditions).astype(jnp.bfloat16)
    silu_own = lax.dynamic_slice_in_dim(silu_all, ring_rank * rows, rows, 1)
    if compact:
        first_shards = rotations(first_shard, ring_size)
        *first_parts, second_shard, silu_late = gather_along_z(
            first_shards, place, handed=(second_shard, silu_own)
        )
        first_parts += first_flips(*first_parts, ring_size)
    else:
        silu_late = silu_own

    products = matmul(silu_late, modulation_weight[0])
    own_bias = jnp.broadcast_to(biases.astype(jnp.float32), (products.shape[0], bias_count))
    products = jnp.repeat(jnp.concatenate([products, own_bias], axis=1), sharers, axis=0)
    products = lax.all_to_all(
        products[:, None], ("section", "dp", "seq"), 0, 0, tiled=True
    ).reshape(sections, ring_size, 6 * width + bias_count)
    first_modulation, second_modulation = jnp.split(
        jnp.sum(products[:, :, : 6 * width], axis=1), 2, axis=0
    )
    first_bias, second_bias = products[0, :, 6 * width :], products[1, :, 6 * width :]

    if compact:
        second_parts = gather_along_z(
            rotations(second_shard, ring_size), place, after=(both, *first_parts[2:])
        )
        second_parts += first_flips(*second_parts, ring_size)
        first_pack = gather_across(*first_parts, place, ring_size)
        second_pack = gather_across(*second_parts, place, ring_size)
    else:
        first_pack = lax.all_gather(first_shard, RING, axis=0, tiled=True)
        second_pack = lax.all_gather(second_shard, RING, axis=0, tiled=True)
    first_halves = (first_pack, pair_swap(first_pack, "section"))
    second_halves = (second_pack, pair_swap(second_pack, "section"))

    first_low, *first_saved = run_section(
        layout, rank, first_input, first_halves, (first_modulation, first_bias)
    )
    second_low, second_grad, second_dmod, second_sums, second_keep, second_send = run_section(
        layout, rank, first_low, second_halves, (second_modulation, second_bias), dy=last_grad
    )
    second_got = pair_swap(second_send, "section")

    def ring_terms(term):
        return term.reshape(ring_size, rows, half)

    first_grad, first_dmod, first_sums, first_keep, first_send = run_section(
        layout, rank, first_input, first_halves, saved=first_saved, dy=second_grad
    )
    first_got = pair_swap(first_send, "section")

    shard = jax.ShapeDtypeStruct((rows, half), jnp.float32)
    if compact:
        second_sorted = scatter_first(
            ring_terms(second_keep), ring_terms(second_got), place, ring_size
        )
        second_received = scatter_flips(second_sorted, ring_size)
        *first_sorted, first_dmod, first_sums = scatter_first(
            ring_terms(first_keep),
            ring_terms(first_got),
            place,
            ring_size,
            handed=(first_dmod, first_sums),
            after=(second_sorted[0],),
        )
        first_received = scatter_flips(first_sorted, ring_size)
        second_turned, _ = scatter_second(second_received, place, ring_size)
        second_sent = scatter_third(second_turned, place, ring_size)
        second_pieces = scatter_along_z(second_sent, ring_size)
        first_turned, (first_grad,) = scatter_second(
            first_received, place, ring_size, handed=(first_grad,), after=(second_sent[0],)
        )
        first_sent = scatter_third(first_turned, place, ring_size, tuple(second_pieces[1:]))
        first_pieces = scatter_along_z(first_sent, ring_size)
    else:

        def chip_sum(keep, got):
            return ring_terms(low(added(keep, got)))

        first_pieces, second_pieces = [
            [scatter_sum(chip_sum(keep, got), ring_rank, ring_size)]
            for keep, got in ((first_keep, first_got), (second_keep, second_got))
        ]
    rows_back = jnp.concatenate(
        [
            jnp.concatenate(
                [jnp.broadcast_to(dmod, (ring_size, 6 * width)), sums], axis=1
            )
            for dmod, sums in ((first_dmod, first_sums), (second_dmod, second_sums))
        ]
    )
    every = lax.all_to_all(rows_back[:, None], ("section", "dp", "seq"), 0, 0, tiled=True)
    every = every[::sharers, 0]
    bias_grad = jnp.sum(every[:, 6 * width :], axis=0)
    modulation_rows = low(every[:, : 6 * width])
    modulation_grad = outer_sum(silu_own, modulation_rows)
    columns = matmul_transposed(modulation_rows, modulation_weight[0])
    if compact:
        columns = hand_on(rank, columns, (second_pieces[1],))
    columns = jnp.broadcast_to(columns.reshape(1, 1, -1), (sections * ring_size, 1, columns.size))
    columns = lax.all_to_all(columns, ("section", "dp", "seq"), 0, 0, tiled=True)

    outputs_ready = (first_low * live, second_low * live)
    if compact:
        block = jnp.stack([outputs_ready[0], first_grad, outputs_ready[1], second_grad])
        block = block.reshape(4, 2, tokens, width)
        mine = lax.dynamic_index_in_dim(block, seq_rank, 1, keepdims=True)
        sent = lax.dynamic_index_in_dim(block, 1 - seq_rank, 1, keepdims=True)
        block = side_by_side(mine, pair_swap(sent, "seq"), 1)
        per_first, per_second = block[:2], block[2:]
        mine = jnp.where(is_first, per_first, per_second)
        got = pair_swap(jnp.where(is_first, per_second, per_first), "section")
        outputs = jnp.where(is_first, jnp.stack([mine, got], 1), jnp.stack([got, mine], 1))
    else:
        pieces = jnp.stack([outputs_ready[0], first_grad, outputs_ready[1], second_grad])
        pieces = jnp.swapaxes(pieces.reshape(2, 2, seq_size, tokens, width), 1, 2)
        pieces = pieces.reshape(2 * seq_size, 2, tokens, width)
        pieces = lax.all_to_all(pieces, ("section", "seq"), 0, 0, tiled=True)
        pieces = pieces.reshape(batches, slots, sharers, 2, tokens, width)[:, :, 0]
        outputs = jnp.moveaxis(pieces, 2, 0)
    activations = outputs[0]
    input_grads = outputs[1].astype(jnp.float32)

    mine, send = in_memory(
        partial(close_kernel, len(first_pieces)),
        [shard, shard],
        [rank, *first_pieces, *second_pieces],
        after=(columns,),
    )
    att, out, up, down = in_memory(
        spread_kernel,
        [
            jax.ShapeDtypeStruct(extent, jnp.float32)
            for extent in (
                (rows, 3 * width),
                (rows, width),
                (rows, hidden),
                (rows * ratio, width),
            )
        ],
        [rank, mine, pair_swap(send, "section")],
    )

    columns = jnp.sum(columns.reshape(sections, ring_size, -1, rows), axis=0)
    products_back = jnp.swapaxes(columns, 0, 1).reshape(-1, width)
    _, silu_back = jax.vjp(jax.nn.silu, conditions)
    table_grad = lax.dot_general(
        selector.astype(jnp.float32),
        silu_back(products_back)[0],
        (((0,), (0,)), ((), ())),
        precision=lax.Precision.HIGHEST,
        preferred_element_type=jnp.float32,
    )
    return (
        activations[None],
        input_grads[None],
        table_grad,
        modulation_grad[None],
        att[None],
        out[None],
        up[None],
        down[None],
        bias_grad[None],
    )


def solution(mesh):
    shard = P("section", ("dp", "seq"), None)
    in_specs = (
        P(None, "dp", "seq", None),
        P(None, "dp", "seq", None),
        P(),
        P(None, "dp"),
        P(),
        shard,
        shard,
        shard,
        shard,
        shard,
        P("section", ("dp", "seq")),
    )
    out_specs = (
        P("section", None, "dp", "seq", None),
        P("section", None, "dp", "seq", None),
        P(),
        shard,
        shard,
        shard,
        shard,
        shard,
        P("section", ("dp", "seq")),
    )
    return jax.shard_map(
        per_device, mesh=mesh, in_specs=in_specs, out_specs=out_specs, check_vma=False
    )
```
